32 devices in a mesh: expert: 8 (over z, x), shard: 4 (over y, core).
Axes of the slice: x: 2, y: 2, z: 4, core: 2. Of those that a mesh axis runs over, the one named last changes fastest.
Arguments:
- hidden_in: bfloat16 [8, 1024, 768], P('expert', 'shard'), may hold values from -6 to 6
- gain_attn: bfloat16 [768], P('shard'), may hold values from 0.25 to 1.75
- gain_ffn: bfloat16 [768], P('shard'), may hold values from 0.25 to 1.75
- w_query: bfloat16 [768, 768], P('shard'), may hold values from -0.21875 to 0.21875
- w_key: bfloat16 [768, 768], P('shard'), may hold values from -0.21875 to 0.21875
- w_value: bfloat16 [768, 768], P('shard'), may hold values from -0.21875 to 0.21875
- w_out: bfloat16 [768, 768], P('shard'), may hold values from -1.25 to 1.25
- shared_gate: bfloat16 [768, 2048], P('shard'), may hold values from -0.21875 to 0.21875
- shared_up: bfloat16 [768, 2048], P('shard'), may hold values from -0.21875 to 0.21875
- shared_down: bfloat16 [2048, 768], P('shard'), may hold values from -0.125 to 0.125
- expert_gate: bfloat16 [8, 768, 2048], P('expert', 'shard'), may hold values from -0.21875 to 0.21875
- expert_up: bfloat16 [8, 768, 2048], P('expert', 'shard'), may hold values from -0.21875 to 0.21875
- expert_down: bfloat16 [8, 2048, 768], P('expert', 'shard'), may hold values from -0.125 to 0.125
- gate_logits: float32 [8, 1024, 2], P('expert', 'shard'), may hold values from -3.5 to 3.5
- routes: int32 [8, 1024, 2], P('expert', 'shard'), may hold values from 0 to 7, all different within a row; in each aligned block of 256 rows (0 to 255, 256 to 511, ..., all dimensions but the last counted through in order) at most 128 rows name the same one
- segment: int32 [8, 1024], P('expert'), may hold values from 0 to 2, as said below
- padding: int32 [8, 1024], P('expert'), may hold values 0 or 1
- cotangent: bfloat16 [8, 1024, 768], P('expert', 'shard'), may hold values from -6 to 6
Outputs:
- output: bfloat16 [8, 1024, 768], P('expert', 'shard')
- input_grad: float32 [8, 1024, 768], P('expert', 'shard')
- logit_grad: float32 [8, 1024, 2], P('expert', 'shard')
- gain_attn_grad: float32 [768], P('shard')
- gain_ffn_grad: float32 [768], P('shard')
- w_query_grad: float32 [768, 768], P('shard')
- w_key_grad: float32 [768, 768], P('shard')
- w_value_grad: float32 [768, 768], P('shard')
- w_out_grad: float32 [768, 768], P('shard')
- shared_gate_grad: float32 [768, 2048], P('shard')
- shared_up_grad: float32 [768, 2048], P('shard')
- shared_down_grad: float32 [2048, 768], P('shard')
- expert_gate_grad: float32 [8, 768, 2048], P('expert', 'shard')
- expert_up_grad: float32 [8, 768, 2048], P('expert', 'shard')
- expert_down_grad: float32 [8, 2048, 768], P('expert', 'shard')
The draws below stay inside these ranges and needn't reach their ends.
Inputs may be any that keep to these rules, and one draw needn't show every extreme that they name: `routes`: in every aligned block of 256 tokens of a row (the tokens of one device) no expert is named more than 128 times, and in some blocks one is named exactly 128 times; a token's 2 experts differ. `segment`: within each row the numbers never fall and rise exactly twice: once at a position from 1 to 255 and once at a position from 769 to 1023.
All inputs are finite; a program needn't handle non-finite values. No bound on the sum of `padding` on one device may be relied on, other than what follows from the above.
Results may differ from the reference program's by a relative error of at most 0.02.
Values may be sent and summed in bfloat16 or wider, within the bound.
A program may use at most 256 MiB of HBM per device.

```python
import math
import jax
import jax.numpy as jnp
import numpy as np
from jax import lax

D = 768
HEADS = 12
HEAD = 64
FF = 2048
SFF = 2048
TOP = 2
WINDOW = 1024
TOK_DEV = 256
EXPERTS = 8
SEQ = 1024
SEQS = 8
CAP = 128


def draw_segment(key, part):
    key = jax.random.fold_in(key, 5)
    first_key, second_key = jax.random.split(key)
    first_cut = jax.random.randint(first_key, (SEQS, 1), 1, TOK_DEV)
    second_cut = jax.random.randint(second_key, (SEQS, 1), SEQ - TOK_DEV + 1, SEQ)
    positions = jnp.arange(SEQ, dtype=jnp.int32)[None, :]
    return (positions >= first_cut).astype(jnp.int32) + (positions >= second_cut).astype(jnp.int32)


def set_ends(values, key, least, largest):
    longest = values.shape.index(max(values.shape))
    spots = []
    for shift in (0, 1):
        where = [jax.random.randint(jax.random.fold_in(key, axis), (), 0, length) for axis, length in enumerate(values.shape)]
        where[longest] = (where[longest] + shift) % values.shape[longest]
        spots.append(tuple(where))
    return values.at[spots[0]].set(least).at[spots[1]].set(largest)


def level_of(own_key, shape, cuts, least, top_value):
    factor_of = 1.0
    for dim, blocks in cuts:
        steps = jax.random.uniform(jax.random.fold_in(jax.random.fold_in(own_key, 6), dim), (blocks,), jnp.float32, least / len(cuts), top_value / len(cuts))
        factor_of = factor_of * jnp.repeat(jnp.exp(steps), shape[dim] // blocks).reshape((-1,) + (1,) * (len(shape) - 1 - dim))
    return factor_of


def deal_out(own_key, own, number, rows, count, top, reach, skew):
    order = jax.random.permutation(own_key, count)
    heavy_load, common = load_shares(count, rows * top, reach, skew, True), load_shares(count, rows * top, reach, skew, False)
    places = jnp.arange(count)

    def named(lengths, rotation):
        used = int((lengths > 0).sum())
        fixed = max(1, used // 4)
        shifted = fixed + (places - fixed + rotation * (used - fixed)) % max(1, count - fixed)
        return jnp.zeros((count,), jnp.int32).at[order[jnp.where(places < fixed, places, shifted)]].set(jnp.asarray(lengths, jnp.int32))

    lengths = jnp.where(number % 4 == 0, named(heavy_load, number // 4), named(common, number - number // 4 - 1))
    mixed = jax.random.permutation(jax.random.fold_in(own, 3), count)
    source_of, taker = mixed[0:count // 2 * 2:2], mixed[1:count // 2 * 2:2]
    margin = jnp.minimum(lengths[source_of] - 1, reach - lengths[taker]) // 2
    margin = jnp.where((source_of == order[0]) | (taker == order[0]) | (lengths[taker] == 0), 0, jnp.maximum(margin, 0))
    shifted = jax.random.randint(jax.random.fold_in(own, 4), (count // 2,), 0, 1 << 20) % (margin + 1)
    lengths = lengths.at[source_of].add(-shifted).at[taker].add(shifted)
    members = jnp.searchsorted(jnp.cumsum(lengths), jnp.arange(rows * top), side="right").astype(jnp.int32)
    table = members.reshape(top, rows).T
    table = table[jax.random.permutation(jax.random.fold_in(own, 1), rows)]
    rotation = jax.random.randint(jax.random.fold_in(own, 2), (rows, 1), 0, top)
    return jnp.take_along_axis(table, (jnp.arange(top)[None, :] + rotation) % top, axis=1)


def load_shares(number_of, total, reach, lean, full):
    weights = [(1 << 20) // math.isqrt(grade ** lean) + 1 for grade in range(1, number_of + 1)]
    largest = reach if full else min(reach, max(-(-total // number_of), total * weights[0] // sum(weights)))
    least = 1 if total - largest >= number_of - 1 else 0
    counts, surplus = [largest] + [least] * (number_of - 1), total - largest - least * (number_of - 1)
    while surplus > 0:
        free = [i for i in range(1, number_of) if counts[i] < largest] or [i for i in range(1, number_of) if counts[i] < reach]
        whole, left = sum([weights[i] for i in free]), surplus
        for i in free:
            extra = min(reach - counts[i], max(1, left * weights[i] // whole), surplus)
            counts[i] = counts[i] + extra
            surplus = surplus - extra
    return np.array(counts)


def scatter_about(key, dims, spread, most, cuts=(), held_as=jnp.bfloat16):
    values = jax.random.normal(key, dims, jnp.float32) * spread
    if len(cuts) > 0:
        values = level_of(key, dims, cuts, -0.22, 0.18) * values
    return jnp.clip(values, min=-most, max=most).astype(held_as)


def setup_inputs(seed: int = 0) -> dict:
    key_of = jax.random.split(jax.random.key(seed), 19)
    hidden_in = scatter_about(key_of[0], (SEQS, SEQ, D), 1.0, 6.0, ((0, 8), (1, 4)))
    gain_attn = jnp.clip(1.0 + 0.15 * jax.random.normal(key_of[1], (D,), jnp.float32), 0.25, 1.75).astype(jnp.bfloat16)
    gain_ffn = jnp.clip(1.0 + 0.15 * jax.random.normal(key_of[2], (D,), jnp.float32), 0.25, 1.75).astype(jnp.bfloat16)
    w_query = scatter_about(key_of[3], (D, D), D ** -0.5, 0.21875, ((0, 4),))
    w_key = scatter_about(key_of[4], (D, D), D ** -0.5, 0.21875, ((0, 4),))
    w_value = scatter_about(key_of[5], (D, D), D ** -0.5, 0.21875, ((0, 4),))
    w_out = scatter_about(key_of[6], (D, D), (D // 32) ** -0.5, 1.25, ((0, 4),))
    shared_gate = scatter_about(key_of[7], (D, SFF), D ** -0.5, 0.21875, ((0, 4),))
    shared_up = scatter_about(key_of[8], (D, SFF), D ** -0.5, 0.21875, ((0, 4),))
    shared_down = scatter_about(key_of[9], (SFF, D), SFF ** -0.5, 0.125, ((0, 4),))
    expert_gate = scatter_about(key_of[10], (EXPERTS, D, FF), D ** -0.5, 0.21875, ((0, 8), (1, 4)))
    expert_up = scatter_about(key_of[11], (EXPERTS, D, FF), D ** -0.5, 0.21875, ((0, 8), (1, 4)))
    expert_down = scatter_about(key_of[12], (EXPERTS, FF, D), FF ** -0.5, 0.125, ((0, 8), (1, 4)))
    gate_logits = scatter_about(key_of[13], (SEQS, SEQ, TOP), 0.7, 3.5, ((0, 8), (1, 4)), jnp.float32)
    routes_keys = jax.random.split(jax.random.fold_in(key_of[14], 1), SEQS * SEQ // TOK_DEV)
    routes_turns = jax.random.permutation(jax.random.fold_in(key_of[14], 3), SEQS * SEQ // TOK_DEV)
    routes = jax.vmap(lambda own, number: deal_out(jax.random.fold_in(key_of[14], 2), own, number, TOK_DEV, EXPERTS, TOP, CAP, 2))(routes_keys, routes_turns).reshape((SEQS, SEQ, TOP))
    segment = draw_segment(jax.random.fold_in(key_of[18], 71), 0)
    padding = set_ends((jax.random.randint(key_of[16], (SEQS, SEQ), 0, 8) < 7).astype(jnp.int32), jax.random.fold_in(key_of[16], 1), 0, 1)
    cotangent = scatter_about(key_of[17], (SEQS, SEQ, D), 1.0, 6.0, ((0, 8), (1, 4)))
    return dict(hidden_in=hidden_in, gain_attn=gain_attn, gain_ffn=gain_ffn, w_query=w_query, w_key=w_key, w_value=w_value, w_out=w_out, shared_gate=shared_gate, shared_up=shared_up, shared_down=shared_down, expert_gate=expert_gate, expert_up=expert_up, expert_down=expert_down, gate_logits=gate_logits, routes=routes, segment=segment, padding=padding, cotangent=cotangent)


@jax.custom_vjp
def low(v):
    return lax.optimization_barrier(v.astype(jnp.bfloat16)).astype(jnp.float32)

@jax.custom_vjp
def low_back(v):
    return v

def low_keep(v):
    return (low(v), None)

def low_pass(kept, grad):
    return (grad,)

def back_keep(v):
    return (v, None)

def back_low(kept, grad):
    return (low(grad),)
low.defvjp(low_keep, low_pass)
low_back.defvjp(back_keep, back_low)
norm_eps = 1e-06
neg_fill = -1e+30
rope_base = 10000.0

def product(left, right):
    return jnp.dot(left, right, precision=lax.Precision.HIGHEST, preferred_element_type=jnp.float32)

def rms_scale(values):
    return lax.rsqrt(lax.optimization_barrier(jnp.mean(values * values, axis=-1, keepdims=True)) + norm_eps)

def rotate(values, positions):
    half_size = values.shape[-1] // 2
    frequency = rope_base ** (-jnp.arange(half_size, dtype=jnp.float32) / half_size)
    angles = positions[:, None] * frequency[None, :]
    cosine = jnp.cos(angles)[:, None, :]
    sine_part = jnp.sin(angles)[:, None, :]
    first_half = values[..., :half_size]
    second_half = values[..., half_size:]
    return jnp.concatenate([first_half * cosine - second_half * sine_part, second_half * cosine + first_half * sine_part], axis=-1)

def attention(query_all, keys_all, values_all, segment, padding):
    row_count = query_all.shape[0]
    length = query_all.shape[1]
    block_rows = min(512, length)
    per_row = length // block_rows
    key_positions = jnp.arange(length, dtype=jnp.int32)
    score_scale = HEAD ** (-0.5)

    def one_block(block_index):
        row_index = block_index // per_row
        row_start = block_index % per_row * block_rows
        query_rows = lax.dynamic_slice_in_dim(lax.dynamic_index_in_dim(query_all, row_index, 0, False), row_start, block_rows, 0)
        key_rows = lax.dynamic_index_in_dim(keys_all, row_index, 0, False)
        value_rows = lax.dynamic_index_in_dim(values_all, row_index, 0, False)
        segment_row = lax.dynamic_index_in_dim(segment, row_index, 0, False)
        padding_row = lax.dynamic_index_in_dim(padding, row_index, 0, False)
        query_positions = row_start + jnp.arange(block_rows, dtype=jnp.int32)
        query_segment = lax.dynamic_slice_in_dim(segment_row, row_start, block_rows, 0)
        distance = query_positions[:, None] - key_positions[None, :]
        allowed = (query_segment[:, None] == segment_row[None, :]) & (distance >= 0) & (distance < WINDOW) & ((padding_row[None, :] == 1) | (distance == 0))
        scores = jnp.einsum('qhd,khd->hqk', query_rows, key_rows, precision=lax.Precision.HIGHEST) * score_scale
        scores = low_back(jnp.where(allowed[None], scores, neg_fill))
        softmaxed = jax.nn.softmax(scores, axis=-1)
        return jnp.einsum('hqk,khd->qhd', low(softmaxed), value_rows, precision=lax.Precision.HIGHEST)
    blocks = lax.map(jax.checkpoint(one_block), jnp.arange(row_count * per_row, dtype=jnp.int32))
    return blocks.reshape(row_count, length, HEADS, HEAD)

def routed_experts(normed_ffn, gate_logits, routes, expert_gate, expert_up, expert_down):
    token_count = normed_ffn.shape[0]
    route_flat = routes.reshape(-1)
    route_total = route_flat.shape[0]
    onehot = (route_flat[:, None] == jnp.arange(EXPERTS, dtype=jnp.int32)[None, :]).astype(jnp.int32)
    slot_rank = lax.optimization_barrier(jnp.sum((jnp.cumsum(onehot, axis=0) - onehot) * onehot, axis=1))
    slot_count = token_count // TOK_DEV * CAP
    places = route_flat * slot_count + slot_rank
    slot_table = jnp.full((EXPERTS * slot_count,), route_total, dtype=jnp.int32).at[places].set(jnp.arange(route_total, dtype=jnp.int32))
    token_table = (slot_table // TOP).reshape(EXPERTS, slot_count)
    padded_rows = jnp.concatenate([normed_ffn, jnp.zeros((1, normed_ffn.shape[1]), jnp.float32)], axis=0)

    def one_expert(inputs):
        expert_index, token_rows = inputs
        slot_rows = low_back(padded_rows[token_rows])
        gate_pre = low_back(product(slot_rows, lax.dynamic_index_in_dim(expert_gate, expert_index, 0, False)))
        up_pre = low_back(product(slot_rows, lax.dynamic_index_in_dim(expert_up, expert_index, 0, False)))
        middle = low(jax.nn.silu(gate_pre) * up_pre)
        return low(low_back(product(middle, lax.dynamic_index_in_dim(expert_down, expert_index, 0, False))))
    results = lax.map(jax.checkpoint(one_expert), (jnp.arange(EXPERTS, dtype=jnp.int32), token_table))
    per_route = results.reshape(EXPERTS * slot_count, -1)[places].reshape(token_count, TOP, -1)
    gate_probs = jax.nn.softmax(gate_logits, axis=-1)
    return lax.optimization_barrier(jnp.sum(gate_probs[:, :, None] * per_route, axis=1))

def layer_forward(params, hidden_rows, gate_logits, routes, segment, padding):
    gain_attn, gain_ffn, w_query, w_key, w_value, w_out, shared_gate, shared_up, shared_down, expert_gate, expert_up, expert_down = params
    row_count, length, model_width = hidden_rows.shape
    flat_in = hidden_rows.reshape(row_count * length, model_width)
    normed = low(flat_in * rms_scale(flat_in) * gain_attn)
    positions = jnp.arange(length).astype(jnp.float32)
    head_shape = (row_count, length, HEADS, HEAD)
    query_all = low(rotate(low_back(product(normed, w_query)).reshape(head_shape), positions))
    keys_all = low(rotate(low_back(product(normed, w_key)).reshape(head_shape), positions))
    values_all = low(low_back(product(normed, w_value))).reshape(head_shape)
    attended = attention(query_all, keys_all, values_all, segment, padding)
    attended = low(low_back(attended.reshape(row_count * length, model_width)))
    mixed_rows = flat_in + low_back(product(attended, w_out))
    normed_ffn = low(mixed_rows * rms_scale(mixed_rows) * gain_ffn)
    shared_pre = low_back(product(normed_ffn, shared_gate))
    shared_lin = low_back(product(normed_ffn, shared_up))
    shared_out = product(low(jax.nn.silu(shared_pre) * shared_lin), shared_down)
    routed = routed_experts(normed_ffn, gate_logits.reshape(-1, TOP), routes.reshape(-1, TOP), expert_gate, expert_up, expert_down)
    return (mixed_rows + shared_out + routed).reshape(row_count, length, model_width)

def reference(hidden_in, gain_attn, gain_ffn, w_query, w_key, w_value, w_out, shared_gate, shared_up, shared_down, expert_gate, expert_up, expert_down, gate_logits, routes, segment, padding, cotangent):
    params = tuple((weight.astype(jnp.float32) for weight in (gain_attn, gain_ffn, w_query, w_key, w_value, w_out, shared_gate, shared_up, shared_down, expert_gate, expert_up, expert_down)))
    group_size = math.gcd(SEQS, max(1, 4096 // SEQ))
    group_count = SEQS // group_size

    def regroup(source):
        return source.reshape((group_count, group_size) + source.shape[1:])

    def one_group(totals, inputs):
        group_in, group_logits, group_routes, group_segment, group_padding, group_cotangent = inputs

        def forward(weights, rows_in, logits_in):
            return layer_forward(weights, rows_in, logits_in, group_routes, group_segment, group_padding)
        result, pullback = jax.vjp(forward, params, group_in.astype(jnp.float32), group_logits.astype(jnp.float32))
        weight_grads, rows_grad, logits_grad = pullback(group_cotangent.astype(jnp.float32))
        totals = jax.tree.map(jnp.add, totals, weight_grads)
        return (totals, (result.astype(jnp.bfloat16), rows_grad, logits_grad))
    zero_grads = jax.tree.map(jnp.zeros_like, params)
    totals, (output, input_grad, logit_grad) = lax.scan(one_group, zero_grads, tuple((regroup(source) for source in (hidden_in, gate_logits, routes, segment, padding, cotangent))))
    output = output.reshape(SEQS, SEQ, D)
    input_grad = input_grad.reshape(SEQS, SEQ, D)
    logit_grad = logit_grad.reshape(SEQS, SEQ, TOP)
    return (output, input_grad, logit_grad, totals[0], totals[1], totals[2], totals[3], totals[4], totals[5], totals[6], totals[7], totals[8], totals[9], totals[10], totals[11])
```

```python
import functools

import jax
import jax.numpy as jnp
from jax import lax
from jax.experimental import pallas as pl
from jax.experimental.pallas import tpu as pltpu
from jax.sharding import PartitionSpec as P

HEADS = 12
TOP = 2
WINDOW = 1024
MESH = pl.DeviceIdType.MESH
NAMES = ("wq", "wk", "wv", "wo", "gains", "sg", "su", "sd", "eg", "eu", "ed")
EARLY = ("wq", "wk", "wv")
SPREAD = ("wo", "gains", "sg", "su", "sd")
LATE = ("eg", "eu", "ed")


norm_eps = 1e-06
neg_fill = -1e30
rope_base = 10000.0


def from_behind(value, axis, steps):
    count = lax.axis_size(axis)
    first, last = (max(0, -steps), min(count, count - steps))
    return lax.ppermute(value, axis, [(source, source + steps) for source in range(first, last)])


def dense_product(left, right):
    return jnp.dot(left, right, preferred_element_type=jnp.float32)


def rms_scale(values):
    return lax.rsqrt(jnp.mean(values * values, axis=-1, keepdims=True) + norm_eps)


def rotate(values, positions, direction):
    half_size = values.shape[-1] // 2
    frequency = rope_base ** (-jnp.arange(half_size, dtype=jnp.float32) / half_size)
    angles = positions.astype(jnp.float32)[:, None] * frequency[None, :]
    cosine = jnp.cos(angles)[:, None, :]
    sine_part = direction * jnp.sin(angles)[:, None, :]
    first_half = values[..., :half_size]
    second_half = values[..., half_size:]
    return jnp.concatenate(
        [
            first_half * cosine - second_half * sine_part,
            second_half * cosine + first_half * sine_part,
        ],
        axis=-1,
    )


def swiglu_back(grad_middle, gate_pre, up_pre):
    sigmoid_gate = jax.nn.sigmoid(gate_pre)
    activated = gate_pre * sigmoid_gate
    grad_gate = grad_middle * up_pre * sigmoid_gate * (1.0 + gate_pre * (1.0 - sigmoid_gate))
    grad_up = grad_middle * activated
    return (grad_gate.astype(jnp.bfloat16), grad_up.astype(jnp.bfloat16))


def gather_kernel(*refs):
    count = len(NAMES)
    own = dict(zip(NAMES, refs[:count]))
    full = dict(zip(NAMES, refs[count : 2 * count]))
    (own_sem, y_send, y_recv, x_send, x_recv, z_send, z_recv, core_send, core_recv) = refs[2 * count :]
    number = {name: index for index, name in enumerate(NAMES)}
    expert, shard = (lax.axis_index("expert"), lax.axis_index("shard"))
    zed, ex = (expert // 2, expert % 2)
    other = (shard + 2) % 4
    y_peer = (expert, other)
    core_peer = (expert, shard + 1 - 2 * (shard % 2))
    x_peer = (expert + 1 - 2 * ex, shard)
    z_up, z_down = (((expert + 2) % 8, shard), ((expert + 6) % 8, shard))

    barrier = pltpu.get_barrier_semaphore()
    for peer in (y_peer, core_peer, x_peer):
        pl.semaphore_signal(barrier, inc=1, device_id=peer, device_id_type=MESH)

    @pl.when(zed < 3)
    def _():
        pl.semaphore_signal(barrier, inc=1, device_id=z_up, device_id_type=MESH)

    @pl.when(zed > 0)
    def _():
        pl.semaphore_signal(barrier, inc=1, device_id=z_down, device_id_type=MESH)

    pl.semaphore_wait(barrier, 3 + jnp.minimum(3 - zed, 1) + jnp.minimum(zed, 1))

    def place(name, slot, at_z=None, at_x=None):
        whole, rows = (full[name], own[name].shape[0])
        base = slot * rows
        if at_z is None and at_x is None:
            return whole.at[pl.ds(base, rows)]
        if name in EARLY:
            return whole.at[pl.ds(base + at_x * (rows // 2), rows // 2)]
        if name in ("sg", "su"):
            width = whole.shape[1] // 4
            if at_x is None:
                return whole.at[pl.ds(base, rows), pl.ds(at_z * width, width)]
            half = width // 2
            return whole.at[pl.ds(base, rows), pl.ds(at_z * width + at_x * half, half)]
        size = rows // 4
        if name == "sd" and at_x is not None:
            return whole.at[pl.ds(base + at_z * size + at_x * (size // 2), size // 2)]
        return whole.at[pl.ds(base + at_z * size, size)]

    def mine(name, at_z=None, at_x=None):
        block, rows = (own[name], own[name].shape[0])
        if at_z is None and at_x is None:
            return block
        if name in EARLY:
            return block.at[pl.ds(at_x * (rows // 2), rows // 2)]
        if name in ("sg", "su"):
            half = block.shape[1] // 8
            return block.at[:, pl.ds((at_z * 2 + at_x) * half, half)]
        size = rows // 4
        if name == "sd":
            return block.at[pl.ds(at_z * size + at_x * (size // 2), size // 2)]
        return block.at[pl.ds(at_z * size, size)]

    def send(source, target, send_sem, recv_sem, peer):
        copy = pltpu.make_async_remote_copy(
            src_ref=source, dst_ref=target, send_sem=send_sem, recv_sem=recv_sem,
            device_id=peer, device_id_type=MESH,
        )
        copy.start()
        return copy

    def wait_recv(target, recv_sem):
        pltpu.make_async_remote_copy(
            src_ref=target, dst_ref=target, send_sem=recv_sem, recv_sem=recv_sem,
            device_id=core_peer, device_id_type=MESH,
        ).wait_recv()

    def wait_send(source, send_sem):
        pltpu.make_async_remote_copy(
            src_ref=source, dst_ref=source, send_sem=send_sem, recv_sem=send_sem,
            device_id=core_peer, device_id_type=MESH,
        ).wait_send()

    def cross(name, at_z=None, at_x=None):
        n = number[name]
        send(mine(name, at_z, at_x), place(name, shard, at_z, at_x), y_send.at[n], y_recv.at[n], y_peer)

    def to_core(name, step, at_z=None, at_x=None):
        n = number[name]
        part = place(name, other, at_z, at_x)
        send(part, part, core_send.at[n, 1 + step], core_recv.at[n, 1 + step], core_peer)

    split_x = tuple(name for name in ("sg", "su", "sd") if name in SPREAD)
    for name in EARLY:
        cross(name, None, ex)
    for name in SPREAD:
        cross(name, zed, ex if name in split_x else None)
    for name in NAMES:
        n = number[name]
        send(own[name], place(name, shard), core_send.at[n, 0], core_recv.at[n, 0], core_peer)
        pltpu.make_async_copy(own[name], place(name, shard), own_sem.at[n]).start()

    for name in EARLY:
        n = number[name]
        part = place(name, other, None, ex)
        wait_recv(part, y_recv.at[n])
        send(part, part, x_send.at[n, 0], x_recv.at[n, 0], x_peer)
        to_core(name, 0, None, ex)
    for name in LATE:
        cross(name)
    for name in EARLY:
        n = number[name]
        wait_recv(place(name, other, None, 1 - ex), x_recv.at[n, 0])
        to_core(name, 1, None, 1 - ex)

    def on_part(name, at_z, step):
        n = number[name]
        at_x = ex if name in split_x else None
        part = place(name, other, at_z, at_x)
        if name in split_x:
            send(part, part, x_send.at[n, step], x_recv.at[n, step], x_peer)
        to_core(name, step, at_z, at_x)

    for name in SPREAD:
        n = number[name]
        wait_recv(place(name, other, zed, ex if name in split_x else None), y_recv.at[n])
    for step in range(3):
        def forward(direction, cond, at_z, peer):
            @pl.when(cond)
            def _():
                for name in SPREAD:
                    n = number[name]
                    part = place(name, other, at_z, ex if name in split_x else None)
                    send(part, part, z_send.at[n, direction, step], z_recv.at[n, direction, step], peer)

        forward(0, (zed < 3) & (zed >= step), zed - step, z_up)
        forward(1, (zed > 0) & (zed + step <= 3), zed + step, z_down)
        if step == 0:
            for name in SPREAD:
                on_part(name, zed, 0)

        def arrived(direction, cond, at_z):
            @pl.when(cond)
            def _():
                for name in SPREAD:
                    n = number[name]
                    at_x = ex if name in split_x else None
                    wait_recv(place(name, other, at_z, at_x), z_recv.at[n, direction, step])
                    on_part(name, at_z, 1 + direction * 3 + step)

        arrived(0, zed >= step + 1, zed - 1 - step)
        arrived(1, zed + 1 + step <= 3, zed + 1 + step)

    def from_x(cond, at_z, step):
        @pl.when(cond)
        def _():
            for name in split_x:
                n = number[name]
                wait_recv(place(name, other, at_z, 1 - ex), x_recv.at[n, step])
                to_core(name, 7 + step, at_z, 1 - ex)

    from_x(zed >= 0, zed, 0)
    for step in range(3):
        from_x(zed >= step + 1, zed - 1 - step, 1 + step)
        from_x(zed + 1 + step <= 3, zed + 1 + step, 4 + step)

    for name in LATE:
        n = number[name]
        wait_recv(place(name, other), y_recv.at[n])
        to_core(name, 0)

    far = shard + 1 - 2 * (shard % 2)
    far_other = (far + 2) % 4
    for name in NAMES:
        n = number[name]
        pltpu.make_async_copy(own[name], place(name, shard), own_sem.at[n]).wait()
        wait_recv(place(name, far), core_recv.at[n, 0])
        wait_send(own[name], core_send.at[n, 0])

    def finish(name, step, at_z, at_x):
        n = number[name]
        wait_recv(place(name, far_other, at_z, at_x), core_recv.at[n, 1 + step])
        wait_send(place(name, other, at_z, at_x), core_send.at[n, 1 + step])

    for name in EARLY:
        n = number[name]
        wait_send(mine(name, None, ex), y_send.at[n])
        wait_send(place(name, other, None, ex), x_send.at[n, 0])
        finish(name, 0, None, ex)
        finish(name, 1, None, 1 - ex)
    for name in LATE:
        n = number[name]
        wait_send(own[name], y_send.at[n])
        finish(name, 0, None, None)

    def finish_spread(cond, at_z, step):
        @pl.when(cond)
        def _():
            for name in SPREAD:
                n = number[name]
                at_x = ex if name in split_x else None
                finish(name, step, at_z, at_x)
                if name in split_x:
                    wait_send(place(name, other, at_z, ex), x_send.at[n, step])
                    finish(name, 7 + step, at_z, 1 - ex)

    for name in SPREAD:
        n = number[name]
        wait_send(mine(name, zed, ex if name in split_x else None), y_send.at[n])
    finish_spread(zed >= 0, zed, 0)
    for step in range(3):
        finish_spread(zed >= step + 1, zed - 1 - step, 1 + step)
        finish_spread(zed + 1 + step <= 3, zed + 1 + step, 4 + step)

        def sent(direction, cond, at_z):
            @pl.when(cond)
            def _():
                for name in SPREAD:
                    n = number[name]
                    at_x = ex if name in split_x else None
                    wait_send(place(name, other, at_z, at_x), z_send.at[n, direction, step])

        sent(0, (zed < 3) & (zed >= step), zed - step)
        sent(1, (zed > 0) & (zed + step <= 3), zed + step)


def gather_weights(blocks):
    count = len(NAMES)
    shapes = [jax.ShapeDtypeStruct((4 * block.shape[0], block.shape[1]), block.dtype) for block in blocks]
    dma = pltpu.SemaphoreType.DMA
    return pl.pallas_call(
        gather_kernel,
        out_shape=shapes,
        in_specs=[pl.BlockSpec(memory_space=pltpu.VMEM)] * count,
        out_specs=[pl.BlockSpec(memory_space=pl.ANY)] * count,
        scratch_shapes=[
            dma((count,)), dma((count,)), dma((count,)), dma((count, 7)), dma((count, 7)),
            dma((count, 2, 3)), dma((count, 2, 3)), dma((count, 15)), dma((count, 15)),
        ],
        compiler_params=pltpu.CompilerParams(collective_id=0, has_side_effects=True, vmem_limit_bytes=48 << 20),
        cost_estimate=pl.CostEstimate(flops=0, bytes_accessed=47000000, transcendentals=0),
    )(*blocks)


def whole_weights(gain_attn, gain_ffn, dense, experts):
    expert_count, shard_count = (lax.axis_size("expert"), lax.axis_size("shard"))
    if (expert_count, shard_count) == (8, 4):
        gains = jnp.zeros((64, gain_attn.shape[0]), jnp.bfloat16)
        gains = gains.at[0].set(gain_attn).at[1].set(gain_ffn)
        blocks = dense[:4] + (gains,) + dense[4:] + tuple(weight[0] for weight in experts)
        out = gather_weights(blocks)
        gains = out[4].reshape(4, 64, -1)[:, :2].transpose(1, 0, 2).reshape(2, -1)
        return gains, tuple(out[:4]) + tuple(out[5:8]), tuple(out[8:])
    gather = functools.partial(lax.all_gather, axis_name="shard", tiled=True)
    gains = jnp.stack([gather(gain_attn), gather(gain_ffn)])
    return gains, tuple(gather(weight) for weight in dense), tuple(gather(weight[0]) for weight in experts)


def swap(value, axis, bit):
    size = lax.axis_size(axis)
    return lax.ppermute(value, axis, [(index, index ^ bit) for index in range(size)])


def halves(value, bit_set, dim):
    half = value.shape[dim] // 2
    keep = lax.dynamic_slice_in_dim(value, bit_set * half, half, dim)
    give = lax.dynamic_slice_in_dim(value, (1 - bit_set) * half, half, dim)
    return keep, give


def fold(value, axis, bit, dim):
    bit_set = (lax.axis_index(axis) // bit) % 2
    keep, give = halves(value, bit_set, dim)
    return (keep.astype(jnp.float32) + swap(give.astype(jnp.bfloat16), axis, bit).astype(jnp.float32)).astype(jnp.bfloat16)


def unfold(value, axis, bit, dim):
    bit_set = (lax.axis_index(axis) // bit) % 2
    come = swap(value, axis, bit)
    return jnp.where(bit_set == 0, jnp.concatenate([value, come], dim), jnp.concatenate([come, value], dim))


def bits_of(axis):
    size = lax.axis_size(axis)
    return [1 << place for place in range(size.bit_length() - 1)]


def scatter_shards(value):
    count = lax.axis_size("shard")
    blocks = value.reshape((count // 2, 2, value.shape[0] // count) + value.shape[1:])
    blocks = fold(blocks, "shard", 1, 1)[:, 0]
    for bit in reversed(bits_of("shard")[1:]):
        blocks = fold(blocks, "shard", bit, 0)
    return blocks[0]


def sum_plane(value, dim):
    bits = bits_of("expert")
    for bit in bits:
        value = fold(value, "expert", bit, dim)
    for bit in reversed(bits):
        value = unfold(value, "expert", bit, dim)
    return value.astype(jnp.float32)


def shards(
    hidden_in,
    gain_attn,
    gain_ffn,
    w_query,
    w_key,
    w_value,
    w_out,
    shared_gate,
    shared_up,
    shared_down,
    expert_gate,
    expert_up,
    expert_down,
    gate_logits,
    routes,
    segment,
    padding,
    cotangent,
):
    bfloat = jnp.bfloat16
    tokens = hidden_in.shape[1]
    model_width = hidden_in.shape[2]
    head_size = model_width // HEADS
    experts = lax.axis_size("expert")
    capacity = max(2, 2 * tokens * TOP // experts)
    shard_count = lax.axis_size("shard")
    shard_index = lax.axis_index("shard")
    key_reach = min((WINDOW + tokens - 2) // tokens, shard_count - 1)
    key_rows = (key_reach + 1) * tokens
    score_scale = head_size ** (-0.5)
    head_shape = (tokens, HEADS, head_size)
    gains, dense_all, expert_all = whole_weights(
        gain_attn,
        gain_ffn,
        (w_query, w_key, w_value, w_out, shared_gate, shared_up, shared_down),
        (expert_gate, expert_up, expert_down),
    )
    dense_all = (gains[0], gains[1]) + dense_all
    dense_back = dense_all
    gain_first = dense_all[0].astype(jnp.float32)
    gain_second = dense_all[1].astype(jnp.float32)
    gate_expert_all = expert_all[0]
    up_expert_all = expert_all[1]
    down_expert_all = expert_all[2]
    rows_in = hidden_in[0].astype(jnp.float32)
    scale_first = rms_scale(rows_in)
    normed = (rows_in * scale_first * gain_first).astype(bfloat)
    positions = shard_index * tokens + jnp.arange(tokens, dtype=jnp.int32)
    query_low = rotate(
        dense_product(normed, dense_all[2]).reshape(head_shape), positions, 1.0
    ).astype(bfloat)
    key_low = (
        rotate(dense_product(normed, dense_all[3]).reshape(head_shape), positions, 1.0)
        .astype(bfloat)
        .reshape(tokens, model_width)
    )
    value_low = dense_product(normed, dense_all[4]).astype(bfloat)
    key_parts = [key_low]
    value_parts = [value_low]
    for offset in range(1, key_reach + 1):
        earlier = from_behind((key_low, value_low), "shard", offset)
        key_parts.insert(0, earlier[0])
        value_parts.insert(0, earlier[1])
    keys_all = jnp.concatenate(key_parts, axis=0).reshape(key_rows, HEADS, head_size)
    values_all = jnp.concatenate(value_parts, axis=0).reshape(key_rows, HEADS, head_size)
    segment_row = segment[0]
    padding_row = padding[0]
    lead_rows = key_reach * tokens
    segment_ext = jnp.concatenate([jnp.full((lead_rows,), -1, jnp.int32), segment_row])
    padding_ext = jnp.concatenate([jnp.zeros((lead_rows,), jnp.int32), padding_row])
    key_segment = lax.dynamic_slice_in_dim(segment_ext, shard_index * tokens, key_rows)
    key_padding = lax.dynamic_slice_in_dim(padding_ext, shard_index * tokens, key_rows)
    query_segment = lax.dynamic_slice_in_dim(segment_row, shard_index * tokens, tokens)
    key_positions = (shard_index - key_reach) * tokens + jnp.arange(key_rows, dtype=jnp.int32)
    distance = positions[:, None] - key_positions[None, :]
    allowed = (
        (query_segment[:, None] == key_segment[None, :])
        & (distance >= 0)
        & (distance < WINDOW)
        & ((key_padding[None, :] == 1) | (distance == 0))
    )

    def score_block():
        raw_scores = (
            jnp.einsum("qhd,khd->hqk", query_low, keys_all, preferred_element_type=jnp.float32)
            * score_scale
        )
        return jnp.where(allowed[None], raw_scores, neg_fill)

    scores = score_block()
    top_score = jnp.max(scores, axis=-1, keepdims=True)
    exponent = jnp.exp(scores - top_score)
    exp_total = jnp.sum(exponent, axis=-1, keepdims=True)
    attn_probs = exponent / exp_total
    log_total = top_score + jnp.log(exp_total)
    attended = (
        jnp.einsum(
            "hqk,khd->qhd",
            attn_probs.astype(bfloat),
            values_all,
            preferred_element_type=jnp.float32,
        )
        .astype(bfloat)
        .reshape(tokens, model_width)
    )
    mixed_rows = rows_in + dense_product(attended, dense_all[5])
    scale_second = rms_scale(mixed_rows)
    normed_ffn = (mixed_rows * scale_second * gain_second).astype(bfloat)
    shared_pre = dense_product(normed_ffn, dense_all[6])
    shared_lin = dense_product(normed_ffn, dense_all[7])
    shared_mid = (jax.nn.silu(shared_pre) * shared_lin).astype(bfloat)
    shared_out = dense_product(shared_mid, dense_all[8])
    route_flat = routes[0].reshape(-1)
    route_total = tokens * TOP
    onehot = (route_flat[:, None] == jnp.arange(experts, dtype=jnp.int32)[None, :]).astype(
        jnp.int32
    )
    slot_rank = jnp.sum((jnp.cumsum(onehot, axis=0) - onehot) * onehot, axis=1)
    places = route_flat * capacity + slot_rank
    slot_table = (
        jnp.full((experts * capacity,), route_total, dtype=jnp.int32)
        .at[places]
        .set(jnp.arange(route_total, dtype=jnp.int32))
    )
    padded_rows = jnp.concatenate([normed_ffn, jnp.zeros((1, model_width), bfloat)], axis=0)
    send_rows = padded_rows[slot_table // TOP].reshape(experts, capacity, model_width)
    received = lax.all_to_all(send_rows, "expert", split_axis=0, concat_axis=0, tiled=True)
    gate_pre = jnp.einsum(
        "sid,df->sif", received, gate_expert_all, preferred_element_type=jnp.float32
    )
    up_pre = jnp.einsum("sid,df->sif", received, up_expert_all, preferred_element_type=jnp.float32)
    middle = (jax.nn.silu(gate_pre) * up_pre).astype(bfloat)
    result = jnp.einsum(
        "sif,fd->sid", middle, down_expert_all, preferred_element_type=jnp.float32
    ).astype(bfloat)
    returned = lax.all_to_all(result, "expert", split_axis=0, concat_axis=0, tiled=True)
    outcome = (returned, received, gate_pre, up_pre)
    per_route = (
        outcome[0]
        .reshape(experts * capacity, model_width)[places]
        .astype(jnp.float32)
        .reshape(tokens, TOP, model_width)
    )
    gate_probs = jax.nn.softmax(gate_logits[0], axis=-1)
    routed = jnp.sum(gate_probs[:, :, None] * per_route, axis=1)
    output = (mixed_rows + shared_out + routed).astype(bfloat)
    grad_low = cotangent[0]
    grad_out = grad_low.astype(jnp.float32)
    contrib = jnp.sum(per_route * grad_out[:, None, :], axis=-1)
    logit_grad = gate_probs * (contrib - jnp.sum(gate_probs * contrib, axis=-1, keepdims=True))
    route_grad = (
        (gate_probs[:, :, None] * grad_out[:, None, :])
        .astype(bfloat)
        .reshape(route_total, model_width)
    )
    route_padded = jnp.concatenate([route_grad, jnp.zeros((1, model_width), bfloat)], axis=0)
    send_grad = route_padded[slot_table].reshape(experts, capacity, model_width)
    gate_expert_back = gate_expert_all
    up_expert_back = up_expert_all
    down_expert_back = down_expert_all
    grad_received = lax.all_to_all(send_grad, "expert", split_axis=0, concat_axis=0, tiled=True)
    received = outcome[1]
    gate_pre = outcome[2]
    up_pre = outcome[3]
    middle = (jax.nn.silu(gate_pre) * up_pre).astype(bfloat)
    grad_middle = jnp.einsum(
        "sid,fd->sif", grad_received, down_expert_back, preferred_element_type=jnp.float32
    )
    grad_gate_pre, grad_up_pre = swiglu_back(grad_middle, gate_pre, up_pre)
    expert_down_grad = jnp.einsum(
        "sif,sid->fd", middle, grad_received, preferred_element_type=jnp.float32
    )
    expert_gate_grad = jnp.einsum(
        "sid,sif->df", received, grad_gate_pre, preferred_element_type=jnp.float32
    )
    expert_up_grad = jnp.einsum(
        "sid,sif->df", received, grad_up_pre, preferred_element_type=jnp.float32
    )
    grad_rows = (
        jnp.einsum(
            "sif,df->sid", grad_gate_pre, gate_expert_back, preferred_element_type=jnp.float32
        )
        + jnp.einsum("sif,df->sid", grad_up_pre, up_expert_back, preferred_element_type=jnp.float32)
    ).astype(bfloat)
    grad_back = lax.all_to_all(grad_rows, "expert", split_axis=0, concat_axis=0, tiled=True)
    expert_grads = tuple(
        scatter_shards(grad.astype(bfloat))[None].astype(jnp.float32)
        for grad in (expert_gate_grad, expert_up_grad, expert_down_grad)
    )
    grad_routes = (
        grad_back.reshape(experts * capacity, model_width)[places]
        .astype(jnp.float32)
        .reshape(tokens, TOP, model_width)
    )
    grad_normed_ffn = jnp.sum(grad_routes, axis=1)
    grad_shared_mid = dense_product(grad_low, dense_back[8].T)
    grad_shared_pre, grad_shared_lin = swiglu_back(grad_shared_mid, shared_pre, shared_lin)
    shared_down_grad = dense_product(shared_mid.T, grad_low)
    shared_gate_grad = dense_product(normed_ffn.T, grad_shared_pre)
    shared_up_grad = dense_product(normed_ffn.T, grad_shared_lin)
    grad_normed_ffn = (
        grad_normed_ffn
        + dense_product(grad_shared_pre, dense_back[6].T)
        + dense_product(grad_shared_lin, dense_back[7].T)
    )
    gain_ffn_grad = jnp.sum(grad_normed_ffn * mixed_rows * scale_second, axis=0)
    scaled_second = grad_normed_ffn * dense_back[1].astype(jnp.float32)
    grad_mixed = (
        grad_out
        + scale_second * scaled_second
        - mixed_rows
        * scale_second**3
        * jnp.mean(scaled_second * mixed_rows, axis=-1, keepdims=True)
    )
    grad_mixed_low = grad_mixed.astype(bfloat)
    w_out_grad = dense_product(attended.T, grad_mixed_low)
    grad_attended = (
        dense_product(grad_mixed_low, dense_back[5].T).astype(bfloat).reshape(head_shape)
    )
    attn_probs = jnp.exp(score_block() - log_total)
    grad_probs = jnp.einsum(
        "qhd,khd->hqk", grad_attended, values_all, preferred_element_type=jnp.float32
    )
    delta_rows = jnp.sum(attn_probs * grad_probs, axis=-1, keepdims=True)
    grad_scores = (attn_probs * (grad_probs - delta_rows)).astype(bfloat)
    grad_query = (
        jnp.einsum("hqk,khd->qhd", grad_scores, keys_all, preferred_element_type=jnp.float32)
        * score_scale
    )
    grad_keys = (
        jnp.einsum("hqk,qhd->khd", grad_scores, query_low, preferred_element_type=jnp.float32)
        * score_scale
    ).reshape(key_reach + 1, tokens, model_width)
    grad_values = jnp.einsum(
        "hqk,qhd->khd", attn_probs.astype(bfloat), grad_attended, preferred_element_type=jnp.float32
    ).reshape(key_reach + 1, tokens, model_width)
    key_total = grad_keys[key_reach]
    value_total = grad_values[key_reach]
    for offset in range(1, key_reach + 1):
        from_later = (
            from_behind(
                grad_keys[key_reach - offset].astype(jnp.bfloat16), "shard", -offset
            ).astype(jnp.float32),
            from_behind(
                grad_values[key_reach - offset].astype(jnp.bfloat16), "shard", -offset
            ).astype(jnp.float32),
        )
        key_total = key_total + from_later[0]
        value_total = value_total + from_later[1]
    grad_query_low = rotate(grad_query, positions, -1.0).astype(bfloat).reshape(tokens, model_width)
    grad_key_low = (
        rotate(key_total.reshape(head_shape), positions, -1.0)
        .astype(bfloat)
        .reshape(tokens, model_width)
    )
    grad_value_low = value_total.astype(bfloat)
    w_query_grad = dense_product(normed.T, grad_query_low)
    w_key_grad = dense_product(normed.T, grad_key_low)
    w_value_grad = dense_product(normed.T, grad_value_low)
    grad_normed = (
        dense_product(grad_query_low, dense_back[2].T)
        + dense_product(grad_key_low, dense_back[3].T)
        + dense_product(grad_value_low, dense_back[4].T)
    )
    gain_attn_grad = jnp.sum(grad_normed * rows_in * scale_first, axis=0)
    scaled_first = grad_normed * dense_back[0].astype(jnp.float32)
    input_grad = (
        grad_mixed
        + scale_first * scaled_first
        - rows_in * scale_first**3 * jnp.mean(scaled_first * rows_in, axis=-1, keepdims=True)
    )
    gain_rows = jnp.stack([gain_attn_grad, gain_ffn_grad], axis=1).astype(bfloat)
    gain_total = lax.psum(scatter_shards(gain_rows), "expert").astype(jnp.float32)
    attn_grads = jnp.stack([w_query_grad, w_key_grad, w_value_grad, w_out_grad]).astype(bfloat)
    attn_rows = scatter_shards(attn_grads.transpose(1, 0, 2)).transpose(1, 0, 2)
    attn_total = sum_plane(attn_rows.reshape(-1, model_width), 0).reshape(attn_rows.shape)
    totals = (
        gain_total[:, 0],
        gain_total[:, 1],
        attn_total[0],
        attn_total[1],
        attn_total[2],
        attn_total[3],
        sum_plane(scatter_shards(shared_gate_grad.astype(bfloat)), 1),
        sum_plane(scatter_shards(shared_up_grad.astype(bfloat)), 1),
        sum_plane(scatter_shards(shared_down_grad.astype(bfloat)), 0),
    )
    return (
        output[None],
        input_grad[None],
        logit_grad[None],
        totals[0],
        totals[1],
        totals[2],
        totals[3],
        totals[4],
        totals[5],
        totals[6],
        totals[7],
        totals[8],
        expert_grads[0],
        expert_grads[1],
        expert_grads[2],
    )


def solution(mesh):
    placed = (
        P("expert", "shard", None),
        P("shard"),
        P("shard"),
        P("shard", None),
        P("shard", None),
        P("shard", None),
        P("shard", None),
        P("shard", None),
        P("shard", None),
        P("shard", None),
        P("expert", "shard", None),
        P("expert", "shard", None),
        P("expert", "shard", None),
        P("expert", "shard", None),
        P("expert", "shard", None),
        P("expert", None),
        P("expert", None),
        P("expert", "shard", None),
    )
    return jax.shard_map(
        shards,
        mesh=mesh,
        in_specs=placed,
        out_specs=(
            P("expert", "shard", None),
            P("expert", "shard", None),
            P("expert", "shard", None),
            P("shard"),
            P("shard"),
            P("shard", None),
            P("shard", None),
            P("shard", None),
            P("shard", None),
            P("shard", None),
            P("shard", None),
            P("shard", None),
            P("expert", "shard", None),
            P("expert", "shard", None),
            P("expert", "shard", None),
        ),
        check_vma=False,
    )
```

```python
import functools

import jax
import jax.numpy as jnp
import numpy as np
from jax import lax
from jax.experimental import pallas as pl
from jax.experimental.pallas import tpu as pltpu
from jax.sharding import PartitionSpec as P

HEADS = 12
TOP = 2
WINDOW = 1024
MESH = pl.DeviceIdType.MESH
norm_eps = 1e-06
neg_fill = -1e30
rope_base = 10000.0

DIRECT = ("hid", "gains")
EARLY = ("wk", "wv", "wq")
SPREAD = ("wo", "sg", "su", "sd")
SPLIT_X = ("sg", "su", "sd")
LATE = ("eg", "eu", "ed")
NAMES = DIRECT + EARLY + SPREAD + LATE
IN_VMEM = DIRECT + EARLY + ("wo",)


def dense_product(left, right):
    return jnp.dot(left, right, preferred_element_type=jnp.float32)


def product_t(left, right):
    return lax.dot_general(left, right, (((1,), (1,)), ((), ())), preferred_element_type=jnp.float32)


def t_product(left, right):
    return lax.dot_general(left, right, (((0,), (0,)), ((), ())), preferred_element_type=jnp.float32)


def rms_scale(values):
    return lax.rsqrt(jnp.mean(values * values, axis=-1, keepdims=True) + norm_eps)


def rotary_tables(length, head_size):
    half = head_size // 2
    frequency = np.float32(rope_base) ** (-np.arange(half, dtype=np.float32) / np.float32(half))
    angles = np.arange(length, dtype=np.float32)[:, None] * frequency[None, :]
    cosine, sine = np.cos(angles).astype(np.float32), np.sin(angles).astype(np.float32)
    return np.concatenate([cosine] * 4, axis=1), np.concatenate([-sine, sine] * 2, axis=1)


def rotate_pair(values, cosine, sine):
    lane = lax.broadcasted_iota(jnp.int32, values.shape, 1)
    partner = jnp.where(lane % 64 < 32, pltpu.roll(values, 96, 1), pltpu.roll(values, 32, 1))
    return values * cosine + partner * sine


def rotate(values, positions, direction):
    half_size = values.shape[-1] // 2
    frequency = rope_base ** (-jnp.arange(half_size, dtype=jnp.float32) / half_size)
    angles = positions.astype(jnp.float32)[:, None] * frequency[None, :]
    cosine = jnp.cos(angles)[:, None, :]
    sine_part = direction * jnp.sin(angles)[:, None, :]
    first_half = values[..., :half_size]
    second_half = values[..., half_size:]
    return jnp.concatenate(
        [
            first_half * cosine - second_half * sine_part,
            second_half * cosine + first_half * sine_part,
        ],
        axis=-1,
    )


def swiglu_back(grad_middle, gate_pre, up_pre):
    sigmoid_gate = jax.nn.sigmoid(gate_pre)
    activated = gate_pre * sigmoid_gate
    grad_gate = grad_middle * up_pre * sigmoid_gate * (1.0 + gate_pre * (1.0 - sigmoid_gate))
    grad_up = grad_middle * activated
    return (grad_gate.astype(jnp.bfloat16), grad_up.astype(jnp.bfloat16))


def from_behind(value, axis, steps):
    count = lax.axis_size(axis)
    first, last = (max(0, -steps), min(count, count - steps))
    return lax.ppermute(value, axis, [(source, source + steps) for source in range(first, last)])


def send(source, target, send_sem, recv_sem, peer):
    pltpu.make_async_remote_copy(
        src_ref=source,
        dst_ref=target,
        send_sem=send_sem,
        recv_sem=recv_sem,
        device_id=peer,
        device_id_type=MESH,
    ).start()


def wait_for(ref, sem):
    pltpu.make_async_copy(ref, ref, sem).wait()


def first_kernel(*refs):
    count = len(NAMES)
    own = dict(zip(NAMES, refs[:count]))
    segment_row, segment_col, padding_row, cosine_ref, sine_ref = refs[count : count + 5]
    refs = refs[count + 5 :]
    full = dict(zip(NAMES, refs[:count]))
    gain_ref, normed_ref, query_ref, key_ref, value_ref, lse_ref, attended_ref, mixed_ref, ffn_ref = refs[count : count + 9]
    (own_sem, y_send, y_recv, x_send, x_recv, z_send, z_recv, core_send, core_recv) = refs[count + 9 :]
    number = {name: index for index, name in enumerate(NAMES)}
    expert, shard = (lax.axis_index("expert"), lax.axis_index("shard"))
    zed, ex = (expert // 2, expert % 2)
    other = (shard + 2) % 4
    y_peer = (expert, other)
    core_peer = (expert, shard + 1 - 2 * (shard % 2))
    x_peer = (expert + 1 - 2 * ex, shard)
    z_up, z_down = (((expert + 2) % 8, shard), ((expert + 6) % 8, shard))

    barrier = pltpu.get_barrier_semaphore()
    for peer in (y_peer, core_peer, x_peer):
        pl.semaphore_signal(barrier, inc=1, device_id=peer, device_id_type=MESH)

    @pl.when(zed < 3)
    def _():
        pl.semaphore_signal(barrier, inc=1, device_id=z_up, device_id_type=MESH)

    @pl.when(zed > 0)
    def _():
        pl.semaphore_signal(barrier, inc=1, device_id=z_down, device_id_type=MESH)

    pl.semaphore_wait(barrier, 3 + jnp.minimum(3 - zed, 1) + jnp.minimum(zed, 1))

    def part_of(block, base, name, at_z, at_x):
        rows = own[name].shape[0]
        if at_z is None and at_x is None:
            return block.at[pl.ds(base, rows)]
        if name in EARLY:
            return block.at[pl.ds(base + at_x * (rows // 2), rows // 2)]
        if name in ("sg", "su"):
            half = block.shape[1] // 8
            return block.at[pl.ds(base, rows), pl.ds((at_z * 2 + at_x) * half, half)]
        size = rows // 4
        if name == "sd":
            return block.at[pl.ds(base + at_z * size + at_x * (size // 2), size // 2)]
        return block.at[pl.ds(base + at_z * size, size)]

    def place(name, slot, at_z=None, at_x=None):
        return part_of(full[name], slot * own[name].shape[0], name, at_z, at_x)

    def mine(name, at_z=None, at_x=None):
        return part_of(own[name], 0, name, at_z, at_x)

    def ex_of(name):
        return ex if name in SPLIT_X else None

    def cross(name, at_z=None, at_x=None):
        n = number[name]
        send(mine(name, at_z, at_x), place(name, shard, at_z, at_x), y_send.at[n], y_recv.at[n], y_peer)

    def to_core(name, step, at_z=None, at_x=None):
        n = number[name]
        part = place(name, other, at_z, at_x)
        send(part, part, core_send.at[n, 1 + step], core_recv.at[n, 1 + step], core_peer)

    far = shard + 1 - 2 * (shard % 2)
    far_other = (far + 2) % 4

    def settle_own(names):
        for name in names:
            n = number[name]
            pltpu.make_async_copy(own[name], place(name, shard), own_sem.at[n]).wait()
            wait_for(place(name, far), core_recv.at[n, 0])
            wait_for(own[name], core_send.at[n, 0])

    def settle_core(name, step, at_z=None, at_x=None):
        n = number[name]
        wait_for(place(name, far_other, at_z, at_x), core_recv.at[n, 1 + step])
        wait_for(place(name, other, at_z, at_x), core_send.at[n, 1 + step])

    for name in DIRECT:
        cross(name)
    for name in EARLY:
        cross(name, None, ex)
    for name in SPREAD:
        cross(name, zed, ex_of(name))
    for name in NAMES:
        n = number[name]
        send(own[name], place(name, shard), core_send.at[n, 0], core_recv.at[n, 0], core_peer)
        pltpu.make_async_copy(own[name], place(name, shard), own_sem.at[n]).start()

    for name in DIRECT:
        wait_for(place(name, other), y_recv.at[number[name]])
        to_core(name, 0)
    for name in EARLY:
        n = number[name]
        part = place(name, other, None, ex)
        wait_for(part, y_recv.at[n])
        send(part, part, x_send.at[n, 0], x_recv.at[n, 0], x_peer)
        to_core(name, 0, None, ex)
    for name in LATE:
        cross(name)

    def on_part(name, at_z, step):
        n = number[name]
        part = place(name, other, at_z, ex_of(name))
        if name in SPLIT_X:
            send(part, part, x_send.at[n, step], x_recv.at[n, step], x_peer)
        to_core(name, step, at_z, ex_of(name))

    def forward(step, direction, condition, at_z, peer):
        @pl.when(condition)
        def _():
            for name in SPREAD:
                n = number[name]
                part = place(name, other, at_z, ex_of(name))
                send(part, part, z_send.at[n, direction, step], z_recv.at[n, direction, step], peer)

    def arrive(step, direction, condition, at_z):
        @pl.when(condition)
        def _():
            for name in SPREAD:
                n = number[name]
                wait_for(place(name, other, at_z, ex_of(name)), z_recv.at[n, direction, step])
                on_part(name, at_z, 1 + direction * 3 + step)

    def ring_send(step):
        forward(step, 0, (zed < 3) & (zed >= step), zed - step, z_up)
        forward(step, 1, (zed > 0) & (zed + step <= 3), zed + step, z_down)

    def ring_arrive(step):
        arrive(step, 0, zed >= step + 1, zed - 1 - step)
        arrive(step, 1, zed + 1 + step <= 3, zed + 1 + step)

    for name in SPREAD:
        wait_for(place(name, other, zed, ex_of(name)), y_recv.at[number[name]])
    ring_send(0)
    for name in SPREAD:
        on_part(name, zed, 0)

    settle_own(DIRECT)
    for name in DIRECT:
        settle_core(name, 0)
    tokens, width = own["hid"].shape
    gain_rows = sum(full["gains"][pl.ds(slot * 16, 16), :].astype(jnp.float32) for slot in range(4))
    gain_ref[...] = gain_rows
    gain_first, gain_second = gain_rows[0:1], gain_rows[1:2]

    def norm_block(block, carry):
        rows = pl.ds(pl.multiple_of(block * tokens, tokens), tokens)
        values = full["hid"][rows, :].astype(jnp.float32)
        normed_ref[rows, :] = (values * rms_scale(values) * gain_first).astype(jnp.bfloat16)
        return carry

    lax.fori_loop(0, 4, norm_block, 0)

    for name in EARLY:
        wait_for(place(name, other, None, 1 - ex), x_recv.at[number[name], 0])
        to_core(name, 1, None, 1 - ex)
    settle_own(EARLY)
    for name in EARLY:
        settle_core(name, 0, None, ex)
        settle_core(name, 1, None, 1 - ex)
        wait_for(mine(name, None, ex), y_send.at[number[name]])
        wait_for(place(name, other, None, ex), x_send.at[number[name], 0])

    def key_block(block, carry):
        rows = pl.ds(pl.multiple_of(block * tokens, tokens), tokens)
        normed = normed_ref[rows, :]
        value_ref[rows, :] = dense_product(normed, full["wv"][...]).astype(jnp.bfloat16)
        raw = dense_product(normed, full["wk"][...])
        cosine, sine = cosine_ref[rows, :], sine_ref[rows, :]
        for start in range(0, width, 128):
            key_ref[rows, start : start + 128] = rotate_pair(raw[:, start : start + 128], cosine, sine).astype(jnp.bfloat16)
        return carry

    lax.fori_loop(0, 4, key_block, 0)
    ring_arrive(0)
    ring_send(1)
    here = pl.ds(pl.multiple_of(shard * tokens, tokens), tokens)
    raw = dense_product(normed_ref[here, :], full["wq"][...])
    cosine, sine = cosine_ref[here, :], sine_ref[here, :]
    for start in range(0, width, 128):
        query_ref[:, start : start + 128] = rotate_pair(raw[:, start : start + 128], cosine, sine).astype(jnp.bfloat16)

    def head_pair(pair, carry):
        lanes = pl.ds(pl.multiple_of(pair * 128, 128), 128)
        query, keys, values = query_ref[:, lanes], key_ref[:, lanes], value_ref[:, lanes]
        allowed = allowed_mask(shard * tokens, 0, segment_col[here, :], segment_row[...], padding_row[...])
        lane = lax.broadcasted_iota(jnp.int32, query.shape, 1)
        results = []
        for half in range(2):
            chosen = (lane >= 64) if half else (lane < 64)
            scores = product_t(jnp.where(chosen, query, jnp.zeros_like(query)), keys) * 0.125
            scores = jnp.where(allowed, scores, neg_fill)
            top_score = jnp.max(scores, axis=-1, keepdims=True)
            exponent = jnp.exp(scores - top_score)
            exp_total = jnp.sum(exponent, axis=-1, keepdims=True)
            lse_ref[2 * pair + half] = top_score + jnp.log(exp_total)
            results.append(dense_product((exponent / exp_total).astype(jnp.bfloat16), values))
        attended_ref[:, lanes] = jnp.where(lane < 64, results[0], results[1]).astype(jnp.bfloat16)
        return carry

    lax.fori_loop(0, 3, head_pair, 0)
    ring_arrive(1)
    ring_send(2)
    lax.fori_loop(3, 6, head_pair, 0)
    ring_arrive(2)

    def from_x(condition, at_z, step):
        @pl.when(condition)
        def _():
            for name in SPLIT_X:
                wait_for(place(name, other, at_z, 1 - ex), x_recv.at[number[name], step])
                to_core(name, 7 + step, at_z, 1 - ex)

    from_x(zed >= 0, zed, 0)
    for step in range(3):
        from_x(zed >= step + 1, zed - 1 - step, 1 + step)
        from_x(zed + 1 + step <= 3, zed + 1 + step, 4 + step)

    def settle_spread(names, condition, at_z, step):
        @pl.when(condition)
        def _():
            for name in names:
                settle_core(name, step, at_z, ex_of(name))
                if name in SPLIT_X:
                    wait_for(place(name, other, at_z, ex), x_send.at[number[name], step])
                    settle_core(name, 7 + step, at_z, 1 - ex)

    def settle_ring(names):
        settle_own(names)
        for name in names:
            wait_for(mine(name, zed, ex_of(name)), y_send.at[number[name]])
        settle_spread(names, zed >= 0, zed, 0)
        for step in range(3):
            settle_spread(names, zed >= step + 1, zed - 1 - step, 1 + step)
            settle_spread(names, zed + 1 + step <= 3, zed + 1 + step, 4 + step)

    settle_ring(("wo",))
    rows_in = own["hid"][...].astype(jnp.float32)
    mixed = rows_in + dense_product(attended_ref[...], full["wo"][...])
    mixed_ref[...] = mixed
    ffn_ref[...] = (mixed * rms_scale(mixed) * gain_second).astype(jnp.bfloat16)

    for name in LATE:
        wait_for(place(name, other), y_recv.at[number[name]])
        to_core(name, 0)
    settle_ring(SPLIT_X)

    def sent(step, direction, condition, at_z):
        @pl.when(condition)
        def _():
            for name in SPREAD:
                wait_for(place(name, other, at_z, ex_of(name)), z_send.at[number[name], direction, step])

    for step in range(3):
        sent(step, 0, (zed < 3) & (zed >= step), zed - step)
        sent(step, 1, (zed > 0) & (zed + step <= 3), zed + step)
    for name in DIRECT:
        wait_for(own[name], y_send.at[number[name]])
    settle_own(LATE)
    for name in LATE:
        wait_for(own[name], y_send.at[number[name]])
        settle_core(name, 0)


def allowed_mask(query_start, key_start, query_segment, key_segment, key_padding):
    shape = (query_segment.shape[0], key_segment.shape[1])
    query_at = query_start + lax.broadcasted_iota(jnp.int32, shape, 0)
    key_at = key_start + lax.broadcasted_iota(jnp.int32, shape, 1)
    distance = query_at - key_at
    return (
        (query_segment == key_segment)
        & (distance >= 0)
        & (distance < WINDOW)
        & ((key_padding == 1) | (distance == 0))
    )


def first_part(hidden, gains, dense, experts, segment, padding):
    tokens, width = hidden.shape
    bfloat, single = jnp.bfloat16, jnp.float32
    wq, wk, wv, wo, sg, su, sd = dense
    blocks = dict(hid=hidden, gains=jnp.pad(gains, ((0, 14), (0, 0))), wq=wq, wk=wk, wv=wv, wo=wo, sg=sg, su=su, sd=sd)
    blocks.update(zip(LATE, experts))
    blocks = [blocks[name] for name in NAMES]
    count = len(NAMES)
    cosine, sine = rotary_tables(4 * tokens, width // HEADS)
    in_hbm, in_vmem = pl.BlockSpec(memory_space=pl.ANY), pl.BlockSpec(memory_space=pltpu.VMEM)
    dma = pltpu.SemaphoreType.DMA
    shape = jax.ShapeDtypeStruct
    out = pl.pallas_call(
        first_kernel,
        out_shape=[shape((4 * block.shape[0], block.shape[1]), block.dtype) for block in blocks]
        + [
            shape((16, width), single),
            shape((4 * tokens, width), bfloat),
            shape((tokens, width), bfloat),
            shape((4 * tokens, width), bfloat),
            shape((4 * tokens, width), bfloat),
            shape((HEADS, tokens, 1), single),
            shape((tokens, width), bfloat),
            shape((tokens, width), single),
            shape((tokens, width), bfloat),
        ],
        in_specs=[in_vmem] * (count + 5),
        out_specs=[in_vmem if name in IN_VMEM else in_hbm for name in NAMES] + [in_vmem] * 9,
        scratch_shapes=[
            dma((count,)),
            dma((count,)),
            dma((count,)),
            dma((count, 7)),
            dma((count, 7)),
            dma((count, 2, 3)),
            dma((count, 2, 3)),
            dma((count, 15)),
            dma((count, 15)),
        ],
        compiler_params=pltpu.CompilerParams(collective_id=0, has_side_effects=True, vmem_limit_bytes=56 << 20),
        cost_estimate=pl.CostEstimate(flops=5000000000, bytes_accessed=47000000, transcendentals=3000000),
    )(
        *blocks,
        segment[None, :],
        segment[:, None],
        padding[None, :],
        jnp.asarray(cosine),
        jnp.asarray(sine),
    )
    return dict(zip(NAMES, out[:count])), out[count:]


def swap(value, axis, bit):
    size = lax.axis_size(axis)
    return lax.ppermute(value, axis, [(index, index ^ bit) for index in range(size)])


def halves(value, bit_set, dim):
    half = value.shape[dim] // 2
    keep = lax.dynamic_slice_in_dim(value, bit_set * half, half, dim)
    give = lax.dynamic_slice_in_dim(value, (1 - bit_set) * half, half, dim)
    return keep, give


def fold(value, axis, bit, dim):
    bit_set = (lax.axis_index(axis) // bit) % 2
    keep, give = halves(value, bit_set, dim)
    return (keep.astype(jnp.float32) + swap(give.astype(jnp.bfloat16), axis, bit).astype(jnp.float32)).astype(jnp.bfloat16)


def unfold(value, axis, bit, dim):
    bit_set = (lax.axis_index(axis) // bit) % 2
    come = swap(value, axis, bit)
    return jnp.where(bit_set == 0, jnp.concatenate([value, come], dim), jnp.concatenate([come, value], dim))


def bits_of(axis):
    size = lax.axis_size(axis)
    return [1 << place for place in range(size.bit_length() - 1)]


def scatter_shards(value):
    count = lax.axis_size("shard")
    blocks = value.reshape((count // 2, 2, value.shape[0] // count) + value.shape[1:])
    blocks = fold(blocks, "shard", 1, 1)[:, 0]
    for bit in reversed(bits_of("shard")[1:]):
        blocks = fold(blocks, "shard", bit, 0)
    return blocks[0]


def sum_plane(value, dim):
    bits = bits_of("expert")
    for bit in bits:
        value = fold(value, "expert", bit, dim)
    for bit in reversed(bits):
        value = unfold(value, "expert", bit, dim)
    return value.astype(jnp.float32)


def shards(
    hidden_in,
    gain_attn,
    gain_ffn,
    w_query,
    w_key,
    w_value,
    w_out,
    shared_gate,
    shared_up,
    shared_down,
    expert_gate,
    expert_up,
    expert_down,
    gate_logits,
    routes,
    segment,
    padding,
    cotangent,
):
    bfloat = jnp.bfloat16
    tokens = hidden_in.shape[1]
    model_width = hidden_in.shape[2]
    head_size = model_width // HEADS
    experts = lax.axis_size("expert")
    capacity = max(2, 2 * tokens * TOP // experts)
    shard_count = lax.axis_size("shard")
    shard_index = lax.axis_index("shard")
    score_scale = head_size ** (-0.5)
    head_shape = (tokens, HEADS, head_size)
    fast = (experts, shard_count, WINDOW) == (8, 4, 4 * tokens)
    dense_own = (w_query, w_key, w_value, w_out, shared_gate, shared_up, shared_down)
    expert_own = (expert_gate[0], expert_up[0], expert_down[0])
    rows_in = hidden_in[0].astype(jnp.float32)
    scale_first = rms_scale(rows_in)
    positions = shard_index * tokens + jnp.arange(tokens, dtype=jnp.int32)
    segment_row, padding_row = segment[0], padding[0]
    query_segment = lax.dynamic_slice_in_dim(segment_row, shard_index * tokens, tokens)
    if fast:
        gain_own = lax.dynamic_update_slice(
            jnp.zeros((2, model_width), bfloat),
            jnp.stack([gain_attn, gain_ffn]),
            (0, shard_index * gain_attn.shape[0]),
        )
        full, rest = first_part(hidden_in[0], gain_own, dense_own, expert_own, segment_row, padding_row)
        gains, normed_ctx, query_low, keys_ctx, values_ctx, log_total, attended, mixed_rows, normed_ffn = rest
        gain_first, gain_second = gains[0], gains[1]
        w_q, w_k, w_v, w_o, s_gate, s_up, s_down = (full[name] for name in ("wq", "wk", "wv", "wo", "sg", "su", "sd"))
        e_gate, e_up, e_down = (full[name] for name in LATE)
        reach, key_start = shard_count - 1, 0
        key_segment, key_padding = segment_row, padding_row
        key_positions = jnp.arange(4 * tokens, dtype=jnp.int32)
        allowed = allowed_mask(shard_index * tokens, 0, query_segment[:, None], key_segment[None], key_padding[None])
    else:
        gather = functools.partial(lax.all_gather, axis_name="shard", tiled=True)
        w_q, w_k, w_v, w_o, s_gate, s_up, s_down = (gather(weight) for weight in dense_own)
        e_gate, e_up, e_down = (gather(weight) for weight in expert_own)
        gain_first, gain_second = (gather(gain).astype(jnp.float32) for gain in (gain_attn, gain_ffn))
        reach = min((WINDOW + tokens - 2) // tokens, shard_count - 1)
        lead_rows, key_rows = reach * tokens, (reach + 1) * tokens
        context = [from_behind(hidden_in[0], "shard", offset) for offset in range(reach, 0, -1)] + [hidden_in[0]]
        context = jnp.concatenate(context, axis=0).astype(jnp.float32)
        normed_ctx = (context * rms_scale(context) * gain_first).astype(bfloat)
        key_positions = (shard_index - reach) * tokens + jnp.arange(key_rows, dtype=jnp.int32)
        query_low = rotate(
            dense_product(normed_ctx[lead_rows:], w_q).reshape(head_shape), positions, 1.0
        ).astype(bfloat)
        keys_ctx = rotate(
            dense_product(normed_ctx, w_k).reshape(key_rows, HEADS, head_size), key_positions, 1.0
        ).astype(bfloat)
        values_ctx = dense_product(normed_ctx, w_v).astype(bfloat)
        segment_ext = jnp.concatenate([jnp.full((lead_rows,), -1, jnp.int32), segment_row])
        padding_ext = jnp.concatenate([jnp.zeros((lead_rows,), jnp.int32), padding_row])
        key_segment = lax.dynamic_slice_in_dim(segment_ext, shard_index * tokens, key_rows)
        key_padding = lax.dynamic_slice_in_dim(padding_ext, shard_index * tokens, key_rows)
        allowed = allowed_mask(
            shard_index * tokens,
            (shard_index - reach) * tokens,
            query_segment[:, None],
            key_segment[None],
            key_padding[None],
        )
    key_rows = (reach + 1) * tokens
    query_heads = query_low.reshape(head_shape)
    keys_all = keys_ctx.reshape(key_rows, HEADS, head_size)
    values_all = values_ctx.reshape(key_rows, HEADS, head_size)

    def score_block():
        raw_scores = (
            jnp.einsum("qhd,khd->hqk", query_heads, keys_all, preferred_element_type=jnp.float32)
            * score_scale
        )
        return jnp.where(allowed[None], raw_scores, neg_fill)

    if not fast:
        scores = score_block()
        top_score = jnp.max(scores, axis=-1, keepdims=True)
        exponent = jnp.exp(scores - top_score)
        exp_total = jnp.sum(exponent, axis=-1, keepdims=True)
        log_total = top_score + jnp.log(exp_total)
        attended = (
            jnp.einsum(
                "hqk,khd->qhd",
                (exponent / exp_total).astype(bfloat),
                values_all,
                preferred_element_type=jnp.float32,
            )
            .astype(bfloat)
            .reshape(tokens, model_width)
        )
        mixed_rows = rows_in + dense_product(attended, w_o)
        normed_ffn = (mixed_rows * rms_scale(mixed_rows) * gain_second).astype(bfloat)
    scale_second = rms_scale(mixed_rows)
    shared_pre = dense_product(normed_ffn, s_gate)
    shared_lin = dense_product(normed_ffn, s_up)
    shared_mid = (jax.nn.silu(shared_pre) * shared_lin).astype(bfloat)
    shared_out = dense_product(shared_mid, s_down)
    route_flat = routes[0].reshape(-1)
    route_total = tokens * TOP
    onehot = (route_flat[:, None] == jnp.arange(experts, dtype=jnp.int32)[None, :]).astype(
        jnp.int32
    )
    slot_rank = jnp.sum((jnp.cumsum(onehot, axis=0) - onehot) * onehot, axis=1)
    places = route_flat * capacity + slot_rank
    slot_table = (
        jnp.full((experts * capacity,), route_total, dtype=jnp.int32)
        .at[places]
        .set(jnp.arange(route_total, dtype=jnp.int32))
    )
    padded_rows = jnp.concatenate([normed_ffn, jnp.zeros((1, model_width), bfloat)], axis=0)
    send_rows = padded_rows[slot_table // TOP].reshape(experts, capacity, model_width)
    received = lax.all_to_all(send_rows, "expert", split_axis=0, concat_axis=0, tiled=True)
    gate_pre = jnp.einsum("sid,df->sif", received, e_gate, preferred_element_type=jnp.float32)
    up_pre = jnp.einsum("sid,df->sif", received, e_up, preferred_element_type=jnp.float32)
    middle = (jax.nn.silu(gate_pre) * up_pre).astype(bfloat)
    result = jnp.einsum("sif,fd->sid", middle, e_down, preferred_element_type=jnp.float32).astype(bfloat)
    returned = lax.all_to_all(result, "expert", split_axis=0, concat_axis=0, tiled=True)
    per_route = (
        returned.reshape(experts * capacity, model_width)[places]
        .astype(jnp.float32)
        .reshape(tokens, TOP, model_width)
    )
    gate_probs = jax.nn.softmax(gate_logits[0], axis=-1)
    routed = jnp.sum(gate_probs[:, :, None] * per_route, axis=1)
    output = (mixed_rows + shared_out + routed).astype(bfloat)
    grad_low = cotangent[0]
    grad_out = grad_low.astype(jnp.float32)
    contrib = jnp.sum(per_route * grad_out[:, None, :], axis=-1)
    logit_grad = gate_probs * (contrib - jnp.sum(gate_probs * contrib, axis=-1, keepdims=True))
    route_grad = (
        (gate_probs[:, :, None] * grad_out[:, None, :])
        .astype(bfloat)
        .reshape(route_total, model_width)
    )
    route_padded = jnp.concatenate([route_grad, jnp.zeros((1, model_width), bfloat)], axis=0)
    send_grad = route_padded[slot_table].reshape(experts, capacity, model_width)
    grad_received = lax.all_to_all(send_grad, "expert", split_axis=0, concat_axis=0, tiled=True)
    grad_middle = jnp.einsum(
        "sid,fd->sif", grad_received, e_down, preferred_element_type=jnp.float32
    )
    grad_gate_pre, grad_up_pre = swiglu_back(grad_middle, gate_pre, up_pre)
    expert_down_grad = jnp.einsum(
        "sif,sid->fd", middle, grad_received, preferred_element_type=jnp.float32
    )
    expert_gate_grad = jnp.einsum(
        "sid,sif->df", received, grad_gate_pre, preferred_element_type=jnp.float32
    )
    expert_up_grad = jnp.einsum(
        "sid,sif->df", received, grad_up_pre, preferred_element_type=jnp.float32
    )
    grad_rows = (
        jnp.einsum("sif,df->sid", grad_gate_pre, e_gate, preferred_element_type=jnp.float32)
        + jnp.einsum("sif,df->sid", grad_up_pre, e_up, preferred_element_type=jnp.float32)
    ).astype(bfloat)
    grad_back = lax.all_to_all(grad_rows, "expert", split_axis=0, concat_axis=0, tiled=True)
    expert_grads = tuple(
        scatter_shards(grad.astype(bfloat))[None].astype(jnp.float32)
        for grad in (expert_gate_grad, expert_up_grad, expert_down_grad)
    )
    grad_routes = (
        grad_back.reshape(experts * capacity, model_width)[places]
        .astype(jnp.float32)
        .reshape(tokens, TOP, model_width)
    )
    grad_normed_ffn = jnp.sum(grad_routes, axis=1)
    grad_shared_mid = product_t(grad_low, s_down)
    grad_shared_pre, grad_shared_lin = swiglu_back(grad_shared_mid, shared_pre, shared_lin)
    shared_down_grad = dense_product(shared_mid.T, grad_low)
    shared_gate_grad = dense_product(normed_ffn.T, grad_shared_pre)
    shared_up_grad = dense_product(normed_ffn.T, grad_shared_lin)
    grad_normed_ffn = (
        grad_normed_ffn + product_t(grad_shared_pre, s_gate) + product_t(grad_shared_lin, s_up)
    )
    gain_ffn_grad = jnp.sum(grad_normed_ffn * mixed_rows * scale_second, axis=0)
    scaled_second = grad_normed_ffn * gain_second
    grad_mixed = (
        grad_out
        + scale_second * scaled_second
        - mixed_rows
        * scale_second**3
        * jnp.mean(scaled_second * mixed_rows, axis=-1, keepdims=True)
    )
    grad_mixed_low = grad_mixed.astype(bfloat)
    w_out_grad = dense_product(attended.T, grad_mixed_low)
    grad_attended = product_t(grad_mixed_low, w_o).astype(bfloat).reshape(head_shape)
    attn_probs = jnp.exp(score_block() - log_total)
    grad_probs = jnp.einsum(
        "qhd,khd->hqk", grad_attended, values_all, preferred_element_type=jnp.float32
    )
    delta_rows = jnp.sum(attn_probs * grad_probs, axis=-1, keepdims=True)
    grad_scores = (attn_probs * (grad_probs - delta_rows)).astype(bfloat)
    grad_query = (
        jnp.einsum("hqk,khd->qhd", grad_scores, keys_all, preferred_element_type=jnp.float32)
        * score_scale
    )
    grad_keys = (
        jnp.einsum("hqk,qhd->khd", grad_scores, query_heads, preferred_element_type=jnp.float32)
        * score_scale
    )
    grad_values = jnp.einsum(
        "hqk,qhd->khd", attn_probs.astype(bfloat), grad_attended, preferred_element_type=jnp.float32
    )
    grad_query_low = rotate(grad_query, positions, -1.0).astype(bfloat).reshape(tokens, model_width)
    grad_key_low = rotate(grad_keys, key_positions, -1.0).astype(bfloat).reshape(key_rows, model_width)
    grad_value_low = grad_values.astype(bfloat).reshape(key_rows, model_width)
    if fast:
        normed = lax.dynamic_slice_in_dim(normed_ctx, shard_index * tokens, tokens)
    else:
        normed = normed_ctx[reach * tokens :]
    w_query_grad = dense_product(normed.T, grad_query_low)
    w_key_grad = dense_product(normed_ctx.T, grad_key_low)
    w_value_grad = dense_product(normed_ctx.T, grad_value_low)
    grad_context = product_t(grad_key_low, w_k) + product_t(grad_value_low, w_v)
    grad_normed = product_t(grad_query_low, w_q)
    if fast:
        grad_normed = grad_normed + scatter_shards(grad_context.astype(bfloat)).astype(jnp.float32)
    else:
        grad_normed = grad_normed + grad_context[reach * tokens :]
        for offset in range(1, reach + 1):
            sent = grad_context[(reach - offset) * tokens :][:tokens].astype(bfloat)
            grad_normed = grad_normed + from_behind(sent, "shard", -offset).astype(jnp.float32)
    gain_attn_grad = jnp.sum(grad_normed * rows_in * scale_first, axis=0)
    scaled_first = grad_normed * gain_first
    input_grad = (
        grad_mixed
        + scale_first * scaled_first
        - rows_in * scale_first**3 * jnp.mean(scaled_first * rows_in, axis=-1, keepdims=True)
    )
    gain_rows = jnp.stack([gain_attn_grad, gain_ffn_grad], axis=1).astype(bfloat)
    gain_total = lax.psum(scatter_shards(gain_rows), "expert").astype(jnp.float32)
    attn_grads = jnp.stack([w_query_grad, w_key_grad, w_value_grad, w_out_grad]).astype(bfloat)
    attn_rows = scatter_shards(attn_grads.transpose(1, 0, 2)).transpose(1, 0, 2)
    attn_total = sum_plane(attn_rows.reshape(-1, model_width), 0).reshape(attn_rows.shape)
    return (
        output[None],
        input_grad[None],
        logit_grad[None],
        gain_total[:, 0],
        gain_total[:, 1],
        attn_total[0],
        attn_total[1],
        attn_total[2],
        attn_total[3],
        sum_plane(scatter_shards(shared_gate_grad.astype(bfloat)), 1),
        sum_plane(scatter_shards(shared_up_grad.astype(bfloat)), 1),
        sum_plane(scatter_shards(shared_down_grad.astype(bfloat)), 0),
        expert_grads[0],
        expert_grads[1],
        expert_grads[2],
    )


def solution(mesh):
    placed = (
        P("expert", "shard", None),
        P("shard"),
        P("shard"),
        P("shard", None),
        P("shard", None),
        P("shard", None),
        P("shard", None),
        P("shard", None),
        P("shard", None),
        P("shard", None),
        P("expert", "shard", None),
        P("expert", "shard", None),
        P("expert", "shard", None),
        P("expert", "shard", None),
        P("expert", "shard", None),
        P("expert", None),
        P("expert", None),
        P("expert", "shard", None),
    )
    return jax.shard_map(
        shards,
        mesh=mesh,
        in_specs=placed,
        out_specs=(
            P("expert", "shard", None),
            P("expert", "shard", None),
            P("expert", "shard", None),
            P("shard"),
            P("shard"),
            P("shard", None),
            P("shard", None),
            P("shard", None),
            P("shard", None),
            P("shard", None),
            P("shard", None),
            P("shard", None),
            P("expert", "shard", None),
            P("expert", "shard", None),
            P("expert", "shard", None),
        ),
        check_vma=False,
    )
```

```python
import functools

import jax
import jax.numpy as jnp
import numpy as np
from jax import lax
from jax.experimental import pallas as pl
from jax.experimental.pallas import tpu as pltpu
from jax.sharding import PartitionSpec as P

HEADS = 12
TOP = 2
WINDOW = 1024
MESH = pl.DeviceIdType.MESH
norm_eps = 1e-06
neg_fill = -1e30
rope_base = 10000.0

DIRECT = ("hid", "gains")
EARLY = ("wk", "wv", "wq")
SPREAD = ("wo", "sg", "su", "sd")
SPLIT_X = ("sg", "su", "sd")
LATE = ("eg", "eu", "ed")
NAMES = DIRECT + EARLY + SPREAD + LATE
PASSING = DIRECT + ("sg", "su", "sd")
KEPT = EARLY + ("wo",) + LATE


def dense_product(left, right):
    return jnp.dot(left, right, preferred_element_type=jnp.float32)


def product_t(left, right):
    return lax.dot_general(left, right, (((1,), (1,)), ((), ())), preferred_element_type=jnp.float32)


def t_product(left, right):
    return lax.dot_general(left, right, (((0,), (0,)), ((), ())), preferred_element_type=jnp.float32)


def rms_scale(values):
    return lax.rsqrt(jnp.mean(values * values, axis=-1, keepdims=True) + norm_eps)


def rotary_tables(length, head_size):
    half = head_size // 2
    frequency = np.float32(rope_base) ** (-np.arange(half, dtype=np.float32) / np.float32(half))
    angles = np.arange(length, dtype=np.float32)[:, None] * frequency[None, :]
    cosine, sine = np.cos(angles).astype(np.float32), np.sin(angles).astype(np.float32)
    return np.concatenate([cosine] * 4, axis=1), np.concatenate([-sine, sine] * 2, axis=1)


def rotate_pair(values, cosine, sine):
    lane = lax.broadcasted_iota(jnp.int32, values.shape, 1)
    partner = jnp.where(lane % 64 < 32, pltpu.roll(values, 96, 1), pltpu.roll(values, 32, 1))
    return values * cosine + partner * sine


def rotate(values, positions, direction):
    half_size = values.shape[-1] // 2
    frequency = rope_base ** (-jnp.arange(half_size, dtype=jnp.float32) / half_size)
    angles = positions.astype(jnp.float32)[:, None] * frequency[None, :]
    cosine = jnp.cos(angles)[:, None, :]
    sine_part = direction * jnp.sin(angles)[:, None, :]
    first_half = values[..., :half_size]
    second_half = values[..., half_size:]
    return jnp.concatenate(
        [
            first_half * cosine - second_half * sine_part,
            second_half * cosine + first_half * sine_part,
        ],
        axis=-1,
    )


def swiglu_back(grad_middle, gate_pre, up_pre):
    sigmoid_gate = jax.nn.sigmoid(gate_pre)
    activated = gate_pre * sigmoid_gate
    grad_gate = grad_middle * up_pre * sigmoid_gate * (1.0 + gate_pre * (1.0 - sigmoid_gate))
    grad_up = grad_middle * activated
    return (grad_gate.astype(jnp.bfloat16), grad_up.astype(jnp.bfloat16))


def from_behind(value, axis, steps):
    count = lax.axis_size(axis)
    first, last = (max(0, -steps), min(count, count - steps))
    return lax.ppermute(value, axis, [(source, source + steps) for source in range(first, last)])


def send(source, target, send_sem, recv_sem, peer):
    pltpu.make_async_remote_copy(
        src_ref=source,
        dst_ref=target,
        send_sem=send_sem,
        recv_sem=recv_sem,
        device_id=peer,
        device_id_type=MESH,
    ).start()


def wait_for(ref, sem):
    pltpu.make_async_copy(ref, ref, sem).wait()


def first_kernel(*refs):
    count = len(NAMES)
    own = dict(zip(NAMES, refs[:count]))
    segment_row, segment_col, padding_row, cosine_ref, sine_ref, cot_ref, logit_ref, route_ref, lane_route_ref = refs[
        count : count + 9
    ]
    refs = refs[count + 9 :]
    full = dict(zip(KEPT, refs[: len(KEPT)]))
    refs = refs[len(KEPT) :]
    gain_ref, normed_ref, query_ref, key_ref, value_ref, lse_ref, attended_ref, mixed_ref, ffn_ref = refs[:9]
    rows_got, grads_got, shared_ref, ffn_grad_ref, *shared_work = refs[9:16]
    refs = refs[16:]
    full.update(zip(PASSING, refs[: len(PASSING)]))
    refs = refs[len(PASSING) :]
    shared_core = refs[:3]
    refs = refs[3:]
    rows_put, grads_put = refs[:2]
    (own_sem, y_send, y_recv, x_send, x_recv, z_send, z_recv, core_send, core_recv) = refs[2:11]
    row_sems, grad_sems, share_send, share_recv = refs[11:13], refs[13:15], refs[15], refs[16]
    number = {name: index for index, name in enumerate(NAMES)}
    expert, shard = (lax.axis_index("expert"), lax.axis_index("shard"))
    zed, ex = (expert // 2, expert % 2)
    other = (shard + 2) % 4
    y_peer = (expert, other)
    core_peer = (expert, shard + 1 - 2 * (shard % 2))
    x_peer = (expert + 1 - 2 * ex, shard)
    z_up, z_down = (((expert + 2) % 8, shard), ((expert + 6) % 8, shard))

    barrier = pltpu.get_barrier_semaphore()
    for peer in (y_peer, core_peer) + tuple(((expert + step) % 8, shard) for step in range(1, 8)):
        pl.semaphore_signal(barrier, inc=1, device_id=peer, device_id_type=MESH)
    pl.semaphore_wait(barrier, 9)

    def part_of(block, base, name, at_z, at_x):
        rows = own[name].shape[0]
        if at_z is None and at_x is None:
            return block.at[pl.ds(base, rows)]
        if name in EARLY:
            return block.at[pl.ds(base + at_x * (rows // 2), rows // 2)]
        if name in ("sg", "su"):
            half = block.shape[1] // 8
            return block.at[pl.ds(base, rows), pl.ds((at_z * 2 + at_x) * half, half)]
        size = rows // 4
        if name == "sd":
            return block.at[pl.ds(base + at_z * size + at_x * (size // 2), size // 2)]
        return block.at[pl.ds(base + at_z * size, size)]

    def place(name, slot, at_z=None, at_x=None):
        return part_of(full[name], slot * own[name].shape[0], name, at_z, at_x)

    def mine(name, at_z=None, at_x=None):
        return part_of(own[name], 0, name, at_z, at_x)

    def ex_of(name):
        return ex if name in SPLIT_X else None

    def cross(name, at_z=None, at_x=None):
        n = number[name]
        send(mine(name, at_z, at_x), place(name, shard, at_z, at_x), y_send.at[n], y_recv.at[n], y_peer)

    def to_core(name, step, at_z=None, at_x=None):
        n = number[name]
        part = place(name, other, at_z, at_x)
        send(part, part, core_send.at[n, 1 + step], core_recv.at[n, 1 + step], core_peer)

    far = shard + 1 - 2 * (shard % 2)
    far_other = (far + 2) % 4

    def settle_own(names):
        for name in names:
            n = number[name]
            pltpu.make_async_copy(own[name], place(name, shard), own_sem.at[n]).wait()
            wait_for(place(name, far), core_recv.at[n, 0])
            wait_for(own[name], core_send.at[n, 0])

    def settle_core(name, step, at_z=None, at_x=None):
        n = number[name]
        wait_for(place(name, far_other, at_z, at_x), core_recv.at[n, 1 + step])
        wait_for(place(name, other, at_z, at_x), core_send.at[n, 1 + step])

    for name in DIRECT:
        cross(name)
    for name in EARLY:
        cross(name, None, ex)
    for name in SPREAD:
        cross(name, zed, ex_of(name))
    for name in NAMES:
        n = number[name]
        send(own[name], place(name, shard), core_send.at[n, 0], core_recv.at[n, 0], core_peer)
        pltpu.make_async_copy(own[name], place(name, shard), own_sem.at[n]).start()

    for name in DIRECT:
        wait_for(place(name, other), y_recv.at[number[name]])
        to_core(name, 0)
    for name in EARLY:
        n = number[name]
        part = place(name, other, None, ex)
        wait_for(part, y_recv.at[n])
        send(part, part, x_send.at[n, 0], x_recv.at[n, 0], x_peer)
        to_core(name, 0, None, ex)
    for name in LATE:
        cross(name)

    def on_part(name, at_z, step):
        n = number[name]
        part = place(name, other, at_z, ex_of(name))
        if name in SPLIT_X:
            send(part, part, x_send.at[n, step], x_recv.at[n, step], x_peer)
        to_core(name, step, at_z, ex_of(name))

    def forward(step, direction, condition, at_z, peer):
        @pl.when(condition)
        def _():
            for name in SPREAD:
                n = number[name]
                part = place(name, other, at_z, ex_of(name))
                send(part, part, z_send.at[n, direction, step], z_recv.at[n, direction, step], peer)

    def arrive(step, direction, condition, at_z):
        @pl.when(condition)
        def _():
            for name in SPREAD:
                n = number[name]
                wait_for(place(name, other, at_z, ex_of(name)), z_recv.at[n, direction, step])
                on_part(name, at_z, 1 + direction * 3 + step)

    def ring_send(step):
        forward(step, 0, (zed < 3) & (zed >= step), zed - step, z_up)
        forward(step, 1, (zed > 0) & (zed + step <= 3), zed + step, z_down)

    def ring_arrive(step):
        arrive(step, 0, zed >= step + 1, zed - 1 - step)
        arrive(step, 1, zed + 1 + step <= 3, zed + 1 + step)

    for name in SPREAD:
        wait_for(place(name, other, zed, ex_of(name)), y_recv.at[number[name]])
    ring_send(0)
    for name in SPREAD:
        on_part(name, zed, 0)

    settle_own(DIRECT)
    for name in DIRECT:
        settle_core(name, 0)
    tokens, width = own["hid"].shape
    gain_rows = sum(full["gains"][pl.ds(slot * 16, 16), :].astype(jnp.float32) for slot in range(4))
    gain_ref[...] = gain_rows
    gain_first, gain_second = gain_rows[0:1], gain_rows[1:2]

    def norm_block(block, carry):
        rows = pl.ds(pl.multiple_of(block * tokens, tokens), tokens)
        values = full["hid"][rows, :].astype(jnp.float32)
        normed_ref[rows, :] = (values * rms_scale(values) * gain_first).astype(jnp.bfloat16)
        return carry

    lax.fori_loop(0, 4, norm_block, 0)

    for name in EARLY:
        wait_for(place(name, other, None, 1 - ex), x_recv.at[number[name], 0])
        to_core(name, 1, None, 1 - ex)
    settle_own(EARLY)
    for name in EARLY:
        settle_core(name, 0, None, ex)
        settle_core(name, 1, None, 1 - ex)
        wait_for(mine(name, None, ex), y_send.at[number[name]])
        wait_for(place(name, other, None, ex), x_send.at[number[name], 0])

    lane_routes = lane_route_ref[...]
    expert_at = lax.broadcasted_iota(jnp.int32, (8, tokens), 0)
    named = ((lane_routes[0:1] == expert_at) | (lane_routes[1:2] == expert_at)).astype(jnp.float32)
    before = lax.broadcasted_iota(jnp.int32, (tokens, tokens), 0) < lax.broadcasted_iota(jnp.int32, (tokens, tokens), 1)
    rank = dense_product(named.astype(jnp.bfloat16), before.astype(jnp.bfloat16))
    slot_of = jnp.where(named > 0.0, rank, -1.0).astype(jnp.int32)
    capacity = rows_put.shape[1]

    def picks(target):
        slot_at = lax.broadcasted_iota(jnp.int32, (capacity, tokens), 0)
        return slot_at == slot_of[target : target + 1]

    def dispatch(put, got, sems):
        for step in range(1, 8):
            target = (expert + step) % 8
            send(put.at[target], got.at[expert], sems[0].at[step], sems[1].at[step], (target, shard))
        got[pl.ds(expert, 1)] = put[pl.ds(expert, 1)]

    def settle_dispatch(put, got, sems):
        for step in range(1, 8):
            wait_for(put.at[(expert + step) % 8], sems[0].at[step])
            wait_for(got.at[(expert + 8 - step) % 8], sems[1].at[step])

    gate_probs = gate_columns(logit_ref[...])
    cot = cot_ref[...]
    route_grads = [(gate * cot.astype(jnp.float32)).astype(jnp.bfloat16) for gate in gate_probs]
    for target in range(8):
        chosen = picks(target)
        grads_put[target] = sum(
            dense_product((chosen & (lane_routes[k : k + 1] == target)).astype(jnp.bfloat16), route_grads[k])
            for k in range(TOP)
        ).astype(jnp.bfloat16)
    dispatch(grads_put, grads_got, grad_sems)

    def key_block(block, carry):
        rows = pl.ds(pl.multiple_of(block * tokens, tokens), tokens)
        normed = normed_ref[rows, :]
        value_ref[rows, :] = dense_product(normed, full["wv"][...]).astype(jnp.bfloat16)
        raw = dense_product(normed, full["wk"][...])
        cosine, sine = cosine_ref[rows, :], sine_ref[rows, :]
        for start in range(0, width, 128):
            key_ref[rows, start : start + 128] = rotate_pair(raw[:, start : start + 128], cosine, sine).astype(jnp.bfloat16)
        return carry

    lax.fori_loop(0, 4, key_block, 0)
    ring_arrive(0)
    ring_send(1)
    here = pl.ds(pl.multiple_of(shard * tokens, tokens), tokens)
    raw = dense_product(normed_ref[here, :], full["wq"][...])
    cosine, sine = cosine_ref[here, :], sine_ref[here, :]
    for start in range(0, width, 128):
        query_ref[:, start : start + 128] = rotate_pair(raw[:, start : start + 128], cosine, sine).astype(jnp.bfloat16)

    def head_pair(pair, carry):
        lanes = pl.ds(pl.multiple_of(pair * 128, 128), 128)
        query, keys, values = query_ref[:, lanes], key_ref[:, lanes], value_ref[:, lanes]
        allowed = allowed_mask(shard * tokens, 0, segment_col[here, :], segment_row[...], padding_row[...])
        lane = lax.broadcasted_iota(jnp.int32, query.shape, 1)
        results = []
        for half in range(2):
            chosen = (lane >= 64) if half else (lane < 64)
            scores = product_t(jnp.where(chosen, query, jnp.zeros_like(query)), keys) * 0.125
            scores = jnp.where(allowed, scores, neg_fill)
            top_score = jnp.max(scores, axis=-1, keepdims=True)
            exponent = jnp.exp(scores - top_score)
            exp_total = jnp.sum(exponent, axis=-1, keepdims=True)
            lse_ref[2 * pair + half] = top_score + jnp.log(exp_total)
            results.append(dense_product((exponent / exp_total).astype(jnp.bfloat16), values))
        attended_ref[:, lanes] = jnp.where(lane < 64, results[0], results[1]).astype(jnp.bfloat16)
        return carry

    lax.fori_loop(0, 3, head_pair, 0)
    ring_arrive(1)
    ring_send(2)
    lax.fori_loop(3, 6, head_pair, 0)
    ring_arrive(2)

    def from_x(condition, at_z, step):
        @pl.when(condition)
        def _():
            for name in SPLIT_X:
                wait_for(place(name, other, at_z, 1 - ex), x_recv.at[number[name], step])
                to_core(name, 7 + step, at_z, 1 - ex)

    from_x(zed >= 0, zed, 0)
    for step in range(3):
        from_x(zed >= step + 1, zed - 1 - step, 1 + step)
        from_x(zed + 1 + step <= 3, zed + 1 + step, 4 + step)

    def settle_spread(names, condition, at_z, step):
        @pl.when(condition)
        def _():
            for name in names:
                settle_core(name, step, at_z, ex_of(name))
                if name in SPLIT_X:
                    wait_for(place(name, other, at_z, ex), x_send.at[number[name], step])
                    settle_core(name, 7 + step, at_z, 1 - ex)

    def settle_ring(names):
        settle_own(names)
        for name in names:
            wait_for(mine(name, zed, ex_of(name)), y_send.at[number[name]])
        settle_spread(names, zed >= 0, zed, 0)
        for step in range(3):
            settle_spread(names, zed >= step + 1, zed - 1 - step, 1 + step)
            settle_spread(names, zed + 1 + step <= 3, zed + 1 + step, 4 + step)

    settle_ring(("wo",))
    rows_in = own["hid"][...].astype(jnp.float32)
    mixed = rows_in + dense_product(attended_ref[...], full["wo"][...])
    mixed_ref[...] = mixed
    ffn = (mixed * rms_scale(mixed) * gain_second).astype(jnp.bfloat16)
    ffn_ref[...] = ffn
    for target in range(8):
        rows_put[target] = dense_product(picks(target).astype(jnp.bfloat16), ffn).astype(jnp.bfloat16)
    dispatch(rows_put, rows_got, row_sems)

    settle_ring(SPLIT_X)

    def sent(step, direction, condition, at_z):
        @pl.when(condition)
        def _():
            for name in SPREAD:
                wait_for(place(name, other, at_z, ex_of(name)), z_send.at[number[name], direction, step])

    for step in range(3):
        sent(step, 0, (zed < 3) & (zed >= step), zed - step)
        sent(step, 1, (zed > 0) & (zed + step <= 3), zed + step)
    shared_ref[...] = jnp.zeros_like(shared_ref)
    ffn_grad_ref[...] = jnp.zeros_like(ffn_grad_ref)

    def shared_block(block, carry):
        cut = pl.ds(pl.multiple_of(block * 512, 512), 512)
        normed = ffn_ref[...]
        gate, up, down = full["sg"][:, cut], full["su"][:, cut], full["sd"][cut, :]
        pre, lin = dense_product(normed, gate), dense_product(normed, up)
        middle = (jax.nn.silu(pre) * lin).astype(jnp.bfloat16)
        shared_ref[...] += dense_product(middle, down)
        pre_grad, lin_grad = swiglu_back(product_t(cot_ref[...], down), pre, lin)
        ffn_grad_ref[...] += product_t(pre_grad, gate) + product_t(lin_grad, up)
        full["sg"][:, cut] = t_product(normed, pre_grad).astype(jnp.bfloat16)
        full["su"][:, cut] = t_product(normed, lin_grad).astype(jnp.bfloat16)
        full["sd"][cut, :] = t_product(middle, cot_ref[...]).astype(jnp.bfloat16)
        return carry

    lax.fori_loop(0, full["sg"].shape[1] // 512, shared_block, 0)

    def shard_rows(ref, y_of, core_of):
        rows = ref.shape[0] // 4
        return ref.at[pl.ds((y_of * 2 + core_of) * rows, rows)]

    core = shard % 2
    shared_grads = (full["sg"], full["su"], full["sd"])
    for index in range(3):
        for y_of in range(2):
            send(
                shard_rows(shared_grads[index], y_of, 1 - core),
                shared_core[index].at[y_of],
                share_send.at[index, y_of],
                share_recv.at[index, y_of],
                core_peer,
            )

    for name in LATE:
        wait_for(place(name, other), y_recv.at[number[name]])
        to_core(name, 0)

    for name in DIRECT:
        wait_for(own[name], y_send.at[number[name]])
    settle_own(LATE)
    for name in LATE:
        wait_for(own[name], y_send.at[number[name]])
        settle_core(name, 0)
    for index in range(3):
        for y_of in range(2):
            wait_for(shared_core[index].at[y_of], share_recv.at[index, y_of])
            add_rows(shared_work[index].at[y_of], shard_rows(shared_grads[index], y_of, core), shared_core[index].at[y_of])
            wait_for(shard_rows(shared_grads[index], y_of, 1 - core), share_send.at[index, y_of])
    settle_dispatch(grads_put, grads_got, grad_sems)
    settle_dispatch(rows_put, rows_got, row_sems)


def gate_columns(logits):
    first, second = logits[:, 0:1], logits[:, 1:2]
    top = jnp.maximum(first, second)
    first, second = jnp.exp(first - top), jnp.exp(second - top)
    total = first + second
    return first / total, second / total


def allowed_mask(query_start, key_start, query_segment, key_segment, key_padding):
    shape = (query_segment.shape[0], key_segment.shape[1])
    query_at = query_start + lax.broadcasted_iota(jnp.int32, shape, 0)
    key_at = key_start + lax.broadcasted_iota(jnp.int32, shape, 1)
    distance = query_at - key_at
    return (
        (query_segment == key_segment)
        & (distance >= 0)
        & (distance < WINDOW)
        & ((key_padding == 1) | (distance == 0))
    )


def first_part(hidden, gains, dense, experts, segment, padding, cotangent, logits, routes):
    tokens, width = hidden.shape
    bfloat, single = jnp.bfloat16, jnp.float32
    wq, wk, wv, wo, sg, su, sd = dense
    blocks = dict(hid=hidden, gains=jnp.pad(gains, ((0, 14), (0, 0))), wq=wq, wk=wk, wv=wv, wo=wo, sg=sg, su=su, sd=sd)
    blocks.update(zip(LATE, experts))
    blocks = [blocks[name] for name in NAMES]
    count = len(NAMES)
    cosine, sine = rotary_tables(4 * tokens, width // HEADS)
    in_hbm, in_vmem = pl.BlockSpec(memory_space=pl.ANY), pl.BlockSpec(memory_space=pltpu.VMEM)
    dma = pltpu.SemaphoreType.DMA
    shape = jax.ShapeDtypeStruct
    whole = {name: shape((4 * block.shape[0], block.shape[1]), block.dtype) for name, block in zip(NAMES, blocks)}
    middle = sg.shape[1]
    capacity = max(2, 2 * tokens * TOP // 8)
    routed = (8, capacity, width)
    halved = [(2,) + block.shape for block in (sg, su, sd)]
    out = pl.pallas_call(
        first_kernel,
        out_shape=[whole[name] for name in KEPT]
        + [
            shape((16, width), single),
            shape((4 * tokens, width), bfloat),
            shape((tokens, width), bfloat),
            shape((4 * tokens, width), bfloat),
            shape((4 * tokens, width), bfloat),
            shape((HEADS, tokens, 1), single),
            shape((tokens, width), bfloat),
            shape((tokens, width), single),
            shape((tokens, width), bfloat),
            shape(routed, bfloat),
            shape(routed, bfloat),
            shape((tokens, width), single),
            shape((tokens, width), single),
        ]
        + [shape(one, bfloat) for one in halved],
        in_specs=[in_vmem] * (count + 9),
        out_specs=[in_hbm if name in LATE else in_vmem for name in KEPT] + [in_vmem] * 16,
        scratch_shapes=[pltpu.VMEM(whole[name].shape, whole[name].dtype) for name in PASSING]
        + [pltpu.VMEM(one, bfloat) for one in halved]
        + [pltpu.VMEM(routed, bfloat)] * 2
        + [
            dma((count,)),
            dma((count,)),
            dma((count,)),
            dma((count, 7)),
            dma((count, 7)),
            dma((count, 2, 3)),
            dma((count, 2, 3)),
            dma((count, 15)),
            dma((count, 15)),
        ]
        + [dma((8,))] * 4
        + [dma((3, 2))] * 2,
        compiler_params=pltpu.CompilerParams(collective_id=0, has_side_effects=True, vmem_limit_bytes=60 << 20),
        cost_estimate=pl.CostEstimate(flops=15000000000, bytes_accessed=47000000, transcendentals=3000000),
    )(
        *blocks,
        segment[None, :],
        segment[:, None],
        padding[None, :],
        jnp.asarray(cosine),
        jnp.asarray(sine),
        cotangent,
        logits,
        routes,
        routes.T,
    )
    return dict(zip(KEPT, out)), out[len(KEPT) :]


def add_into(target, first, second):
    rows = first.shape[-2]
    strip = 64

    def body(index, carry):
        at = pl.ds(pl.multiple_of(index * strip, strip), strip)
        for lead in range(first.shape[0]):
            total = first[lead, at, :].astype(jnp.float32) + second[lead, at, :].astype(jnp.float32)
            target[lead, at, :] = total.astype(target.dtype)
        return carry

    lax.fori_loop(0, rows // strip, body, 0)


class PlaneSum:
    def __init__(self, work, out, receive, send_sem, recv_sem, bits, peers, order, by_rows):
        self.work, self.out, self.receive = work, out, receive
        self.send_sem, self.recv_sem, self.bits, self.peers, self.order = send_sem, recv_sem, bits, peers, order
        self.by_rows = by_rows
        self.whole_y = True
        self.size = work.shape[1 if by_rows else 2]
        self.offset = 0
        self.trail = []

    def region(self, ref, offset, size, y=None):
        lead = pl.ds(0, ref.shape[0]) if y is None else pl.ds(y, 1)
        unit = 16 if self.by_rows else 128
        at = pl.ds(offset if isinstance(offset, int) else pl.multiple_of(offset, unit), size)
        return ref.at[lead, at, :] if self.by_rows else ref.at[lead, :, at]

    def halves(self, axis):
        bit = self.bits[axis]
        if axis == "y":
            return (self.offset, self.size, bit), (self.offset, self.size, 1 - bit)
        half = self.size // 2
        y = None if self.whole_y else self.bits["y"]
        return (self.offset + bit * half, half, y), (self.offset + (1 - bit) * half, half, y)

    def start(self, step):
        axis = self.order[step]
        _, give = self.halves(axis)
        send(
            self.region(self.work, *give),
            self.receive[step],
            self.send_sem.at[step],
            self.recv_sem.at[step],
            self.peers[axis],
        )

    def finish(self, step):
        axis = self.order[step]
        keep, give = self.halves(axis)
        wait_for(self.receive[step], self.recv_sem.at[step])
        last = step == len(self.order) - 1
        kept = self.region(self.work, *keep)
        target = self.region(self.out, keep[0], keep[1]) if last else kept
        add_into(target, kept, self.receive[step])
        wait_for(self.region(self.work, *give), self.send_sem.at[step])
        if axis == "y":
            self.whole_y = False
        else:
            self.trail.append((axis, self.offset, self.size))
            self.offset, self.size = keep[0], keep[1]

    def back_start(self, step):
        axis, _, _ = self.trail[-1 - step]
        part = self.region(self.out, self.offset, self.size)
        at = len(self.order) + step
        send(part, part, self.send_sem.at[at], self.recv_sem.at[at], self.peers[axis])

    def back_finish(self, step):
        axis, offset, size = self.trail[-1 - step]
        at = len(self.order) + step
        half = size // 2
        wait_for(self.region(self.out, self.offset, self.size), self.send_sem.at[at])
        wait_for(self.region(self.out, offset + (1 - self.bits[axis]) * half, half), self.recv_sem.at[at])
        self.offset, self.size = offset, size


def receive_shapes(shape, order, by_rows):
    lead, rows, columns = shape
    result = []
    for axis in order:
        if axis == "y":
            lead = 1
        elif by_rows:
            rows //= 2
        else:
            columns //= 2
        result.append((lead, rows, columns))
    return result


SHARED_ORDER = (("y", "x", "z1", "z2"), ("x", "z1", "y", "z2"), ("z1", "y", "x", "z2"))


def plane_places():
    expert, shard = (lax.axis_index("expert"), lax.axis_index("shard"))
    zed, ex, why, core = (expert // 2, expert % 2, shard // 2, shard % 2)
    bits = {"x": ex, "z1": zed % 2, "z2": zed // 2, "y": why}
    peers = {
        "x": (expert + 1 - 2 * ex, shard),
        "z1": (expert + 2 - 4 * (zed % 2), shard),
        "z2": ((expert + 4) % 8, shard),
        "y": (expert, (shard + 2) % 4),
        "core": (expert, shard + 1 - 2 * core),
    }
    return expert, shard, zed, core, bits, peers


def enter(peers):
    barrier = pltpu.get_barrier_semaphore()
    for peer in peers:
        pl.semaphore_signal(barrier, inc=1, device_id=peer, device_id_type=MESH)
    pl.semaphore_wait(barrier, len(peers))


def second_kernel(*refs):
    rows_ref, grads_ref, *weights_in = refs[:5]
    shared_in = refs[5:8]
    rows_back, grads_back = refs[8:10]
    expert_out, shared_out = refs[10:13], refs[13:16]
    weights, shared_work = refs[16:19], refs[19:22]
    rows_put, grads_put, middle_ref, pre_ref, lin_ref, out_sum, grad_sum = refs[22:29]
    expert_core, expert_y = refs[29:32], refs[32:35]
    receive = [refs[35 + 4 * index : 39 + 4 * index] for index in range(3)]
    load_sem, shared_sem, out_send, out_recv, grad_send, grad_recv, core_send, core_recv, y_send, y_recv, sum_send, sum_recv = refs[47:]
    expert, shard, zed, core, bits, peers = plane_places()
    why = bits["y"]
    for index in range(3):
        pltpu.make_async_copy(weights_in[index], weights[index], load_sem.at[index]).start()
        pltpu.make_async_copy(shared_in[index], shared_work[index], shared_sem.at[index]).start()
    enter((peers["y"], peers["core"]) + tuple(((expert + step) % 8, shard) for step in range(1, 8)))
    sums = [
        PlaneSum(
            shared_work[index],
            shared_out[index],
            receive[index],
            sum_send.at[index],
            sum_recv.at[index],
            bits,
            peers,
            SHARED_ORDER[index],
            index == 2,
        )
        for index in range(3)
    ]
    for index in range(3):
        pltpu.make_async_copy(shared_in[index], shared_work[index], shared_sem.at[index]).wait()
        sums[index].start(0)
    for index in range(3):
        pltpu.make_async_copy(weights_in[index], weights[index], load_sem.at[index]).wait()

    _, capacity, width = rows_ref.shape
    gate_ref, up_ref, down_ref = weights
    middle = gate_ref.shape[1]
    cuts = middle // 512

    def block(z_from):
        pair = pl.ds(2 * z_from, 2)
        rows = rows_ref[pair].reshape(2 * capacity, width)
        grads = grads_ref[pair].reshape(2 * capacity, width)
        here = pl.ds(pl.multiple_of(z_from * 2 * capacity, 2 * capacity), 2 * capacity)
        out_sum[...] = jnp.zeros_like(out_sum)
        grad_sum[...] = jnp.zeros_like(grad_sum)

        def body(index, carry):
            cut = pl.ds(pl.multiple_of(index * 512, 512), 512)
            gate, up, down = gate_ref[:, cut], up_ref[:, cut], down_ref[cut, :]
            pre, lin = dense_product(rows, gate), dense_product(rows, up)
            mid = (jax.nn.silu(pre) * lin).astype(jnp.bfloat16)
            out_sum[...] += dense_product(mid, down)
            pre_grad, lin_grad = swiglu_back(product_t(grads, down), pre, lin)
            grad_sum[...] += product_t(pre_grad, gate) + product_t(lin_grad, up)
            middle_ref[here, cut] = mid
            pre_ref[here, cut] = pre_grad
            lin_ref[here, cut] = lin_grad
            return carry

        lax.fori_loop(0, cuts, body, 0)
        rows_put[pair] = out_sum[...].astype(jnp.bfloat16).reshape(2, capacity, width)
        grads_put[pair] = grad_sum[...].astype(jnp.bfloat16).reshape(2, capacity, width)
        for side in range(2):
            source = 2 * z_from + side

            @pl.when(source != expert)
            def _():
                send(grads_put.at[source], grads_back.at[expert], grad_send.at[source], grad_recv.at[expert], (source, shard))
                send(rows_put.at[source], rows_back.at[expert], out_send.at[source], out_recv.at[expert], (source, shard))

            @pl.when(source == expert)
            def _():
                rows_back[pl.ds(source, 1)] = rows_put[pl.ds(source, 1)]
                grads_back[pl.ds(source, 1)] = grads_put[pl.ds(source, 1)]

    z_order = ((zed + 2) % 4, 3 - zed, zed + 1 - 2 * (zed % 2), zed)
    for step in range(4):
        block(z_order[step])
        for one in sums:
            one.finish(step)
            if step < 3:
                one.start(step + 1)
            else:
                one.back_start(0)

    rows_all, grads_all = rows_ref, grads_ref

    def weight_grad(index):
        def body(step, carry):
            cut = pl.ds(pl.multiple_of(step * 512, 512), 512)
            if index == 2:
                left, right = middle_ref[:, cut], grads_all[...].reshape(8 * capacity, width)
                down_ref[cut, :] = t_product(left, right).astype(jnp.bfloat16)
            else:
                left, right = rows_all[...].reshape(8 * capacity, width), (pre_ref, lin_ref)[index][:, cut]
                weights[index][:, cut] = t_product(left, right).astype(jnp.bfloat16)
            return carry

        lax.fori_loop(0, cuts, body, 0)

    def shard_rows(index, y_of, core_of):
        rows = weights[index].shape[0] // 4
        return weights[index].at[pl.ds((y_of * 2 + core_of) * rows, rows)]

    def core_start(index):
        for y_of in range(2):
            send(
                shard_rows(index, y_of, 1 - core),
                expert_core[index].at[y_of],
                core_send.at[index, y_of],
                core_recv.at[index, y_of],
                peers["core"],
            )

    def core_finish(index):
        for y_of in range(2):
            wait_for(expert_core[index].at[y_of], core_recv.at[index, y_of])
            wait_for(shard_rows(index, y_of, 1 - core), core_send.at[index, y_of])
        for y_of in range(2):
            kept = shard_rows(index, y_of, core)
            add_rows(expert_core[index].at[y_of], kept, expert_core[index].at[y_of])
        send(expert_core[index].at[1 - why], expert_y[index], y_send.at[index], y_recv.at[index], peers["y"])

    def y_finish(index):
        wait_for(expert_y[index], y_recv.at[index])
        add_rows(expert_out[index], expert_core[index].at[why], expert_y[index])
        wait_for(expert_core[index].at[1 - why], y_send.at[index])

    weight_grad(0)
    core_start(0)
    weight_grad(1)
    core_finish(0)
    core_start(1)
    for one in sums:
        one.back_finish(0)
        one.back_start(1)
    weight_grad(2)
    core_finish(1)
    core_start(2)
    for one in sums:
        one.back_finish(1)
        one.back_start(2)
    core_finish(2)
    for one in sums:
        one.back_finish(2)
    for step in range(1, 8):
        target, origin = (expert + step) % 8, (expert + 8 - step) % 8
        wait_for(rows_put.at[target], out_send.at[target])
        wait_for(grads_put.at[target], grad_send.at[target])
        wait_for(rows_back.at[origin], out_recv.at[origin])
        wait_for(grads_back.at[origin], grad_recv.at[origin])
    for index in range(3):
        y_finish(index)


def add_rows(target, first, second):
    def body(index, carry):
        at = pl.ds(pl.multiple_of(index * 64, 64), 64)
        target[at, :] = (first[at, :].astype(jnp.float32) + second[at, :].astype(jnp.float32)).astype(target.dtype)
        return carry

    lax.fori_loop(0, first.shape[0] // 64, body, 0)


def second_part(rows, grads, weights, shared):
    in_hbm, in_vmem = pl.BlockSpec(memory_space=pl.ANY), pl.BlockSpec(memory_space=pltpu.VMEM)
    dma, bfloat = pltpu.SemaphoreType.DMA, jnp.bfloat16
    shape = jax.ShapeDtypeStruct
    count, capacity, width = rows.shape
    middle = weights[0].shape[1]
    quarter = [(weight.shape[0] // 4, weight.shape[1]) for weight in weights]
    own = [(1,) + work.shape[1:] for work in shared]
    blocks = (count * capacity, middle)
    return pl.pallas_call(
        second_kernel,
        out_shape=[shape(rows.shape, bfloat)] * 2
        + [shape(one, bfloat) for one in quarter]
        + [shape(one, bfloat) for one in own],
        in_specs=[in_vmem] * 2 + [in_hbm] * 6,
        out_specs=[in_vmem] * 8,
        scratch_shapes=[pltpu.VMEM(weight.shape, bfloat) for weight in weights]
        + [pltpu.VMEM(work.shape, bfloat) for work in shared]
        + [pltpu.VMEM(rows.shape, bfloat)] * 2
        + [pltpu.VMEM(blocks, bfloat)] * 3
        + [pltpu.VMEM((2 * capacity, width), jnp.float32)] * 2
        + [pltpu.VMEM((2,) + one, bfloat) for one in quarter]
        + [pltpu.VMEM(one, bfloat) for one in quarter]
        + [
            pltpu.VMEM(one, bfloat)
            for index in range(3)
            for one in receive_shapes(shared[index].shape, SHARED_ORDER[index], index == 2)
        ]
        + [dma((3,)), dma((3,))]
        + [dma((8,))] * 4
        + [dma((3, 2)), dma((3, 2)), dma((3,)), dma((3,)), dma((3, 7)), dma((3, 7))],
        compiler_params=pltpu.CompilerParams(collective_id=1, has_side_effects=True, vmem_limit_bytes=62 << 20),
        cost_estimate=pl.CostEstimate(flops=29000000000, bytes_accessed=30000000, transcendentals=2000000),
    )(rows, grads, *weights, *shared)


def swap(value, axis, bit):
    size = lax.axis_size(axis)
    return lax.ppermute(value, axis, [(index, index ^ bit) for index in range(size)])


def halves(value, bit_set, dim):
    half = value.shape[dim] // 2
    keep = lax.dynamic_slice_in_dim(value, bit_set * half, half, dim)
    give = lax.dynamic_slice_in_dim(value, (1 - bit_set) * half, half, dim)
    return keep, give


def fold(value, axis, bit, dim):
    bit_set = (lax.axis_index(axis) // bit) % 2
    keep, give = halves(value, bit_set, dim)
    return (keep.astype(jnp.float32) + swap(give.astype(jnp.bfloat16), axis, bit).astype(jnp.float32)).astype(jnp.bfloat16)


def unfold(value, axis, bit, dim):
    bit_set = (lax.axis_index(axis) // bit) % 2
    come = swap(value, axis, bit)
    return jnp.where(bit_set == 0, jnp.concatenate([value, come], dim), jnp.concatenate([come, value], dim))


def bits_of(axis):
    size = lax.axis_size(axis)
    return [1 << place for place in range(size.bit_length() - 1)]


def scatter_shards(value):
    count = lax.axis_size("shard")
    blocks = value.reshape((count // 2, 2, value.shape[0] // count) + value.shape[1:])
    blocks = fold(blocks, "shard", 1, 1)[:, 0]
    for bit in reversed(bits_of("shard")[1:]):
        blocks = fold(blocks, "shard", bit, 0)
    return blocks[0]


def sum_plane(value, dim):
    bits = bits_of("expert")
    for bit in bits:
        value = fold(value, "expert", bit, dim)
    for bit in reversed(bits):
        value = unfold(value, "expert", bit, dim)
    return value.astype(jnp.float32)


def shards(
    hidden_in,
    gain_attn,
    gain_ffn,
    w_query,
    w_key,
    w_value,
    w_out,
    shared_gate,
    shared_up,
    shared_down,
    expert_gate,
    expert_up,
    expert_down,
    gate_logits,
    routes,
    segment,
    padding,
    cotangent,
):
    bfloat = jnp.bfloat16
    tokens = hidden_in.shape[1]
    model_width = hidden_in.shape[2]
    head_size = model_width // HEADS
    experts = lax.axis_size("expert")
    capacity = max(2, 2 * tokens * TOP // experts)
    shard_count = lax.axis_size("shard")
    shard_index = lax.axis_index("shard")
    score_scale = head_size ** (-0.5)
    head_shape = (tokens, HEADS, head_size)
    fast = (experts, shard_count, WINDOW) == (8, 4, 4 * tokens)
    dense_own = (w_query, w_key, w_value, w_out, shared_gate, shared_up, shared_down)
    expert_own = (expert_gate[0], expert_up[0], expert_down[0])
    rows_in = hidden_in[0].astype(jnp.float32)
    scale_first = rms_scale(rows_in)
    positions = shard_index * tokens + jnp.arange(tokens, dtype=jnp.int32)
    segment_row, padding_row = segment[0], padding[0]
    query_segment = lax.dynamic_slice_in_dim(segment_row, shard_index * tokens, tokens)
    if fast:
        gain_own = lax.dynamic_update_slice(
            jnp.zeros((2, model_width), bfloat),
            jnp.stack([gain_attn, gain_ffn]),
            (0, shard_index * gain_attn.shape[0]),
        )
        full, rest = first_part(
            hidden_in[0],
            gain_own,
            dense_own,
            expert_own,
            segment_row,
            padding_row,
            cotangent[0],
            gate_logits[0],
            routes[0],
        )
        gains, normed_ctx, query_low, keys_ctx, values_ctx, log_total, attended, mixed_rows, normed_ffn = rest[:9]
        received, grad_received, shared_out, ffn_grad_shared, *shared_work = rest[9:]
        gain_first, gain_second = gains[0], gains[1]
        w_q, w_k, w_v, w_o = (full[name] for name in ("wq", "wk", "wv", "wo"))
        e_gate, e_up, e_down = (full[name] for name in LATE)
        reach, key_start = shard_count - 1, 0
        key_segment, key_padding = segment_row, padding_row
        key_positions = jnp.arange(4 * tokens, dtype=jnp.int32)
        allowed = allowed_mask(shard_index * tokens, 0, query_segment[:, None], key_segment[None], key_padding[None])
    else:
        gather = functools.partial(lax.all_gather, axis_name="shard", tiled=True)
        w_q, w_k, w_v, w_o, s_gate, s_up, s_down = (gather(weight) for weight in dense_own)
        e_gate, e_up, e_down = (gather(weight) for weight in expert_own)
        gain_first, gain_second = (gather(gain).astype(jnp.float32) for gain in (gain_attn, gain_ffn))
        reach = min((WINDOW + tokens - 2) // tokens, shard_count - 1)
        lead_rows, key_rows = reach * tokens, (reach + 1) * tokens
        context = [from_behind(hidden_in[0], "shard", offset) for offset in range(reach, 0, -1)] + [hidden_in[0]]
        context = jnp.concatenate(context, axis=0).astype(jnp.float32)
        normed_ctx = (context * rms_scale(context) * gain_first).astype(bfloat)
        key_positions = (shard_index - reach) * tokens + jnp.arange(key_rows, dtype=jnp.int32)
        query_low = rotate(
            dense_product(normed_ctx[lead_rows:], w_q).reshape(head_shape), positions, 1.0
        ).astype(bfloat)
        keys_ctx = rotate(
            dense_product(normed_ctx, w_k).reshape(key_rows, HEADS, head_size), key_positions, 1.0
        ).astype(bfloat)
        values_ctx = dense_product(normed_ctx, w_v).astype(bfloat)
        segment_ext = jnp.concatenate([jnp.full((lead_rows,), -1, jnp.int32), segment_row])
        padding_ext = jnp.concatenate([jnp.zeros((lead_rows,), jnp.int32), padding_row])
        key_segment = lax.dynamic_slice_in_dim(segment_ext, shard_index * tokens, key_rows)
        key_padding = lax.dynamic_slice_in_dim(padding_ext, shard_index * tokens, key_rows)
        allowed = allowed_mask(
            shard_index * tokens,
            (shard_index - reach) * tokens,
            query_segment[:, None],
            key_segment[None],
            key_padding[None],
        )
    key_rows = (reach + 1) * tokens
    query_heads = query_low.reshape(head_shape)
    keys_all = keys_ctx.reshape(key_rows, HEADS, head_size)
    values_all = values_ctx.reshape(key_rows, HEADS, head_size)

    def score_block():
        raw_scores = (
            jnp.einsum("qhd,khd->hqk", query_heads, keys_all, preferred_element_type=jnp.float32)
            * score_scale
        )
        return jnp.where(allowed[None], raw_scores, neg_fill)

    if not fast:
        scores = score_block()
        top_score = jnp.max(scores, axis=-1, keepdims=True)
        exponent = jnp.exp(scores - top_score)
        exp_total = jnp.sum(exponent, axis=-1, keepdims=True)
        log_total = top_score + jnp.log(exp_total)
        attended = (
            jnp.einsum(
                "hqk,khd->qhd",
                (exponent / exp_total).astype(bfloat),
                values_all,
                preferred_element_type=jnp.float32,
            )
            .astype(bfloat)
            .reshape(tokens, model_width)
        )
        mixed_rows = rows_in + dense_product(attended, w_o)
        normed_ffn = (mixed_rows * rms_scale(mixed_rows) * gain_second).astype(bfloat)
    scale_second = rms_scale(mixed_rows)
    grad_low = cotangent[0]
    grad_out = grad_low.astype(jnp.float32)
    gate_probs = jax.nn.softmax(gate_logits[0], axis=-1)
    route_flat = routes[0].reshape(-1)
    route_total = tokens * TOP
    onehot = (route_flat[:, None] == jnp.arange(experts, dtype=jnp.int32)[None, :]).astype(
        jnp.int32
    )
    slot_rank = jnp.sum((jnp.cumsum(onehot, axis=0) - onehot) * onehot, axis=1)
    places = route_flat * capacity + slot_rank
    if not fast:
        shared_pre = dense_product(normed_ffn, s_gate)
        shared_lin = dense_product(normed_ffn, s_up)
        shared_mid = (jax.nn.silu(shared_pre) * shared_lin).astype(bfloat)
        shared_out = dense_product(shared_mid, s_down)
        grad_shared_mid = product_t(grad_low, s_down)
        grad_shared_pre, grad_shared_lin = swiglu_back(grad_shared_mid, shared_pre, shared_lin)
        shared_down_grad = dense_product(shared_mid.T, grad_low)
        shared_gate_grad = dense_product(normed_ffn.T, grad_shared_pre)
        shared_up_grad = dense_product(normed_ffn.T, grad_shared_lin)
        ffn_grad_shared = product_t(grad_shared_pre, s_gate) + product_t(grad_shared_lin, s_up)
        slot_table = (
            jnp.full((experts * capacity,), route_total, dtype=jnp.int32)
            .at[places]
            .set(jnp.arange(route_total, dtype=jnp.int32))
        )
        padded_rows = jnp.concatenate([normed_ffn, jnp.zeros((1, model_width), bfloat)], axis=0)
        send_rows = padded_rows[slot_table // TOP].reshape(experts, capacity, model_width)
        received = lax.all_to_all(send_rows, "expert", split_axis=0, concat_axis=0, tiled=True)
        route_grad = (
            (gate_probs[:, :, None] * grad_out[:, None, :])
            .astype(bfloat)
            .reshape(route_total, model_width)
        )
        route_padded = jnp.concatenate([route_grad, jnp.zeros((1, model_width), bfloat)], axis=0)
        send_grad = route_padded[slot_table].reshape(experts, capacity, model_width)
        grad_received = lax.all_to_all(send_grad, "expert", split_axis=0, concat_axis=0, tiled=True)
    if fast:
        returned, grad_back, *sums = second_part(received, grad_received, (e_gate, e_up, e_down), shared_work)
        expert_grads = tuple(grad[None].astype(jnp.float32) for grad in sums[:3])
        shared_grads = tuple(grad[0].astype(jnp.float32) for grad in sums[3:])
    else:
        gate_pre = jnp.einsum("sid,df->sif", received, e_gate, preferred_element_type=jnp.float32)
        up_pre = jnp.einsum("sid,df->sif", received, e_up, preferred_element_type=jnp.float32)
        middle = (jax.nn.silu(gate_pre) * up_pre).astype(bfloat)
        result = jnp.einsum("sif,fd->sid", middle, e_down, preferred_element_type=jnp.float32).astype(bfloat)
        returned = lax.all_to_all(result, "expert", split_axis=0, concat_axis=0, tiled=True)
        grad_middle = jnp.einsum(
            "sid,fd->sif", grad_received, e_down, preferred_element_type=jnp.float32
        )
        grad_gate_pre, grad_up_pre = swiglu_back(grad_middle, gate_pre, up_pre)
        expert_down_grad = jnp.einsum(
            "sif,sid->fd", middle, grad_received, preferred_element_type=jnp.float32
        )
        expert_gate_grad = jnp.einsum(
            "sid,sif->df", received, grad_gate_pre, preferred_element_type=jnp.float32
        )
        expert_up_grad = jnp.einsum(
            "sid,sif->df", received, grad_up_pre, preferred_element_type=jnp.float32
        )
        grad_rows = (
            jnp.einsum("sif,df->sid", grad_gate_pre, e_gate, preferred_element_type=jnp.float32)
            + jnp.einsum("sif,df->sid", grad_up_pre, e_up, preferred_element_type=jnp.float32)
        ).astype(bfloat)
        grad_back = lax.all_to_all(grad_rows, "expert", split_axis=0, concat_axis=0, tiled=True)
        expert_grads = tuple(
            scatter_shards(grad.astype(bfloat))[None].astype(jnp.float32)
            for grad in (expert_gate_grad, expert_up_grad, expert_down_grad)
        )
        shared_grads = (
            sum_plane(scatter_shards(shared_gate_grad.astype(bfloat)), 1),
            sum_plane(scatter_shards(shared_up_grad.astype(bfloat)), 1),
            sum_plane(scatter_shards(shared_down_grad.astype(bfloat)), 0),
        )
    per_route = (
        returned.reshape(experts * capacity, model_width)[places]
        .astype(jnp.float32)
        .reshape(tokens, TOP, model_width)
    )
    routed = jnp.sum(gate_probs[:, :, None] * per_route, axis=1)
    output = (mixed_rows + shared_out + routed).astype(bfloat)
    contrib = jnp.sum(per_route * grad_out[:, None, :], axis=-1)
    logit_grad = gate_probs * (contrib - jnp.sum(gate_probs * contrib, axis=-1, keepdims=True))
    grad_routes = (
        grad_back.reshape(experts * capacity, model_width)[places]
        .astype(jnp.float32)
        .reshape(tokens, TOP, model_width)
    )
    grad_normed_ffn = jnp.sum(grad_routes, axis=1) + ffn_grad_shared
    gain_ffn_grad = jnp.sum(grad_normed_ffn * mixed_rows * scale_second, axis=0)
    scaled_second = grad_normed_ffn * gain_second
    grad_mixed = (
        grad_out
        + scale_second * scaled_second
        - mixed_rows
        * scale_second**3
        * jnp.mean(scaled_second * mixed_rows, axis=-1, keepdims=True)
    )
    grad_mixed_low = grad_mixed.astype(bfloat)
    w_out_grad = dense_product(attended.T, grad_mixed_low)
    grad_attended = product_t(grad_mixed_low, w_o).astype(bfloat).reshape(head_shape)
    attn_probs = jnp.exp(score_block() - log_total)
    grad_probs = jnp.einsum(
        "qhd,khd->hqk", grad_attended, values_all, preferred_element_type=jnp.float32
    )
    delta_rows = jnp.sum(attn_probs * grad_probs, axis=-1, keepdims=True)
    grad_scores = (attn_probs * (grad_probs - delta_rows)).astype(bfloat)
    grad_query = (
        jnp.einsum("hqk,khd->qhd", grad_scores, keys_all, preferred_element_type=jnp.float32)
        * score_scale
    )
    grad_keys = (
        jnp.einsum("hqk,qhd->khd", grad_scores, query_heads, preferred_element_type=jnp.float32)
        * score_scale
    )
    grad_values = jnp.einsum(
        "hqk,qhd->khd", attn_probs.astype(bfloat), grad_attended, preferred_element_type=jnp.float32
    )
    grad_query_low = rotate(grad_query, positions, -1.0).astype(bfloat).reshape(tokens, model_width)
    grad_key_low = rotate(grad_keys, key_positions, -1.0).astype(bfloat).reshape(key_rows, model_width)
    grad_value_low = grad_values.astype(bfloat).reshape(key_rows, model_width)
    if fast:
        normed = lax.dynamic_slice_in_dim(normed_ctx, shard_index * tokens, tokens)
    else:
        normed = normed_ctx[reach * tokens :]
    w_query_grad = dense_product(normed.T, grad_query_low)
    w_key_grad = dense_product(normed_ctx.T, grad_key_low)
    w_value_grad = dense_product(normed_ctx.T, grad_value_low)
    grad_context = product_t(grad_key_low, w_k) + product_t(grad_value_low, w_v)
    grad_normed = product_t(grad_query_low, w_q)
    if fast:
        grad_normed = grad_normed + scatter_shards(grad_context.astype(bfloat)).astype(jnp.float32)
    else:
        grad_normed = grad_normed + grad_context[reach * tokens :]
        for offset in range(1, reach + 1):
            sent = grad_context[(reach - offset) * tokens :][:tokens].astype(bfloat)
            grad_normed = grad_normed + from_behind(sent, "shard", -offset).astype(jnp.float32)
    gain_attn_grad = jnp.sum(grad_normed * rows_in * scale_first, axis=0)
    scaled_first = grad_normed * gain_first
    input_grad = (
        grad_mixed
        + scale_first * scaled_first
        - rows_in * scale_first**3 * jnp.mean(scaled_first * rows_in, axis=-1, keepdims=True)
    )
    gain_rows = jnp.stack([gain_attn_grad, gain_ffn_grad], axis=1).astype(bfloat)
    gain_total = lax.psum(scatter_shards(gain_rows), "expert").astype(jnp.float32)
    attn_grads = jnp.stack([w_query_grad, w_key_grad, w_value_grad, w_out_grad]).astype(bfloat)
    attn_rows = scatter_shards(attn_grads.transpose(1, 0, 2)).transpose(1, 0, 2)
    attn_total = sum_plane(attn_rows.reshape(-1, model_width), 0).reshape(attn_rows.shape)
    return (
        output[None],
        input_grad[None],
        logit_grad[None],
        gain_total[:, 0],
        gain_total[:, 1],
        attn_total[0],
        attn_total[1],
        attn_total[2],
        attn_total[3],
        shared_grads[0],
        shared_grads[1],
        shared_grads[2],
        expert_grads[0],
        expert_grads[1],
        expert_grads[2],
    )


def solution(mesh):
    placed = (
        P("expert", "shard", None),
        P("shard"),
        P("shard"),
        P("shard", None),
        P("shard", None),
        P("shard", None),
        P("shard", None),
        P("shard", None),
        P("shard", None),
        P("shard", None),
        P("expert", "shard", None),
        P("expert", "shard", None),
        P("expert", "shard", None),
        P("expert", "shard", None),
        P("expert", "shard", None),
        P("expert", None),
        P("expert", None),
        P("expert", "shard", None),
    )
    return jax.shard_map(
        shards,
        mesh=mesh,
        in_specs=placed,
        out_specs=(
            P("expert", "shard", None),
            P("expert", "shard", None),
            P("expert", "shard", None),
            P("shard"),
            P("shard"),
            P("shard", None),
            P("shard", None),
            P("shard", None),
            P("shard", None),
            P("shard", None),
            P("shard", None),
            P("shard", None),
            P("expert", "shard", None),
            P("expert", "shard", None),
            P("expert", "shard", None),
        ),
        check_vma=False,
    )
```

```python
import functools
import math

import jax
import jax.numpy as jnp
import numpy as np
from jax import lax
from jax.experimental import pallas as pl
from jax.experimental.pallas import tpu as pltpu
from jax.sharding import PartitionSpec as P

HEADS = 12
TOP = 2
WINDOW = 1024
MESH = pl.DeviceIdType.MESH
norm_eps = 1e-06
neg_fill = -1e30
rope_base = 10000.0

DIRECT = ("hid", "gains")
EARLY = ("wk", "wv", "wq")
SPREAD = ("wo", "sg", "su", "sd")
SPLIT_X = ("sg", "su", "sd")
LATE = ("eg", "eu", "ed")
NAMES = DIRECT + EARLY + SPREAD + LATE
PASSING = DIRECT + ("sg", "su", "sd")
KEPT = EARLY + ("wo",) + LATE


def dense_product(left, right):
    return jnp.dot(left, right, preferred_element_type=jnp.float32)


def product_t(left, right):
    return lax.dot_general(left, right, (((1,), (1,)), ((), ())), preferred_element_type=jnp.float32)


def t_product(left, right):
    return lax.dot_general(left, right, (((0,), (0,)), ((), ())), preferred_element_type=jnp.float32)


def rms_scale(values):
    return lax.rsqrt(jnp.mean(values * values, axis=-1, keepdims=True) + norm_eps)


def rotary_tables(length, head_size):
    half = head_size // 2
    frequency = np.float32(rope_base) ** (-np.arange(half, dtype=np.float32) / np.float32(half))
    angles = np.arange(length, dtype=np.float32)[:, None] * frequency[None, :]
    cosine, sine = np.cos(angles).astype(np.float32), np.sin(angles).astype(np.float32)
    return np.concatenate([cosine] * 4, axis=1), np.concatenate([-sine, sine] * 2, axis=1)


def rotate_pair(values, cosine, sine):
    lane = lax.broadcasted_iota(jnp.int32, values.shape, 1)
    partner = jnp.where(lane % 64 < 32, pltpu.roll(values, 96, 1), pltpu.roll(values, 32, 1))
    return values * cosine + partner * sine


def rotate(values, positions, direction):
    half_size = values.shape[-1] // 2
    frequency = rope_base ** (-jnp.arange(half_size, dtype=jnp.float32) / half_size)
    angles = positions.astype(jnp.float32)[:, None] * frequency[None, :]
    cosine = jnp.cos(angles)[:, None, :]
    sine_part = direction * jnp.sin(angles)[:, None, :]
    first_half = values[..., :half_size]
    second_half = values[..., half_size:]
    return jnp.concatenate(
        [
            first_half * cosine - second_half * sine_part,
            second_half * cosine + first_half * sine_part,
        ],
        axis=-1,
    )


def swiglu_back(grad_middle, gate_pre, up_pre):
    sigmoid_gate = jax.nn.sigmoid(gate_pre)
    activated = gate_pre * sigmoid_gate
    grad_gate = grad_middle * up_pre * sigmoid_gate * (1.0 + gate_pre * (1.0 - sigmoid_gate))
    grad_up = grad_middle * activated
    return (grad_gate.astype(jnp.bfloat16), grad_up.astype(jnp.bfloat16))


def from_behind(value, axis, steps):
    count = lax.axis_size(axis)
    first, last = (max(0, -steps), min(count, count - steps))
    return lax.ppermute(value, axis, [(source, source + steps) for source in range(first, last)])


def send(source, target, send_sem, recv_sem, peer):
    pltpu.make_async_remote_copy(
        src_ref=source,
        dst_ref=target,
        send_sem=send_sem,
        recv_sem=recv_sem,
        device_id=peer,
        device_id_type=MESH,
    ).start()


def wait_for(ref, sem):
    pltpu.make_async_copy(ref, ref, sem).wait()


def first_kernel(*refs):
    count = len(NAMES)
    own = dict(zip(NAMES, refs[:count]))
    segment_row, segment_col, padding_row, cosine_ref, sine_ref, cot_ref, logit_ref, route_ref, lane_route_ref = refs[
        count : count + 9
    ]
    refs = refs[count + 9 :]
    full = dict(zip(KEPT, refs[: len(KEPT)]))
    refs = refs[len(KEPT) :]
    gain_ref, normed_ref, query_ref, key_ref, value_ref, lse_ref, attended_ref, mixed_ref, ffn_ref = refs[:9]
    rows_got, grads_got, shared_ref, ffn_grad_ref, *shared_work = refs[9:16]
    refs = refs[16:]
    full.update(zip(PASSING, refs[: len(PASSING)]))
    refs = refs[len(PASSING) :]
    shared_core = refs[:3]
    refs = refs[3:]
    rows_put, grads_put = refs[:2]
    (own_sem, y_send, y_recv, x_send, x_recv, z_send, z_recv, core_send, core_recv) = refs[2:11]
    row_sems, grad_sems, share_send, share_recv = refs[11:13], refs[13:15], refs[15], refs[16]
    number = {name: index for index, name in enumerate(NAMES)}
    expert, shard = (lax.axis_index("expert"), lax.axis_index("shard"))
    zed, ex = (expert // 2, expert % 2)
    other = (shard + 2) % 4
    y_peer = (expert, other)
    core_peer = (expert, shard + 1 - 2 * (shard % 2))
    x_peer = (expert + 1 - 2 * ex, shard)
    z_up, z_down = (((expert + 2) % 8, shard), ((expert + 6) % 8, shard))

    barrier = pltpu.get_barrier_semaphore()
    for peer in (y_peer, core_peer) + tuple(((expert + step) % 8, shard) for step in range(1, 8)):
        pl.semaphore_signal(barrier, inc=1, device_id=peer, device_id_type=MESH)
    pl.semaphore_wait(barrier, 9)

    def part_of(block, base, name, at_z, at_x):
        rows = own[name].shape[0]
        if at_z is None and at_x is None:
            return block.at[pl.ds(base, rows)]
        if name in EARLY:
            return block.at[pl.ds(base + at_x * (rows // 2), rows // 2)]
        if name in ("sg", "su"):
            half = block.shape[1] // 8
            return block.at[pl.ds(base, rows), pl.ds((at_z * 2 + at_x) * half, half)]
        size = rows // 4
        if name == "sd":
            return block.at[pl.ds(base + at_z * size + at_x * (size // 2), size // 2)]
        return block.at[pl.ds(base + at_z * size, size)]

    def place(name, slot, at_z=None, at_x=None):
        return part_of(full[name], slot * own[name].shape[0], name, at_z, at_x)

    def mine(name, at_z=None, at_x=None):
        return part_of(own[name], 0, name, at_z, at_x)

    def ex_of(name):
        return ex if name in SPLIT_X else None

    def cross(name, at_z=None, at_x=None):
        n = number[name]
        send(mine(name, at_z, at_x), place(name, shard, at_z, at_x), y_send.at[n], y_recv.at[n], y_peer)

    def to_core(name, step, at_z=None, at_x=None):
        n = number[name]
        part = place(name, other, at_z, at_x)
        send(part, part, core_send.at[n, 1 + step], core_recv.at[n, 1 + step], core_peer)

    far = shard + 1 - 2 * (shard % 2)
    far_other = (far + 2) % 4

    def settle_own(names):
        for name in names:
            n = number[name]
            pltpu.make_async_copy(own[name], place(name, shard), own_sem.at[n]).wait()
            wait_for(place(name, far), core_recv.at[n, 0])
            wait_for(own[name], core_send.at[n, 0])

    def settle_core(name, step, at_z=None, at_x=None):
        n = number[name]
        wait_for(place(name, far_other, at_z, at_x), core_recv.at[n, 1 + step])
        wait_for(place(name, other, at_z, at_x), core_send.at[n, 1 + step])

    for name in DIRECT:
        cross(name)
    for name in EARLY:
        cross(name, None, ex)
    for name in SPREAD:
        cross(name, zed, ex_of(name))
    for name in NAMES:
        n = number[name]
        send(own[name], place(name, shard), core_send.at[n, 0], core_recv.at[n, 0], core_peer)
        pltpu.make_async_copy(own[name], place(name, shard), own_sem.at[n]).start()

    for name in DIRECT:
        wait_for(place(name, other), y_recv.at[number[name]])
        to_core(name, 0)
    for name in EARLY:
        n = number[name]
        part = place(name, other, None, ex)
        wait_for(part, y_recv.at[n])
        send(part, part, x_send.at[n, 0], x_recv.at[n, 0], x_peer)
        to_core(name, 0, None, ex)
    for name in LATE:
        cross(name)

    def on_part(name, at_z, step):
        n = number[name]
        part = place(name, other, at_z, ex_of(name))
        if name in SPLIT_X:
            send(part, part, x_send.at[n, step], x_recv.at[n, step], x_peer)
        to_core(name, step, at_z, ex_of(name))

    def forward(step, direction, condition, at_z, peer):
        @pl.when(condition)
        def _():
            for name in SPREAD:
                n = number[name]
                part = place(name, other, at_z, ex_of(name))
                send(part, part, z_send.at[n, direction, step], z_recv.at[n, direction, step], peer)

    def arrive(step, direction, condition, at_z):
        @pl.when(condition)
        def _():
            for name in SPREAD:
                n = number[name]
                wait_for(place(name, other, at_z, ex_of(name)), z_recv.at[n, direction, step])
                on_part(name, at_z, 1 + direction * 3 + step)

    def ring_send(step):
        forward(step, 0, (zed < 3) & (zed >= step), zed - step, z_up)
        forward(step, 1, (zed > 0) & (zed + step <= 3), zed + step, z_down)

    def ring_arrive(step):
        arrive(step, 0, zed >= step + 1, zed - 1 - step)
        arrive(step, 1, zed + 1 + step <= 3, zed + 1 + step)

    for name in SPREAD:
        wait_for(place(name, other, zed, ex_of(name)), y_recv.at[number[name]])
    ring_send(0)
    for name in SPREAD:
        on_part(name, zed, 0)

    settle_own(DIRECT)
    for name in DIRECT:
        settle_core(name, 0)
    tokens, width = own["hid"].shape
    gain_rows = sum(full["gains"][pl.ds(slot * 16, 16), :].astype(jnp.float32) for slot in range(4))
    gain_ref[...] = gain_rows
    gain_first, gain_second = gain_rows[0:1], gain_rows[1:2]

    def norm_block(block, carry):
        rows = pl.ds(pl.multiple_of(block * tokens, tokens), tokens)
        values = full["hid"][rows, :].astype(jnp.float32)
        normed_ref[rows, :] = (values * rms_scale(values) * gain_first).astype(jnp.bfloat16)
        return carry

    lax.fori_loop(0, 4, norm_block, 0)

    for name in EARLY:
        wait_for(place(name, other, None, 1 - ex), x_recv.at[number[name], 0])
        to_core(name, 1, None, 1 - ex)
    settle_own(EARLY)
    for name in EARLY:
        settle_core(name, 0, None, ex)
        settle_core(name, 1, None, 1 - ex)
        wait_for(mine(name, None, ex), y_send.at[number[name]])
        wait_for(place(name, other, None, ex), x_send.at[number[name], 0])

    lane_routes = lane_route_ref[...]
    expert_at = lax.broadcasted_iota(jnp.int32, (8, tokens), 0)
    named = ((lane_routes[0:1] == expert_at) | (lane_routes[1:2] == expert_at)).astype(jnp.float32)
    before = lax.broadcasted_iota(jnp.int32, (tokens, tokens), 0) < lax.broadcasted_iota(jnp.int32, (tokens, tokens), 1)
    rank = dense_product(named.astype(jnp.bfloat16), before.astype(jnp.bfloat16))
    slot_of = jnp.where(named > 0.0, rank, -1.0).astype(jnp.int32)
    capacity = rows_put.shape[1]

    def picks(target):
        slot_at = lax.broadcasted_iota(jnp.int32, (capacity, tokens), 0)
        return slot_at == slot_of[target : target + 1]

    def dispatch(put, got, sems):
        for step in range(1, 8):
            target = (expert + step) % 8
            send(put.at[target], got.at[expert], sems[0].at[step], sems[1].at[step], (target, shard))
        got[pl.ds(expert, 1)] = put[pl.ds(expert, 1)]

    def settle_dispatch(put, got, sems):
        for step in range(1, 8):
            wait_for(put.at[(expert + step) % 8], sems[0].at[step])
            wait_for(got.at[(expert + 8 - step) % 8], sems[1].at[step])

    gate_probs = gate_columns(logit_ref[...])
    cot = cot_ref[...]
    route_grads = [(gate * cot.astype(jnp.float32)).astype(jnp.bfloat16) for gate in gate_probs]
    for target in range(8):
        chosen = picks(target)
        grads_put[target] = sum(
            dense_product((chosen & (lane_routes[k : k + 1] == target)).astype(jnp.bfloat16), route_grads[k])
            for k in range(TOP)
        ).astype(jnp.bfloat16)
    dispatch(grads_put, grads_got, grad_sems)

    def key_block(block, carry):
        rows = pl.ds(pl.multiple_of(block * tokens, tokens), tokens)
        normed = normed_ref[rows, :]
        value_ref[rows, :] = dense_product(normed, full["wv"][...]).astype(jnp.bfloat16)
        raw = dense_product(normed, full["wk"][...])
        cosine, sine = cosine_ref[rows, :], sine_ref[rows, :]
        for start in range(0, width, 128):
            key_ref[rows, start : start + 128] = rotate_pair(raw[:, start : start + 128], cosine, sine).astype(jnp.bfloat16)
        return carry

    lax.fori_loop(0, 4, key_block, 0)
    ring_arrive(0)
    ring_send(1)
    here = pl.ds(pl.multiple_of(shard * tokens, tokens), tokens)
    raw = dense_product(normed_ref[here, :], full["wq"][...])
    cosine, sine = cosine_ref[here, :], sine_ref[here, :]
    for start in range(0, width, 128):
        query_ref[:, start : start + 128] = rotate_pair(raw[:, start : start + 128], cosine, sine).astype(jnp.bfloat16)

    def head_pair(pair, carry):
        lanes = pl.ds(pl.multiple_of(pair * 128, 128), 128)
        query, keys, values = query_ref[:, lanes], key_ref[:, lanes], value_ref[:, lanes]
        allowed = allowed_mask(shard * tokens, 0, segment_col[here, :], segment_row[...], padding_row[...])
        lane = lax.broadcasted_iota(jnp.int32, query.shape, 1)
        results = []
        for half in range(2):
            chosen = (lane >= 64) if half else (lane < 64)
            scores = product_t(jnp.where(chosen, query, jnp.zeros_like(query)), keys) * 0.125
            scores = jnp.where(allowed, scores, neg_fill)
            top_score = jnp.max(scores, axis=-1, keepdims=True)
            exponent = jnp.exp(scores - top_score)
            exp_total = jnp.sum(exponent, axis=-1, keepdims=True)
            lse_ref[2 * pair + half] = top_score + jnp.log(exp_total)
            results.append(dense_product((exponent / exp_total).astype(jnp.bfloat16), values))
        attended_ref[:, lanes] = jnp.where(lane < 64, results[0], results[1]).astype(jnp.bfloat16)
        return carry

    lax.fori_loop(0, 3, head_pair, 0)
    ring_arrive(1)
    ring_send(2)
    lax.fori_loop(3, 6, head_pair, 0)
    ring_arrive(2)

    def from_x(condition, at_z, step):
        @pl.when(condition)
        def _():
            for name in SPLIT_X:
                wait_for(place(name, other, at_z, 1 - ex), x_recv.at[number[name], step])
                to_core(name, 7 + step, at_z, 1 - ex)

    from_x(zed >= 0, zed, 0)
    for step in range(3):
        from_x(zed >= step + 1, zed - 1 - step, 1 + step)
        from_x(zed + 1 + step <= 3, zed + 1 + step, 4 + step)

    def settle_spread(names, condition, at_z, step):
        @pl.when(condition)
        def _():
            for name in names:
                settle_core(name, step, at_z, ex_of(name))
                if name in SPLIT_X:
                    wait_for(place(name, other, at_z, ex), x_send.at[number[name], step])
                    settle_core(name, 7 + step, at_z, 1 - ex)

    def settle_ring(names):
        settle_own(names)
        for name in names:
            wait_for(mine(name, zed, ex_of(name)), y_send.at[number[name]])
        settle_spread(names, zed >= 0, zed, 0)
        for step in range(3):
            settle_spread(names, zed >= step + 1, zed - 1 - step, 1 + step)
            settle_spread(names, zed + 1 + step <= 3, zed + 1 + step, 4 + step)

    settle_ring(("wo",))
    rows_in = own["hid"][...].astype(jnp.float32)
    mixed = rows_in + dense_product(attended_ref[...], full["wo"][...])
    mixed_ref[...] = mixed
    ffn = (mixed * rms_scale(mixed) * gain_second).astype(jnp.bfloat16)
    ffn_ref[...] = ffn
    for target in range(8):
        rows_put[target] = dense_product(picks(target).astype(jnp.bfloat16), ffn).astype(jnp.bfloat16)
    dispatch(rows_put, rows_got, row_sems)

    settle_ring(SPLIT_X)

    def sent(step, direction, condition, at_z):
        @pl.when(condition)
        def _():
            for name in SPREAD:
                wait_for(place(name, other, at_z, ex_of(name)), z_send.at[number[name], direction, step])

    for step in range(3):
        sent(step, 0, (zed < 3) & (zed >= step), zed - step)
        sent(step, 1, (zed > 0) & (zed + step <= 3), zed + step)
    shared_ref[...] = jnp.zeros_like(shared_ref)
    ffn_grad_ref[...] = jnp.zeros_like(ffn_grad_ref)

    def shared_block(block, carry):
        cut = pl.ds(pl.multiple_of(block * 512, 512), 512)
        normed = ffn_ref[...]
        gate, up, down = full["sg"][:, cut], full["su"][:, cut], full["sd"][cut, :]
        pre, lin = dense_product(normed, gate), dense_product(normed, up)
        middle = (jax.nn.silu(pre) * lin).astype(jnp.bfloat16)
        shared_ref[...] += dense_product(middle, down)
        pre_grad, lin_grad = swiglu_back(product_t(cot_ref[...], down), pre, lin)
        ffn_grad_ref[...] += product_t(pre_grad, gate) + product_t(lin_grad, up)
        full["sg"][:, cut] = t_product(normed, pre_grad).astype(jnp.bfloat16)
        full["su"][:, cut] = t_product(normed, lin_grad).astype(jnp.bfloat16)
        full["sd"][cut, :] = t_product(middle, cot_ref[...]).astype(jnp.bfloat16)
        return carry

    lax.fori_loop(0, full["sg"].shape[1] // 512, shared_block, 0)

    def shard_rows(ref, y_of, core_of):
        rows = ref.shape[0] // 4
        return ref.at[pl.ds((y_of * 2 + core_of) * rows, rows)]

    core = shard % 2
    shared_grads = (full["sg"], full["su"], full["sd"])
    for index in range(3):
        for y_of in range(2):
            send(
                shard_rows(shared_grads[index], y_of, 1 - core),
                shared_core[index].at[y_of],
                share_send.at[index, y_of],
                share_recv.at[index, y_of],
                core_peer,
            )

    for name in LATE:
        wait_for(place(name, other), y_recv.at[number[name]])
        to_core(name, 0)

    for name in DIRECT:
        wait_for(own[name], y_send.at[number[name]])
    settle_own(LATE)
    for name in LATE:
        wait_for(own[name], y_send.at[number[name]])
        settle_core(name, 0)
    for index in range(3):
        for y_of in range(2):
            wait_for(shared_core[index].at[y_of], share_recv.at[index, y_of])
            add_rows(shared_work[index].at[y_of], shard_rows(shared_grads[index], y_of, core), shared_core[index].at[y_of])
            wait_for(shard_rows(shared_grads[index], y_of, 1 - core), share_send.at[index, y_of])
    settle_dispatch(grads_put, grads_got, grad_sems)
    settle_dispatch(rows_put, rows_got, row_sems)


def gate_columns(logits):
    first, second = logits[:, 0:1], logits[:, 1:2]
    top = jnp.maximum(first, second)
    first, second = jnp.exp(first - top), jnp.exp(second - top)
    total = first + second
    return first / total, second / total


def allowed_mask(query_start, key_start, query_segment, key_segment, key_padding):
    shape = (query_segment.shape[0], key_segment.shape[1])
    query_at = query_start + lax.broadcasted_iota(jnp.int32, shape, 0)
    key_at = key_start + lax.broadcasted_iota(jnp.int32, shape, 1)
    distance = query_at - key_at
    return (
        (query_segment == key_segment)
        & (distance >= 0)
        & (distance < WINDOW)
        & ((key_padding == 1) | (distance == 0))
    )


def first_part(hidden, gains, dense, experts, segment, padding, cotangent, logits, routes):
    tokens, width = hidden.shape
    bfloat, single = jnp.bfloat16, jnp.float32
    wq, wk, wv, wo, sg, su, sd = dense
    blocks = dict(hid=hidden, gains=jnp.pad(gains, ((0, 14), (0, 0))), wq=wq, wk=wk, wv=wv, wo=wo, sg=sg, su=su, sd=sd)
    blocks.update(zip(LATE, experts))
    blocks = [blocks[name] for name in NAMES]
    count = len(NAMES)
    cosine, sine = rotary_tables(4 * tokens, width // HEADS)
    in_hbm, in_vmem = pl.BlockSpec(memory_space=pl.ANY), pl.BlockSpec(memory_space=pltpu.VMEM)
    dma = pltpu.SemaphoreType.DMA
    shape = jax.ShapeDtypeStruct
    whole = {name: shape((4 * block.shape[0], block.shape[1]), block.dtype) for name, block in zip(NAMES, blocks)}
    middle = sg.shape[1]
    capacity = max(2, 2 * tokens * TOP // 8)
    routed = (8, capacity, width)
    halved = [(2,) + block.shape for block in (sg, su, sd)]
    out = pl.pallas_call(
        first_kernel,
        out_shape=[whole[name] for name in KEPT]
        + [
            shape((16, width), single),
            shape((4 * tokens, width), bfloat),
            shape((tokens, width), bfloat),
            shape((4 * tokens, width), bfloat),
            shape((4 * tokens, width), bfloat),
            shape((HEADS, tokens, 1), single),
            shape((tokens, width), bfloat),
            shape((tokens, width), single),
            shape((tokens, width), bfloat),
            shape(routed, bfloat),
            shape(routed, bfloat),
            shape((tokens, width), single),
            shape((tokens, width), single),
        ]
        + [shape(one, bfloat) for one in halved],
        in_specs=[in_vmem] * (count + 9),
        out_specs=[in_hbm if name in LATE else in_vmem for name in KEPT] + [in_vmem] * 16,
        scratch_shapes=[pltpu.VMEM(whole[name].shape, whole[name].dtype) for name in PASSING]
        + [pltpu.VMEM(one, bfloat) for one in halved]
        + [pltpu.VMEM(routed, bfloat)] * 2
        + [
            dma((count,)),
            dma((count,)),
            dma((count,)),
            dma((count, 7)),
            dma((count, 7)),
            dma((count, 2, 3)),
            dma((count, 2, 3)),
            dma((count, 15)),
            dma((count, 15)),
        ]
        + [dma((8,))] * 4
        + [dma((3, 2))] * 2,
        compiler_params=pltpu.CompilerParams(collective_id=0, has_side_effects=True, vmem_limit_bytes=60 << 20),
        cost_estimate=pl.CostEstimate(flops=15000000000, bytes_accessed=47000000, transcendentals=3000000),
    )(
        *blocks,
        segment[None, :],
        segment[:, None],
        padding[None, :],
        jnp.asarray(cosine),
        jnp.asarray(sine),
        cotangent,
        logits,
        routes,
        routes.T,
    )
    return dict(zip(KEPT, out)), out[len(KEPT) :]


def add_into(target, first, second):
    rows = first.shape[-2]
    strip = math.gcd(rows, 64)

    def body(index, carry):
        at = pl.ds(pl.multiple_of(index * strip, strip), strip)
        for lead in range(first.shape[0]):
            total = first[lead, at, :].astype(jnp.float32) + second[lead, at, :].astype(jnp.float32)
            target[lead, at, :] = total.astype(target.dtype)
        return carry

    lax.fori_loop(0, rows // strip, body, 0)


class PlaneSum:
    def __init__(self, work, out, receive, send_sem, recv_sem, bits, peers, order):
        self.work, self.out, self.receive = work, out, receive
        self.send_sem, self.recv_sem, self.bits, self.peers, self.order = send_sem, recv_sem, bits, peers, order
        self.at = [(0, 2), (0, work.shape[1]), (0, work.shape[2])]
        self.trail = []

    def region(self, ref, at):
        starts = [pl.multiple_of(start, unit) if unit > 1 and not isinstance(start, int) else start for (start, _), unit in zip(at, (1, 16, 128))]
        first = pl.ds(0, 1) if ref.shape[0] == 1 else pl.ds(starts[0], at[0][1])
        return ref.at[first, pl.ds(starts[1], at[1][1]), pl.ds(starts[2], at[2][1])]

    def halves(self, step):
        axis, dim = self.order[step]
        bit, half = self.bits[axis], self.at[dim][1] // 2
        keep, give = list(self.at), list(self.at)
        keep[dim] = (self.at[dim][0] + bit * half, half)
        give[dim] = (self.at[dim][0] + (1 - bit) * half, half)
        return keep, give

    def start(self, step):
        _, give = self.halves(step)
        peer = self.peers[self.order[step][0]]
        send(self.region(self.work, give), self.receive[step], self.send_sem.at[step], self.recv_sem.at[step], peer)

    def finish(self, step):
        keep, give = self.halves(step)
        wait_for(self.receive[step], self.recv_sem.at[step])
        kept = self.region(self.work, keep)
        target = self.region(self.out, keep) if step == len(self.order) - 1 else kept
        add_into(target, kept, self.receive[step])
        wait_for(self.region(self.work, give), self.send_sem.at[step])
        if self.order[step][0] != "y":
            self.trail.append((step, self.at))
        self.at = keep

    def back_start(self, step):
        forth, _ = self.trail[-1 - step]
        part, at = self.region(self.out, self.at), len(self.order) + step
        send(part, part, self.send_sem.at[at], self.recv_sem.at[at], self.peers[self.order[forth][0]])

    def back_finish(self, step):
        forth, whole = self.trail[-1 - step]
        at = len(self.order) + step
        wait_for(self.region(self.out, self.at), self.send_sem.at[at])
        dim = self.order[forth][1]
        start, size = self.at[dim]
        other = list(self.at)
        other[dim] = (2 * whole[dim][0] + size - start, size)
        wait_for(self.region(self.out, other), self.recv_sem.at[at])
        self.at = list(self.at)
        self.at[dim] = whole[dim]


def receive_shapes(shape, order):
    result, shape = [], list(shape)
    for _, dim in order:
        shape[dim] //= 2
        result.append(tuple(shape))
    return result


def ordered(axes, dims):
    return tuple((axis, 0 if axis == "y" else dims[axis]) for axis in axes)


BY_COLUMNS, BY_ROWS = dict(x=2, z1=2, z2=2), dict(x=1, z1=1, z2=1)
BY_BOTH = dict(x=2, z1=1, z2=1)
SHARED_ORDER = (
    ordered(("y", "x", "z1", "z2"), BY_COLUMNS),
    ordered(("x", "z1", "y", "z2"), BY_COLUMNS),
    ordered(("z1", "y", "x", "z2"), BY_ROWS),
)
ATTENTION_ORDER = (
    ordered(("y", "x", "z1", "z2"), BY_BOTH),
    ordered(("x", "z1", "y", "z2"), BY_BOTH),
    ordered(("z1", "y", "x", "z2"), BY_BOTH),
    ordered(("y", "x", "z1", "z2"), BY_BOTH),
)


def plane_places():
    expert, shard = (lax.axis_index("expert"), lax.axis_index("shard"))
    zed, ex, why, core = (expert // 2, expert % 2, shard // 2, shard % 2)
    bits = {"x": ex, "z1": zed % 2, "z2": zed // 2, "y": why}
    peers = {
        "x": (expert + 1 - 2 * ex, shard),
        "z1": (expert + 2 - 4 * (zed % 2), shard),
        "z2": ((expert + 4) % 8, shard),
        "y": (expert, (shard + 2) % 4),
        "core": (expert, shard + 1 - 2 * core),
    }
    return expert, shard, zed, core, bits, peers


def enter(peers):
    barrier = pltpu.get_barrier_semaphore()
    for peer in peers:
        pl.semaphore_signal(barrier, inc=1, device_id=peer, device_id_type=MESH)
    pl.semaphore_wait(barrier, len(peers))


def second_kernel(*refs):
    rows_ref, grads_ref, *weights_in = refs[:5]
    shared_in = refs[5:8]
    rows_back, grads_back = refs[8:10]
    expert_out, shared_out = refs[10:13], refs[13:16]
    weights, shared_work = refs[16:19], refs[19:22]
    rows_put, grads_put, middle_ref, pre_ref, lin_ref, out_sum, grad_sum = refs[22:29]
    expert_core, expert_y = refs[29:32], refs[32:35]
    receive = [refs[35 + 4 * index : 39 + 4 * index] for index in range(3)]
    load_sem, shared_sem, out_send, out_recv, grad_send, grad_recv, core_send, core_recv, y_send, y_recv, sum_send, sum_recv = refs[47:]
    expert, shard, zed, core, bits, peers = plane_places()
    why = bits["y"]
    for index in range(3):
        pltpu.make_async_copy(weights_in[index], weights[index], load_sem.at[index]).start()
        pltpu.make_async_copy(shared_in[index], shared_work[index], shared_sem.at[index]).start()
    enter((peers["y"], peers["core"]) + tuple(((expert + step) % 8, shard) for step in range(1, 8)))
    sums = [
        PlaneSum(
            shared_work[index],
            shared_out[index],
            receive[index],
            sum_send.at[index],
            sum_recv.at[index],
            bits,
            peers,
            SHARED_ORDER[index],
        )
        for index in range(3)
    ]
    for index in range(3):
        pltpu.make_async_copy(shared_in[index], shared_work[index], shared_sem.at[index]).wait()
        sums[index].start(0)
    for index in range(3):
        pltpu.make_async_copy(weights_in[index], weights[index], load_sem.at[index]).wait()

    _, capacity, width = rows_ref.shape
    gate_ref, up_ref, down_ref = weights
    middle = gate_ref.shape[1]
    cuts = middle // 512

    def block(z_from):
        pair = pl.ds(2 * z_from, 2)
        rows = rows_ref[pair].reshape(2 * capacity, width)
        grads = grads_ref[pair].reshape(2 * capacity, width)
        here = pl.ds(pl.multiple_of(z_from * 2 * capacity, 2 * capacity), 2 * capacity)
        out_sum[...] = jnp.zeros_like(out_sum)
        grad_sum[...] = jnp.zeros_like(grad_sum)

        def body(index, carry):
            cut = pl.ds(pl.multiple_of(index * 512, 512), 512)
            gate, up, down = gate_ref[:, cut], up_ref[:, cut], down_ref[cut, :]
            pre, lin = dense_product(rows, gate), dense_product(rows, up)
            mid = (jax.nn.silu(pre) * lin).astype(jnp.bfloat16)
            out_sum[...] += dense_product(mid, down)
            pre_grad, lin_grad = swiglu_back(product_t(grads, down), pre, lin)
            grad_sum[...] += product_t(pre_grad, gate) + product_t(lin_grad, up)
            middle_ref[here, cut] = mid
            pre_ref[here, cut] = pre_grad
            lin_ref[here, cut] = lin_grad
            return carry

        lax.fori_loop(0, cuts, body, 0)
        rows_put[pair] = out_sum[...].astype(jnp.bfloat16).reshape(2, capacity, width)
        grads_put[pair] = grad_sum[...].astype(jnp.bfloat16).reshape(2, capacity, width)
        for side in range(2):
            source = 2 * z_from + side

            @pl.when(source != expert)
            def _():
                send(grads_put.at[source], grads_back.at[expert], grad_send.at[source], grad_recv.at[expert], (source, shard))
                send(rows_put.at[source], rows_back.at[expert], out_send.at[source], out_recv.at[expert], (source, shard))

            @pl.when(source == expert)
            def _():
                rows_back[pl.ds(source, 1)] = rows_put[pl.ds(source, 1)]
                grads_back[pl.ds(source, 1)] = grads_put[pl.ds(source, 1)]

    z_order = ((zed + 2) % 4, 3 - zed, zed + 1 - 2 * (zed % 2), zed)
    for step in range(4):
        block(z_order[step])
        for one in sums:
            one.finish(step)
            if step < 3:
                one.start(step + 1)
            else:
                one.back_start(0)

    rows_all, grads_all = rows_ref, grads_ref

    def weight_grad(index):
        def body(step, carry):
            cut = pl.ds(pl.multiple_of(step * 512, 512), 512)
            if index == 2:
                left, right = middle_ref[:, cut], grads_all[...].reshape(8 * capacity, width)
                down_ref[cut, :] = t_product(left, right).astype(jnp.bfloat16)
            else:
                left, right = rows_all[...].reshape(8 * capacity, width), (pre_ref, lin_ref)[index][:, cut]
                weights[index][:, cut] = t_product(left, right).astype(jnp.bfloat16)
            return carry

        lax.fori_loop(0, cuts, body, 0)

    def shard_rows(index, y_of, core_of):
        rows = weights[index].shape[0] // 4
        return weights[index].at[pl.ds((y_of * 2 + core_of) * rows, rows)]

    def core_start(index):
        for y_of in range(2):
            send(
                shard_rows(index, y_of, 1 - core),
                expert_core[index].at[y_of],
                core_send.at[index, y_of],
                core_recv.at[index, y_of],
                peers["core"],
            )

    def core_finish(index):
        for y_of in range(2):
            wait_for(expert_core[index].at[y_of], core_recv.at[index, y_of])
            wait_for(shard_rows(index, y_of, 1 - core), core_send.at[index, y_of])
        for y_of in range(2):
            kept = shard_rows(index, y_of, core)
            add_rows(expert_core[index].at[y_of], kept, expert_core[index].at[y_of])
        send(expert_core[index].at[1 - why], expert_y[index], y_send.at[index], y_recv.at[index], peers["y"])

    def y_finish(index):
        wait_for(expert_y[index], y_recv.at[index])
        add_rows(expert_out[index], expert_core[index].at[why], expert_y[index])
        wait_for(expert_core[index].at[1 - why], y_send.at[index])

    weight_grad(0)
    core_start(0)
    weight_grad(1)
    core_finish(0)
    core_start(1)
    for one in sums:
        one.back_finish(0)
        one.back_start(1)
    weight_grad(2)
    core_finish(1)
    core_start(2)
    for one in sums:
        one.back_finish(1)
        one.back_start(2)
    core_finish(2)
    for one in sums:
        one.back_finish(2)
    for step in range(1, 8):
        target, origin = (expert + step) % 8, (expert + 8 - step) % 8
        wait_for(rows_put.at[target], out_send.at[target])
        wait_for(grads_put.at[target], grad_send.at[target])
        wait_for(rows_back.at[origin], out_recv.at[origin])
        wait_for(grads_back.at[origin], grad_recv.at[origin])
    for index in range(3):
        y_finish(index)


def add_rows(target, first, second):
    def body(index, carry):
        at = pl.ds(pl.multiple_of(index * 64, 64), 64)
        target[at, :] = (first[at, :].astype(jnp.float32) + second[at, :].astype(jnp.float32)).astype(target.dtype)
        return carry

    lax.fori_loop(0, first.shape[0] // 64, body, 0)


def second_part(rows, grads, weights, shared):
    in_hbm, in_vmem = pl.BlockSpec(memory_space=pl.ANY), pl.BlockSpec(memory_space=pltpu.VMEM)
    dma, bfloat = pltpu.SemaphoreType.DMA, jnp.bfloat16
    shape = jax.ShapeDtypeStruct
    count, capacity, width = rows.shape
    middle = weights[0].shape[1]
    quarter = [(weight.shape[0] // 4, weight.shape[1]) for weight in weights]
    own = [(1,) + work.shape[1:] for work in shared]
    blocks = (count * capacity, middle)
    return pl.pallas_call(
        second_kernel,
        out_shape=[shape(rows.shape, bfloat)] * 2
        + [shape(one, bfloat) for one in quarter]
        + [shape(one, bfloat) for one in own],
        in_specs=[in_vmem] * 2 + [in_hbm] * 6,
        out_specs=[in_vmem] * 8,
        scratch_shapes=[pltpu.VMEM(weight.shape, bfloat) for weight in weights]
        + [pltpu.VMEM(work.shape, bfloat) for work in shared]
        + [pltpu.VMEM(rows.shape, bfloat)] * 2
        + [pltpu.VMEM(blocks, bfloat)] * 3
        + [pltpu.VMEM((2 * capacity, width), jnp.float32)] * 2
        + [pltpu.VMEM((2,) + one, bfloat) for one in quarter]
        + [pltpu.VMEM(one, bfloat) for one in quarter]
        + [
            pltpu.VMEM(one, bfloat)
            for index in range(3)
            for one in receive_shapes(shared[index].shape, SHARED_ORDER[index])
        ]
        + [dma((3,)), dma((3,))]
        + [dma((8,))] * 4
        + [dma((3, 2)), dma((3, 2)), dma((3,)), dma((3,)), dma((3, 7)), dma((3, 7))],
        compiler_params=pltpu.CompilerParams(collective_id=1, has_side_effects=True, vmem_limit_bytes=62 << 20),
        cost_estimate=pl.CostEstimate(flops=29000000000, bytes_accessed=30000000, transcendentals=2000000),
    )(rows, grads, *weights, *shared)


def third_kernel(*refs):
    rows_back, grads_back, mixed_ref, shared_ref, ffn_grad_ref, cot_ref, hidden_ref, logit_ref, route_ref, gain_ref = refs[:10]
    normed_ref, query_ref, key_ref, value_ref, lse_ref, attended_ref = refs[10:16]
    segment_row, segment_col, padding_row, cosine_ref, sine_ref = refs[16:21]
    wq_ref, wk_ref, wv_ref, wo_ref = refs[21:25]
    output_ref, input_grad_ref, logit_grad_ref, gain_out = refs[25:29]
    sums_out = refs[29:33]
    query_grad, key_grad, value_grad, context_grad, attended_grad, mixed_grad_ref = refs[33:39]
    weight_grads = refs[39:43]
    weight_work = refs[43:47]
    context_core, context_y = refs[47:49]
    receive = [refs[49 + 4 * index : 53 + 4 * index] for index in range(4)]
    gain_parts, gain_recv = refs[65:67]
    core_send, core_recv, sum_send, sum_recv, ctx_send, ctx_recv, gain_send, gain_got = refs[67:]
    expert, shard, zed, core, bits, peers = plane_places()
    why = bits["y"]
    enter(tuple(peers[axis] for axis in ("core", "y", "x", "z1", "z2")))
    tokens, width = hidden_ref.shape
    here = pl.ds(pl.multiple_of(shard * tokens, tokens), tokens)
    single, bfloat = jnp.float32, jnp.bfloat16

    experts, capacity = rows_back.shape[0], rows_back.shape[1]
    slots = experts * capacity
    expert_at = lax.broadcasted_iota(jnp.int32, (tokens, 128), 1)
    choices = [route_ref[:, k : k + 1] for k in range(TOP)]
    named = ((choices[0] == expert_at) | (choices[1] == expert_at)).astype(bfloat)
    before = lax.broadcasted_iota(jnp.int32, (tokens, tokens), 1) < lax.broadcasted_iota(jnp.int32, (tokens, tokens), 0)
    rank = dense_product(before.astype(bfloat), named)
    slot_at = lax.broadcasted_iota(jnp.int32, (tokens, slots), 1)

    def slot_column(k):
        slot = rank + expert_at.astype(single) * float(capacity)
        return jnp.sum(jnp.where(choices[k] == expert_at, slot, 0.0), axis=1, keepdims=True).astype(jnp.int32)

    picks = [slot_at == slot_column(k) for k in range(TOP)]
    gate_probs = gate_columns(logit_ref[...])
    grad_out = cot_ref[...].astype(single)
    results = rows_back[...].reshape(slots, width)
    per_route = [dense_product(pick.astype(bfloat), results) for pick in picks]
    mixed = mixed_ref[...]
    routed = gate_probs[0] * per_route[0] + gate_probs[1] * per_route[1]
    output_ref[...] = (mixed + shared_ref[...] + routed).astype(bfloat)
    contrib = [jnp.sum(rows * grad_out, axis=1, keepdims=True) for rows in per_route]
    mean_contrib = gate_probs[0] * contrib[0] + gate_probs[1] * contrib[1]
    logit_grad = [gate * (value - mean_contrib) for gate, value in zip(gate_probs, contrib)]
    choice_at = lax.broadcasted_iota(jnp.int32, logit_grad_ref.shape, 1)
    logit_grad_ref[...] = jnp.where(choice_at == 0, logit_grad[0], logit_grad[1])

    ffn_grad = ffn_grad_ref[...] + dense_product((picks[0] | picks[1]).astype(bfloat), grads_back[...].reshape(slots, width))
    scale_second = rms_scale(mixed)
    gain_parts[0] = jnp.zeros_like(gain_parts[0])
    gain_parts[0, 1:2, :] = jnp.sum(ffn_grad * mixed * scale_second, axis=0, keepdims=True)
    scaled = ffn_grad * gain_ref[1:2, :]
    mixed_grad = (
        grad_out
        + scale_second * scaled
        - mixed * (scale_second * scale_second * scale_second) * jnp.mean(scaled * mixed, axis=-1, keepdims=True)
    )
    mixed_grad_ref[...] = mixed_grad
    mixed_low = mixed_grad.astype(bfloat)
    attended_grad[...] = product_t(mixed_low, wo_ref[...]).astype(bfloat)

    def shard_rows(ref, y_of, core_of):
        rows = ref.shape[0] // 4
        return ref.at[pl.ds((y_of * 2 + core_of) * rows, rows)]

    def core_start(index):
        for y_of in range(2):
            send(
                shard_rows(weight_grads[index], y_of, 1 - core),
                weight_work[index].at[y_of],
                core_send.at[index, y_of],
                core_recv.at[index, y_of],
                peers["core"],
            )

    def core_finish(index):
        for y_of in range(2):
            wait_for(weight_work[index].at[y_of], core_recv.at[index, y_of])
            wait_for(shard_rows(weight_grads[index], y_of, 1 - core), core_send.at[index, y_of])
            add_rows(weight_work[index].at[y_of], shard_rows(weight_grads[index], y_of, core), weight_work[index].at[y_of])

    sums = [
        PlaneSum(
            weight_work[index],
            sums_out[index],
            receive[index],
            sum_send.at[index],
            sum_recv.at[index],
            bits,
            peers,
            ATTENTION_ORDER[index],
        )
        for index in range(4)
    ]
    weight_grads[3][...] = t_product(attended_ref[...], mixed_low).astype(bfloat)
    core_start(3)

    def head_pair(pair, carry):
        lanes = pl.ds(pl.multiple_of(pair * 128, 128), 128)
        query, keys, values, grads = query_ref[:, lanes], key_ref[:, lanes], value_ref[:, lanes], attended_grad[:, lanes]
        allowed = allowed_mask(shard * tokens, 0, segment_col[here, :], segment_row[...], padding_row[...])
        lane = lax.broadcasted_iota(jnp.int32, query.shape, 1)
        from_keys = []
        key_total = value_total = None
        for half in range(2):
            chosen = (lane >= 64) if half else (lane < 64)
            one_query = jnp.where(chosen, query, jnp.zeros_like(query))
            one_grad = jnp.where(chosen, grads, jnp.zeros_like(grads))
            scores = jnp.where(allowed, product_t(one_query, keys) * 0.125, neg_fill)
            probs = jnp.exp(scores - lse_ref[2 * pair + half])
            probs_grad = product_t(one_grad, values)
            delta = jnp.sum(probs * probs_grad, axis=1, keepdims=True)
            scores_grad = (probs * (probs_grad - delta)).astype(bfloat)
            from_keys.append(dense_product(scores_grad, keys))
            key_part = t_product(scores_grad, one_query)
            value_part = t_product(probs.astype(bfloat), one_grad)
            key_total = key_part if key_total is None else key_total + key_part
            value_total = value_part if value_total is None else value_total + value_part
        back = jnp.where(lane < 64, from_keys[0], from_keys[1]) * 0.125
        query_grad[:, lanes] = rotate_pair(back, cosine_ref[here, :], -sine_ref[here, :]).astype(bfloat)
        key_grad[:, lanes] = rotate_pair(key_total * 0.125, cosine_ref[...], -sine_ref[...]).astype(bfloat)
        value_grad[:, lanes] = value_total.astype(bfloat)
        return carry

    lax.fori_loop(0, 3, head_pair, 0)
    core_finish(3)
    sums[3].start(0)
    lax.fori_loop(3, 6, head_pair, 0)

    weight_grads[1][...] = t_product(normed_ref[...], key_grad[...]).astype(bfloat)
    core_start(1)
    weight_grads[2][...] = t_product(normed_ref[...], value_grad[...]).astype(bfloat)
    core_start(2)
    core_finish(1)
    sums[1].start(0)
    weight_grads[0][...] = t_product(normed_ref[here, :], query_grad[...]).astype(bfloat)
    core_start(0)
    core_finish(2)
    sums[2].start(0)

    def context_block(block, carry):
        rows = pl.ds(pl.multiple_of(block * tokens, tokens), tokens)
        total = product_t(key_grad[rows, :], wk_ref[...]) + product_t(value_grad[rows, :], wv_ref[...])
        context_grad[rows, :] = total.astype(bfloat)
        return carry

    lax.fori_loop(0, 4, context_block, 0)
    for y_of in range(2):
        send(
            shard_rows(context_grad, y_of, 1 - core),
            context_core.at[y_of],
            ctx_send.at[y_of],
            ctx_recv.at[y_of],
            peers["core"],
        )
    core_finish(0)
    sums[0].start(0)
    for y_of in range(2):
        wait_for(context_core.at[y_of], ctx_recv.at[y_of])
        wait_for(shard_rows(context_grad, y_of, 1 - core), ctx_send.at[y_of])
        add_rows(context_core.at[y_of], shard_rows(context_grad, y_of, core), context_core.at[y_of])
    send(context_core.at[1 - why], context_y, ctx_send.at[2], ctx_recv.at[2], peers["y"])
    normed_grad = product_t(query_grad[...], wq_ref[...])

    def step_all(step):
        for one in (sums[3], sums[1], sums[2], sums[0]):
            one.finish(step)
            if step < 3:
                one.start(step + 1)
            else:
                one.back_start(0)

    step_all(0)
    wait_for(context_y, ctx_recv.at[2])
    wait_for(context_core.at[1 - why], ctx_send.at[2])
    normed_grad = normed_grad + context_core[pl.ds(why, 1)].reshape(tokens, width).astype(single) + context_y[...].astype(single)
    rows_in = hidden_ref[...].astype(single)
    scale_first = rms_scale(rows_in)
    gain_parts[0, 0:1, :] = jnp.sum(normed_grad * rows_in * scale_first, axis=0, keepdims=True)

    def gain_start(step):
        peer = peers[("core", "y", "x", "z1", "z2")[step]]
        send(gain_parts.at[step], gain_recv.at[step], gain_send.at[step], gain_got.at[step], peer)

    def gain_finish(step):
        wait_for(gain_recv.at[step], gain_got.at[step])
        gain_parts[step + 1] = gain_parts[step] + gain_recv[step]

    gain_start(0)
    scaled = normed_grad * gain_ref[0:1, :]
    input_grad_ref[...] = (
        mixed_grad_ref[...]
        + scale_first * scaled
        - rows_in * (scale_first * scale_first * scale_first) * jnp.mean(scaled * rows_in, axis=-1, keepdims=True)
    )
    gain_finish(0)
    gain_start(1)
    step_all(1)
    gain_finish(1)
    gain_start(2)
    step_all(2)
    gain_finish(2)
    gain_start(3)
    step_all(3)
    gain_finish(3)
    gain_start(4)
    for step in range(3):
        for one in (sums[3], sums[1], sums[2], sums[0]):
            one.back_finish(step)
            if step < 2:
                one.back_start(step + 1)
    gain_finish(4)
    gain_out[...] = gain_parts[5]
    for step in range(5):
        wait_for(gain_parts.at[step], gain_send.at[step])


def third_part(back, mixed, shared_out, ffn_grad, cotangent, hidden, logits, routes, gains, kept, segment, padding, weights):
    tokens, width = hidden.shape
    bfloat, single = jnp.bfloat16, jnp.float32
    in_vmem = pl.BlockSpec(memory_space=pltpu.VMEM)
    dma, shape, vmem = pltpu.SemaphoreType.DMA, jax.ShapeDtypeStruct, pltpu.VMEM
    cosine, sine = rotary_tables(4 * tokens, width // HEADS)
    work = (2, width // 4, width)
    arguments = (
        *back,
        mixed,
        shared_out,
        ffn_grad,
        cotangent,
        hidden,
        logits,
        routes,
        gains,
        *kept,
        segment[None, :],
        segment[:, None],
        padding[None, :],
        jnp.asarray(cosine),
        jnp.asarray(sine),
        *weights,
    )
    return pl.pallas_call(
        third_kernel,
        out_shape=[
            shape((tokens, width), bfloat),
            shape((tokens, width), single),
            shape((tokens, TOP), single),
            shape((8, width), single),
        ]
        + [shape((1,) + work[1:], bfloat)] * 4,
        in_specs=[in_vmem] * len(arguments),
        out_specs=[in_vmem] * 8,
        scratch_shapes=[vmem((tokens, width), bfloat)]
        + [vmem((4 * tokens, width), bfloat)] * 3
        + [vmem((tokens, width), bfloat), vmem((tokens, width), single)]
        + [vmem((width, width), bfloat)] * 4
        + [vmem(work, bfloat)] * 4
        + [vmem((2, tokens, width), bfloat), vmem((tokens, width), bfloat)]
        + [vmem(one, bfloat) for order in ATTENTION_ORDER for one in receive_shapes(work, order)]
        + [vmem((6, 8, width), single), vmem((5, 8, width), single)]
        + [dma((4, 2)), dma((4, 2)), dma((4, 7)), dma((4, 7)), dma((3,)), dma((3,)), dma((5,)), dma((5,))],
        compiler_params=pltpu.CompilerParams(collective_id=2, has_side_effects=True, vmem_limit_bytes=60 << 20),
        cost_estimate=pl.CostEstimate(flops=12000000000, bytes_accessed=25000000, transcendentals=3000000),
    )(*arguments)


def swap(value, axis, bit):
    size = lax.axis_size(axis)
    return lax.ppermute(value, axis, [(index, index ^ bit) for index in range(size)])


def halves(value, bit_set, dim):
    half = value.shape[dim] // 2
    keep = lax.dynamic_slice_in_dim(value, bit_set * half, half, dim)
    give = lax.dynamic_slice_in_dim(value, (1 - bit_set) * half, half, dim)
    return keep, give


def fold(value, axis, bit, dim):
    bit_set = (lax.axis_index(axis) // bit) % 2
    keep, give = halves(value, bit_set, dim)
    return (keep.astype(jnp.float32) + swap(give.astype(jnp.bfloat16), axis, bit).astype(jnp.float32)).astype(jnp.bfloat16)


def unfold(value, axis, bit, dim):
    bit_set = (lax.axis_index(axis) // bit) % 2
    come = swap(value, axis, bit)
    return jnp.where(bit_set == 0, jnp.concatenate([value, come], dim), jnp.concatenate([come, value], dim))


def bits_of(axis):
    size = lax.axis_size(axis)
    return [1 << place for place in range(size.bit_length() - 1)]


def scatter_shards(value):
    count = lax.axis_size("shard")
    blocks = value.reshape((count // 2, 2, value.shape[0] // count) + value.shape[1:])
    blocks = fold(blocks, "shard", 1, 1)[:, 0]
    for bit in reversed(bits_of("shard")[1:]):
        blocks = fold(blocks, "shard", bit, 0)
    return blocks[0]


def sum_plane(value, dim):
    bits = bits_of("expert")
    for bit in bits:
        value = fold(value, "expert", bit, dim)
    for bit in reversed(bits):
        value = unfold(value, "expert", bit, dim)
    return value.astype(jnp.float32)


def shards(
    hidden_in,
    gain_attn,
    gain_ffn,
    w_query,
    w_key,
    w_value,
    w_out,
    shared_gate,
    shared_up,
    shared_down,
    expert_gate,
    expert_up,
    expert_down,
    gate_logits,
    routes,
    segment,
    padding,
    cotangent,
):
    bfloat = jnp.bfloat16
    tokens = hidden_in.shape[1]
    model_width = hidden_in.shape[2]
    head_size = model_width // HEADS
    experts = lax.axis_size("expert")
    capacity = max(2, 2 * tokens * TOP // experts)
    shard_count = lax.axis_size("shard")
    shard_index = lax.axis_index("shard")
    score_scale = head_size ** (-0.5)
    head_shape = (tokens, HEADS, head_size)
    fast = (experts, shard_count, WINDOW) == (8, 4, 4 * tokens)
    dense_own = (w_query, w_key, w_value, w_out, shared_gate, shared_up, shared_down)
    expert_own = (expert_gate[0], expert_up[0], expert_down[0])
    rows_in = hidden_in[0].astype(jnp.float32)
    scale_first = rms_scale(rows_in)
    positions = shard_index * tokens + jnp.arange(tokens, dtype=jnp.int32)
    segment_row, padding_row = segment[0], padding[0]
    query_segment = lax.dynamic_slice_in_dim(segment_row, shard_index * tokens, tokens)
    if fast:
        gain_own = lax.dynamic_update_slice(
            jnp.zeros((2, model_width), bfloat),
            jnp.stack([gain_attn, gain_ffn]),
            (0, shard_index * gain_attn.shape[0]),
        )
        full, rest = first_part(
            hidden_in[0],
            gain_own,
            dense_own,
            expert_own,
            segment_row,
            padding_row,
            cotangent[0],
            gate_logits[0],
            routes[0],
        )
        gains, normed_ctx, query_low, keys_ctx, values_ctx, log_total, attended, mixed_rows, normed_ffn = rest[:9]
        received, grad_received, shared_out, ffn_grad_shared, *shared_work = rest[9:]
        gain_first, gain_second = gains[0], gains[1]
        w_q, w_k, w_v, w_o = (full[name] for name in ("wq", "wk", "wv", "wo"))
        e_gate, e_up, e_down = (full[name] for name in LATE)
        reach, key_start = shard_count - 1, 0
        key_segment, key_padding = segment_row, padding_row
        key_positions = jnp.arange(4 * tokens, dtype=jnp.int32)
        allowed = allowed_mask(shard_index * tokens, 0, query_segment[:, None], key_segment[None], key_padding[None])
    else:
        gather = functools.partial(lax.all_gather, axis_name="shard", tiled=True)
        w_q, w_k, w_v, w_o, s_gate, s_up, s_down = (gather(weight) for weight in dense_own)
        e_gate, e_up, e_down = (gather(weight) for weight in expert_own)
        gain_first, gain_second = (gather(gain).astype(jnp.float32) for gain in (gain_attn, gain_ffn))
        reach = min((WINDOW + tokens - 2) // tokens, shard_count - 1)
        lead_rows, key_rows = reach * tokens, (reach + 1) * tokens
        context = [from_behind(hidden_in[0], "shard", offset) for offset in range(reach, 0, -1)] + [hidden_in[0]]
        context = jnp.concatenate(context, axis=0).astype(jnp.float32)
        normed_ctx = (context * rms_scale(context) * gain_first).astype(bfloat)
        key_positions = (shard_index - reach) * tokens + jnp.arange(key_rows, dtype=jnp.int32)
        query_low = rotate(
            dense_product(normed_ctx[lead_rows:], w_q).reshape(head_shape), positions, 1.0
        ).astype(bfloat)
        keys_ctx = rotate(
            dense_product(normed_ctx, w_k).reshape(key_rows, HEADS, head_size), key_positions, 1.0
        ).astype(bfloat)
        values_ctx = dense_product(normed_ctx, w_v).astype(bfloat)
        segment_ext = jnp.concatenate([jnp.full((lead_rows,), -1, jnp.int32), segment_row])
        padding_ext = jnp.concatenate([jnp.zeros((lead_rows,), jnp.int32), padding_row])
        key_segment = lax.dynamic_slice_in_dim(segment_ext, shard_index * tokens, key_rows)
        key_padding = lax.dynamic_slice_in_dim(padding_ext, shard_index * tokens, key_rows)
        allowed = allowed_mask(
            shard_index * tokens,
            (shard_index - reach) * tokens,
            query_segment[:, None],
            key_segment[None],
            key_padding[None],
        )
    key_rows = (reach + 1) * tokens
    query_heads = query_low.reshape(head_shape)
    keys_all = keys_ctx.reshape(key_rows, HEADS, head_size)
    values_all = values_ctx.reshape(key_rows, HEADS, head_size)

    def score_block():
        raw_scores = (
            jnp.einsum("qhd,khd->hqk", query_heads, keys_all, preferred_element_type=jnp.float32)
            * score_scale
        )
        return jnp.where(allowed[None], raw_scores, neg_fill)

    if not fast:
        scores = score_block()
        top_score = jnp.max(scores, axis=-1, keepdims=True)
        exponent = jnp.exp(scores - top_score)
        exp_total = jnp.sum(exponent, axis=-1, keepdims=True)
        log_total = top_score + jnp.log(exp_total)
        attended = (
            jnp.einsum(
                "hqk,khd->qhd",
                (exponent / exp_total).astype(bfloat),
                values_all,
                preferred_element_type=jnp.float32,
            )
            .astype(bfloat)
            .reshape(tokens, model_width)
        )
        mixed_rows = rows_in + dense_product(attended, w_o)
        normed_ffn = (mixed_rows * rms_scale(mixed_rows) * gain_second).astype(bfloat)
    scale_second = rms_scale(mixed_rows)
    grad_low = cotangent[0]
    grad_out = grad_low.astype(jnp.float32)
    gate_probs = jax.nn.softmax(gate_logits[0], axis=-1)
    route_flat = routes[0].reshape(-1)
    route_total = tokens * TOP
    onehot = (route_flat[:, None] == jnp.arange(experts, dtype=jnp.int32)[None, :]).astype(
        jnp.int32
    )
    slot_rank = jnp.sum((jnp.cumsum(onehot, axis=0) - onehot) * onehot, axis=1)
    places = route_flat * capacity + slot_rank
    if not fast:
        shared_pre = dense_product(normed_ffn, s_gate)
        shared_lin = dense_product(normed_ffn, s_up)
        shared_mid = (jax.nn.silu(shared_pre) * shared_lin).astype(bfloat)
        shared_out = dense_product(shared_mid, s_down)
        grad_shared_mid = product_t(grad_low, s_down)
        grad_shared_pre, grad_shared_lin = swiglu_back(grad_shared_mid, shared_pre, shared_lin)
        shared_down_grad = dense_product(shared_mid.T, grad_low)
        shared_gate_grad = dense_product(normed_ffn.T, grad_shared_pre)
        shared_up_grad = dense_product(normed_ffn.T, grad_shared_lin)
        ffn_grad_shared = product_t(grad_shared_pre, s_gate) + product_t(grad_shared_lin, s_up)
        slot_table = (
            jnp.full((experts * capacity,), route_total, dtype=jnp.int32)
            .at[places]
            .set(jnp.arange(route_total, dtype=jnp.int32))
        )
        padded_rows = jnp.concatenate([normed_ffn, jnp.zeros((1, model_width), bfloat)], axis=0)
        send_rows = padded_rows[slot_table // TOP].reshape(experts, capacity, model_width)
        received = lax.all_to_all(send_rows, "expert", split_axis=0, concat_axis=0, tiled=True)
        route_grad = (
            (gate_probs[:, :, None] * grad_out[:, None, :])
            .astype(bfloat)
            .reshape(route_total, model_width)
        )
        route_padded = jnp.concatenate([route_grad, jnp.zeros((1, model_width), bfloat)], axis=0)
        send_grad = route_padded[slot_table].reshape(experts, capacity, model_width)
        grad_received = lax.all_to_all(send_grad, "expert", split_axis=0, concat_axis=0, tiled=True)
    if fast:
        returned, grad_back, *sums = second_part(received, grad_received, (e_gate, e_up, e_down), shared_work)
        output, input_grad, logit_grad, gain_grads, *attention_grads = third_part(
            (returned, grad_back),
            mixed_rows,
            shared_out,
            ffn_grad_shared,
            grad_low,
            hidden_in[0],
            gate_logits[0],
            routes[0],
            gains,
            (normed_ctx, query_low, keys_ctx, values_ctx, log_total, attended),
            segment_row,
            padding_row,
            (w_q, w_k, w_v, w_o),
        )
        gain_grads = lax.dynamic_slice_in_dim(gain_grads, shard_index * gain_attn.shape[0], gain_attn.shape[0], 1)
        return (
            output[None],
            input_grad[None],
            logit_grad[None],
            gain_grads[0],
            gain_grads[1],
            *(grad[0].astype(jnp.float32) for grad in attention_grads),
            *(grad[0].astype(jnp.float32) for grad in sums[3:]),
            *(grad[None].astype(jnp.float32) for grad in sums[:3]),
        )
    else:
        gate_pre = jnp.einsum("sid,df->sif", received, e_gate, preferred_element_type=jnp.float32)
        up_pre = jnp.einsum("sid,df->sif", received, e_up, preferred_element_type=jnp.float32)
        middle = (jax.nn.silu(gate_pre) * up_pre).astype(bfloat)
        result = jnp.einsum("sif,fd->sid", middle, e_down, preferred_element_type=jnp.float32).astype(bfloat)
        returned = lax.all_to_all(result, "expert", split_axis=0, concat_axis=0, tiled=True)
        grad_middle = jnp.einsum(
            "sid,fd->sif", grad_received, e_down, preferred_element_type=jnp.float32
        )
        grad_gate_pre, grad_up_pre = swiglu_back(grad_middle, gate_pre, up_pre)
        expert_down_grad = jnp.einsum(
            "sif,sid->fd", middle, grad_received, preferred_element_type=jnp.float32
        )
        expert_gate_grad = jnp.einsum(
            "sid,sif->df", received, grad_gate_pre, preferred_element_type=jnp.float32
        )
        expert_up_grad = jnp.einsum(
            "sid,sif->df", received, grad_up_pre, preferred_element_type=jnp.float32
        )
        grad_rows = (
            jnp.einsum("sif,df->sid", grad_gate_pre, e_gate, preferred_element_type=jnp.float32)
            + jnp.einsum("sif,df->sid", grad_up_pre, e_up, preferred_element_type=jnp.float32)
        ).astype(bfloat)
        grad_back = lax.all_to_all(grad_rows, "expert", split_axis=0, concat_axis=0, tiled=True)
        expert_grads = tuple(
            scatter_shards(grad.astype(bfloat))[None].astype(jnp.float32)
            for grad in (expert_gate_grad, expert_up_grad, expert_down_grad)
        )
        shared_grads = (
            sum_plane(scatter_shards(shared_gate_grad.astype(bfloat)), 1),
            sum_plane(scatter_shards(shared_up_grad.astype(bfloat)), 1),
            sum_plane(scatter_shards(shared_down_grad.astype(bfloat)), 0),
        )
    per_route = (
        returned.reshape(experts * capacity, model_width)[places]
        .astype(jnp.float32)
        .reshape(tokens, TOP, model_width)
    )
    routed = jnp.sum(gate_probs[:, :, None] * per_route, axis=1)
    output = (mixed_rows + shared_out + routed).astype(bfloat)
    contrib = jnp.sum(per_route * grad_out[:, None, :], axis=-1)
    logit_grad = gate_probs * (contrib - jnp.sum(gate_probs * contrib, axis=-1, keepdims=True))
    grad_routes = (
        grad_back.reshape(experts * capacity, model_width)[places]
        .astype(jnp.float32)
        .reshape(tokens, TOP, model_width)
    )
    grad_normed_ffn = jnp.sum(grad_routes, axis=1) + ffn_grad_shared
    gain_ffn_grad = jnp.sum(grad_normed_ffn * mixed_rows * scale_second, axis=0)
    scaled_second = grad_normed_ffn * gain_second
    grad_mixed = (
        grad_out
        + scale_second * scaled_second
        - mixed_rows
        * scale_second**3
        * jnp.mean(scaled_second * mixed_rows, axis=-1, keepdims=True)
    )
    grad_mixed_low = grad_mixed.astype(bfloat)
    w_out_grad = dense_product(attended.T, grad_mixed_low)
    grad_attended = product_t(grad_mixed_low, w_o).astype(bfloat).reshape(head_shape)
    attn_probs = jnp.exp(score_block() - log_total)
    grad_probs = jnp.einsum(
        "qhd,khd->hqk", grad_attended, values_all, preferred_element_type=jnp.float32
    )
    delta_rows = jnp.sum(attn_probs * grad_probs, axis=-1, keepdims=True)
    grad_scores = (attn_probs * (grad_probs - delta_rows)).astype(bfloat)
    grad_query = (
        jnp.einsum("hqk,khd->qhd", grad_scores, keys_all, preferred_element_type=jnp.float32)
        * score_scale
    )
    grad_keys = (
        jnp.einsum("hqk,qhd->khd", grad_scores, query_heads, preferred_element_type=jnp.float32)
        * score_scale
    )
    grad_values = jnp.einsum(
        "hqk,qhd->khd", attn_probs.astype(bfloat), grad_attended, preferred_element_type=jnp.float32
    )
    grad_query_low = rotate(grad_query, positions, -1.0).astype(bfloat).reshape(tokens, model_width)
    grad_key_low = rotate(grad_keys, key_positions, -1.0).astype(bfloat).reshape(key_rows, model_width)
    grad_value_low = grad_values.astype(bfloat).reshape(key_rows, model_width)
    if fast:
        normed = lax.dynamic_slice_in_dim(normed_ctx, shard_index * tokens, tokens)
    else:
        normed = normed_ctx[reach * tokens :]
    w_query_grad = dense_product(normed.T, grad_query_low)
    w_key_grad = dense_product(normed_ctx.T, grad_key_low)
    w_value_grad = dense_product(normed_ctx.T, grad_value_low)
    grad_context = product_t(grad_key_low, w_k) + product_t(grad_value_low, w_v)
    grad_normed = product_t(grad_query_low, w_q)
    if fast:
        grad_normed = grad_normed + scatter_shards(grad_context.astype(bfloat)).astype(jnp.float32)
    else:
        grad_normed = grad_normed + grad_context[reach * tokens :]
        for offset in range(1, reach + 1):
            sent = grad_context[(reach - offset) * tokens :][:tokens].astype(bfloat)
            grad_normed = grad_normed + from_behind(sent, "shard", -offset).astype(jnp.float32)
    gain_attn_grad = jnp.sum(grad_normed * rows_in * scale_first, axis=0)
    scaled_first = grad_normed * gain_first
    input_grad = (
        grad_mixed
        + scale_first * scaled_first
        - rows_in * scale_first**3 * jnp.mean(scaled_first * rows_in, axis=-1, keepdims=True)
    )
    gain_rows = jnp.stack([gain_attn_grad, gain_ffn_grad], axis=1).astype(bfloat)
    gain_total = lax.psum(scatter_shards(gain_rows), "expert").astype(jnp.float32)
    attn_grads = jnp.stack([w_query_grad, w_key_grad, w_value_grad, w_out_grad]).astype(bfloat)
    attn_rows = scatter_shards(attn_grads.transpose(1, 0, 2)).transpose(1, 0, 2)
    attn_total = sum_plane(attn_rows.reshape(-1, model_width), 0).reshape(attn_rows.shape)
    return (
        output[None],
        input_grad[None],
        logit_grad[None],
        gain_total[:, 0],
        gain_total[:, 1],
        attn_total[0],
        attn_total[1],
        attn_total[2],
        attn_total[3],
        shared_grads[0],
        shared_grads[1],
        shared_grads[2],
        expert_grads[0],
        expert_grads[1],
        expert_grads[2],
    )


def solution(mesh):
    placed = (
        P("expert", "shard", None),
        P("shard"),
        P("shard"),
        P("shard", None),
        P("shard", None),
        P("shard", None),
        P("shard", None),
        P("shard", None),
        P("shard", None),
        P("shard", None),
        P("expert", "shard", None),
        P("expert", "shard", None),
        P("expert", "shard", None),
        P("expert", "shard", None),
        P("expert", "shard", None),
        P("expert", None),
        P("expert", None),
        P("expert", "shard", None),
    )
    return jax.shard_map(
        shards,
        mesh=mesh,
        in_specs=placed,
        out_specs=(
            P("expert", "shard", None),
            P("expert", "shard", None),
            P("expert", "shard", None),
            P("shard"),
            P("shard"),
            P("shard", None),
            P("shard", None),
            P("shard", None),
            P("shard", None),
            P("shard", None),
            P("shard", None),
            P("shard", None),
            P("expert", "shard", None),
            P("expert", "shard", None),
            P("expert", "shard", None),
        ),
        check_vma=False,
    )
```

```python
import functools
import math

import jax
import jax.numpy as jnp
import numpy as np
from jax import lax
from jax.experimental import pallas as pl
from jax.experimental.pallas import tpu as pltpu
from jax.sharding import PartitionSpec as P

HEADS = 12
TOP = 2
WINDOW = 1024
MESH = pl.DeviceIdType.MESH
norm_eps = 1e-06
neg_fill = -1e30
rope_base = 10000.0

DIRECT = ("hid", "gains")
EARLY = ("wk", "wv", "wq", "wo")
SPREAD = ("sg", "su", "sd")
LATE = ("eg", "eu", "ed")
NAMES = DIRECT + EARLY + SPREAD + LATE
PASSING = DIRECT + EARLY + SPREAD
SAVED = 11


def dense_product(left, right):
    return jnp.dot(left, right, preferred_element_type=jnp.float32)


def product_t(left, right):
    return lax.dot_general(left, right, (((1,), (1,)), ((), ())), preferred_element_type=jnp.float32)


def t_product(left, right):
    return lax.dot_general(left, right, (((0,), (0,)), ((), ())), preferred_element_type=jnp.float32)


def rms_scale(values):
    return lax.rsqrt(jnp.mean(values * values, axis=-1, keepdims=True) + norm_eps)


def rotary_tables(length, head_size):
    half = head_size // 2
    frequency = np.float32(rope_base) ** (-np.arange(half, dtype=np.float32) / np.float32(half))
    angles = np.arange(length, dtype=np.float32)[:, None] * frequency[None, :]
    cosine, sine = np.cos(angles).astype(np.float32), np.sin(angles).astype(np.float32)
    return np.concatenate([cosine] * 4, axis=1), np.concatenate([-sine, sine] * 2, axis=1)


def rotate_pair(values, cosine, sine):
    lane = lax.broadcasted_iota(jnp.int32, values.shape, 1)
    partner = jnp.where(lane % 64 < 32, pltpu.roll(values, 96, 1), pltpu.roll(values, 32, 1))
    return values * cosine + partner * sine


def rotate(values, positions, direction):
    half_size = values.shape[-1] // 2
    frequency = rope_base ** (-jnp.arange(half_size, dtype=jnp.float32) / half_size)
    angles = positions.astype(jnp.float32)[:, None] * frequency[None, :]
    cosine = jnp.cos(angles)[:, None, :]
    sine_part = direction * jnp.sin(angles)[:, None, :]
    first_half = values[..., :half_size]
    second_half = values[..., half_size:]
    return jnp.concatenate(
        [
            first_half * cosine - second_half * sine_part,
            second_half * cosine + first_half * sine_part,
        ],
        axis=-1,
    )


def swiglu_back(grad_middle, gate_pre, up_pre):
    sigmoid_gate = jax.nn.sigmoid(gate_pre)
    activated = gate_pre * sigmoid_gate
    grad_gate = grad_middle * up_pre * sigmoid_gate * (1.0 + gate_pre * (1.0 - sigmoid_gate))
    grad_up = grad_middle * activated
    return (grad_gate.astype(jnp.bfloat16), grad_up.astype(jnp.bfloat16))


def from_behind(value, axis, steps):
    count = lax.axis_size(axis)
    first, last = (max(0, -steps), min(count, count - steps))
    return lax.ppermute(value, axis, [(source, source + steps) for source in range(first, last)])


def send(source, target, send_sem, recv_sem, peer):
    pltpu.make_async_remote_copy(
        src_ref=source,
        dst_ref=target,
        send_sem=send_sem,
        recv_sem=recv_sem,
        device_id=peer,
        device_id_type=MESH,
    ).start()


def wait_for(ref, sem):
    pltpu.make_async_copy(ref, ref, sem).wait()


def first_kernel(*refs):
    count = len(NAMES)
    own = dict(zip(NAMES, refs[:count]))
    segment_row, segment_col, padding_row, cosine_ref, sine_ref, cot_ref, meta_ref = refs[
        count : count + 7
    ]
    refs = refs[count + 7 :]
    full = dict(zip(LATE, refs[: len(LATE)]))
    refs = refs[len(LATE) :]
    saved, refs = refs[:SAVED], refs[SAVED:]
    gain_ref, rows_got, grads_got, shared_ref, ffn_grad_ref, *shared_work = refs[:8]
    refs = refs[8:]
    full.update(zip(PASSING, refs[: len(PASSING)]))
    refs = refs[len(PASSING) :]
    normed_ref, query_ref, key_ref, value_ref, lse_ref, attended_ref, mixed_ref, ffn_ref = refs[:8]
    refs = refs[8:]
    shared_core = refs[:3]
    refs = refs[3:]
    rows_put, grads_put = refs[:2]
    (own_sem, y_send, y_recv, x_send, x_recv, z_send, z_recv, core_send, core_recv) = refs[2:11]
    row_sems, grad_sems, share_send, share_recv, save_sem = refs[11:13], refs[13:15], refs[15], refs[16], refs[17]
    far_send, far_recv, slot_ref, meta_far, cot_far, ffn_far = refs[18:]
    number = {name: index for index, name in enumerate(NAMES)}
    expert, shard = (lax.axis_index("expert"), lax.axis_index("shard"))
    zed, ex = (expert // 2, expert % 2)
    other = (shard + 2) % 4
    y_peer = (expert, other)
    core_peer = (expert, shard + 1 - 2 * (shard % 2))
    x_peer = (expert + 1 - 2 * ex, shard)
    z_up, z_down = (((expert + 2) % 8, shard), ((expert + 6) % 8, shard))

    barrier = pltpu.get_barrier_semaphore()
    for peer in (y_peer, core_peer) + tuple(((expert + step) % 8, shard) for step in range(1, 8)):
        pl.semaphore_signal(barrier, inc=1, device_id=peer, device_id_type=MESH)
    pl.semaphore_wait(barrier, 9)

    def part_of(block, base, name, at_z, at_x):
        rows = own[name].shape[0]
        if at_z is None and at_x is None:
            return block.at[pl.ds(base, rows)]
        if name in EARLY:
            return block.at[pl.ds(base + at_x * (rows // 2), rows // 2)]
        if name in ("sg", "su"):
            half = block.shape[1] // 8
            return block.at[pl.ds(base, rows), pl.ds((at_z * 2 + at_x) * half, half)]
        size = rows // 8
        return block.at[pl.ds(base + (at_z * 2 + at_x) * size, size)]

    def place(name, slot, at_z=None, at_x=None):
        return part_of(full[name], slot * own[name].shape[0], name, at_z, at_x)

    def mine(name, at_z=None, at_x=None):
        return part_of(own[name], 0, name, at_z, at_x)

    def cross(name, at_z=None, at_x=None):
        n = number[name]
        send(mine(name, at_z, at_x), place(name, shard, at_z, at_x), y_send.at[n], y_recv.at[n], y_peer)

    def to_core(name, step, at_z=None, at_x=None):
        n = number[name]
        part = place(name, other, at_z, at_x)
        send(part, part, core_send.at[n, 1 + step], core_recv.at[n, 1 + step], core_peer)

    far = shard + 1 - 2 * (shard % 2)
    far_other = (far + 2) % 4

    def settle_own(names):
        for name in names:
            n = number[name]
            pltpu.make_async_copy(own[name], place(name, shard), own_sem.at[n]).wait()
            wait_for(place(name, far), core_recv.at[n, 0])
            wait_for(own[name], core_send.at[n, 0])

    def settle_core(name, step, at_z=None, at_x=None):
        n = number[name]
        wait_for(place(name, far_other, at_z, at_x), core_recv.at[n, 1 + step])
        wait_for(place(name, other, at_z, at_x), core_send.at[n, 1 + step])

    def own_to_core(names):
        for name in names:
            n = number[name]
            send(own[name], place(name, shard), core_send.at[n, 0], core_recv.at[n, 0], core_peer)
            pltpu.make_async_copy(own[name], place(name, shard), own_sem.at[n]).start()

    for name in DIRECT:
        cross(name)
    for name in ("wk", "wv", "wq"):
        cross(name, None, ex)
    for name in SPREAD:
        cross(name, zed, ex)
    cross("wo", None, ex)
    for name in LATE:
        cross(name)
    own_to_core(DIRECT + EARLY)

    tokens, width = own["hid"].shape
    capacity = rows_put.shape[1]
    far_expert, half_start, in_half = (expert + 4) % 8, 4 * (expert // 4), expert % 4
    far_peer = (far_expert, shard)

    def to_far(index, ref, target):
        send(ref, target, far_send.at[index], far_recv.at[index], far_peer)

    def settle_far(index, ref):
        wait_for(ref, far_send.at[index])
        wait_for(ref, far_recv.at[index])

    to_far(0, meta_ref, meta_far)
    to_far(1, cot_ref, cot_far)

    def fill_slots(block, meta):
        expert_at = lax.broadcasted_iota(jnp.int32, (8, tokens), 0).astype(jnp.float32)
        named = ((meta[0:1] == expert_at) | (meta[1:2] == expert_at)).astype(jnp.float32)
        row_at = lax.broadcasted_iota(jnp.int32, (tokens, tokens), 0)
        before = row_at < lax.broadcasted_iota(jnp.int32, (tokens, tokens), 1)
        rank = dense_product(named.astype(jnp.bfloat16), before.astype(jnp.bfloat16))
        slot_ref[block] = jnp.where(named > 0.0, rank, -1.0)

    def picks(block, target):
        slot_at = lax.broadcasted_iota(jnp.int32, (capacity, tokens), 0)
        return slot_at == slot_ref[block, pl.ds(target, 1), :].astype(jnp.int32)

    def put_grads(block, meta, cot):
        gates = [as_column(gate) for gate in gate_pair(meta[2:3], meta[3:4])]
        route_grads = [(gate * cot.astype(jnp.float32)).astype(jnp.bfloat16) for gate in gates]
        for index in range(4):
            target = half_start + index
            chosen = picks(block, target)
            grads_put[4 * block + index] = sum(
                dense_product(
                    (chosen & (meta[k : k + 1].astype(jnp.int32) == target)).astype(jnp.bfloat16), route_grads[k]
                )
                for k in range(TOP)
            ).astype(jnp.bfloat16)

    def put_rows(block, ffn):
        for index in range(4):
            chosen = picks(block, half_start + index).astype(jnp.bfloat16)
            rows_put[4 * block + index] = dense_product(chosen, ffn).astype(jnp.bfloat16)

    def dispatch(block, put, got, sems):
        source = far_expert if block else expert
        for step in range(1, 4):
            index = (in_half + step) % 4
            at = 4 * block + step
            send(put.at[4 * block + index], got.at[source], sems[0].at[at], sems[1].at[at], (half_start + index, shard))
        pltpu.make_async_copy(put.at[4 * block + in_half], got.at[source], sems[0].at[4 * block]).start()

    def settle_dispatch(put, got, sems):
        for block in range(2):
            for step in range(4):
                wait_for(put.at[4 * block + (in_half + step) % 4], sems[0].at[4 * block + step])
            for step in range(1, 4):
                sender = half_start + (in_half + 4 - step) % 4
                wait_for(got.at[(sender + 4 * block) % 8], sems[1].at[4 * block + step])

    fill_slots(0, meta_ref[...])
    put_grads(0, meta_ref[...], cot_ref[...])
    dispatch(0, grads_put, grads_got, grad_sems)
    for name in DIRECT:
        wait_for(place(name, other), y_recv.at[number[name]])
        to_core(name, 0)

    def early_out(name):
        n = number[name]
        part = place(name, other, None, ex)
        wait_for(part, y_recv.at[n])
        send(part, part, x_send.at[n, 0], x_recv.at[n, 0], x_peer)
        to_core(name, 0, None, ex)

    for name in ("wk", "wv", "wq"):
        early_out(name)
    own_to_core(SPREAD + LATE)

    def on_part(name, at_z, step):
        n = number[name]
        part = place(name, other, at_z, ex)
        send(part, part, x_send.at[n, step], x_recv.at[n, step], x_peer)
        to_core(name, step, at_z, ex)

    def forward(step, direction, condition, at_z, peer):
        @pl.when(condition)
        def _():
            for name in SPREAD:
                n = number[name]
                part = place(name, other, at_z, ex)
                send(part, part, z_send.at[n, direction, step], z_recv.at[n, direction, step], peer)

    def arrive(step, direction, condition, at_z):
        @pl.when(condition)
        def _():
            for name in SPREAD:
                n = number[name]
                wait_for(place(name, other, at_z, ex), z_recv.at[n, direction, step])
                on_part(name, at_z, 1 + direction * 3 + step)

    def ring_send(step):
        forward(step, 0, (zed < 3) & (zed >= step), zed - step, z_up)
        forward(step, 1, (zed > 0) & (zed + step <= 3), zed + step, z_down)

    def ring_arrive(step):
        arrive(step, 0, zed >= step + 1, zed - 1 - step)
        arrive(step, 1, zed + 1 + step <= 3, zed + 1 + step)

    settle_own(DIRECT)
    for name in DIRECT:
        settle_core(name, 0)
    gain_rows = sum(full["gains"][pl.ds(slot * 16, 16), :].astype(jnp.float32) for slot in range(4))
    gain_ref[...] = gain_rows
    gain_first, gain_second = gain_rows[0:1], gain_rows[1:2]

    def norm_block(block, carry):
        rows = pl.ds(pl.multiple_of(block * tokens, tokens), tokens)
        values = full["hid"][rows, :].astype(jnp.float32)
        normed_ref[rows, :] = (values * rms_scale(values) * gain_first).astype(jnp.bfloat16)
        return carry

    lax.fori_loop(0, 4, norm_block, 0)

    def settle_early(names):
        settle_own(names)
        for name in names:
            settle_core(name, 0, None, ex)
            settle_core(name, 1, None, 1 - ex)
            wait_for(mine(name, None, ex), y_send.at[number[name]])
            wait_for(place(name, other, None, ex), x_send.at[number[name], 0])

    def pass_early(name):
        wait_for(place(name, other, None, 1 - ex), x_recv.at[number[name], 0])
        to_core(name, 1, None, 1 - ex)

    pass_early("wk")
    pass_early("wv")
    settle_early(("wk",))

    def key_block(block, carry):
        rows = pl.ds(pl.multiple_of(block * tokens, tokens), tokens)
        raw = dense_product(normed_ref[rows, :], full["wk"][...])
        cosine, sine = cosine_ref[rows, :], sine_ref[rows, :]
        for start in range(0, width, 128):
            key_ref[rows, start : start + 128] = rotate_pair(raw[:, start : start + 128], cosine, sine).astype(jnp.bfloat16)
        return carry

    def value_block(block, carry):
        rows = pl.ds(pl.multiple_of(block * tokens, tokens), tokens)
        value_ref[rows, :] = dense_product(normed_ref[rows, :], full["wv"][...]).astype(jnp.bfloat16)
        return carry

    lax.fori_loop(0, 4, key_block, 0)
    pass_early("wq")
    settle_early(("wv",))
    lax.fori_loop(0, 4, value_block, 0)
    settle_early(("wq",))
    here = pl.ds(pl.multiple_of(shard * tokens, tokens), tokens)
    raw = dense_product(normed_ref[here, :], full["wq"][...])
    cosine, sine = cosine_ref[here, :], sine_ref[here, :]
    for start in range(0, width, 128):
        query_ref[:, start : start + 128] = rotate_pair(raw[:, start : start + 128], cosine, sine).astype(jnp.bfloat16)
    for name in SPREAD:
        wait_for(place(name, other, zed, ex), y_recv.at[number[name]])
    ring_send(0)
    for name in SPREAD:
        on_part(name, zed, 0)
    early_out("wo")

    def head_pair(pair, carry):
        lanes = pl.ds(pl.multiple_of(pair * 128, 128), 128)
        query, keys, values = query_ref[:, lanes], key_ref[:, lanes], value_ref[:, lanes]
        allowed = allowed_mask(shard * tokens, 0, segment_col[here, :], segment_row[...], padding_row[...])
        lane = lax.broadcasted_iota(jnp.int32, query.shape, 1)
        results = []
        for half in range(2):
            chosen = (lane >= 64) if half else (lane < 64)
            scores = product_t(jnp.where(chosen, query, jnp.zeros_like(query)), keys) * 0.125
            scores = jnp.where(allowed, scores, neg_fill)
            top_score = jnp.max(scores, axis=-1, keepdims=True)
            exponent = jnp.exp(scores - top_score)
            exp_total = jnp.sum(exponent, axis=-1, keepdims=True)
            lse_ref[2 * pair + half] = top_score + jnp.log(exp_total)
            results.append(dense_product((exponent / exp_total).astype(jnp.bfloat16), values))
        attended_ref[:, lanes] = jnp.where(lane < 64, results[0], results[1]).astype(jnp.bfloat16)
        return carry

    lax.fori_loop(0, 3, head_pair, 0)
    ring_arrive(0)
    ring_send(1)
    settle_far(0, meta_far)
    settle_far(1, cot_far)
    fill_slots(1, meta_far[...])
    put_grads(1, meta_far[...], cot_far[...])
    dispatch(1, grads_put, grads_got, grad_sems)
    pass_early("wo")
    lax.fori_loop(3, 6, head_pair, 0)
    ring_arrive(1)
    ring_send(2)
    settle_early(("wo",))
    rows_in = own["hid"][...].astype(jnp.float32)
    mixed = rows_in + dense_product(attended_ref[...], full["wo"][...])
    mixed_ref[...] = mixed
    ffn = (mixed * rms_scale(mixed) * gain_second).astype(jnp.bfloat16)
    ffn_ref[...] = ffn
    to_far(2, ffn_ref, ffn_far)
    put_rows(0, ffn)
    dispatch(0, rows_put, rows_got, row_sems)
    keep = [full[name] for name in EARLY]
    keep += [normed_ref, query_ref, key_ref, value_ref, lse_ref, attended_ref, mixed_ref]
    for index, ref in enumerate(keep):
        pltpu.make_async_copy(ref, saved[index], save_sem.at[index]).start()
    ring_arrive(2)

    def from_x(condition, at_z, step):
        @pl.when(condition)
        def _():
            for name in SPREAD:
                wait_for(place(name, other, at_z, 1 - ex), x_recv.at[number[name], step])
                to_core(name, 7 + step, at_z, 1 - ex)

    from_x(zed >= 0, zed, 0)
    for step in range(3):
        from_x(zed >= step + 1, zed - 1 - step, 1 + step)
        from_x(zed + 1 + step <= 3, zed + 1 + step, 4 + step)

    def settle_spread(names, condition, at_z, step):
        @pl.when(condition)
        def _():
            for name in names:
                settle_core(name, step, at_z, ex)
                wait_for(place(name, other, at_z, ex), x_send.at[number[name], step])
                settle_core(name, 7 + step, at_z, 1 - ex)

    def settle_ring(names):
        settle_own(names)
        for name in names:
            wait_for(mine(name, zed, ex), y_send.at[number[name]])
        settle_spread(names, zed >= 0, zed, 0)
        for step in range(3):
            settle_spread(names, zed >= step + 1, zed - 1 - step, 1 + step)
            settle_spread(names, zed + 1 + step <= 3, zed + 1 + step, 4 + step)

    settle_ring(SPREAD)

    def sent(step, direction, condition, at_z):
        @pl.when(condition)
        def _():
            for name in SPREAD:
                wait_for(place(name, other, at_z, ex), z_send.at[number[name], direction, step])

    for step in range(3):
        sent(step, 0, (zed < 3) & (zed >= step), zed - step)
        sent(step, 1, (zed > 0) & (zed + step <= 3), zed + step)
    shared_ref[...] = jnp.zeros_like(shared_ref)
    ffn_grad_ref[...] = jnp.zeros_like(ffn_grad_ref)

    def shared_block(block, carry):
        cut = pl.ds(pl.multiple_of(block * 512, 512), 512)
        normed = ffn_ref[...]
        gate, up, down = full["sg"][:, cut], full["su"][:, cut], full["sd"][cut, :]
        pre, lin = dense_product(normed, gate), dense_product(normed, up)
        middle = (jax.nn.silu(pre) * lin).astype(jnp.bfloat16)
        shared_ref[...] += dense_product(middle, down)
        pre_grad, lin_grad = swiglu_back(product_t(cot_ref[...], down), pre, lin)
        ffn_grad_ref[...] += product_t(pre_grad, gate) + product_t(lin_grad, up)
        full["sg"][:, cut] = t_product(normed, pre_grad).astype(jnp.bfloat16)
        full["su"][:, cut] = t_product(normed, lin_grad).astype(jnp.bfloat16)
        full["sd"][cut, :] = t_product(middle, cot_ref[...]).astype(jnp.bfloat16)
        return carry

    cuts = full["sg"].shape[1] // 512
    lax.fori_loop(0, cuts // 2, shared_block, 0)
    settle_far(2, ffn_far)
    put_rows(1, ffn_far[...])
    dispatch(1, rows_put, rows_got, row_sems)
    lax.fori_loop(cuts // 2, cuts, shared_block, 0)

    def shard_rows(ref, y_of, core_of):
        rows = ref.shape[0] // 4
        return ref.at[pl.ds((y_of * 2 + core_of) * rows, rows)]

    core = shard % 2
    shared_grads = (full["sg"], full["su"], full["sd"])
    for index in range(3):
        for y_of in range(2):
            send(
                shard_rows(shared_grads[index], y_of, 1 - core),
                shared_core[index].at[y_of],
                share_send.at[index, y_of],
                share_recv.at[index, y_of],
                core_peer,
            )

    for name in LATE:
        wait_for(place(name, other), y_recv.at[number[name]])
        to_core(name, 0)

    for name in DIRECT:
        wait_for(own[name], y_send.at[number[name]])
    settle_own(LATE)
    for name in LATE:
        wait_for(own[name], y_send.at[number[name]])
        settle_core(name, 0)
    for index in range(3):
        for y_of in range(2):
            wait_for(shared_core[index].at[y_of], share_recv.at[index, y_of])
            add_rows(shared_work[index].at[y_of], shard_rows(shared_grads[index], y_of, core), shared_core[index].at[y_of])
            wait_for(shard_rows(shared_grads[index], y_of, 1 - core), share_send.at[index, y_of])
    settle_dispatch(grads_put, grads_got, grad_sems)
    settle_dispatch(rows_put, rows_got, row_sems)
    for index, ref in enumerate(keep):
        wait_for(ref, save_sem.at[index])


def as_column(row):
    shape = (row.shape[1], row.shape[1])
    same = lax.broadcasted_iota(jnp.int32, shape, 0) == lax.broadcasted_iota(jnp.int32, shape, 1)
    return jnp.sum(jnp.where(same, row, 0.0), axis=1, keepdims=True)


def gate_pair(first, second):
    top = jnp.maximum(first, second)
    first, second = jnp.exp(first - top), jnp.exp(second - top)
    total = first + second
    return first / total, second / total


def allowed_mask(query_start, key_start, query_segment, key_segment, key_padding):
    shape = (query_segment.shape[0], key_segment.shape[1])
    query_at = query_start + lax.broadcasted_iota(jnp.int32, shape, 0)
    key_at = key_start + lax.broadcasted_iota(jnp.int32, shape, 1)
    distance = query_at - key_at
    return (
        (query_segment == key_segment)
        & (distance >= 0)
        & (distance < WINDOW)
        & ((key_padding == 1) | (distance == 0))
    )


def first_part(hidden, gains, dense, experts, segment, padding, cotangent, meta):
    tokens, width = hidden.shape
    bfloat, single = jnp.bfloat16, jnp.float32
    wq, wk, wv, wo, sg, su, sd = dense
    blocks = dict(hid=hidden, gains=jnp.pad(gains, ((0, 14), (0, 0))), wq=wq, wk=wk, wv=wv, wo=wo, sg=sg, su=su, sd=sd)
    blocks.update(zip(LATE, experts))
    blocks = [blocks[name] for name in NAMES]
    count = len(NAMES)
    cosine, sine = rotary_tables(4 * tokens, width // HEADS)
    in_hbm, in_vmem = pl.BlockSpec(memory_space=pl.ANY), pl.BlockSpec(memory_space=pltpu.VMEM)
    dma = pltpu.SemaphoreType.DMA
    shape = jax.ShapeDtypeStruct
    whole = {name: shape((4 * block.shape[0], block.shape[1]), block.dtype) for name, block in zip(NAMES, blocks)}
    middle = sg.shape[1]
    capacity = max(2, 2 * tokens * TOP // 8)
    routed = (8, capacity, width)
    halved = [(2,) + block.shape for block in (sg, su, sd)]
    inner = [
        shape((4 * tokens, width), bfloat),
        shape((tokens, width), bfloat),
        shape((4 * tokens, width), bfloat),
        shape((4 * tokens, width), bfloat),
        shape((HEADS, tokens, 1), single),
        shape((tokens, width), bfloat),
        shape((tokens, width), single),
        shape((tokens, width), bfloat),
    ]
    out = pl.pallas_call(
        first_kernel,
        out_shape=[whole[name] for name in LATE]
        + [whole[name] for name in EARLY]
        + inner[:7]
        + [
            shape((16, width), single),
            shape(routed, bfloat),
            shape(routed, bfloat),
            shape((tokens, width), single),
            shape((tokens, width), single),
        ]
        + [shape(one, bfloat) for one in halved],
        in_specs=[in_vmem] * (count + 7),
        out_specs=[in_hbm] * (len(LATE) + SAVED) + [in_vmem] + [in_hbm] * 2 + [in_vmem] * 5,
        scratch_shapes=[pltpu.VMEM(whole[name].shape, whole[name].dtype) for name in PASSING]
        + [pltpu.VMEM(one.shape, one.dtype) for one in inner]
        + [pltpu.VMEM(one, bfloat) for one in halved]
        + [pltpu.VMEM(routed, bfloat)] * 2
        + [
            dma((count,)),
            dma((count,)),
            dma((count,)),
            dma((count, 7)),
            dma((count, 7)),
            dma((count, 2, 3)),
            dma((count, 2, 3)),
            dma((count, 15)),
            dma((count, 15)),
        ]
        + [dma((8,))] * 4
        + [dma((3, 2))] * 2
        + [
            dma((SAVED,)),
            dma((3,)),
            dma((3,)),
            pltpu.VMEM((2, 8, tokens), single),
            pltpu.VMEM((8, tokens), single),
            pltpu.VMEM((tokens, width), bfloat),
            pltpu.VMEM((tokens, width), bfloat),
        ],
        compiler_params=pltpu.CompilerParams(collective_id=0, has_side_effects=True, vmem_limit_bytes=60 << 20),
        cost_estimate=pl.CostEstimate(flops=15000000000, bytes_accessed=47000000, transcendentals=3000000),
    )(
        *blocks,
        segment[None, :],
        segment[:, None],
        padding[None, :],
        jnp.asarray(cosine),
        jnp.asarray(sine),
        cotangent,
        meta,
    )
    return dict(zip(LATE + EARLY, out)), out[len(LATE + EARLY) :]


def add_into(target, first, second):
    rows = first.shape[-2]
    strip = math.gcd(rows, 64)

    def body(index, carry):
        at = pl.ds(pl.multiple_of(index * strip, strip), strip)
        for lead in range(first.shape[0]):
            total = first[lead, at, :].astype(jnp.float32) + second[lead, at, :].astype(jnp.float32)
            target[lead, at, :] = total.astype(target.dtype)
        return carry

    lax.fori_loop(0, rows // strip, body, 0)


class PlaneSum:
    def __init__(self, shape, work, receive, send_sem, recv_sem, bits, peers, order, out=None, done=0):
        self.work, self.receive, self.out = work, receive, out
        self.send_sem, self.recv_sem, self.bits, self.peers, self.order = send_sem, recv_sem, bits, peers, order
        self.at = [(0, size) for size in shape]
        self.inside = [0, 0, 0]
        self.trail = []
        for step in range(done):
            self.narrow(step)
        self.inside = [0, 0, 0]
        self.step = done

    def region(self, ref, starts, sizes):
        starts = [
            start if isinstance(start, int) or unit == 1 else pl.multiple_of(start, unit)
            for start, unit in zip(starts, (1, 16, 128))
        ]
        return ref.at[tuple(pl.ds(start, size) for start, size in zip(starts, sizes))]

    def working(self, bit_of):
        axis, dim = self.order[self.step]
        starts, sizes = list(self.inside), [size for _, size in self.at]
        sizes[dim] //= 2
        starts[dim] = starts[dim] + bit_of(self.bits[axis]) * sizes[dim]
        return self.region(self.work, starts, sizes)

    def final(self, at):
        return self.region(self.out, [0] + [start for start, _ in at[1:]], [1] + [size for _, size in at[1:]])

    def narrow(self, step):
        axis, dim = self.order[step]
        if axis != "y":
            self.trail.append((step, self.at))
        (start, size), self.at = self.at[dim], list(self.at)
        self.at[dim] = (start + self.bits[axis] * (size // 2), size // 2)
        self.inside[dim] = self.inside[dim] + self.bits[axis] * (size // 2)

    def start(self):
        step = self.step
        peer = self.peers[self.order[step][0]]
        send(self.working(lambda bit: 1 - bit), self.receive[step], self.send_sem.at[step], self.recv_sem.at[step], peer)

    def finish(self, target=None):
        step = self.step
        wait_for(self.receive[step], self.recv_sem.at[step])
        kept, gone = self.working(lambda bit: bit), self.working(lambda bit: 1 - bit)
        self.narrow(step)
        if step == len(self.order) - 1:
            target = self.final(self.at)
        add_into(kept if target is None else target, kept, self.receive[step])
        wait_for(gone, self.send_sem.at[step])
        self.step = step + 1

    def back_start(self):
        step, _ = self.trail[-1]
        part, at = self.final(self.at), self.step
        send(part, part, self.send_sem.at[at], self.recv_sem.at[at], self.peers[self.order[step][0]])

    def back_finish(self):
        step, whole = self.trail.pop()
        wait_for(self.final(self.at), self.send_sem.at[self.step])
        dim = self.order[step][1]
        start, size = self.at[dim]
        other = list(self.at)
        other[dim] = (2 * whole[dim][0] + size - start, size)
        wait_for(self.final(other), self.recv_sem.at[self.step])
        self.at = list(self.at)
        self.at[dim] = whole[dim]
        self.step += 1

    def advance(self):
        if self.step < len(self.order):
            self.finish()
        else:
            self.back_finish()
        if self.step < len(self.order):
            self.start()
        elif self.trail:
            self.back_start()


def receive_shapes(shape, order):
    result, shape = [], list(shape)
    for _, dim in order:
        shape[dim] //= 2
        result.append(tuple(shape))
    return result


def ordered(axes, dims):
    return tuple((axis, 0 if axis == "y" else dims[axis]) for axis in axes)


BY_COLUMNS, BY_ROWS = dict(x=2, z1=2, z2=2), dict(x=1, z1=1, z2=1)
BY_BOTH = dict(x=2, z1=1, z2=1)
SHARED_ORDER = (
    ordered(("y", "x", "z1", "z2"), BY_COLUMNS),
    ordered(("x", "y", "z1", "z2"), BY_COLUMNS),
    ordered(("z1", "y", "x", "z2"), BY_ROWS),
)
SHARED_DONE = 2
ATTENTION_ORDER = (
    ordered(("z1", "x", "y", "z2"), BY_BOTH),
    ordered(("y", "x", "z1", "z2"), BY_BOTH),
    ordered(("x", "z1", "y", "z2"), BY_BOTH),
    ordered(("x", "z1", "y", "z2"), BY_BOTH),
)


def plane_places():
    expert, shard = (lax.axis_index("expert"), lax.axis_index("shard"))
    zed, ex, why, core = (expert // 2, expert % 2, shard // 2, shard % 2)
    bits = {"x": ex, "z1": zed % 2, "z2": zed // 2, "y": why}
    peers = {
        "x": (expert + 1 - 2 * ex, shard),
        "z1": (expert + 2 - 4 * (zed % 2), shard),
        "z2": ((expert + 4) % 8, shard),
        "y": (expert, (shard + 2) % 4),
        "core": (expert, shard + 1 - 2 * core),
    }
    return expert, shard, zed, core, bits, peers


def enter(peers):
    barrier = pltpu.get_barrier_semaphore()
    for peer in peers:
        pl.semaphore_signal(barrier, inc=1, device_id=peer, device_id_type=MESH)
    pl.semaphore_wait(barrier, len(peers))


def second_kernel(*refs):
    rows_ref, grads_ref, *weights_in = refs[:5]
    shared_in = refs[5:8]
    rows_back, grads_back = refs[8:10]
    expert_out, left_over, shared_out, late_ref = refs[10], refs[11:13], refs[13:16], refs[16]
    weights, shared_work = refs[17:20], refs[20:23]
    rows_put, grads_put, middle_ref, pre_ref, lin_ref, out_sum, grad_sum = refs[23:30]
    expert_core, expert_y = (refs[30],) + tuple(left_over), refs[31]
    refs = refs[32:]
    receive = [refs[SHARED_DONE * index : SHARED_DONE * (index + 1)] for index in range(3)]
    refs = refs[3 * SHARED_DONE :]
    load_sem, shared_sem, out_send, out_recv, grad_send, grad_recv, core_send, core_recv, y_send, y_recv, sum_send, sum_recv = refs
    expert, shard, zed, core, bits, peers = plane_places()
    why = bits["y"]
    for index in range(3):
        pltpu.make_async_copy(weights_in[index], weights[index], load_sem.at[index]).start()
        pltpu.make_async_copy(shared_in[index], shared_work[index], shared_sem.at[index]).start()
    enter((peers["y"], peers["core"]) + tuple(((expert + step) % 8, shard) for step in range(1, 8)))
    sums = [
        PlaneSum(
            shared_work[index].shape,
            shared_work[index],
            receive[index],
            sum_send.at[index],
            sum_recv.at[index],
            bits,
            peers,
            SHARED_ORDER[index],
        )
        for index in range(3)
    ]
    for index in range(3):
        pltpu.make_async_copy(shared_in[index], shared_work[index], shared_sem.at[index]).wait()
        sums[index].start()
    for index in range(3):
        pltpu.make_async_copy(weights_in[index], weights[index], load_sem.at[index]).wait()

    _, capacity, width = rows_ref.shape
    gate_ref, up_ref, down_ref = weights
    middle = gate_ref.shape[1]
    cuts = middle // 512

    def block(z_from):
        pair = pl.ds(2 * z_from, 2)
        rows = rows_ref[pair].reshape(2 * capacity, width)
        grads = grads_ref[pair].reshape(2 * capacity, width)
        here = pl.ds(pl.multiple_of(z_from * 2 * capacity, 2 * capacity), 2 * capacity)
        out_sum[...] = jnp.zeros_like(out_sum)
        grad_sum[...] = jnp.zeros_like(grad_sum)

        def body(index, carry):
            cut = pl.ds(pl.multiple_of(index * 512, 512), 512)
            gate, up, down = gate_ref[:, cut], up_ref[:, cut], down_ref[cut, :]
            pre, lin = dense_product(rows, gate), dense_product(rows, up)
            mid = (jax.nn.silu(pre) * lin).astype(jnp.bfloat16)
            out_sum[...] += dense_product(mid, down)
            pre_grad, lin_grad = swiglu_back(product_t(grads, down), pre, lin)
            grad_sum[...] += product_t(pre_grad, gate) + product_t(lin_grad, up)
            middle_ref[here, cut] = mid
            pre_ref[here, cut] = pre_grad
            lin_ref[here, cut] = lin_grad
            return carry

        lax.fori_loop(0, cuts, body, 0)
        rows_put[pair] = out_sum[...].astype(jnp.bfloat16).reshape(2, capacity, width)
        grads_put[pair] = grad_sum[...].astype(jnp.bfloat16).reshape(2, capacity, width)
        give_back(z_from, grads_put, grads_back, grad_send, grad_recv)

    def give_back(z_from, put, back, send_sem, recv_sem):
        for side in range(2):
            source = 2 * z_from + side

            @pl.when(source != expert)
            def _():
                send(put.at[source], back.at[expert], send_sem.at[source], recv_sem.at[expert], (source, shard))

            @pl.when(source == expert)
            def _():
                back[pl.ds(source, 1)] = put[pl.ds(source, 1)]

    z_order = ((zed + 2) % 4, 3 - zed, zed + 1 - 2 * (zed % 2), zed)
    rows_back[pl.ds(2 * z_order[1], 2)] = jnp.zeros_like(late_ref)
    block(z_order[0])
    block(z_order[1])
    for one in sums:
        one.advance()
    block(z_order[2])
    block(z_order[3])
    for turn in (0, 2, 3):
        give_back(z_order[turn], rows_put, rows_back, out_send, out_recv)
    late_ref[...] = rows_put[pl.ds(2 * z_order[1], 2)]
    for one, target in zip(sums, shared_out):
        one.finish(target)

    rows_all, grads_all = rows_ref, grads_ref

    def weight_grad(index):
        def body(step, carry):
            cut = pl.ds(pl.multiple_of(step * 512, 512), 512)
            if index == 2:
                left, right = middle_ref[:, cut], grads_all[...].reshape(8 * capacity, width)
                down_ref[cut, :] = t_product(left, right).astype(jnp.bfloat16)
            else:
                left, right = rows_all[...].reshape(8 * capacity, width), (pre_ref, lin_ref)[index][:, cut]
                weights[index][:, cut] = t_product(left, right).astype(jnp.bfloat16)
            return carry

        lax.fori_loop(0, cuts, body, 0)

    def shard_rows(index, y_of, core_of):
        rows = weights[index].shape[0] // 4
        return weights[index].at[pl.ds((y_of * 2 + core_of) * rows, rows)]

    def core_start(index):
        for y_of in range(2):
            send(
                shard_rows(index, y_of, 1 - core),
                expert_core[index].at[y_of],
                core_send.at[index, y_of],
                core_recv.at[index, y_of],
                peers["core"],
            )

    def core_finish(index):
        for y_of in range(2):
            wait_for(expert_core[index].at[y_of], core_recv.at[index, y_of])
            wait_for(shard_rows(index, y_of, 1 - core), core_send.at[index, y_of])
        for y_of in range(2):
            kept = shard_rows(index, y_of, core)
            add_rows(expert_core[index].at[y_of], kept, expert_core[index].at[y_of])

    weight_grad(0)
    core_start(0)
    weight_grad(1)
    core_start(1)
    core_finish(0)
    send(expert_core[0].at[1 - why], expert_y, y_send, y_recv, peers["y"])
    weight_grad(2)
    core_start(2)
    core_finish(1)
    core_finish(2)
    for step in range(1, 8):
        target, origin = (expert + step) % 8, (expert + 8 - step) % 8
        wait_for(grads_put.at[target], grad_send.at[target])
        wait_for(grads_back.at[origin], grad_recv.at[origin])

        @pl.when(target // 2 != z_order[1])
        def _():
            wait_for(rows_put.at[target], out_send.at[target])

        @pl.when(origin // 2 != z_order[1])
        def _():
            wait_for(rows_back.at[origin], out_recv.at[origin])

    wait_for(expert_y, y_recv)
    add_rows(expert_out, expert_core[0].at[why], expert_y)
    wait_for(expert_core[0].at[1 - why], y_send)


def add_rows(target, first, second):
    def body(index, carry):
        at = pl.ds(pl.multiple_of(index * 64, 64), 64)
        target[at, :] = (first[at, :].astype(jnp.float32) + second[at, :].astype(jnp.float32)).astype(target.dtype)
        return carry

    lax.fori_loop(0, first.shape[0] // 64, body, 0)


def second_part(rows, grads, weights, shared):
    in_hbm, in_vmem = pl.BlockSpec(memory_space=pl.ANY), pl.BlockSpec(memory_space=pltpu.VMEM)
    dma, bfloat = pltpu.SemaphoreType.DMA, jnp.bfloat16
    shape = jax.ShapeDtypeStruct
    count, capacity, width = rows.shape
    middle = weights[0].shape[1]
    quarter = [(weight.shape[0] // 4, weight.shape[1]) for weight in weights]
    steps = [receive_shapes(work.shape, order)[:SHARED_DONE] for work, order in zip(shared, SHARED_ORDER)]
    blocks = (count * capacity, middle)
    return pl.pallas_call(
        second_kernel,
        out_shape=[shape(rows.shape, bfloat)] * 2
        + [shape(quarter[0], bfloat)]
        + [shape((2,) + one, bfloat) for one in quarter[1:]]
        + [shape(one[-1], bfloat) for one in steps]
        + [shape((2, capacity, width), bfloat)],
        in_specs=[in_vmem] * 2 + [in_hbm] * 6,
        out_specs=[in_vmem] * 9,
        scratch_shapes=[pltpu.VMEM(weight.shape, bfloat) for weight in weights]
        + [pltpu.VMEM(work.shape, bfloat) for work in shared]
        + [pltpu.VMEM(rows.shape, bfloat)] * 2
        + [pltpu.VMEM(blocks, bfloat)] * 3
        + [pltpu.VMEM((2 * capacity, width), jnp.float32)] * 2
        + [pltpu.VMEM((2,) + quarter[0], bfloat), pltpu.VMEM(quarter[0], bfloat)]
        + [pltpu.VMEM(one, bfloat) for group in steps for one in group]
        + [dma((3,)), dma((3,))]
        + [dma((8,))] * 4
        + [dma((3, 2)), dma((3, 2)), dma(()), dma(()), dma((3, SHARED_DONE)), dma((3, SHARED_DONE))],
        compiler_params=pltpu.CompilerParams(collective_id=1, has_side_effects=True, vmem_limit_bytes=62 << 20),
        cost_estimate=pl.CostEstimate(flops=29000000000, bytes_accessed=30000000, transcendentals=2000000),
    )(rows, grads, *weights, *shared)


STORED = 15


def third_kernel(*refs):
    rows_back, grads_back, mixed_ref, shared_ref, ffn_grad_ref, cot_ref, hidden_ref, gain_ref, meta_ref = refs[:9]
    segment_row, segment_col, padding_row = refs[9:12]
    stored, left_over, late_put = refs[12 : 12 + STORED], refs[12 + STORED : 14 + STORED], refs[14 + STORED]
    output_ref, input_grad_ref, logit_grad_ref, gain_out = refs[30:34]
    sums_out, shared_out, expert_out = refs[34:38], refs[38:41], refs[41:43]
    query_grad, key_grad, value_grad, context_grad, attended_grad, mixed_grad_ref = refs[43:49]
    weight_grads, weight_work = refs[49:53], refs[53:57]
    context_core, context_y, late_got = refs[57:60]
    expert_y = refs[60:62]
    refs = refs[62:]
    receive = [refs[4 * index : 4 * index + 4] for index in range(4)]
    refs = refs[16:]
    rest = 4 - SHARED_DONE
    shared_receive = [(None,) * SHARED_DONE + refs[rest * index : rest * index + rest] for index in range(3)]
    refs = refs[3 * rest :]
    loaded, left_mine = refs[:STORED], refs[STORED : STORED + 2]
    wo_ref, attended_ref, cosine_ref, sine_ref, query_ref, key_ref, value_ref, lse_ref, normed_ref, wk_ref, wv_ref, wq_ref = loaded[3:]
    shared_work = loaded[:3]
    refs = refs[STORED + 2 :]
    gain_parts, gain_recv = refs[:2]
    core_send, core_recv, sum_send, sum_recv, share_send, share_recv, ctx_send, ctx_recv, gain_send, gain_got, late_send, late_recv, load_sem, left_sem = refs[2:]
    expert, shard, zed, core, bits, peers = plane_places()
    why = bits["y"]
    for index in range(STORED):
        pltpu.make_async_copy(stored[index], loaded[index], load_sem.at[index]).start()
    mirror = 2 * (3 - zed)
    enter(tuple(peers[axis] for axis in ("core", "y", "x", "z1", "z2")) + ((mirror, shard), (mirror + 1, shard)))
    for index in range(2):
        send(left_over[index].at[1 - why], expert_y[index], ctx_send.at[3 + index], ctx_recv.at[3 + index], peers["y"])
        pltpu.make_async_copy(left_over[index].at[why], left_mine[index], left_sem.at[index]).start()
    shared_sums = [
        PlaneSum(
            (2,) + shared_out[index].shape[1:],
            shared_work[index],
            shared_receive[index],
            share_send.at[index],
            share_recv.at[index],
            bits,
            peers,
            SHARED_ORDER[index],
            shared_out[index],
            SHARED_DONE,
        )
        for index in range(3)
    ]
    for index, one in enumerate(shared_sums):
        wait_for(loaded[index], load_sem.at[index])
        one.start()
    tokens, width = hidden_ref.shape
    here = pl.ds(pl.multiple_of(shard * tokens, tokens), tokens)
    single, bfloat = jnp.float32, jnp.bfloat16

    experts, capacity = rows_back.shape[0], rows_back.shape[1]
    slots = experts * capacity
    expert_at = lax.broadcasted_iota(jnp.int32, (tokens, 128), 1)
    choices = [as_column(meta_ref[k : k + 1, :]).astype(jnp.int32) for k in range(TOP)]
    named = ((choices[0] == expert_at) | (choices[1] == expert_at)).astype(bfloat)
    before = lax.broadcasted_iota(jnp.int32, (tokens, tokens), 1) < lax.broadcasted_iota(jnp.int32, (tokens, tokens), 0)
    rank = dense_product(before.astype(bfloat), named)
    slot_at = lax.broadcasted_iota(jnp.int32, (tokens, slots), 1)

    def slot_column(k):
        slot = rank + expert_at.astype(single) * float(capacity)
        return jnp.sum(jnp.where(choices[k] == expert_at, slot, 0.0), axis=1, keepdims=True).astype(jnp.int32)

    slots_taken = [slot_column(k) for k in range(TOP)]
    grad_out = cot_ref[...].astype(single)
    mixed = mixed_ref[...]
    picks = (slot_at == slots_taken[0]) | (slot_at == slots_taken[1])
    ffn_grad = ffn_grad_ref[...] + dense_product(picks.astype(bfloat), grads_back[...].reshape(slots, width))
    scale_second = rms_scale(mixed)
    gain_parts[0] = jnp.zeros_like(gain_parts[0])
    gain_parts[0, 1:2, :] = jnp.sum(ffn_grad * mixed * scale_second, axis=0, keepdims=True)
    scaled = ffn_grad * gain_ref[1:2, :]
    mixed_grad = (
        grad_out
        + scale_second * scaled
        - mixed * (scale_second * scale_second * scale_second) * jnp.mean(scaled * mixed, axis=-1, keepdims=True)
    )
    mixed_grad_ref[...] = mixed_grad
    mixed_low = mixed_grad.astype(bfloat)
    for index in range(3, 5):
        wait_for(loaded[index], load_sem.at[index])
    attended_grad[...] = product_t(mixed_low, wo_ref[...]).astype(bfloat)

    def shard_rows(ref, y_of, core_of):
        rows = ref.shape[0] // 4
        return ref.at[pl.ds((y_of * 2 + core_of) * rows, rows)]

    def core_start(index):
        for y_of in range(2):
            send(
                shard_rows(weight_grads[index], y_of, 1 - core),
                weight_work[index].at[y_of],
                core_send.at[index, y_of],
                core_recv.at[index, y_of],
                peers["core"],
            )

    def core_finish(index):
        for y_of in range(2):
            wait_for(weight_work[index].at[y_of], core_recv.at[index, y_of])
            wait_for(shard_rows(weight_grads[index], y_of, 1 - core), core_send.at[index, y_of])
            add_rows(weight_work[index].at[y_of], shard_rows(weight_grads[index], y_of, core), weight_work[index].at[y_of])

    sums = [
        PlaneSum(
            weight_work[index].shape,
            weight_work[index],
            receive[index],
            sum_send.at[index],
            sum_recv.at[index],
            bits,
            peers,
            ATTENTION_ORDER[index],
            sums_out[index],
        )
        for index in range(4)
    ]
    weight_grads[3][...] = t_product(attended_ref[...], mixed_low).astype(bfloat)
    core_start(3)

    for index in range(5, STORED):
        wait_for(loaded[index], load_sem.at[index])

    def head_pair(pair, carry):
        lanes = pl.ds(pl.multiple_of(pair * 128, 128), 128)
        query, keys, values, grads = query_ref[:, lanes], key_ref[:, lanes], value_ref[:, lanes], attended_grad[:, lanes]
        allowed = allowed_mask(shard * tokens, 0, segment_col[here, :], segment_row[...], padding_row[...])
        lane = lax.broadcasted_iota(jnp.int32, query.shape, 1)
        from_keys = []
        key_total = value_total = None
        for half in range(2):
            chosen = (lane >= 64) if half else (lane < 64)
            one_query = jnp.where(chosen, query, jnp.zeros_like(query))
            one_grad = jnp.where(chosen, grads, jnp.zeros_like(grads))
            scores = jnp.where(allowed, product_t(one_query, keys) * 0.125, neg_fill)
            probs = jnp.exp(scores - lse_ref[2 * pair + half])
            probs_grad = product_t(one_grad, values)
            delta = jnp.sum(probs * probs_grad, axis=1, keepdims=True)
            scores_grad = (probs * (probs_grad - delta)).astype(bfloat)
            from_keys.append(dense_product(scores_grad, keys))
            key_part = t_product(scores_grad, one_query)
            value_part = t_product(probs.astype(bfloat), one_grad)
            key_total = key_part if key_total is None else key_total + key_part
            value_total = value_part if value_total is None else value_total + value_part
        back = jnp.where(lane < 64, from_keys[0], from_keys[1]) * 0.125
        query_grad[:, lanes] = rotate_pair(back, cosine_ref[here, :], -sine_ref[here, :]).astype(bfloat)
        key_grad[:, lanes] = rotate_pair(key_total * 0.125, cosine_ref[...], -sine_ref[...]).astype(bfloat)
        value_grad[:, lanes] = value_total.astype(bfloat)
        return carry

    def group_grads(group):
        cut = slice(256 * group, 256 * group + 256)
        weight_grads[group][:, 0:256] = t_product(normed_ref[here, :], query_grad[:, cut]).astype(bfloat)
        weight_grads[group][:, 256:512] = t_product(normed_ref[...], key_grad[:, cut]).astype(bfloat)
        weight_grads[group][:, 512:768] = t_product(normed_ref[...], value_grad[:, cut]).astype(bfloat)
        core_start(group)

    def combine():
        for side in range(2):
            wait_for(late_got.at[side], late_recv.at[side])
        slots_late = late_got.shape[0] * capacity
        late_at = lax.broadcasted_iota(jnp.int32, (tokens, slots_late), 1) + mirror * capacity
        gate_probs = [as_column(gate) for gate in gate_pair(meta_ref[2:3, :], meta_ref[3:4, :])]
        per_route = [
            dense_product((slot_at == slot).astype(bfloat), rows_back[...].reshape(slots, width))
            + dense_product((late_at == slot).astype(bfloat), late_got[...].reshape(slots_late, width))
            for slot in slots_taken
        ]
        routed = gate_probs[0] * per_route[0] + gate_probs[1] * per_route[1]
        output_ref[...] = (mixed_ref[...] + shared_ref[...] + routed).astype(bfloat)
        contrib = [jnp.sum(rows * grad_out, axis=1, keepdims=True) for rows in per_route]
        mean_contrib = gate_probs[0] * contrib[0] + gate_probs[1] * contrib[1]
        logit_grad = [gate * (value - mean_contrib) for gate, value in zip(gate_probs, contrib)]
        choice_at = lax.broadcasted_iota(jnp.int32, logit_grad_ref.shape, 1)
        logit_grad_ref[...] = jnp.where(choice_at == 0, logit_grad[0], logit_grad[1])

    gate_sum, up_sum, down_sum = shared_sums
    first, second, third, out_sum = sums

    def take(*items):
        for one in items:
            if one.step < len(one.order) or one.trail:
                one.advance()

    lax.fori_loop(0, 2, head_pair, 0)
    take(gate_sum, up_sum, down_sum)
    core_finish(3)
    out_sum.start()
    group_grads(0)
    lax.fori_loop(2, 4, head_pair, 0)
    core_finish(0)
    first.start()
    take(out_sum, gate_sum, up_sum, down_sum)
    for side in range(2):
        send(late_put.at[side], late_got.at[bits["x"]], late_send.at[side], late_recv.at[bits["x"]], (mirror + side, shard))
    group_grads(1)
    lax.fori_loop(4, 6, head_pair, 0)
    core_finish(1)
    second.start()
    group_grads(2)

    def context_block(block, carry):
        rows = pl.ds(pl.multiple_of(block * tokens, tokens), tokens)
        total = product_t(key_grad[rows, :], wk_ref[...]) + product_t(value_grad[rows, :], wv_ref[...])
        context_grad[rows, :] = total.astype(bfloat)
        return carry

    lax.fori_loop(0, 4, context_block, 0)
    for y_of in range(2):
        send(
            shard_rows(context_grad, y_of, 1 - core),
            context_core.at[y_of],
            ctx_send.at[y_of],
            ctx_recv.at[y_of],
            peers["core"],
        )
    core_finish(2)
    third.start()
    for y_of in range(2):
        wait_for(context_core.at[y_of], ctx_recv.at[y_of])
        wait_for(shard_rows(context_grad, y_of, 1 - core), ctx_send.at[y_of])
        add_rows(context_core.at[y_of], shard_rows(context_grad, y_of, core), context_core.at[y_of])
    send(context_core.at[1 - why], context_y, ctx_send.at[2], ctx_recv.at[2], peers["y"])
    normed_grad = product_t(query_grad[...], wq_ref[...])
    take(first, out_sum, gate_sum, up_sum)
    take(down_sum, third, second, first, out_sum)
    wait_for(context_y, ctx_recv.at[2])
    wait_for(context_core.at[1 - why], ctx_send.at[2])
    normed_grad = normed_grad + context_core[pl.ds(why, 1)].reshape(tokens, width).astype(single) + context_y[...].astype(single)
    rows_in = hidden_ref[...].astype(single)
    scale_first = rms_scale(rows_in)
    gain_parts[0, 0:1, :] = jnp.sum(normed_grad * rows_in * scale_first, axis=0, keepdims=True)

    def gain_start(step):
        peer = peers[("core", "y", "x", "z1", "z2")[step]]
        send(gain_parts.at[step], gain_recv.at[step], gain_send.at[step], gain_got.at[step], peer)

    def gain_finish(step):
        wait_for(gain_recv.at[step], gain_got.at[step])
        gain_parts[step + 1] = gain_parts[step] + gain_recv[step]

    gain_start(0)
    scaled = normed_grad * gain_ref[0:1, :]
    input_grad_ref[...] = (
        mixed_grad_ref[...]
        + scale_first * scaled
        - rows_in * (scale_first * scale_first * scale_first) * jnp.mean(scaled * rows_in, axis=-1, keepdims=True)
    )
    everything = (third, second, first, out_sum, gate_sum, up_sum, down_sum)
    for step in range(5):
        take(*everything)
        gain_finish(step)
        if step < 4:
            gain_start(step + 1)
        if step == 0:
            combine()
    left = [third, second, first, out_sum, gate_sum, up_sum, down_sum]
    while any(one.trail for one in left):
        take(*[one for one in left if one.trail])
    for index in range(2):
        wait_for(expert_y[index], ctx_recv.at[3 + index])
        wait_for(left_mine[index], left_sem.at[index])
        add_rows(expert_out[index], left_mine[index], expert_y[index])
        wait_for(left_over[index].at[1 - why], ctx_send.at[3 + index])
        wait_for(late_put.at[index], late_send.at[index])
    gain_out[...] = gain_parts[5]
    for step in range(5):
        wait_for(gain_parts.at[step], gain_send.at[step])


def third_part(back, mixed, shared_out, ffn_grad, cotangent, hidden, gains, meta, kept, segment, padding, weights, left_over, shared, late, shared_own):
    tokens, width = hidden.shape
    bfloat, single = jnp.bfloat16, jnp.float32
    in_vmem = pl.BlockSpec(memory_space=pltpu.VMEM)
    dma, shape, vmem = pltpu.SemaphoreType.DMA, jax.ShapeDtypeStruct, pltpu.VMEM
    cosine, sine = rotary_tables(4 * tokens, width // HEADS)
    work = (2, width // 4, width)
    normed, query, keys, values, lse, attended = kept
    wq, wk, wv, wo = weights
    cosine, sine = jnp.asarray(cosine), jnp.asarray(sine)
    stored = (*shared, wo, attended, cosine, sine, query, keys, values, lse, normed, wk, wv, wq)
    arguments = (
        *back,
        mixed,
        shared_out,
        ffn_grad,
        cotangent,
        hidden,
        gains,
        meta,
        segment[None, :],
        segment[:, None],
        padding[None, :],
        *stored,
        *left_over,
        late,
    )
    in_hbm = pl.BlockSpec(memory_space=pl.ANY)
    return pl.pallas_call(
        third_kernel,
        out_shape=[
            shape((tokens, width), bfloat),
            shape((tokens, width), single),
            shape((tokens, TOP), single),
            shape((8, width), single),
        ]
        + [shape((1,) + work[1:], bfloat)] * 4
        + [shape((1,) + one, bfloat) for one in shared_own]
        + [shape(one.shape[1:], bfloat) for one in left_over],
        in_specs=[in_vmem] * 12 + [in_hbm] * (STORED + 3),
        out_specs=[in_vmem] * 13,
        scratch_shapes=[vmem((tokens, width), bfloat)]
        + [vmem((4 * tokens, width), bfloat)] * 3
        + [vmem((tokens, width), bfloat), vmem((tokens, width), single)]
        + [vmem((width, width), bfloat)] * 4
        + [vmem(work, bfloat)] * 4
        + [vmem((2, tokens, width), bfloat), vmem((tokens, width), bfloat), vmem(late.shape, bfloat)]
        + [vmem(one.shape[1:], bfloat) for one in left_over]
        + [vmem(one, bfloat) for order in ATTENTION_ORDER for one in receive_shapes(work, order)]
        + [
            vmem(one, bfloat)
            for own, order in zip(shared_own, SHARED_ORDER)
            for one in receive_shapes((2,) + own, order)[SHARED_DONE:]
        ]
        + [vmem(one.shape, one.dtype) for one in stored]
        + [vmem(one.shape[1:], bfloat) for one in left_over]
        + [vmem((6, 8, width), single), vmem((5, 8, width), single)]
        + [dma((4, 2)), dma((4, 2)), dma((4, 7)), dma((4, 7)), dma((3, 7)), dma((3, 7)), dma((5,)), dma((5,)), dma((5,)), dma((5,)), dma((2,)), dma((2,)), dma((STORED,)), dma((2,))],
        compiler_params=pltpu.CompilerParams(collective_id=2, has_side_effects=True, vmem_limit_bytes=60 << 20),
        cost_estimate=pl.CostEstimate(flops=12000000000, bytes_accessed=25000000, transcendentals=3000000),
    )(*arguments)


def swap(value, axis, bit):
    size = lax.axis_size(axis)
    return lax.ppermute(value, axis, [(index, index ^ bit) for index in range(size)])


def halves(value, bit_set, dim):
    half = value.shape[dim] // 2
    keep = lax.dynamic_slice_in_dim(value, bit_set * half, half, dim)
    give = lax.dynamic_slice_in_dim(value, (1 - bit_set) * half, half, dim)
    return keep, give


def fold(value, axis, bit, dim):
    bit_set = (lax.axis_index(axis) // bit) % 2
    keep, give = halves(value, bit_set, dim)
    return (keep.astype(jnp.float32) + swap(give.astype(jnp.bfloat16), axis, bit).astype(jnp.float32)).astype(jnp.bfloat16)


def unfold(value, axis, bit, dim):
    bit_set = (lax.axis_index(axis) // bit) % 2
    come = swap(value, axis, bit)
    return jnp.where(bit_set == 0, jnp.concatenate([value, come], dim), jnp.concatenate([come, value], dim))


def bits_of(axis):
    size = lax.axis_size(axis)
    return [1 << place for place in range(size.bit_length() - 1)]


def scatter_shards(value):
    count = lax.axis_size("shard")
    blocks = value.reshape((count // 2, 2, value.shape[0] // count) + value.shape[1:])
    blocks = fold(blocks, "shard", 1, 1)[:, 0]
    for bit in reversed(bits_of("shard")[1:]):
        blocks = fold(blocks, "shard", bit, 0)
    return blocks[0]


def sum_plane(value, dim):
    bits = bits_of("expert")
    for bit in bits:
        value = fold(value, "expert", bit, dim)
    for bit in reversed(bits):
        value = unfold(value, "expert", bit, dim)
    return value.astype(jnp.float32)


def shards(
    hidden_in,
    gain_attn,
    gain_ffn,
    w_query,
    w_key,
    w_value,
    w_out,
    shared_gate,
    shared_up,
    shared_down,
    expert_gate,
    expert_up,
    expert_down,
    gate_logits,
    routes,
    segment,
    padding,
    cotangent,
):
    bfloat = jnp.bfloat16
    tokens = hidden_in.shape[1]
    model_width = hidden_in.shape[2]
    head_size = model_width // HEADS
    experts = lax.axis_size("expert")
    capacity = max(2, 2 * tokens * TOP // experts)
    shard_count = lax.axis_size("shard")
    shard_index = lax.axis_index("shard")
    score_scale = head_size ** (-0.5)
    head_shape = (tokens, HEADS, head_size)
    fast = (experts, shard_count, WINDOW) == (8, 4, 4 * tokens)
    dense_own = (w_query, w_key, w_value, w_out, shared_gate, shared_up, shared_down)
    expert_own = (expert_gate[0], expert_up[0], expert_down[0])
    rows_in = hidden_in[0].astype(jnp.float32)
    scale_first = rms_scale(rows_in)
    positions = shard_index * tokens + jnp.arange(tokens, dtype=jnp.int32)
    segment_row, padding_row = segment[0], padding[0]
    query_segment = lax.dynamic_slice_in_dim(segment_row, shard_index * tokens, tokens)
    if fast:
        gain_own = lax.dynamic_update_slice(
            jnp.zeros((2, model_width), bfloat),
            jnp.stack([gain_attn, gain_ffn]),
            (0, shard_index * gain_attn.shape[0]),
        )
        meta = [routes[0].T.astype(jnp.float32), gate_logits[0].T, jnp.zeros((8 - 2 * TOP, tokens), jnp.float32)]
        meta = jnp.concatenate(meta, axis=0)
        full, rest = first_part(
            hidden_in[0],
            gain_own,
            dense_own,
            expert_own,
            segment_row,
            padding_row,
            cotangent[0],
            meta,
        )
        normed_ctx, query_low, keys_ctx, values_ctx, log_total, attended, mixed_rows = rest[:7]
        gains, received, grad_received, shared_out, ffn_grad_shared, *shared_work = rest[7:]
        normed_ffn = None
        gain_first, gain_second = gains[0], gains[1]
        w_q, w_k, w_v, w_o = (full[name] for name in ("wq", "wk", "wv", "wo"))
        e_gate, e_up, e_down = (full[name] for name in LATE)
        reach, key_start = shard_count - 1, 0
        key_segment, key_padding = segment_row, padding_row
        key_positions = jnp.arange(4 * tokens, dtype=jnp.int32)
        allowed = allowed_mask(shard_index * tokens, 0, query_segment[:, None], key_segment[None], key_padding[None])
    else:
        gather = functools.partial(lax.all_gather, axis_name="shard", tiled=True)
        w_q, w_k, w_v, w_o, s_gate, s_up, s_down = (gather(weight) for weight in dense_own)
        e_gate, e_up, e_down = (gather(weight) for weight in expert_own)
        gain_first, gain_second = (gather(gain).astype(jnp.float32) for gain in (gain_attn, gain_ffn))
        reach = min((WINDOW + tokens - 2) // tokens, shard_count - 1)
        lead_rows, key_rows = reach * tokens, (reach + 1) * tokens
        context = [from_behind(hidden_in[0], "shard", offset) for offset in range(reach, 0, -1)] + [hidden_in[0]]
        context = jnp.concatenate(context, axis=0).astype(jnp.float32)
        normed_ctx = (context * rms_scale(context) * gain_first).astype(bfloat)
        key_positions = (shard_index - reach) * tokens + jnp.arange(key_rows, dtype=jnp.int32)
        query_low = rotate(
            dense_product(normed_ctx[lead_rows:], w_q).reshape(head_shape), positions, 1.0
        ).astype(bfloat)
        keys_ctx = rotate(
            dense_product(normed_ctx, w_k).reshape(key_rows, HEADS, head_size), key_positions, 1.0
        ).astype(bfloat)
        values_ctx = dense_product(normed_ctx, w_v).astype(bfloat)
        segment_ext = jnp.concatenate([jnp.full((lead_rows,), -1, jnp.int32), segment_row])
        padding_ext = jnp.concatenate([jnp.zeros((lead_rows,), jnp.int32), padding_row])
        key_segment = lax.dynamic_slice_in_dim(segment_ext, shard_index * tokens, key_rows)
        key_padding = lax.dynamic_slice_in_dim(padding_ext, shard_index * tokens, key_rows)
        allowed = allowed_mask(
            shard_index * tokens,
            (shard_index - reach) * tokens,
            query_segment[:, None],
            key_segment[None],
            key_padding[None],
        )
    key_rows = (reach + 1) * tokens
    query_heads = query_low.reshape(head_shape)
    keys_all = keys_ctx.reshape(key_rows, HEADS, head_size)
    values_all = values_ctx.reshape(key_rows, HEADS, head_size)

    def score_block():
        raw_scores = (
            jnp.einsum("qhd,khd->hqk", query_heads, keys_all, preferred_element_type=jnp.float32)
            * score_scale
        )
        return jnp.where(allowed[None], raw_scores, neg_fill)

    if not fast:
        scores = score_block()
        top_score = jnp.max(scores, axis=-1, keepdims=True)
        exponent = jnp.exp(scores - top_score)
        exp_total = jnp.sum(exponent, axis=-1, keepdims=True)
        log_total = top_score + jnp.log(exp_total)
        attended = (
            jnp.einsum(
                "hqk,khd->qhd",
                (exponent / exp_total).astype(bfloat),
                values_all,
                preferred_element_type=jnp.float32,
            )
            .astype(bfloat)
            .reshape(tokens, model_width)
        )
        mixed_rows = rows_in + dense_product(attended, w_o)
        normed_ffn = (mixed_rows * rms_scale(mixed_rows) * gain_second).astype(bfloat)
    scale_second = rms_scale(mixed_rows)
    grad_low = cotangent[0]
    grad_out = grad_low.astype(jnp.float32)
    gate_probs = jax.nn.softmax(gate_logits[0], axis=-1)
    route_flat = routes[0].reshape(-1)
    route_total = tokens * TOP
    onehot = (route_flat[:, None] == jnp.arange(experts, dtype=jnp.int32)[None, :]).astype(
        jnp.int32
    )
    slot_rank = jnp.sum((jnp.cumsum(onehot, axis=0) - onehot) * onehot, axis=1)
    places = route_flat * capacity + slot_rank
    if not fast:
        shared_pre = dense_product(normed_ffn, s_gate)
        shared_lin = dense_product(normed_ffn, s_up)
        shared_mid = (jax.nn.silu(shared_pre) * shared_lin).astype(bfloat)
        shared_out = dense_product(shared_mid, s_down)
        grad_shared_mid = product_t(grad_low, s_down)
        grad_shared_pre, grad_shared_lin = swiglu_back(grad_shared_mid, shared_pre, shared_lin)
        shared_down_grad = dense_product(shared_mid.T, grad_low)
        shared_gate_grad = dense_product(normed_ffn.T, grad_shared_pre)
        shared_up_grad = dense_product(normed_ffn.T, grad_shared_lin)
        ffn_grad_shared = product_t(grad_shared_pre, s_gate) + product_t(grad_shared_lin, s_up)
        slot_table = (
            jnp.full((experts * capacity,), route_total, dtype=jnp.int32)
            .at[places]
            .set(jnp.arange(route_total, dtype=jnp.int32))
        )
        padded_rows = jnp.concatenate([normed_ffn, jnp.zeros((1, model_width), bfloat)], axis=0)
        send_rows = padded_rows[slot_table // TOP].reshape(experts, capacity, model_width)
        received = lax.all_to_all(send_rows, "expert", split_axis=0, concat_axis=0, tiled=True)
        route_grad = (
            (gate_probs[:, :, None] * grad_out[:, None, :])
            .astype(bfloat)
            .reshape(route_total, model_width)
        )
        route_padded = jnp.concatenate([route_grad, jnp.zeros((1, model_width), bfloat)], axis=0)
        send_grad = route_padded[slot_table].reshape(experts, capacity, model_width)
        grad_received = lax.all_to_all(send_grad, "expert", split_axis=0, concat_axis=0, tiled=True)
    if fast:
        returned, grad_back, gate_grad, *left_over = second_part(received, grad_received, (e_gate, e_up, e_down), shared_work)
        output, input_grad, logit_grad, gain_grads, *sums = third_part(
            (returned, grad_back),
            mixed_rows,
            shared_out,
            ffn_grad_shared,
            grad_low,
            hidden_in[0],
            gains,
            meta,
            (normed_ctx, query_low, keys_ctx, values_ctx, log_total, attended),
            segment_row,
            padding_row,
            (w_q, w_k, w_v, w_o),
            left_over[:2],
            left_over[2:5],
            left_over[5],
            (shared_gate.shape, shared_up.shape, shared_down.shape),
        )
        groups = jnp.concatenate(sums[:3], axis=0).reshape(3, -1, 3, model_width // 3)
        attention_grads = [groups[:, :, kind].transpose(1, 0, 2).reshape(-1, model_width) for kind in range(3)]
        attention_grads.append(sums[3][0])
        gain_grads = lax.dynamic_slice_in_dim(gain_grads, shard_index * gain_attn.shape[0], gain_attn.shape[0], 1)
        return (
            output[None],
            input_grad[None],
            logit_grad[None],
            gain_grads[0],
            gain_grads[1],
            *(grad.astype(jnp.float32) for grad in attention_grads),
            *(grad[0].astype(jnp.float32) for grad in sums[4:7]),
            *(grad[None].astype(jnp.float32) for grad in (gate_grad, sums[7], sums[8])),
        )
    else:
        gate_pre = jnp.einsum("sid,df->sif", received, e_gate, preferred_element_type=jnp.float32)
        up_pre = jnp.einsum("sid,df->sif", received, e_up, preferred_element_type=jnp.float32)
        middle = (jax.nn.silu(gate_pre) * up_pre).astype(bfloat)
        result = jnp.einsum("sif,fd->sid", middle, e_down, preferred_element_type=jnp.float32).astype(bfloat)
        returned = lax.all_to_all(result, "expert", split_axis=0, concat_axis=0, tiled=True)
        grad_middle = jnp.einsum(
            "sid,fd->sif", grad_received, e_down, preferred_element_type=jnp.float32
        )
        grad_gate_pre, grad_up_pre = swiglu_back(grad_middle, gate_pre, up_pre)
        expert_down_grad = jnp.einsum(
            "sif,sid->fd", middle, grad_received, preferred_element_type=jnp.float32
        )
        expert_gate_grad = jnp.einsum(
            "sid,sif->df", received, grad_gate_pre, preferred_element_type=jnp.float32
        )
        expert_up_grad = jnp.einsum(
            "sid,sif->df", received, grad_up_pre, preferred_element_type=jnp.float32
        )
        grad_rows = (
            jnp.einsum("sif,df->sid", grad_gate_pre, e_gate, preferred_element_type=jnp.float32)
            + jnp.einsum("sif,df->sid", grad_up_pre, e_up, preferred_element_type=jnp.float32)
        ).astype(bfloat)
        grad_back = lax.all_to_all(grad_rows, "expert", split_axis=0, concat_axis=0, tiled=True)
        expert_grads = tuple(
            scatter_shards(grad.astype(bfloat))[None].astype(jnp.float32)
            for grad in (expert_gate_grad, expert_up_grad, expert_down_grad)
        )
        shared_grads = (
            sum_plane(scatter_shards(shared_gate_grad.astype(bfloat)), 1),
            sum_plane(scatter_shards(shared_up_grad.astype(bfloat)), 1),
            sum_plane(scatter_shards(shared_down_grad.astype(bfloat)), 0),
        )
    per_route = (
        returned.reshape(experts * capacity, model_width)[places]
        .astype(jnp.float32)
        .reshape(tokens, TOP, model_width)
    )
    routed = jnp.sum(gate_probs[:, :, None] * per_route, axis=1)
    output = (mixed_rows + shared_out + routed).astype(bfloat)
    contrib = jnp.sum(per_route * grad_out[:, None, :], axis=-1)
    logit_grad = gate_probs * (contrib - jnp.sum(gate_probs * contrib, axis=-1, keepdims=True))
    grad_routes = (
        grad_back.reshape(experts * capacity, model_width)[places]
        .astype(jnp.float32)
        .reshape(tokens, TOP, model_width)
    )
    grad_normed_ffn = jnp.sum(grad_routes, axis=1) + ffn_grad_shared
    gain_ffn_grad = jnp.sum(grad_normed_ffn * mixed_rows * scale_second, axis=0)
    scaled_second = grad_normed_ffn * gain_second
    grad_mixed = (
        grad_out
        + scale_second * scaled_second
        - mixed_rows
        * scale_second**3
        * jnp.mean(scaled_second * mixed_rows, axis=-1, keepdims=True)
    )
    grad_mixed_low = grad_mixed.astype(bfloat)
    w_out_grad = dense_product(attended.T, grad_mixed_low)
    grad_attended = product_t(grad_mixed_low, w_o).astype(bfloat).reshape(head_shape)
    attn_probs = jnp.exp(score_block() - log_total)
    grad_probs = jnp.einsum(
        "qhd,khd->hqk", grad_attended, values_all, preferred_element_type=jnp.float32
    )
    delta_rows = jnp.sum(attn_probs * grad_probs, axis=-1, keepdims=True)
    grad_scores = (attn_probs * (grad_probs - delta_rows)).astype(bfloat)
    grad_query = (
        jnp.einsum("hqk,khd->qhd", grad_scores, keys_all, preferred_element_type=jnp.float32)
        * score_scale
    )
    grad_keys = (
        jnp.einsum("hqk,qhd->khd", grad_scores, query_heads, preferred_element_type=jnp.float32)
        * score_scale
    )
    grad_values = jnp.einsum(
        "hqk,qhd->khd", attn_probs.astype(bfloat), grad_attended, preferred_element_type=jnp.float32
    )
    grad_query_low = rotate(grad_query, positions, -1.0).astype(bfloat).reshape(tokens, model_width)
    grad_key_low = rotate(grad_keys, key_positions, -1.0).astype(bfloat).reshape(key_rows, model_width)
    grad_value_low = grad_values.astype(bfloat).reshape(key_rows, model_width)
    if fast:
        normed = lax.dynamic_slice_in_dim(normed_ctx, shard_index * tokens, tokens)
    else:
        normed = normed_ctx[reach * tokens :]
    w_query_grad = dense_product(normed.T, grad_query_low)
    w_key_grad = dense_product(normed_ctx.T, grad_key_low)
    w_value_grad = dense_product(normed_ctx.T, grad_value_low)
    grad_context = product_t(grad_key_low, w_k) + product_t(grad_value_low, w_v)
    grad_normed = product_t(grad_query_low, w_q)
    if fast:
        grad_normed = grad_normed + scatter_shards(grad_context.astype(bfloat)).astype(jnp.float32)
    else:
        grad_normed = grad_normed + grad_context[reach * tokens :]
        for offset in range(1, reach + 1):
            sent = grad_context[(reach - offset) * tokens :][:tokens].astype(bfloat)
            grad_normed = grad_normed + from_behind(sent, "shard", -offset).astype(jnp.float32)
    gain_attn_grad = jnp.sum(grad_normed * rows_in * scale_first, axis=0)
    scaled_first = grad_normed * gain_first
    input_grad = (
        grad_mixed
        + scale_first * scaled_first
        - rows_in * scale_first**3 * jnp.mean(scaled_first * rows_in, axis=-1, keepdims=True)
    )
    gain_rows = jnp.stack([gain_attn_grad, gain_ffn_grad], axis=1).astype(bfloat)
    gain_total = lax.psum(scatter_shards(gain_rows), "expert").astype(jnp.float32)
    attn_grads = jnp.stack([w_query_grad, w_key_grad, w_value_grad, w_out_grad]).astype(bfloat)
    attn_rows = scatter_shards(attn_grads.transpose(1, 0, 2)).transpose(1, 0, 2)
    attn_total = sum_plane(attn_rows.reshape(-1, model_width), 0).reshape(attn_rows.shape)
    return (
        output[None],
        input_grad[None],
        logit_grad[None],
        gain_total[:, 0],
        gain_total[:, 1],
        attn_total[0],
        attn_total[1],
        attn_total[2],
        attn_total[3],
        shared_grads[0],
        shared_grads[1],
        shared_grads[2],
        expert_grads[0],
        expert_grads[1],
        expert_grads[2],
    )


def solution(mesh):
    placed = (
        P("expert", "shard", None),
        P("shard"),
        P("shard"),
        P("shard", None),
        P("shard", None),
        P("shard", None),
        P("shard", None),
        P("shard", None),
        P("shard", None),
        P("shard", None),
        P("expert", "shard", None),
        P("expert", "shard", None),
        P("expert", "shard", None),
        P("expert", "shard", None),
        P("expert", "shard", None),
        P("expert", None),
        P("expert", None),
        P("expert", "shard", None),
    )
    return jax.shard_map(
        shards,
        mesh=mesh,
        in_specs=placed,
        out_specs=(
            P("expert", "shard", None),
            P("expert", "shard", None),
            P("expert", "shard", None),
            P("shard"),
            P("shard"),
            P("shard", None),
            P("shard", None),
            P("shard", None),
            P("shard", None),
            P("shard", None),
            P("shard", None),
            P("shard", None),
            P("expert", "shard", None),
            P("expert", "shard", None),
            P("expert", "shard", None),
        ),
        check_vma=False,
    )
```

```python
import functools
import math

import jax
import jax.numpy as jnp
import numpy as np
from jax import lax
from jax.experimental import pallas as pl
from jax.experimental.pallas import tpu as pltpu
from jax.sharding import PartitionSpec as P

HEADS = 12
TOP = 2
WINDOW = 1024
MESH = pl.DeviceIdType.MESH
norm_eps = 1e-06
neg_fill = -1e30
rope_base = 10000.0

DIRECT = ("hid", "gains")
EARLY = ("wk", "wv", "wq", "wo")
SHARED = ("sg", "su", "sd")
SWAP_Z = ("su",)
LATE = ("eg", "eu")
NAMES = DIRECT + EARLY + SHARED + LATE
PASSING = DIRECT + EARLY + SHARED
SAVED = 13


def dense_product(left, right):
    return jnp.dot(left, right, preferred_element_type=jnp.float32)


def product_t(left, right):
    return lax.dot_general(left, right, (((1,), (1,)), ((), ())), preferred_element_type=jnp.float32)


def t_product(left, right):
    return lax.dot_general(left, right, (((0,), (0,)), ((), ())), preferred_element_type=jnp.float32)


def rms_scale(values):
    return lax.rsqrt(jnp.mean(values * values, axis=-1, keepdims=True) + norm_eps)


def rotary_tables(length, head_size):
    half = head_size // 2
    frequency = np.float32(rope_base) ** (-np.arange(half, dtype=np.float32) / np.float32(half))
    angles = np.arange(length, dtype=np.float32)[:, None] * frequency[None, :]
    cosine, sine = np.cos(angles).astype(np.float32), np.sin(angles).astype(np.float32)
    return np.concatenate([cosine] * 4, axis=1), np.concatenate([-sine, sine] * 2, axis=1)


def rotate_pair(values, cosine, sine):
    lane = lax.broadcasted_iota(jnp.int32, values.shape, 1)
    partner = jnp.where(lane % 64 < 32, pltpu.roll(values, 96, 1), pltpu.roll(values, 32, 1))
    return values * cosine + partner * sine


def rotate(values, positions, direction):
    half_size = values.shape[-1] // 2
    frequency = rope_base ** (-jnp.arange(half_size, dtype=jnp.float32) / half_size)
    angles = positions.astype(jnp.float32)[:, None] * frequency[None, :]
    cosine = jnp.cos(angles)[:, None, :]
    sine_part = direction * jnp.sin(angles)[:, None, :]
    first_half = values[..., :half_size]
    second_half = values[..., half_size:]
    return jnp.concatenate(
        [
            first_half * cosine - second_half * sine_part,
            second_half * cosine + first_half * sine_part,
        ],
        axis=-1,
    )


def swiglu_back(grad_middle, gate_pre, up_pre):
    sigmoid_gate = jax.nn.sigmoid(gate_pre)
    activated = gate_pre * sigmoid_gate
    grad_gate = grad_middle * up_pre * sigmoid_gate * (1.0 + gate_pre * (1.0 - sigmoid_gate))
    grad_up = grad_middle * activated
    return (grad_gate.astype(jnp.bfloat16), grad_up.astype(jnp.bfloat16))


def from_behind(value, axis, steps):
    count = lax.axis_size(axis)
    first, last = (max(0, -steps), min(count, count - steps))
    return lax.ppermute(value, axis, [(source, source + steps) for source in range(first, last)])


def send(source, target, send_sem, recv_sem, peer):
    pltpu.make_async_remote_copy(
        src_ref=source,
        dst_ref=target,
        send_sem=send_sem,
        recv_sem=recv_sem,
        device_id=peer,
        device_id_type=MESH,
    ).start()


def wait_for(ref, sem):
    pltpu.make_async_copy(ref, ref, sem).wait()


def first_kernel(*refs):
    count = len(NAMES)
    own = dict(zip(NAMES, refs[:count]))
    segment_row, padding_row, cosine_ref, sine_ref, cot_ref, meta_ref = refs[count : count + 6]
    refs = refs[count + 6 :]
    full = dict(zip(LATE, refs[: len(LATE)]))
    refs = refs[len(LATE) :]
    saved, refs = refs[:SAVED], refs[SAVED:]
    gain_ref, rows_got, grads_got, shared_ref, ffn_grad_ref, *shared_work = refs[:8]
    refs = refs[8:]
    full.update(zip(PASSING, refs[: len(PASSING)]))
    refs = refs[len(PASSING) :]
    normed_ref, query_ref, key_ref, value_ref, lse_ref, attended_ref, mixed_ref, ffn_ref = refs[:8]
    refs = refs[8:]
    shared_core = refs[:3]
    refs = refs[3:]
    rows_put, grads_put = refs[:2]
    (own_sem, y_send, y_recv, swap_send, swap_recv, core_send, core_recv) = refs[2:9]
    row_sems, grad_sems, share_send, share_recv, save_sem = refs[9:11], refs[11:13], refs[13], refs[14], refs[15]
    far_send, far_recv, slot_ref, meta_far, cot_far, ffn_far = refs[16:]
    number = {name: index for index, name in enumerate(NAMES)}
    expert, shard = (lax.axis_index("expert"), lax.axis_index("shard"))
    zed, ex = (expert // 2, expert % 2)
    other = (shard + 2) % 4
    y_peer = (expert, other)
    core_peer = (expert, shard + 1 - 2 * (shard % 2))
    x_peer = (expert + 1 - 2 * ex, shard)
    z_peer = (expert + 2 - 4 * (zed % 2), shard)

    barrier = pltpu.get_barrier_semaphore()
    for peer in (y_peer, core_peer) + tuple(((expert + step) % 8, shard) for step in range(1, 8)):
        pl.semaphore_signal(barrier, inc=1, device_id=peer, device_id_type=MESH)
    pl.semaphore_wait(barrier, 9)

    def side(name):
        return (zed % 2, z_peer) if name in SWAP_Z else (ex, x_peer)

    def part_of(block, base, name, half):
        rows = own[name].shape[0]
        if half is None:
            return block.at[pl.ds(base, rows)]
        return block.at[pl.ds(base + half * (rows // 2), rows // 2)]

    def place(name, slot, half=None):
        return part_of(full[name], slot * own[name].shape[0], name, half)

    def mine(name, half=None):
        return part_of(own[name], 0, name, half)

    def cross(name, half=None):
        n = number[name]
        send(mine(name, half), place(name, shard, half), y_send.at[n], y_recv.at[n], y_peer)

    def to_core(name, step, half=None):
        n = number[name]
        part = place(name, other, half)
        send(part, part, core_send.at[n, 1 + step], core_recv.at[n, 1 + step], core_peer)

    far = shard + 1 - 2 * (shard % 2)
    far_other = (far + 2) % 4

    def settle_own(names):
        for name in names:
            n = number[name]
            pltpu.make_async_copy(own[name], place(name, shard), own_sem.at[n]).wait()
            wait_for(place(name, far), core_recv.at[n, 0])
            wait_for(own[name], core_send.at[n, 0])

    def settle_core(name, step, half=None):
        n = number[name]
        wait_for(place(name, far_other, half), core_recv.at[n, 1 + step])
        wait_for(place(name, other, half), core_send.at[n, 1 + step])

    def own_to_core(names):
        for name in names:
            n = number[name]
            send(own[name], place(name, shard), core_send.at[n, 0], core_recv.at[n, 0], core_peer)
            pltpu.make_async_copy(own[name], place(name, shard), own_sem.at[n]).start()

    for name in DIRECT:
        cross(name)
    for name in EARLY + SHARED:
        cross(name, side(name)[0])
    for name in LATE:
        cross(name)
    own_to_core(DIRECT + EARLY)

    tokens, width = own["hid"].shape
    capacity = rows_put.shape[1]
    far_expert, half_start, in_half = (expert + 4) % 8, 4 * (expert // 4), expert % 4
    far_peer = (far_expert, shard)

    def to_far(index, ref, target):
        send(ref, target, far_send.at[index], far_recv.at[index], far_peer)

    def settle_far(index, ref):
        wait_for(ref, far_send.at[index])
        wait_for(ref, far_recv.at[index])

    to_far(0, meta_ref, meta_far)
    to_far(1, cot_ref, cot_far)

    def fill_slots(block, meta):
        expert_at = lax.broadcasted_iota(jnp.int32, (8, tokens), 0).astype(jnp.float32)
        named = ((meta[0:1] == expert_at) | (meta[1:2] == expert_at)).astype(jnp.float32)
        row_at = lax.broadcasted_iota(jnp.int32, (tokens, tokens), 0)
        before = row_at < lax.broadcasted_iota(jnp.int32, (tokens, tokens), 1)
        rank = dense_product(named.astype(jnp.bfloat16), before.astype(jnp.bfloat16))
        slot_ref[block] = jnp.where(named > 0.0, rank, -1.0)

    def picks(block, target):
        slot_at = lax.broadcasted_iota(jnp.int32, (capacity, tokens), 0)
        return slot_at == slot_ref[block, pl.ds(target, 1), :].astype(jnp.int32)

    def put_grads(block, meta, cot):
        gates = [as_column(gate) for gate in gate_pair(meta[2:3], meta[3:4])]
        route_grads = [(gate * cot.astype(jnp.float32)).astype(jnp.bfloat16) for gate in gates]
        for index in range(4):
            target = half_start + index
            chosen = picks(block, target)
            grads_put[4 * block + index] = sum(
                dense_product(
                    (chosen & (meta[k : k + 1].astype(jnp.int32) == target)).astype(jnp.bfloat16), route_grads[k]
                )
                for k in range(TOP)
            ).astype(jnp.bfloat16)

    def put_rows(block, ffn):
        for index in range(4):
            chosen = picks(block, half_start + index).astype(jnp.bfloat16)
            rows_put[4 * block + index] = dense_product(chosen, ffn).astype(jnp.bfloat16)

    def dispatch(block, put, got, sems):
        source = far_expert if block else expert
        for step in range(1, 4):
            index = (in_half + step) % 4
            at = 4 * block + step
            send(put.at[4 * block + index], got.at[source], sems[0].at[at], sems[1].at[at], (half_start + index, shard))
        pltpu.make_async_copy(put.at[4 * block + in_half], got.at[source], sems[0].at[4 * block]).start()

    def settle_dispatch(put, got, sems):
        for block in range(2):
            for step in range(4):
                wait_for(put.at[4 * block + (in_half + step) % 4], sems[0].at[4 * block + step])
            for step in range(1, 4):
                sender = half_start + (in_half + 4 - step) % 4
                wait_for(got.at[(sender + 4 * block) % 8], sems[1].at[4 * block + step])

    fill_slots(0, meta_ref[...])
    put_grads(0, meta_ref[...], cot_ref[...])
    dispatch(0, grads_put, grads_got, grad_sems)
    for name in DIRECT:
        wait_for(place(name, other), y_recv.at[number[name]])
        to_core(name, 0)

    def early_out(name):
        n, (half, peer) = number[name], side(name)
        part = place(name, other, half)
        wait_for(part, y_recv.at[n])
        send(part, part, swap_send.at[n], swap_recv.at[n], peer)
        to_core(name, 0, half)

    def pass_early(name):
        half, _ = side(name)
        wait_for(place(name, other, 1 - half), swap_recv.at[number[name]])
        to_core(name, 1, 1 - half)

    def settle_early_far(name):
        half, _ = side(name)
        settle_core(name, 0, half)
        settle_core(name, 1, 1 - half)
        wait_for(mine(name, half), y_send.at[number[name]])
        wait_for(place(name, other, half), swap_send.at[number[name]])

    def settle_early(names):
        settle_own(names)
        for name in names:
            settle_early_far(name)

    for name in ("wk", "wv", "wq"):
        early_out(name)
    own_to_core(SHARED + LATE)

    settle_own(DIRECT)
    for name in DIRECT:
        settle_core(name, 0)
    gain_rows = sum(full["gains"][pl.ds(slot * 16, 16), :].astype(jnp.float32) for slot in range(4))
    gain_ref[...] = gain_rows
    gain_first, gain_second = gain_rows[0:1], gain_rows[1:2]

    def norm_block(block, carry):
        rows = pl.ds(pl.multiple_of(block * tokens, tokens), tokens)
        values = full["hid"][rows, :].astype(jnp.float32)
        normed_ref[rows, :] = (values * rms_scale(values) * gain_first).astype(jnp.bfloat16)
        return carry

    lax.fori_loop(0, 4, norm_block, 0)

    pass_early("wk")
    pass_early("wv")
    settle_early(("wk",))

    def key_block(block, carry):
        rows = pl.ds(pl.multiple_of(block * tokens, tokens), tokens)
        raw = dense_product(normed_ref[rows, :], full["wk"][...])
        cosine, sine = cosine_ref[rows, :], sine_ref[rows, :]
        for start in range(0, width, 128):
            key_ref[rows, start : start + 128] = rotate_pair(raw[:, start : start + 128], cosine, sine).astype(jnp.bfloat16)
        return carry

    def value_block(block, carry):
        rows = pl.ds(pl.multiple_of(block * tokens, tokens), tokens)
        value_ref[rows, :] = dense_product(normed_ref[rows, :], full["wv"][...]).astype(jnp.bfloat16)
        return carry

    lax.fori_loop(0, 4, key_block, 0)
    pass_early("wq")
    settle_early(("wv",))
    lax.fori_loop(0, 4, value_block, 0)
    settle_early(("wq",))
    here = pl.ds(pl.multiple_of(shard * tokens, tokens), tokens)
    raw = dense_product(normed_ref[here, :], full["wq"][...])
    cosine, sine = cosine_ref[here, :], sine_ref[here, :]
    for start in range(0, width, 128):
        query_ref[:, start : start + 128] = rotate_pair(raw[:, start : start + 128], cosine, sine).astype(jnp.bfloat16)
    early_out("wo")

    own_segment = as_column(segment_row[:, here].astype(jnp.float32)).astype(jnp.int32)

    def head_pair(pair, carry):
        lanes = pl.ds(pl.multiple_of(pair * 128, 128), 128)
        query, keys, values = query_ref[:, lanes], key_ref[:, lanes], value_ref[:, lanes]
        allowed = allowed_mask(shard * tokens, 0, own_segment, segment_row[...], padding_row[...])
        lane = lax.broadcasted_iota(jnp.int32, query.shape, 1)
        results = []
        for half in range(2):
            chosen = (lane >= 64) if half else (lane < 64)
            scores = product_t(jnp.where(chosen, query, jnp.zeros_like(query)), keys) * 0.125
            scores = jnp.where(allowed, scores, neg_fill)
            top_score = jnp.max(scores, axis=-1, keepdims=True)
            exponent = jnp.exp(scores - top_score)
            exp_total = jnp.sum(exponent, axis=-1, keepdims=True)
            lse_ref[2 * pair + half] = top_score + jnp.log(exp_total)
            results.append(dense_product((exponent / exp_total).astype(jnp.bfloat16), values))
        attended_ref[:, lanes] = jnp.where(lane < 64, results[0], results[1]).astype(jnp.bfloat16)
        return carry

    lax.fori_loop(0, 2, head_pair, 0)
    early_out("sg")
    pass_early("wo")
    lax.fori_loop(2, 5, head_pair, 0)
    early_out("su")
    pass_early("sg")
    lax.fori_loop(5, 6, head_pair, 0)
    settle_far(0, meta_far)
    settle_far(1, cot_far)
    fill_slots(1, meta_far[...])
    put_grads(1, meta_far[...], cot_far[...])
    settle_early(("wo",))
    rows_in = own["hid"][...].astype(jnp.float32)
    mixed = rows_in + dense_product(attended_ref[...], full["wo"][...])
    mixed_ref[...] = mixed
    ffn = (mixed * rms_scale(mixed) * gain_second).astype(jnp.bfloat16)
    ffn_ref[...] = ffn
    to_far(2, ffn_ref, ffn_far)
    put_rows(0, ffn)
    dispatch(0, rows_put, rows_got, row_sems)
    dispatch(1, grads_put, grads_got, grad_sems)
    keep = [full[name] for name in EARLY]
    keep += [normed_ref, query_ref, key_ref, value_ref, lse_ref, attended_ref, mixed_ref, cot_far, meta_far]
    for index, ref in enumerate(keep):
        pltpu.make_async_copy(ref, saved[index], save_sem.at[index]).start()
    early_out("sd")
    pass_early("su")
    settle_early(("sg", "su"))
    settle_own(("sd",))
    shared_ref[...] = jnp.zeros_like(shared_ref)
    ffn_grad_ref[...] = jnp.zeros_like(ffn_grad_ref)

    why = shard // 2

    def shared_block(block, carry):
        cut = pl.ds(pl.multiple_of((block + 2 * why) % 4 * 512, 512), 512)
        normed = ffn_ref[...]
        gate, up, down = full["sg"][:, cut], full["su"][:, cut], full["sd"][cut, :]
        pre, lin = dense_product(normed, gate), dense_product(normed, up)
        middle = (jax.nn.silu(pre) * lin).astype(jnp.bfloat16)
        shared_ref[...] += dense_product(middle, down)
        pre_grad, lin_grad = swiglu_back(product_t(cot_ref[...], down), pre, lin)
        ffn_grad_ref[...] += product_t(pre_grad, gate) + product_t(lin_grad, up)
        full["sg"][:, cut] = t_product(normed, pre_grad).astype(jnp.bfloat16)
        full["su"][:, cut] = t_product(normed, lin_grad).astype(jnp.bfloat16)
        full["sd"][cut, :] = t_product(middle, cot_ref[...]).astype(jnp.bfloat16)
        return carry

    core = shard % 2
    shared_grads = (full["sg"], full["su"], full["sd"])

    def halved(index, turn):
        ref, rows, columns = shared_grads[index], shared_grads[index].shape[0] // 4, shared_grads[index].shape[1]
        part = why if turn == 0 else 1 - why
        picked = (pl.ds(0, rows),)
        if index < 2:
            picked += (pl.ds(pl.multiple_of(part * (columns // 2), 128), columns // 2),)
        for y_of in (part,) if index == 2 else (0, 1):
            far_rows, near_rows = [pl.ds((y_of * 2 + of) * rows, rows) for of in (1 - core, core)]
            at = (y_of,) + picked
            place_of = 2 * turn if index == 2 else 2 * turn + y_of
            yield (
                ref.at[(far_rows,) + picked[1:]],
                shared_core[index].at[at],
                ref.at[(near_rows,) + picked[1:]],
                shared_work[index].at[at],
                place_of,
            )

    def share(part):
        for index in range(3):
            for away, landing, _, _, at in halved(index, part):
                send(away, landing, share_send.at[index, at], share_recv.at[index, at], core_peer)

    def take_share(part):
        for index in range(3):
            for away, landing, near, target, at in halved(index, part):
                wait_for(landing, share_recv.at[index, at])
                add_rows(target, near, landing)
                wait_for(away, share_send.at[index, at])

    cuts = full["sg"].shape[1] // 512
    lax.fori_loop(0, cuts // 2, shared_block, 0)
    share(0)
    pass_early("sd")
    settle_early_far("sd")
    lax.fori_loop(cuts // 2, cuts, shared_block, 0)
    share(1)
    settle_far(2, ffn_far)
    put_rows(1, ffn_far[...])
    dispatch(1, rows_put, rows_got, row_sems)
    take_share(0)

    for name in LATE:
        wait_for(place(name, other), y_recv.at[number[name]])
        to_core(name, 0)

    for name in DIRECT:
        wait_for(own[name], y_send.at[number[name]])
    settle_own(LATE)
    for name in LATE:
        wait_for(own[name], y_send.at[number[name]])
        settle_core(name, 0)
    take_share(1)
    settle_dispatch(grads_put, grads_got, grad_sems)
    settle_dispatch(rows_put, rows_got, row_sems)
    for index, ref in enumerate(keep):
        wait_for(ref, save_sem.at[index])


def as_column(row):
    shape = (row.shape[1], row.shape[1])
    same = lax.broadcasted_iota(jnp.int32, shape, 0) == lax.broadcasted_iota(jnp.int32, shape, 1)
    return jnp.sum(jnp.where(same, row, 0.0), axis=1, keepdims=True)


def as_row(column):
    shape = (column.shape[0], column.shape[0])
    same = lax.broadcasted_iota(jnp.int32, shape, 0) == lax.broadcasted_iota(jnp.int32, shape, 1)
    return jnp.sum(jnp.where(same, column, 0.0), axis=0, keepdims=True)


def gate_pair(first, second):
    top = jnp.maximum(first, second)
    first, second = jnp.exp(first - top), jnp.exp(second - top)
    total = first + second
    return first / total, second / total


def allowed_mask(query_start, key_start, query_segment, key_segment, key_padding):
    shape = (query_segment.shape[0], key_segment.shape[1])
    query_at = query_start + lax.broadcasted_iota(jnp.int32, shape, 0)
    key_at = key_start + lax.broadcasted_iota(jnp.int32, shape, 1)
    distance = query_at - key_at
    return (
        (query_segment == key_segment)
        & (distance >= 0)
        & (distance < WINDOW)
        & ((key_padding == 1) | (distance == 0))
    )


def first_part(hidden, gains, dense, experts, segment, padding, cotangent, meta):
    tokens, width = hidden.shape
    bfloat, single = jnp.bfloat16, jnp.float32
    wq, wk, wv, wo, sg, su, sd = dense
    blocks = dict(hid=hidden, gains=jnp.pad(gains, ((0, 14), (0, 0))), wq=wq, wk=wk, wv=wv, wo=wo, sg=sg, su=su, sd=sd)
    blocks.update(zip(LATE, experts[:2]))
    blocks = [blocks[name] for name in NAMES]
    count = len(NAMES)
    cosine, sine = rotary_tables(4 * tokens, width // HEADS)
    in_hbm, in_vmem = pl.BlockSpec(memory_space=pl.ANY), pl.BlockSpec(memory_space=pltpu.VMEM)
    dma = pltpu.SemaphoreType.DMA
    shape = jax.ShapeDtypeStruct
    whole = {name: shape((4 * block.shape[0], block.shape[1]), block.dtype) for name, block in zip(NAMES, blocks)}
    middle = sg.shape[1]
    capacity = max(2, 2 * tokens * TOP // 8)
    routed = (8, capacity, width)
    halved = [(2,) + block.shape for block in (sg, su, sd)]
    inner = [
        shape((4 * tokens, width), bfloat),
        shape((tokens, width), bfloat),
        shape((4 * tokens, width), bfloat),
        shape((4 * tokens, width), bfloat),
        shape((HEADS, tokens, 1), single),
        shape((tokens, width), bfloat),
        shape((tokens, width), single),
        shape((tokens, width), bfloat),
    ]
    out = pl.pallas_call(
        first_kernel,
        out_shape=[whole[name] for name in LATE]
        + [whole[name] for name in EARLY]
        + inner[:7]
        + [
            shape((tokens, width), bfloat),
            shape((8, tokens), single),
            shape((16, width), single),
            shape(routed, bfloat),
            shape(routed, bfloat),
            shape((tokens, width), single),
            shape((tokens, width), single),
        ]
        + [shape(one, bfloat) for one in halved],
        in_specs=[in_vmem] * (count + 6),
        out_specs=[in_hbm] * (len(LATE) + SAVED) + [in_vmem] + [in_hbm] * 2 + [in_vmem] * 5,
        scratch_shapes=[pltpu.VMEM(whole[name].shape, whole[name].dtype) for name in PASSING]
        + [pltpu.VMEM(one.shape, one.dtype) for one in inner]
        + [pltpu.VMEM(one, bfloat) for one in halved]
        + [pltpu.VMEM(routed, bfloat)] * 2
        + [
            dma((count,)),
            dma((count,)),
            dma((count,)),
            dma((count,)),
            dma((count,)),
            dma((count, 3)),
            dma((count, 3)),
        ]
        + [dma((8,))] * 4
        + [dma((3, 4))] * 2
        + [
            dma((SAVED,)),
            dma((3,)),
            dma((3,)),
            pltpu.VMEM((2, 8, tokens), single),
            pltpu.VMEM((8, tokens), single),
            pltpu.VMEM((tokens, width), bfloat),
            pltpu.VMEM((tokens, width), bfloat),
        ],
        compiler_params=pltpu.CompilerParams(collective_id=0, has_side_effects=True, vmem_limit_bytes=60 << 20),
        cost_estimate=pl.CostEstimate(flops=15000000000, bytes_accessed=47000000, transcendentals=3000000),
    )(
        *blocks,
        segment[None, :],
        padding[None, :],
        jnp.asarray(cosine),
        jnp.asarray(sine),
        cotangent,
        meta,
    )
    return dict(zip(LATE + EARLY, out)), out[len(LATE + EARLY) :]


def add_into(target, first, second):
    rows = first.shape[-2]
    strip = math.gcd(rows, 64)

    def body(index, carry):
        at = pl.ds(pl.multiple_of(index * strip, strip), strip)
        for lead in range(first.shape[0]):
            total = first[lead, at, :].astype(jnp.float32) + second[lead, at, :].astype(jnp.float32)
            target[lead, at, :] = total.astype(target.dtype)
        return carry

    lax.fori_loop(0, rows // strip, body, 0)


class PlaneSum:
    def __init__(self, shape, work, receive, send_sem, recv_sem, bits, peers, order, out=None, done=0):
        self.work, self.receive, self.out = work, receive, out
        self.send_sem, self.recv_sem, self.bits, self.peers, self.order = send_sem, recv_sem, bits, peers, order
        self.at = [(0, size) for size in shape]
        self.inside = [0, 0, 0]
        self.trail = []
        for step in range(done):
            self.narrow(step)
        self.inside = [0, 0, 0]
        self.step = done

    def region(self, ref, starts, sizes):
        starts = [
            start if isinstance(start, int) or unit == 1 else pl.multiple_of(start, unit)
            for start, unit in zip(starts, (1, 16, 128))
        ]
        return ref.at[tuple(pl.ds(start, size) for start, size in zip(starts, sizes))]

    def working(self, bit_of):
        axis, dim = self.order[self.step]
        starts, sizes = list(self.inside), [size for _, size in self.at]
        sizes[dim] //= 2
        starts[dim] = starts[dim] + bit_of(self.bits[axis]) * sizes[dim]
        return self.region(self.work, starts, sizes)

    def final(self, at):
        return self.region(self.out, [0] + [start for start, _ in at[1:]], [1] + [size for _, size in at[1:]])

    def narrow(self, step):
        axis, dim = self.order[step]
        if axis != "y":
            self.trail.append((step, self.at))
        (start, size), self.at = self.at[dim], list(self.at)
        self.at[dim] = (start + self.bits[axis] * (size // 2), size // 2)
        self.inside[dim] = self.inside[dim] + self.bits[axis] * (size // 2)

    def start(self):
        step = self.step
        peer = self.peers[self.order[step][0]]
        send(self.working(lambda bit: 1 - bit), self.receive[step], self.send_sem.at[step], self.recv_sem.at[step], peer)

    def finish(self, target=None):
        step = self.step
        wait_for(self.receive[step], self.recv_sem.at[step])
        kept, gone = self.working(lambda bit: bit), self.working(lambda bit: 1 - bit)
        self.narrow(step)
        if step == len(self.order) - 1:
            target = self.final(self.at)
        add_into(kept if target is None else target, kept, self.receive[step])
        wait_for(gone, self.send_sem.at[step])
        self.step = step + 1

    def back_start(self):
        step, _ = self.trail[-1]
        part, at = self.final(self.at), self.step
        send(part, part, self.send_sem.at[at], self.recv_sem.at[at], self.peers[self.order[step][0]])

    def back_finish(self):
        step, whole = self.trail.pop()
        wait_for(self.final(self.at), self.send_sem.at[self.step])
        dim = self.order[step][1]
        start, size = self.at[dim]
        other = list(self.at)
        other[dim] = (2 * whole[dim][0] + size - start, size)
        wait_for(self.final(other), self.recv_sem.at[self.step])
        self.at = list(self.at)
        self.at[dim] = whole[dim]
        self.step += 1

    def advance(self):
        if self.step < len(self.order):
            self.finish()
        else:
            self.back_finish()
        if self.step < len(self.order):
            self.start()
        elif self.trail:
            self.back_start()


def receive_shapes(shape, order):
    result, shape = [], list(shape)
    for _, dim in order:
        shape[dim] //= 2
        result.append(tuple(shape))
    return result


def ordered(axes, dims):
    return tuple((axis, 0 if axis == "y" else dims[axis]) for axis in axes)


BY_COLUMNS, BY_ROWS = dict(x=2, z1=2, z2=2), dict(x=1, z1=1, z2=1)
BY_BOTH = dict(x=2, z1=1, z2=1)
SHARED_ORDER = (
    ordered(("y", "x", "z1", "z2"), BY_COLUMNS),
    ordered(("x", "y", "z1", "z2"), BY_COLUMNS),
    ordered(("z1", "y", "x", "z2"), BY_ROWS),
)
SHARED_DONE = 2
ATTENTION_ORDER = (
    ordered(("z1", "x", "y", "z2"), BY_BOTH),
    ordered(("y", "x", "z1", "z2"), BY_BOTH),
    ordered(("x", "z1", "y", "z2"), BY_BOTH),
    ordered(("x", "z1", "y", "z2"), BY_BOTH),
)


def plane_places():
    expert, shard = (lax.axis_index("expert"), lax.axis_index("shard"))
    zed, ex, why, core = (expert // 2, expert % 2, shard // 2, shard % 2)
    bits = {"x": ex, "z1": zed % 2, "z2": zed // 2, "y": why}
    peers = {
        "x": (expert + 1 - 2 * ex, shard),
        "z1": (expert + 2 - 4 * (zed % 2), shard),
        "z2": ((expert + 4) % 8, shard),
        "y": (expert, (shard + 2) % 4),
        "core": (expert, shard + 1 - 2 * core),
    }
    return expert, shard, zed, core, bits, peers


def enter(peers):
    barrier = pltpu.get_barrier_semaphore()
    for peer in peers:
        pl.semaphore_signal(barrier, inc=1, device_id=peer, device_id_type=MESH)
    pl.semaphore_wait(barrier, len(peers))


def second_kernel(*refs):
    rows_ref, grads_ref, meta_far, *weights_in, down_own = refs[:6]
    shared_in = refs[6:9]
    rows_back, grads_back, grads_far = refs[9:12]
    expert_core, shared_out = refs[12:15], refs[15:18]
    weights, shared_work = refs[18:21], refs[21:24]
    rows_put, grads_put, middle_ref, pre_ref, lin_ref, out_sum, grad_sum, far_put = refs[24:32]
    refs = refs[32:]
    receive = [refs[SHARED_DONE * index : SHARED_DONE * (index + 1)] for index in range(3)]
    refs = refs[3 * SHARED_DONE :]
    load_sem, shared_sem, out_send, out_recv, grad_send, grad_recv, core_send, core_recv, sum_send, sum_recv, far_send, far_recv, down_send, down_recv = refs
    expert, shard, zed, core, bits, peers = plane_places()
    def down_rows(slot):
        rows = down_own.shape[0]
        return weights[2].at[pl.ds(slot * rows, rows)]

    why = bits["y"]
    other, beside = (shard + 2) % 4, shard + 1 - 2 * core
    for index in range(2):
        pltpu.make_async_copy(weights_in[index], weights[index], load_sem.at[index]).start()
    for index in range(3):
        pltpu.make_async_copy(shared_in[index], shared_work[index], shared_sem.at[index]).start()
    pltpu.make_async_copy(down_own, down_rows(shard), load_sem.at[2]).start()
    enter((peers["y"], peers["core"]) + tuple(((expert + step) % 8, shard) for step in range(1, 8)))
    send(down_own, down_rows(shard), down_send.at[0], down_recv.at[0], peers["y"])
    send(down_own, down_rows(shard), down_send.at[1], down_recv.at[1], peers["core"])
    sums = [
        PlaneSum(
            shared_work[index].shape,
            shared_work[index],
            receive[index],
            sum_send.at[index],
            sum_recv.at[index],
            bits,
            peers,
            SHARED_ORDER[index],
        )
        for index in range(3)
    ]
    for index in range(3):
        pltpu.make_async_copy(shared_in[index], shared_work[index], shared_sem.at[index]).wait()
        sums[index].start()
    for index in range(2):
        pltpu.make_async_copy(weights_in[index], weights[index], load_sem.at[index]).wait()

    _, capacity, width = rows_ref.shape
    gate_ref, up_ref, down_ref = weights
    middle = gate_ref.shape[1]
    cuts = middle // 512

    half, in_half = expert // 4, expert % 4
    lot = 4 * capacity

    def hidden_units(index, carry):
        cut = pl.ds(pl.multiple_of(index * 512, 512), 512)
        rows = rows_ref[...].reshape(2 * lot, width)
        pre, lin = dense_product(rows, gate_ref[:, cut]), dense_product(rows, up_ref[:, cut])
        middle_ref[:, cut] = (jax.nn.silu(pre) * lin).astype(jnp.bfloat16)
        pre_ref[:, cut] = pre.astype(jnp.bfloat16)
        lin_ref[:, cut] = lin.astype(jnp.bfloat16)
        return carry

    def block(of_half, between=None):
        lots, here = pl.ds(4 * of_half, 4), pl.ds(pl.multiple_of(of_half * lot, lot), lot)
        grads = grads_ref[lots].reshape(lot, width)
        out_sum[...] = jnp.zeros_like(out_sum)
        grad_sum[...] = jnp.zeros_like(grad_sum)

        def body(index, carry):
            cut = pl.ds(pl.multiple_of((index + 2 * why) % 4 * 512, 512), 512)
            gate, up, down = gate_ref[:, cut], up_ref[:, cut], down_ref[cut, :]
            pre, lin = pre_ref[here, cut].astype(jnp.float32), lin_ref[here, cut].astype(jnp.float32)
            pre_grad, lin_grad = swiglu_back(product_t(grads, down), pre, lin)
            grad_sum[...] += product_t(pre_grad, gate) + product_t(lin_grad, up)
            out_sum[...] += dense_product(middle_ref[here, cut], down)
            pre_ref[here, cut] = pre_grad
            lin_ref[here, cut] = lin_grad
            return carry

        if between is None:
            lax.fori_loop(0, cuts, body, 0)
        else:
            lax.fori_loop(0, cuts // 2, body, 0)
            between()
            lax.fori_loop(cuts // 2, cuts, body, 0)
        rows_put[lots] = out_sum[...].astype(jnp.bfloat16).reshape(4, capacity, width)
        grads_put[lots] = grad_sum[...].astype(jnp.bfloat16).reshape(4, capacity, width)
        give_back(of_half, grads_put, grads_back, grad_send, grad_recv)
        give_back(of_half, rows_put, rows_back, out_send, out_recv)

    def give_back(of_half, put, back, send_sem, recv_sem):
        slot = 4 * ((of_half + half) % 2) + in_half
        for step in range(1, 4):
            there = (in_half + step) % 4
            source = 4 * of_half + there
            send(put.at[source], back.at[slot], send_sem.at[source], recv_sem.at[slot], (4 * half + there, shard))
        back[pl.ds(slot, 1)] = put[pl.ds(4 * of_half + in_half, 1)]

    def settle_back(put, back, send_sem, recv_sem, far):
        for step in range(1, 4):
            there = (in_half + step) % 4
            source = (4 * half + there + 4 * far) % 8
            wait_for(put.at[source], send_sem.at[source])
            wait_for(back.at[4 * far + there], recv_sem.at[4 * far + there])

    lax.fori_loop(0, cuts, hidden_units, 0)
    wait_for(down_rows(shard), load_sem.at[2])
    wait_for(down_rows(beside), down_recv.at[1])

    def rest_of_down():
        wait_for(down_rows(other), down_recv.at[0])
        send(down_rows(other), down_rows(other), down_send.at[2], down_recv.at[2], peers["core"])
        wait_for(down_rows((beside + 2) % 4), down_recv.at[2])

    block(1 - half, rest_of_down)
    for one in sums:
        one.advance()
    block(half)
    settle_back(grads_put, grads_back, grad_send, grad_recv, 1)
    taken = slots_in_half(meta_far[...], half, capacity)
    slot_at = lax.broadcasted_iota(jnp.int32, (taken[0].shape[0], 4 * capacity), 1)
    chosen = ((slot_at == taken[0]) | (slot_at == taken[1])).astype(jnp.bfloat16)
    far_put[...] = dense_product(chosen, grads_back[4:8].reshape(4 * capacity, width)).astype(jnp.bfloat16)
    send(far_put, grads_far, far_send, far_recv, ((expert + 4) % 8, shard))
    for index, ref in enumerate((down_rows(shard), down_rows(shard), down_rows(other))):
        wait_for(ref, down_send.at[index])

    rows_all, grads_all = rows_ref, grads_ref

    def weight_grad(index):
        def body(step, carry):
            cut = pl.ds(pl.multiple_of(step * 512, 512), 512)
            if index == 2:
                left, right = middle_ref[:, cut], grads_all[...].reshape(8 * capacity, width)
                down_ref[cut, :] = t_product(left, right).astype(jnp.bfloat16)
            else:
                left, right = rows_all[...].reshape(8 * capacity, width), (pre_ref, lin_ref)[index][:, cut]
                weights[index][:, cut] = t_product(left, right).astype(jnp.bfloat16)
            return carry

        lax.fori_loop(0, cuts, body, 0)

    def shard_rows(index, y_of, core_of):
        rows = weights[index].shape[0] // 4
        return weights[index].at[pl.ds((y_of * 2 + core_of) * rows, rows)]

    def core_start(index):
        for y_of in range(2):
            send(
                shard_rows(index, y_of, 1 - core),
                expert_core[index].at[y_of],
                core_send.at[index, y_of],
                core_recv.at[index, y_of],
                peers["core"],
            )

    def core_finish(index):
        for y_of in range(2):
            wait_for(expert_core[index].at[y_of], core_recv.at[index, y_of])
            wait_for(shard_rows(index, y_of, 1 - core), core_send.at[index, y_of])
        for y_of in range(2):
            kept = shard_rows(index, y_of, core)
            add_rows(expert_core[index].at[y_of], kept, expert_core[index].at[y_of])

    weight_grad(0)
    core_start(0)
    weight_grad(1)
    core_start(1)
    core_finish(0)
    for one, target in zip(sums, shared_out):
        one.finish(target)
    weight_grad(2)
    core_start(2)
    core_finish(1)
    settle_back(grads_put, grads_back, grad_send, grad_recv, 0)
    for far in range(2):
        settle_back(rows_put, rows_back, out_send, out_recv, far)
    wait_for(far_put, far_send)
    wait_for(grads_far, far_recv)
    core_finish(2)


def slots_in_half(meta, half, capacity):
    tokens = meta.shape[1]
    expert_at = lax.broadcasted_iota(jnp.int32, (tokens, 128), 1)
    choices = [as_column(meta[k : k + 1]).astype(jnp.int32) for k in range(TOP)]
    named = ((choices[0] == expert_at) | (choices[1] == expert_at)).astype(jnp.bfloat16)
    row_at = lax.broadcasted_iota(jnp.int32, (tokens, tokens), 0)
    before = lax.broadcasted_iota(jnp.int32, (tokens, tokens), 1) < row_at
    rank = dense_product(before.astype(jnp.bfloat16), named).astype(jnp.int32)
    slot = rank + (expert_at - 4 * half) * capacity
    columns = [jnp.sum(jnp.where(choice == expert_at, slot, 0).astype(jnp.float32), axis=1, keepdims=True) for choice in choices]
    return [jnp.where(choice // 4 == half, column.astype(jnp.int32), -1) for choice, column in zip(choices, columns)]


def add_rows(target, first, second):
    def body(index, carry):
        at = pl.ds(pl.multiple_of(index * 64, 64), 64)
        target[at, :] = (first[at, :].astype(jnp.float32) + second[at, :].astype(jnp.float32)).astype(target.dtype)
        return carry

    lax.fori_loop(0, first.shape[0] // 64, body, 0)


def second_part(rows, grads, meta_far, weights, shared):
    in_hbm, in_vmem = pl.BlockSpec(memory_space=pl.ANY), pl.BlockSpec(memory_space=pltpu.VMEM)
    dma, bfloat = pltpu.SemaphoreType.DMA, jnp.bfloat16
    shape = jax.ShapeDtypeStruct
    count, capacity, width = rows.shape
    middle = weights[0].shape[1]
    down_own = weights[2]
    whole = [weights[0].shape, weights[1].shape, (4 * down_own.shape[0], down_own.shape[1])]
    quarter = [(one[0] // 4, one[1]) for one in whole]
    steps = [receive_shapes(work.shape, order)[:SHARED_DONE] for work, order in zip(shared, SHARED_ORDER)]
    blocks = (count * capacity, middle)
    return pl.pallas_call(
        second_kernel,
        out_shape=[shape(rows.shape, bfloat)] * 2
        + [shape((meta_far.shape[1], width), bfloat)]
        + [shape((2,) + one, bfloat) for one in quarter]
        + [shape(one[-1], bfloat) for one in steps],
        in_specs=[in_vmem] * 3 + [in_hbm] * 6,
        out_specs=[in_vmem] * 9,
        scratch_shapes=[pltpu.VMEM(one, bfloat) for one in whole]
        + [pltpu.VMEM(work.shape, bfloat) for work in shared]
        + [pltpu.VMEM(rows.shape, bfloat)] * 2
        + [pltpu.VMEM(blocks, bfloat)] * 3
        + [pltpu.VMEM((4 * capacity, width), jnp.float32)] * 2
        + [pltpu.VMEM((meta_far.shape[1], width), bfloat)]
        + [pltpu.VMEM(one, bfloat) for group in steps for one in group]
        + [dma((3,)), dma((3,))]
        + [dma((8,))] * 4
        + [dma((3, 2)), dma((3, 2)), dma((3, SHARED_DONE)), dma((3, SHARED_DONE)), dma(()), dma(()), dma((3,)), dma((3,))],
        compiler_params=pltpu.CompilerParams(collective_id=1, has_side_effects=True, vmem_limit_bytes=62 << 20),
        cost_estimate=pl.CostEstimate(flops=29000000000, bytes_accessed=30000000, transcendentals=2000000),
    )(rows, grads, meta_far, *weights, *shared)


STORED = 15


def third_kernel(*refs):
    rows_back, grads_back, grads_far, mixed_ref, shared_ref, ffn_grad_ref, cot_ref, hidden_ref, gain_ref, meta_ref = refs[:10]
    segment_row, padding_row, cot_far, meta_far = refs[10:14]
    stored, left_over = refs[14 : 14 + STORED], refs[14 + STORED : 17 + STORED]
    output_ref, input_grad_ref, logit_grad_ref, gain_out = refs[32:36]
    sums_out, shared_out, expert_out = refs[36:40], refs[40:43], refs[43:46]
    query_grad, key_grad, value_grad, context_grad, attended_grad, mixed_grad_ref = refs[46:52]
    weight_grads, weight_work = refs[52:56], refs[56:60]
    context_core, context_y, far_got = refs[60:63]
    expert_y = refs[63:66]
    refs = refs[66:]
    receive = [refs[4 * index : 4 * index + 4] for index in range(4)]
    refs = refs[16:]
    rest = 4 - SHARED_DONE
    shared_receive = [(None,) * SHARED_DONE + refs[rest * index : rest * index + rest] for index in range(3)]
    refs = refs[3 * rest :]
    loaded, left_mine = refs[:STORED], refs[STORED : STORED + 3]
    wo_ref, attended_ref, cosine_ref, sine_ref, query_ref, key_ref, value_ref, lse_ref, normed_ref, wk_ref, wv_ref, wq_ref = loaded[3:]
    shared_work = loaded[:3]
    refs = refs[STORED + 3 :]
    gain_parts, gain_recv = refs[:2]
    core_send, core_recv, sum_send, sum_recv, share_send, share_recv, ctx_send, ctx_recv, gain_send, gain_got, late_send, late_recv, load_sem, left_sem, far_put, part_put, part_got = refs[2:]
    expert, shard, zed, core, bits, peers = plane_places()
    why = bits["y"]
    for index in range(STORED):
        pltpu.make_async_copy(stored[index], loaded[index], load_sem.at[index]).start()
    enter(tuple(peers[axis] for axis in ("core", "y", "x", "z1", "z2")))
    def send_left(index):
        send(left_over[index].at[1 - why], expert_y[index], ctx_send.at[3 + index], ctx_recv.at[3 + index], peers["y"])

    send_left(0)
    send_left(1)
    for index in range(3):
        pltpu.make_async_copy(left_over[index].at[why], left_mine[index], left_sem.at[index]).start()
    shared_sums = [
        PlaneSum(
            (2,) + shared_out[index].shape[1:],
            shared_work[index],
            shared_receive[index],
            share_send.at[index],
            share_recv.at[index],
            bits,
            peers,
            SHARED_ORDER[index],
            shared_out[index],
            SHARED_DONE,
        )
        for index in range(3)
    ]
    for index, one in enumerate(shared_sums):
        wait_for(loaded[index], load_sem.at[index])
        one.start()
    tokens, width = hidden_ref.shape
    here = pl.ds(pl.multiple_of(shard * tokens, tokens), tokens)
    single, bfloat = jnp.float32, jnp.bfloat16

    half, capacity = expert // 4, rows_back.shape[1]
    slots = 4 * capacity
    slot_at = lax.broadcasted_iota(jnp.int32, (tokens, slots), 1)
    slots_taken = slots_in_half(meta_ref[...], half, capacity)
    grad_out = cot_ref[...].astype(single)
    mixed = mixed_ref[...]
    picks = (slot_at == slots_taken[0]) | (slot_at == slots_taken[1])
    ffn_grad = ffn_grad_ref[...] + dense_product(picks.astype(bfloat), grads_back[0:4].reshape(slots, width))
    ffn_grad = ffn_grad + grads_far[...].astype(single)
    scale_second = rms_scale(mixed)
    gain_parts[0] = jnp.zeros_like(gain_parts[0])
    gain_parts[0, 1:2, :] = jnp.sum(ffn_grad * mixed * scale_second, axis=0, keepdims=True)
    scaled = ffn_grad * gain_ref[1:2, :]
    mixed_grad = (
        grad_out
        + scale_second * scaled
        - mixed * (scale_second * scale_second * scale_second) * jnp.mean(scaled * mixed, axis=-1, keepdims=True)
    )
    mixed_grad_ref[...] = mixed_grad
    mixed_low = mixed_grad.astype(bfloat)
    for index in range(3, 5):
        wait_for(loaded[index], load_sem.at[index])
    attended_grad[...] = product_t(mixed_low, wo_ref[...]).astype(bfloat)

    def shard_rows(ref, y_of, core_of):
        rows = ref.shape[0] // 4
        return ref.at[pl.ds((y_of * 2 + core_of) * rows, rows)]

    def core_start(index):
        for y_of in range(2):
            send(
                shard_rows(weight_grads[index], y_of, 1 - core),
                weight_work[index].at[y_of],
                core_send.at[index, y_of],
                core_recv.at[index, y_of],
                peers["core"],
            )

    def core_finish(index):
        for y_of in range(2):
            wait_for(weight_work[index].at[y_of], core_recv.at[index, y_of])
            wait_for(shard_rows(weight_grads[index], y_of, 1 - core), core_send.at[index, y_of])
            add_rows(weight_work[index].at[y_of], shard_rows(weight_grads[index], y_of, core), weight_work[index].at[y_of])

    sums = [
        PlaneSum(
            weight_work[index].shape,
            weight_work[index],
            receive[index],
            sum_send.at[index],
            sum_recv.at[index],
            bits,
            peers,
            ATTENTION_ORDER[index],
            sums_out[index],
        )
        for index in range(4)
    ]
    weight_grads[3][...] = t_product(attended_ref[...], mixed_low).astype(bfloat)
    core_start(3)

    for index in range(5, STORED):
        wait_for(loaded[index], load_sem.at[index])

    own_segment = as_column(segment_row[:, here].astype(single)).astype(jnp.int32)

    def head_pair(pair, carry):
        lanes = pl.ds(pl.multiple_of(pair * 128, 128), 128)
        query, keys, values, grads = query_ref[:, lanes], key_ref[:, lanes], value_ref[:, lanes], attended_grad[:, lanes]
        allowed = allowed_mask(shard * tokens, 0, own_segment, segment_row[...], padding_row[...])
        lane = lax.broadcasted_iota(jnp.int32, query.shape, 1)
        from_keys = []
        key_total = value_total = None
        for half in range(2):
            chosen = (lane >= 64) if half else (lane < 64)
            one_query = jnp.where(chosen, query, jnp.zeros_like(query))
            one_grad = jnp.where(chosen, grads, jnp.zeros_like(grads))
            scores = jnp.where(allowed, product_t(one_query, keys) * 0.125, neg_fill)
            probs = jnp.exp(scores - lse_ref[2 * pair + half])
            probs_grad = product_t(one_grad, values)
            delta = jnp.sum(probs * probs_grad, axis=1, keepdims=True)
            scores_grad = (probs * (probs_grad - delta)).astype(bfloat)
            from_keys.append(dense_product(scores_grad, keys))
            key_part = t_product(scores_grad, one_query)
            value_part = t_product(probs.astype(bfloat), one_grad)
            key_total = key_part if key_total is None else key_total + key_part
            value_total = value_part if value_total is None else value_total + value_part
        back = jnp.where(lane < 64, from_keys[0], from_keys[1]) * 0.125
        query_grad[:, lanes] = rotate_pair(back, cosine_ref[here, :], -sine_ref[here, :]).astype(bfloat)
        key_grad[:, lanes] = rotate_pair(key_total * 0.125, cosine_ref[...], -sine_ref[...]).astype(bfloat)
        value_grad[:, lanes] = value_total.astype(bfloat)
        return carry

    def group_grads(group):
        cut = slice(256 * group, 256 * group + 256)
        weight_grads[group][:, 0:256] = t_product(normed_ref[here, :], query_grad[:, cut]).astype(bfloat)
        weight_grads[group][:, 256:512] = t_product(normed_ref[...], key_grad[:, cut]).astype(bfloat)
        weight_grads[group][:, 512:768] = t_product(normed_ref[...], value_grad[:, cut]).astype(bfloat)
        core_start(group)

    def from_experts(block, taken, meta, grads):
        gates = [as_column(gate) for gate in gate_pair(meta[2:3], meta[3:4])]
        results = rows_back[4 * block : 4 * block + 4].reshape(slots, width)
        per_route = [dense_product((slot_at == slot).astype(bfloat), results) for slot in taken]
        routed = gates[0] * per_route[0] + gates[1] * per_route[1]
        return routed, [as_row(jnp.sum(rows * grads, axis=1, keepdims=True)) for rows in per_route]

    def serve_far():
        meta = meta_far[...]
        routed, contrib = from_experts(1, slots_in_half(meta, half, capacity), meta, cot_far[...].astype(single))
        far_put[...] = routed.astype(bfloat)
        part_put[...] = jnp.zeros_like(part_put)
        for k in range(TOP):
            part_put[k : k + 1, :] = contrib[k]
        send(far_put, far_got, late_send.at[0], late_recv.at[0], peers["z2"])
        send(part_put, part_got, late_send.at[1], late_recv.at[1], peers["z2"])

    def combine():
        meta = meta_ref[...]
        routed, contrib = from_experts(0, slots_taken, meta, grad_out)
        wait_for(far_got, late_recv.at[0])
        wait_for(part_got, late_recv.at[1])
        output_ref[...] = (mixed_ref[...] + shared_ref[...] + routed + far_got[...].astype(single)).astype(bfloat)
        gates = gate_pair(meta[2:3], meta[3:4])
        contrib = [contrib[k] + part_got[k : k + 1, :] for k in range(TOP)]
        mean_contrib = gates[0] * contrib[0] + gates[1] * contrib[1]
        for k in range(TOP):
            logit_grad_ref[k : k + 1, :] = gates[k] * (contrib[k] - mean_contrib)

    gate_sum, up_sum, down_sum = shared_sums
    first, second, third, out_sum = sums

    def take(*items):
        for one in items:
            if one.step < len(one.order) or one.trail:
                one.advance()

    lax.fori_loop(0, 2, head_pair, 0)
    take(gate_sum, up_sum, down_sum)
    core_finish(3)
    out_sum.start()
    group_grads(0)
    lax.fori_loop(2, 4, head_pair, 0)
    core_finish(0)
    first.start()
    take(out_sum, gate_sum, up_sum, down_sum)
    serve_far()
    group_grads(1)
    lax.fori_loop(4, 6, head_pair, 0)
    core_finish(1)
    second.start()
    group_grads(2)

    def context_block(block, carry):
        rows = pl.ds(pl.multiple_of(block * tokens, tokens), tokens)
        total = product_t(key_grad[rows, :], wk_ref[...]) + product_t(value_grad[rows, :], wv_ref[...])
        context_grad[rows, :] = total.astype(bfloat)
        return carry

    lax.fori_loop(0, 4, context_block, 0)
    for y_of in range(2):
        send(
            shard_rows(context_grad, y_of, 1 - core),
            context_core.at[y_of],
            ctx_send.at[y_of],
            ctx_recv.at[y_of],
            peers["core"],
        )
    core_finish(2)
    third.start()
    for y_of in range(2):
        wait_for(context_core.at[y_of], ctx_recv.at[y_of])
        wait_for(shard_rows(context_grad, y_of, 1 - core), ctx_send.at[y_of])
        add_rows(context_core.at[y_of], shard_rows(context_grad, y_of, core), context_core.at[y_of])
    send(context_core.at[1 - why], context_y, ctx_send.at[2], ctx_recv.at[2], peers["y"])
    normed_grad = product_t(query_grad[...], wq_ref[...])
    take(first, out_sum, gate_sum, up_sum)
    take(down_sum, third, second, first, out_sum)
    wait_for(context_y, ctx_recv.at[2])
    wait_for(context_core.at[1 - why], ctx_send.at[2])
    normed_grad = normed_grad + context_core[pl.ds(why, 1)].reshape(tokens, width).astype(single) + context_y[...].astype(single)
    rows_in = hidden_ref[...].astype(single)
    scale_first = rms_scale(rows_in)
    gain_parts[0, 0:1, :] = jnp.sum(normed_grad * rows_in * scale_first, axis=0, keepdims=True)

    def gain_start(step):
        peer = peers[("core", "y", "x", "z1", "z2")[step]]
        send(gain_parts.at[step], gain_recv.at[step], gain_send.at[step], gain_got.at[step], peer)

    def gain_finish(step):
        wait_for(gain_recv.at[step], gain_got.at[step])
        gain_parts[step + 1] = gain_parts[step] + gain_recv[step]

    gain_start(0)
    scaled = normed_grad * gain_ref[0:1, :]
    input_grad_ref[...] = (
        mixed_grad_ref[...]
        + scale_first * scaled
        - rows_in * (scale_first * scale_first * scale_first) * jnp.mean(scaled * rows_in, axis=-1, keepdims=True)
    )
    everything = (third, second, first, out_sum, gate_sum, up_sum, down_sum)
    for step in range(5):
        take(*everything)
        if step == 0:
            send_left(2)
        gain_finish(step)
        if step < 4:
            gain_start(step + 1)
        if step == 0:
            combine()
    left = [third, second, first, out_sum, gate_sum, up_sum, down_sum]
    while any(one.trail for one in left):
        take(*[one for one in left if one.trail])
    wait_for(far_put, late_send.at[0])
    wait_for(part_put, late_send.at[1])
    for index in range(3):
        wait_for(expert_y[index], ctx_recv.at[3 + index])
        wait_for(left_mine[index], left_sem.at[index])
        add_rows(expert_out[index], left_mine[index], expert_y[index])
        wait_for(left_over[index].at[1 - why], ctx_send.at[3 + index])
    gain_out[...] = gain_parts[5]
    for step in range(5):
        wait_for(gain_parts.at[step], gain_send.at[step])


def third_part(back, mixed, shared_out, ffn_grad, cotangent, hidden, gains, meta, kept, segment, padding, weights, left_over, shared, far, shared_own):
    tokens, width = hidden.shape
    bfloat, single = jnp.bfloat16, jnp.float32
    in_vmem = pl.BlockSpec(memory_space=pltpu.VMEM)
    dma, shape, vmem = pltpu.SemaphoreType.DMA, jax.ShapeDtypeStruct, pltpu.VMEM
    cosine, sine = rotary_tables(4 * tokens, width // HEADS)
    work = (2, width // 4, width)
    normed, query, keys, values, lse, attended = kept
    wq, wk, wv, wo = weights
    cosine, sine = jnp.asarray(cosine), jnp.asarray(sine)
    stored = (*shared, wo, attended, cosine, sine, query, keys, values, lse, normed, wk, wv, wq)
    arguments = (
        *back,
        mixed,
        shared_out,
        ffn_grad,
        cotangent,
        hidden,
        gains,
        meta,
        segment[None, :],
        padding[None, :],
        *far,
        *stored,
        *left_over,
    )
    in_hbm = pl.BlockSpec(memory_space=pl.ANY)
    return pl.pallas_call(
        third_kernel,
        out_shape=[
            shape((tokens, width), bfloat),
            shape((tokens, width), single),
            shape((TOP, tokens), single),
            shape((8, width), single),
        ]
        + [shape((1,) + work[1:], bfloat)] * 4
        + [shape((1,) + one, bfloat) for one in shared_own]
        + [shape(one.shape[1:], bfloat) for one in left_over],
        in_specs=[in_vmem] * 14 + [in_hbm] * (STORED + 3),
        out_specs=[in_vmem] * 14,
        scratch_shapes=[vmem((tokens, width), bfloat)]
        + [vmem((4 * tokens, width), bfloat)] * 3
        + [vmem((tokens, width), bfloat), vmem((tokens, width), single)]
        + [vmem((width, width), bfloat)] * 4
        + [vmem(work, bfloat)] * 4
        + [vmem((2, tokens, width), bfloat), vmem((tokens, width), bfloat), vmem((tokens, width), bfloat)]
        + [vmem(one.shape[1:], bfloat) for one in left_over]
        + [vmem(one, bfloat) for order in ATTENTION_ORDER for one in receive_shapes(work, order)]
        + [
            vmem(one, bfloat)
            for own, order in zip(shared_own, SHARED_ORDER)
            for one in receive_shapes((2,) + own, order)[SHARED_DONE:]
        ]
        + [vmem(one.shape, one.dtype) for one in stored]
        + [vmem(one.shape[1:], bfloat) for one in left_over]
        + [vmem((6, 8, width), single), vmem((5, 8, width), single)]
        + [dma((4, 2)), dma((4, 2)), dma((4, 7)), dma((4, 7)), dma((3, 7)), dma((3, 7)), dma((6,)), dma((6,)), dma((5,)), dma((5,)), dma((2,)), dma((2,)), dma((STORED,)), dma((3,))]
        + [vmem((tokens, width), bfloat), vmem((8, tokens), single), vmem((8, tokens), single)],
        compiler_params=pltpu.CompilerParams(collective_id=2, has_side_effects=True, vmem_limit_bytes=60 << 20),
        cost_estimate=pl.CostEstimate(flops=12000000000, bytes_accessed=25000000, transcendentals=3000000),
    )(*arguments)


def last_kernel(*refs):
    groups, rest_in, output_in, input_grad_in = refs[:3], refs[3:10], refs[10], refs[11]
    heads_out, rest_out, output_ref, input_grad_ref = refs[12:15], refs[15:22], refs[22], refs[23]
    for kind, target in enumerate(heads_out):
        for index, group in enumerate(groups):
            target[:, 256 * index : 256 * index + 256] = group[0, :, 256 * kind : 256 * kind + 256].astype(jnp.float32)
    for source, target in zip(rest_in, rest_out):
        target[...] = source[...].reshape(target.shape).astype(jnp.float32)
    output_ref[...] = output_in[...].reshape(output_ref.shape)
    input_grad_ref[...] = input_grad_in[...].reshape(input_grad_ref.shape)


def last_part(attention, shared, experts, output, input_grad):
    steps = 4
    inputs = [*attention, *shared, *experts, output, input_grad]

    def spec(shape):
        if len(shape) == 3:
            return pl.BlockSpec((1, shape[1] // steps, shape[2]), lambda step: (0, step, 0))
        return pl.BlockSpec((shape[0] // steps, shape[1]), lambda step: (step, 0))

    shapes = [one.shape[1:] for one in (attention[0], *attention[:3], *shared)]
    shapes = [shapes[0]] * 4 + shapes[4:] + [(1,) + one.shape for one in experts]
    out_shape = [jax.ShapeDtypeStruct(one, jnp.float32) for one in shapes]
    out_shape += [jax.ShapeDtypeStruct((1,) + one.shape, one.dtype) for one in (output, input_grad)]
    return pl.pallas_call(
        last_kernel,
        grid=(steps,),
        out_shape=out_shape,
        in_specs=[spec(one.shape) for one in inputs],
        out_specs=[spec(one.shape) for one in out_shape],
        compiler_params=pltpu.CompilerParams(vmem_limit_bytes=62 << 20),
    )(*inputs)


def swap(value, axis, bit):
    size = lax.axis_size(axis)
    return lax.ppermute(value, axis, [(index, index ^ bit) for index in range(size)])


def halves(value, bit_set, dim):
    half = value.shape[dim] // 2
    keep = lax.dynamic_slice_in_dim(value, bit_set * half, half, dim)
    give = lax.dynamic_slice_in_dim(value, (1 - bit_set) * half, half, dim)
    return keep, give


def fold(value, axis, bit, dim):
    bit_set = (lax.axis_index(axis) // bit) % 2
    keep, give = halves(value, bit_set, dim)
    return (keep.astype(jnp.float32) + swap(give.astype(jnp.bfloat16), axis, bit).astype(jnp.float32)).astype(jnp.bfloat16)


def unfold(value, axis, bit, dim):
    bit_set = (lax.axis_index(axis) // bit) % 2
    come = swap(value, axis, bit)
    return jnp.where(bit_set == 0, jnp.concatenate([value, come], dim), jnp.concatenate([come, value], dim))


def bits_of(axis):
    size = lax.axis_size(axis)
    return [1 << place for place in range(size.bit_length() - 1)]


def scatter_shards(value):
    count = lax.axis_size("shard")
    blocks = value.reshape((count // 2, 2, value.shape[0] // count) + value.shape[1:])
    blocks = fold(blocks, "shard", 1, 1)[:, 0]
    for bit in reversed(bits_of("shard")[1:]):
        blocks = fold(blocks, "shard", bit, 0)
    return blocks[0]


def sum_plane(value, dim):
    bits = bits_of("expert")
    for bit in bits:
        value = fold(value, "expert", bit, dim)
    for bit in reversed(bits):
        value = unfold(value, "expert", bit, dim)
    return value.astype(jnp.float32)


def shards(
    hidden_in,
    gain_attn,
    gain_ffn,
    w_query,
    w_key,
    w_value,
    w_out,
    shared_gate,
    shared_up,
    shared_down,
    expert_gate,
    expert_up,
    expert_down,
    gate_logits,
    routes,
    segment,
    padding,
    cotangent,
):
    bfloat = jnp.bfloat16
    tokens = hidden_in.shape[1]
    model_width = hidden_in.shape[2]
    head_size = model_width // HEADS
    experts = lax.axis_size("expert")
    capacity = max(2, 2 * tokens * TOP // experts)
    shard_count = lax.axis_size("shard")
    shard_index = lax.axis_index("shard")
    score_scale = head_size ** (-0.5)
    head_shape = (tokens, HEADS, head_size)
    fast = (experts, shard_count, WINDOW) == (8, 4, 4 * tokens)
    dense_own = (w_query, w_key, w_value, w_out, shared_gate, shared_up, shared_down)
    expert_own = (expert_gate[0], expert_up[0], expert_down[0])
    rows_in = hidden_in[0].astype(jnp.float32)
    scale_first = rms_scale(rows_in)
    positions = shard_index * tokens + jnp.arange(tokens, dtype=jnp.int32)
    segment_row, padding_row = segment[0], padding[0]
    query_segment = lax.dynamic_slice_in_dim(segment_row, shard_index * tokens, tokens)
    if fast:
        gain_own = lax.dynamic_update_slice(
            jnp.zeros((2, model_width), bfloat),
            jnp.stack([gain_attn, gain_ffn]),
            (0, shard_index * gain_attn.shape[0]),
        )
        meta = [routes[0].T.astype(jnp.float32), gate_logits[0].T, jnp.zeros((8 - 2 * TOP, tokens), jnp.float32)]
        meta = jnp.concatenate(meta, axis=0)
        full, rest = first_part(
            hidden_in[0],
            gain_own,
            dense_own,
            expert_own,
            segment_row,
            padding_row,
            cotangent[0],
            meta,
        )
        normed_ctx, query_low, keys_ctx, values_ctx, log_total, attended, mixed_rows = rest[:7]
        cot_far, meta_far, gains, received, grad_received, shared_out, ffn_grad_shared, *shared_work = rest[7:]
        normed_ffn = None
        gain_first, gain_second = gains[0], gains[1]
        w_q, w_k, w_v, w_o = (full[name] for name in ("wq", "wk", "wv", "wo"))
        e_gate, e_up = (full[name] for name in LATE)
        reach, key_start = shard_count - 1, 0
        key_segment, key_padding = segment_row, padding_row
        key_positions = jnp.arange(4 * tokens, dtype=jnp.int32)
        allowed = allowed_mask(shard_index * tokens, 0, query_segment[:, None], key_segment[None], key_padding[None])
    else:
        gather = functools.partial(lax.all_gather, axis_name="shard", tiled=True)
        w_q, w_k, w_v, w_o, s_gate, s_up, s_down = (gather(weight) for weight in dense_own)
        e_gate, e_up, e_down = (gather(weight) for weight in expert_own)
        gain_first, gain_second = (gather(gain).astype(jnp.float32) for gain in (gain_attn, gain_ffn))
        reach = min((WINDOW + tokens - 2) // tokens, shard_count - 1)
        lead_rows, key_rows = reach * tokens, (reach + 1) * tokens
        context = [from_behind(hidden_in[0], "shard", offset) for offset in range(reach, 0, -1)] + [hidden_in[0]]
        context = jnp.concatenate(context, axis=0).astype(jnp.float32)
        normed_ctx = (context * rms_scale(context) * gain_first).astype(bfloat)
        key_positions = (shard_index - reach) * tokens + jnp.arange(key_rows, dtype=jnp.int32)
        query_low = rotate(
            dense_product(normed_ctx[lead_rows:], w_q).reshape(head_shape), positions, 1.0
        ).astype(bfloat)
        keys_ctx = rotate(
            dense_product(normed_ctx, w_k).reshape(key_rows, HEADS, head_size), key_positions, 1.0
        ).astype(bfloat)
        values_ctx = dense_product(normed_ctx, w_v).astype(bfloat)
        segment_ext = jnp.concatenate([jnp.full((lead_rows,), -1, jnp.int32), segment_row])
        padding_ext = jnp.concatenate([jnp.zeros((lead_rows,), jnp.int32), padding_row])
        key_segment = lax.dynamic_slice_in_dim(segment_ext, shard_index * tokens, key_rows)
        key_padding = lax.dynamic_slice_in_dim(padding_ext, shard_index * tokens, key_rows)
        allowed = allowed_mask(
            shard_index * tokens,
            (shard_index - reach) * tokens,
            query_segment[:, None],
            key_segment[None],
            key_padding[None],
        )
    key_rows = (reach + 1) * tokens
    query_heads = query_low.reshape(head_shape)
    keys_all = keys_ctx.reshape(key_rows, HEADS, head_size)
    values_all = values_ctx.reshape(key_rows, HEADS, head_size)

    def score_block():
        raw_scores = (
            jnp.einsum("qhd,khd->hqk", query_heads, keys_all, preferred_element_type=jnp.float32)
            * score_scale
        )
        return jnp.where(allowed[None], raw_scores, neg_fill)

    if not fast:
        scores = score_block()
        top_score = jnp.max(scores, axis=-1, keepdims=True)
        exponent = jnp.exp(scores - top_score)
        exp_total = jnp.sum(exponent, axis=-1, keepdims=True)
        log_total = top_score + jnp.log(exp_total)
        attended = (
            jnp.einsum(
                "hqk,khd->qhd",
                (exponent / exp_total).astype(bfloat),
                values_all,
                preferred_element_type=jnp.float32,
            )
            .astype(bfloat)
            .reshape(tokens, model_width)
        )
        mixed_rows = rows_in + dense_product(attended, w_o)
        normed_ffn = (mixed_rows * rms_scale(mixed_rows) * gain_second).astype(bfloat)
    scale_second = rms_scale(mixed_rows)
    grad_low = cotangent[0]
    grad_out = grad_low.astype(jnp.float32)
    gate_probs = jax.nn.softmax(gate_logits[0], axis=-1)
    route_flat = routes[0].reshape(-1)
    route_total = tokens * TOP
    onehot = (route_flat[:, None] == jnp.arange(experts, dtype=jnp.int32)[None, :]).astype(
        jnp.int32
    )
    slot_rank = jnp.sum((jnp.cumsum(onehot, axis=0) - onehot) * onehot, axis=1)
    places = route_flat * capacity + slot_rank
    if not fast:
        shared_pre = dense_product(normed_ffn, s_gate)
        shared_lin = dense_product(normed_ffn, s_up)
        shared_mid = (jax.nn.silu(shared_pre) * shared_lin).astype(bfloat)
        shared_out = dense_product(shared_mid, s_down)
        grad_shared_mid = product_t(grad_low, s_down)
        grad_shared_pre, grad_shared_lin = swiglu_back(grad_shared_mid, shared_pre, shared_lin)
        shared_down_grad = dense_product(shared_mid.T, grad_low)
        shared_gate_grad = dense_product(normed_ffn.T, grad_shared_pre)
        shared_up_grad = dense_product(normed_ffn.T, grad_shared_lin)
        ffn_grad_shared = product_t(grad_shared_pre, s_gate) + product_t(grad_shared_lin, s_up)
        slot_table = (
            jnp.full((experts * capacity,), route_total, dtype=jnp.int32)
            .at[places]
            .set(jnp.arange(route_total, dtype=jnp.int32))
        )
        padded_rows = jnp.concatenate([normed_ffn, jnp.zeros((1, model_width), bfloat)], axis=0)
        send_rows = padded_rows[slot_table // TOP].reshape(experts, capacity, model_width)
        received = lax.all_to_all(send_rows, "expert", split_axis=0, concat_axis=0, tiled=True)
        route_grad = (
            (gate_probs[:, :, None] * grad_out[:, None, :])
            .astype(bfloat)
            .reshape(route_total, model_width)
        )
        route_padded = jnp.concatenate([route_grad, jnp.zeros((1, model_width), bfloat)], axis=0)
        send_grad = route_padded[slot_table].reshape(experts, capacity, model_width)
        grad_received = lax.all_to_all(send_grad, "expert", split_axis=0, concat_axis=0, tiled=True)
    if fast:
        results = second_part(received, grad_received, meta_far, (e_gate, e_up, expert_own[2]), shared_work)
        back, left_over, shared_work = results[:3], results[3:6], results[6:]
        output, input_grad, logit_grad, gain_grads, *sums = third_part(
            back,
            mixed_rows,
            shared_out,
            ffn_grad_shared,
            grad_low,
            hidden_in[0],
            gains,
            meta,
            (normed_ctx, query_low, keys_ctx, values_ctx, log_total, attended),
            segment_row,
            padding_row,
            (w_q, w_k, w_v, w_o),
            left_over,
            shared_work,
            (cot_far, meta_far),
            (shared_gate.shape, shared_up.shape, shared_down.shape),
        )
        *grads, output, input_grad = last_part(sums[:4], sums[4:7], sums[7:], output, input_grad)
        gain_grads = lax.dynamic_slice_in_dim(gain_grads, shard_index * gain_attn.shape[0], gain_attn.shape[0], 1)
        return (output, input_grad, logit_grad.T[None], gain_grads[0], gain_grads[1], *grads)
    else:
        gate_pre = jnp.einsum("sid,df->sif", received, e_gate, preferred_element_type=jnp.float32)
        up_pre = jnp.einsum("sid,df->sif", received, e_up, preferred_element_type=jnp.float32)
        middle = (jax.nn.silu(gate_pre) * up_pre).astype(bfloat)
        result = jnp.einsum("sif,fd->sid", middle, e_down, preferred_element_type=jnp.float32).astype(bfloat)
        returned = lax.all_to_all(result, "expert", split_axis=0, concat_axis=0, tiled=True)
        grad_middle = jnp.einsum(
            "sid,fd->sif", grad_received, e_down, preferred_element_type=jnp.float32
        )
        grad_gate_pre, grad_up_pre = swiglu_back(grad_middle, gate_pre, up_pre)
        expert_down_grad = jnp.einsum(
            "sif,sid->fd", middle, grad_received, preferred_element_type=jnp.float32
        )
        expert_gate_grad = jnp.einsum(
            "sid,sif->df", received, grad_gate_pre, preferred_element_type=jnp.float32
        )
        expert_up_grad = jnp.einsum(
            "sid,sif->df", received, grad_up_pre, preferred_element_type=jnp.float32
        )
        grad_rows = (
            jnp.einsum("sif,df->sid", grad_gate_pre, e_gate, preferred_element_type=jnp.float32)
            + jnp.einsum("sif,df->sid", grad_up_pre, e_up, preferred_element_type=jnp.float32)
        ).astype(bfloat)
        grad_back = lax.all_to_all(grad_rows, "expert", split_axis=0, concat_axis=0, tiled=True)
        expert_grads = tuple(
            scatter_shards(grad.astype(bfloat))[None].astype(jnp.float32)
            for grad in (expert_gate_grad, expert_up_grad, expert_down_grad)
        )
        shared_grads = (
            sum_plane(scatter_shards(shared_gate_grad.astype(bfloat)), 1),
            sum_plane(scatter_shards(shared_up_grad.astype(bfloat)), 1),
            sum_plane(scatter_shards(shared_down_grad.astype(bfloat)), 0),
        )
    per_route = (
        returned.reshape(experts * capacity, model_width)[places]
        .astype(jnp.float32)
        .reshape(tokens, TOP, model_width)
    )
    routed = jnp.sum(gate_probs[:, :, None] * per_route, axis=1)
    output = (mixed_rows + shared_out + routed).astype(bfloat)
    contrib = jnp.sum(per_route * grad_out[:, None, :], axis=-1)
    logit_grad = gate_probs * (contrib - jnp.sum(gate_probs * contrib, axis=-1, keepdims=True))
    grad_routes = (
        grad_back.reshape(experts * capacity, model_width)[places]
        .astype(jnp.float32)
        .reshape(tokens, TOP, model_width)
    )
    grad_normed_ffn = jnp.sum(grad_routes, axis=1) + ffn_grad_shared
    gain_ffn_grad = jnp.sum(grad_normed_ffn * mixed_rows * scale_second, axis=0)
    scaled_second = grad_normed_ffn * gain_second
    grad_mixed = (
        grad_out
        + scale_second * scaled_second
        - mixed_rows
        * scale_second**3
        * jnp.mean(scaled_second * mixed_rows, axis=-1, keepdims=True)
    )
    grad_mixed_low = grad_mixed.astype(bfloat)
    w_out_grad = dense_product(attended.T, grad_mixed_low)
    grad_attended = product_t(grad_mixed_low, w_o).astype(bfloat).reshape(head_shape)
    attn_probs = jnp.exp(score_block() - log_total)
    grad_probs = jnp.einsum(
        "qhd,khd->hqk", grad_attended, values_all, preferred_element_type=jnp.float32
    )
    delta_rows = jnp.sum(attn_probs * grad_probs, axis=-1, keepdims=True)
    grad_scores = (attn_probs * (grad_probs - delta_rows)).astype(bfloat)
    grad_query = (
        jnp.einsum("hqk,khd->qhd", grad_scores, keys_all, preferred_element_type=jnp.float32)
        * score_scale
    )
    grad_keys = (
        jnp.einsum("hqk,qhd->khd", grad_scores, query_heads, preferred_element_type=jnp.float32)
        * score_scale
    )
    grad_values = jnp.einsum(
        "hqk,qhd->khd", attn_probs.astype(bfloat), grad_attended, preferred_element_type=jnp.float32
    )
    grad_query_low = rotate(grad_query, positions, -1.0).astype(bfloat).reshape(tokens, model_width)
    grad_key_low = rotate(grad_keys, key_positions, -1.0).astype(bfloat).reshape(key_rows, model_width)
    grad_value_low = grad_values.astype(bfloat).reshape(key_rows, model_width)
    if fast:
        normed = lax.dynamic_slice_in_dim(normed_ctx, shard_index * tokens, tokens)
    else:
        normed = normed_ctx[reach * tokens :]
    w_query_grad = dense_product(normed.T, grad_query_low)
    w_key_grad = dense_product(normed_ctx.T, grad_key_low)
    w_value_grad = dense_product(normed_ctx.T, grad_value_low)
    grad_context = product_t(grad_key_low, w_k) + product_t(grad_value_low, w_v)
    grad_normed = product_t(grad_query_low, w_q)
    if fast:
        grad_normed = grad_normed + scatter_shards(grad_context.astype(bfloat)).astype(jnp.float32)
    else:
        grad_normed = grad_normed + grad_context[reach * tokens :]
        for offset in range(1, reach + 1):
            sent = grad_context[(reach - offset) * tokens :][:tokens].astype(bfloat)
            grad_normed = grad_normed + from_behind(sent, "shard", -offset).astype(jnp.float32)
    gain_attn_grad = jnp.sum(grad_normed * rows_in * scale_first, axis=0)
    scaled_first = grad_normed * gain_first
    input_grad = (
        grad_mixed
        + scale_first * scaled_first
        - rows_in * scale_first**3 * jnp.mean(scaled_first * rows_in, axis=-1, keepdims=True)
    )
    gain_rows = jnp.stack([gain_attn_grad, gain_ffn_grad], axis=1).astype(bfloat)
    gain_total = lax.psum(scatter_shards(gain_rows), "expert").astype(jnp.float32)
    attn_grads = jnp.stack([w_query_grad, w_key_grad, w_value_grad, w_out_grad]).astype(bfloat)
    attn_rows = scatter_shards(attn_grads.transpose(1, 0, 2)).transpose(1, 0, 2)
    attn_total = sum_plane(attn_rows.reshape(-1, model_width), 0).reshape(attn_rows.shape)
    return (
        output[None],
        input_grad[None],
        logit_grad[None],
        gain_total[:, 0],
        gain_total[:, 1],
        attn_total[0],
        attn_total[1],
        attn_total[2],
        attn_total[3],
        shared_grads[0],
        shared_grads[1],
        shared_grads[2],
        expert_grads[0],
        expert_grads[1],
        expert_grads[2],
    )


def solution(mesh):
    placed = (
        P("expert", "shard", None),
        P("shard"),
        P("shard"),
        P("shard", None),
        P("shard", None),
        P("shard", None),
        P("shard", None),
        P("shard", None),
        P("shard", None),
        P("shard", None),
        P("expert", "shard", None),
        P("expert", "shard", None),
        P("expert", "shard", None),
        P("expert", "shard", None),
        P("expert", "shard", None),
        P("expert", None),
        P("expert", None),
        P("expert", "shard", None),
    )
    return jax.shard_map(
        shards,
        mesh=mesh,
        in_specs=placed,
        out_specs=(
            P("expert", "shard", None),
            P("expert", "shard", None),
            P("expert", "shard", None),
            P("shard"),
            P("shard"),
            P("shard", None),
            P("shard", None),
            P("shard", None),
            P("shard", None),
            P("shard", None),
            P("shard", None),
            P("shard", None),
            P("expert", "shard", None),
            P("expert", "shard", None),
            P("expert", "shard", None),
        ),
        check_vma=False,
    )
```

```python
import functools
import math

import jax
import jax.numpy as jnp
import numpy as np
from jax import lax
from jax.experimental import pallas as pl
from jax.experimental.pallas import tpu as pltpu
from jax.sharding import PartitionSpec as P

HEADS = 12
TOP = 2
WINDOW = 1024
MESH = pl.DeviceIdType.MESH
norm_eps = 1e-06
neg_fill = -1e30
rope_base = 10000.0

DIRECT = ("hid", "gains")
EARLY = ("wk", "wv", "wq", "wo")
SHARED = ("sg", "su", "sd")
SWAP_Z = ("su",)
LATE = ("eg", "eu")
NAMES = DIRECT + EARLY + SHARED + LATE
PASSING = DIRECT + EARLY + SHARED
SAVED = 13


def dense_product(left, right):
    return jnp.dot(left, right, preferred_element_type=jnp.float32)


def product_t(left, right):
    return lax.dot_general(left, right, (((1,), (1,)), ((), ())), preferred_element_type=jnp.float32)


def t_product(left, right):
    return lax.dot_general(left, right, (((0,), (0,)), ((), ())), preferred_element_type=jnp.float32)


def rms_scale(values):
    return lax.rsqrt(jnp.mean(values * values, axis=-1, keepdims=True) + norm_eps)


def rotary_tables(length, head_size):
    half = head_size // 2
    frequency = np.float32(rope_base) ** (-np.arange(half, dtype=np.float32) / np.float32(half))
    angles = np.arange(length, dtype=np.float32)[:, None] * frequency[None, :]
    cosine, sine = np.cos(angles).astype(np.float32), np.sin(angles).astype(np.float32)
    return np.concatenate([cosine] * 4, axis=1), np.concatenate([-sine, sine] * 2, axis=1)


def rotate_pair(values, cosine, sine):
    lane = lax.broadcasted_iota(jnp.int32, values.shape, 1)
    partner = jnp.where(lane % 64 < 32, pltpu.roll(values, 96, 1), pltpu.roll(values, 32, 1))
    return values * cosine + partner * sine


def rotate(values, positions, direction):
    half_size = values.shape[-1] // 2
    frequency = rope_base ** (-jnp.arange(half_size, dtype=jnp.float32) / half_size)
    angles = positions.astype(jnp.float32)[:, None] * frequency[None, :]
    cosine = jnp.cos(angles)[:, None, :]
    sine_part = direction * jnp.sin(angles)[:, None, :]
    first_half = values[..., :half_size]
    second_half = values[..., half_size:]
    return jnp.concatenate(
        [
            first_half * cosine - second_half * sine_part,
            second_half * cosine + first_half * sine_part,
        ],
        axis=-1,
    )


def swiglu_back(grad_middle, gate_pre, up_pre):
    sigmoid_gate = jax.nn.sigmoid(gate_pre)
    activated = gate_pre * sigmoid_gate
    grad_gate = grad_middle * up_pre * sigmoid_gate * (1.0 + gate_pre * (1.0 - sigmoid_gate))
    grad_up = grad_middle * activated
    return (grad_gate.astype(jnp.bfloat16), grad_up.astype(jnp.bfloat16))


def from_behind(value, axis, steps):
    count = lax.axis_size(axis)
    first, last = (max(0, -steps), min(count, count - steps))
    return lax.ppermute(value, axis, [(source, source + steps) for source in range(first, last)])


def send(source, target, send_sem, recv_sem, peer):
    pltpu.make_async_remote_copy(
        src_ref=source,
        dst_ref=target,
        send_sem=send_sem,
        recv_sem=recv_sem,
        device_id=peer,
        device_id_type=MESH,
    ).start()


def wait_for(ref, sem):
    pltpu.make_async_copy(ref, ref, sem).wait()


def first_kernel(*refs):
    count = len(NAMES)
    own = dict(zip(NAMES, refs[:count]))
    segment_row, padding_row, cosine_ref, sine_ref, cot_ref, meta_ref = refs[count : count + 6]
    refs = refs[count + 6 :]
    full = dict(zip(LATE, refs[: len(LATE)]))
    refs = refs[len(LATE) :]
    saved, refs = refs[:SAVED], refs[SAVED:]
    gain_ref, rows_got, grads_got, shared_ref, ffn_grad_ref, *shared_work = refs[:8]
    refs = refs[8:]
    full.update(zip(PASSING, refs[: len(PASSING)]))
    refs = refs[len(PASSING) :]
    normed_ref, query_ref, key_ref, value_ref, lse_ref, attended_ref, mixed_ref, ffn_ref = refs[:8]
    refs = refs[8:]
    shared_core = refs[:3]
    refs = refs[3:]
    rows_put, grads_put = refs[:2]
    (own_sem, y_send, y_recv, swap_send, swap_recv, core_send, core_recv) = refs[2:9]
    row_sems, grad_sems, share_send, share_recv, save_sem = refs[9:11], refs[11:13], refs[13], refs[14], refs[15]
    far_send, far_recv, slot_ref, meta_far, cot_far, ffn_far = refs[16:]
    number = {name: index for index, name in enumerate(NAMES)}
    expert, shard = (lax.axis_index("expert"), lax.axis_index("shard"))
    zed, ex = (expert // 2, expert % 2)
    other = (shard + 2) % 4
    y_peer = (expert, other)
    core_peer = (expert, shard + 1 - 2 * (shard % 2))
    x_peer = (expert + 1 - 2 * ex, shard)
    z_peer = (expert + 2 - 4 * (zed % 2), shard)

    barrier = pltpu.get_barrier_semaphore()
    for peer in (y_peer, core_peer) + tuple(((expert + step) % 8, shard) for step in range(1, 8)):
        pl.semaphore_signal(barrier, inc=1, device_id=peer, device_id_type=MESH)
    pl.semaphore_wait(barrier, 9)

    def side(name):
        return (zed % 2, z_peer) if name in SWAP_Z else (ex, x_peer)

    def part_of(block, base, name, half):
        rows = own[name].shape[0]
        if half is None:
            return block.at[pl.ds(base, rows)]
        return block.at[pl.ds(base + half * (rows // 2), rows // 2)]

    def place(name, slot, half=None):
        return part_of(full[name], slot * own[name].shape[0], name, half)

    def mine(name, half=None):
        return part_of(own[name], 0, name, half)

    def cross(name, half=None):
        n = number[name]
        send(mine(name, half), place(name, shard, half), y_send.at[n], y_recv.at[n], y_peer)

    def to_core(name, step, half=None):
        n = number[name]
        part = place(name, other, half)
        send(part, part, core_send.at[n, 1 + step], core_recv.at[n, 1 + step], core_peer)

    far = shard + 1 - 2 * (shard % 2)
    far_other = (far + 2) % 4

    def settle_own(names):
        for name in names:
            n = number[name]
            pltpu.make_async_copy(own[name], place(name, shard), own_sem.at[n]).wait()
            wait_for(place(name, far), core_recv.at[n, 0])
            wait_for(own[name], core_send.at[n, 0])

    def settle_core(name, step, half=None):
        n = number[name]
        wait_for(place(name, far_other, half), core_recv.at[n, 1 + step])
        wait_for(place(name, other, half), core_send.at[n, 1 + step])

    def own_to_core(names):
        for name in names:
            n = number[name]
            send(own[name], place(name, shard), core_send.at[n, 0], core_recv.at[n, 0], core_peer)
            pltpu.make_async_copy(own[name], place(name, shard), own_sem.at[n]).start()

    for name in DIRECT:
        cross(name)
    for name in EARLY + SHARED:
        cross(name, side(name)[0])
    for name in LATE:
        cross(name)
    own_to_core(DIRECT + EARLY)

    tokens, width = own["hid"].shape
    capacity = rows_put.shape[1]
    far_expert, half_start, in_half = (expert + 4) % 8, 4 * (expert // 4), expert % 4
    far_peer = (far_expert, shard)

    def to_far(index, ref, target):
        send(ref, target, far_send.at[index], far_recv.at[index], far_peer)

    def settle_far(index, ref):
        wait_for(ref, far_send.at[index])
        wait_for(ref, far_recv.at[index])

    to_far(0, meta_ref, meta_far)
    to_far(1, cot_ref, cot_far)

    def fill_slots(block, meta):
        expert_at = lax.broadcasted_iota(jnp.int32, (8, tokens), 0).astype(jnp.float32)
        named = ((meta[0:1] == expert_at) | (meta[1:2] == expert_at)).astype(jnp.float32)
        row_at = lax.broadcasted_iota(jnp.int32, (tokens, tokens), 0)
        before = row_at < lax.broadcasted_iota(jnp.int32, (tokens, tokens), 1)
        rank = dense_product(named.astype(jnp.bfloat16), before.astype(jnp.bfloat16))
        slot_ref[block] = jnp.where(named > 0.0, rank, -1.0)

    def picks(block, target):
        slot_at = lax.broadcasted_iota(jnp.int32, (capacity, tokens), 0)
        return slot_at == slot_ref[block, pl.ds(target, 1), :].astype(jnp.int32)

    def put_grads(block, meta, cot):
        gates = [as_column(gate) for gate in gate_pair(meta[2:3], meta[3:4])]
        route_grads = [(gate * cot.astype(jnp.float32)).astype(jnp.bfloat16) for gate in gates]
        for index in range(4):
            target = half_start + index
            chosen = picks(block, target)
            grads_put[4 * block + index] = sum(
                dense_product(
                    (chosen & (meta[k : k + 1].astype(jnp.int32) == target)).astype(jnp.bfloat16), route_grads[k]
                )
                for k in range(TOP)
            ).astype(jnp.bfloat16)

    def put_rows(block, ffn):
        for index in range(4):
            chosen = picks(block, half_start + index).astype(jnp.bfloat16)
            rows_put[4 * block + index] = dense_product(chosen, ffn).astype(jnp.bfloat16)

    def dispatch(block, put, got, sems):
        source = far_expert if block else expert
        for step in range(1, 4):
            index = (in_half + step) % 4
            at = 4 * block + step
            send(put.at[4 * block + index], got.at[source], sems[0].at[at], sems[1].at[at], (half_start + index, shard))
        pltpu.make_async_copy(put.at[4 * block + in_half], got.at[source], sems[0].at[4 * block]).start()

    def settle_dispatch(put, got, sems):
        for block in range(2):
            for step in range(4):
                wait_for(put.at[4 * block + (in_half + step) % 4], sems[0].at[4 * block + step])
            for step in range(1, 4):
                sender = half_start + (in_half + 4 - step) % 4
                wait_for(got.at[(sender + 4 * block) % 8], sems[1].at[4 * block + step])

    fill_slots(0, meta_ref[...])
    put_grads(0, meta_ref[...], cot_ref[...])
    dispatch(0, grads_put, grads_got, grad_sems)
    for name in DIRECT:
        wait_for(place(name, other), y_recv.at[number[name]])
        to_core(name, 0)

    def early_out(name):
        n, (half, peer) = number[name], side(name)
        part = place(name, other, half)
        wait_for(part, y_recv.at[n])
        send(part, part, swap_send.at[n], swap_recv.at[n], peer)
        to_core(name, 0, half)

    def pass_early(name):
        half, _ = side(name)
        wait_for(place(name, other, 1 - half), swap_recv.at[number[name]])
        to_core(name, 1, 1 - half)

    def settle_early_far(name):
        half, _ = side(name)
        settle_core(name, 0, half)
        settle_core(name, 1, 1 - half)
        wait_for(mine(name, half), y_send.at[number[name]])
        wait_for(place(name, other, half), swap_send.at[number[name]])

    def settle_early(names):
        settle_own(names)
        for name in names:
            settle_early_far(name)

    for name in ("wk", "wv", "wq"):
        early_out(name)
    own_to_core(SHARED + LATE)

    settle_own(DIRECT)
    for name in DIRECT:
        settle_core(name, 0)
    gain_rows = sum(full["gains"][pl.ds(slot * 16, 16), :].astype(jnp.float32) for slot in range(4))
    gain_ref[...] = gain_rows
    gain_first, gain_second = gain_rows[0:1], gain_rows[1:2]

    def norm_block(block, carry):
        rows = pl.ds(pl.multiple_of(block * tokens, tokens), tokens)
        values = full["hid"][rows, :].astype(jnp.float32)
        normed_ref[rows, :] = (values * rms_scale(values) * gain_first).astype(jnp.bfloat16)
        return carry

    lax.fori_loop(0, 4, norm_block, 0)

    pass_early("wk")
    pass_early("wv")
    settle_early(("wk",))

    def key_block(block, carry):
        rows = pl.ds(pl.multiple_of(block * tokens, tokens), tokens)
        raw = dense_product(normed_ref[rows, :], full["wk"][...])
        cosine, sine = cosine_ref[rows, :], sine_ref[rows, :]
        for start in range(0, width, 128):
            key_ref[rows, start : start + 128] = rotate_pair(raw[:, start : start + 128], cosine, sine).astype(jnp.bfloat16)
        return carry

    def value_block(block, carry):
        rows = pl.ds(pl.multiple_of(block * tokens, tokens), tokens)
        value_ref[rows, :] = dense_product(normed_ref[rows, :], full["wv"][...]).astype(jnp.bfloat16)
        return carry

    lax.fori_loop(0, 4, key_block, 0)
    pass_early("wq")
    settle_early(("wv",))
    lax.fori_loop(0, 4, value_block, 0)
    settle_early(("wq",))
    here = pl.ds(pl.multiple_of(shard * tokens, tokens), tokens)
    raw = dense_product(normed_ref[here, :], full["wq"][...])
    cosine, sine = cosine_ref[here, :], sine_ref[here, :]
    for start in range(0, width, 128):
        query_ref[:, start : start + 128] = rotate_pair(raw[:, start : start + 128], cosine, sine).astype(jnp.bfloat16)
    early_out("wo")

    own_segment = as_column(segment_row[:, here].astype(jnp.float32)).astype(jnp.int32)

    def head_pair(pair, carry):
        lanes = pl.ds(pl.multiple_of(pair * 128, 128), 128)
        query, keys, values = query_ref[:, lanes], key_ref[:, lanes], value_ref[:, lanes]
        allowed = allowed_mask(shard * tokens, 0, own_segment, segment_row[...], padding_row[...])
        lane = lax.broadcasted_iota(jnp.int32, query.shape, 1)
        results = []
        for half in range(2):
            chosen = (lane >= 64) if half else (lane < 64)
            scores = product_t(jnp.where(chosen, query, jnp.zeros_like(query)), keys) * 0.125
            scores = jnp.where(allowed, scores, neg_fill)
            top_score = jnp.max(scores, axis=-1, keepdims=True)
            exponent = jnp.exp(scores - top_score)
            exp_total = jnp.sum(exponent, axis=-1, keepdims=True)
            lse_ref[2 * pair + half] = top_score + jnp.log(exp_total)
            results.append(dense_product((exponent / exp_total).astype(jnp.bfloat16), values))
        attended_ref[:, lanes] = jnp.where(lane < 64, results[0], results[1]).astype(jnp.bfloat16)
        return carry

    lax.fori_loop(0, 2, head_pair, 0)
    early_out("sg")
    pass_early("wo")
    lax.fori_loop(2, 5, head_pair, 0)
    early_out("su")
    pass_early("sg")
    lax.fori_loop(5, 6, head_pair, 0)
    settle_far(0, meta_far)
    settle_far(1, cot_far)
    fill_slots(1, meta_far[...])
    put_grads(1, meta_far[...], cot_far[...])
    settle_early(("wo",))
    rows_in = own["hid"][...].astype(jnp.float32)
    mixed = rows_in + dense_product(attended_ref[...], full["wo"][...])
    mixed_ref[...] = mixed
    ffn = (mixed * rms_scale(mixed) * gain_second).astype(jnp.bfloat16)
    ffn_ref[...] = ffn
    to_far(2, ffn_ref, ffn_far)
    put_rows(0, ffn)
    dispatch(0, rows_put, rows_got, row_sems)
    dispatch(1, grads_put, grads_got, grad_sems)
    keep = [full[name] for name in EARLY]
    keep += [normed_ref, query_ref, key_ref, value_ref, lse_ref, attended_ref, mixed_ref, cot_far, meta_far]
    for index, ref in enumerate(keep):
        pltpu.make_async_copy(ref, saved[index], save_sem.at[index]).start()
    early_out("sd")
    pass_early("su")
    settle_early(("sg", "su"))
    settle_own(("sd",))
    shared_ref[...] = jnp.zeros_like(shared_ref)
    ffn_grad_ref[...] = jnp.zeros_like(ffn_grad_ref)

    why = shard // 2

    def shared_block(block, carry):
        cut = pl.ds(pl.multiple_of((block + 2 * why) % 4 * 512, 512), 512)
        normed = ffn_ref[...]
        gate, up, down = full["sg"][:, cut], full["su"][:, cut], full["sd"][cut, :]
        pre, lin = dense_product(normed, gate), dense_product(normed, up)
        middle = (jax.nn.silu(pre) * lin).astype(jnp.bfloat16)
        shared_ref[...] += dense_product(middle, down)
        pre_grad, lin_grad = swiglu_back(product_t(cot_ref[...], down), pre, lin)
        ffn_grad_ref[...] += product_t(pre_grad, gate) + product_t(lin_grad, up)
        full["sg"][:, cut] = t_product(normed, pre_grad).astype(jnp.bfloat16)
        full["su"][:, cut] = t_product(normed, lin_grad).astype(jnp.bfloat16)
        full["sd"][cut, :] = t_product(middle, cot_ref[...]).astype(jnp.bfloat16)
        return carry

    core = shard % 2
    shared_grads = (full["sg"], full["su"], full["sd"])

    def halved(index, turn):
        ref, rows, columns = shared_grads[index], shared_grads[index].shape[0] // 4, shared_grads[index].shape[1]
        part = why if turn == 0 else 1 - why
        picked = (pl.ds(0, rows),)
        if index < 2:
            picked += (pl.ds(pl.multiple_of(part * (columns // 2), 128), columns // 2),)
        for y_of in (part,) if index == 2 else (0, 1):
            far_rows, near_rows = [pl.ds((y_of * 2 + of) * rows, rows) for of in (1 - core, core)]
            at = (y_of,) + picked
            place_of = 2 * turn if index == 2 else 2 * turn + y_of
            yield (
                ref.at[(far_rows,) + picked[1:]],
                shared_core[index].at[at],
                ref.at[(near_rows,) + picked[1:]],
                shared_work[index].at[at],
                place_of,
            )

    def share(part):
        for index in range(3):
            for away, landing, _, _, at in halved(index, part):
                send(away, landing, share_send.at[index, at], share_recv.at[index, at], core_peer)

    def take_share(part):
        for index in range(3):
            for away, landing, near, target, at in halved(index, part):
                wait_for(landing, share_recv.at[index, at])
                add_rows(target, near, landing)
                wait_for(away, share_send.at[index, at])

    cuts = full["sg"].shape[1] // 512
    lax.fori_loop(0, cuts // 2, shared_block, 0)
    share(0)
    pass_early("sd")
    settle_early_far("sd")
    lax.fori_loop(cuts // 2, cuts, shared_block, 0)
    share(1)
    settle_far(2, ffn_far)
    put_rows(1, ffn_far[...])
    dispatch(1, rows_put, rows_got, row_sems)
    take_share(0)

    for name in LATE:
        wait_for(place(name, other), y_recv.at[number[name]])
        to_core(name, 0)

    for name in DIRECT:
        wait_for(own[name], y_send.at[number[name]])
    settle_own(LATE)
    for name in LATE:
        wait_for(own[name], y_send.at[number[name]])
        settle_core(name, 0)
    take_share(1)
    settle_dispatch(grads_put, grads_got, grad_sems)
    settle_dispatch(rows_put, rows_got, row_sems)
    for index, ref in enumerate(keep):
        wait_for(ref, save_sem.at[index])


def as_column(row):
    shape = (row.shape[1], row.shape[1])
    same = lax.broadcasted_iota(jnp.int32, shape, 0) == lax.broadcasted_iota(jnp.int32, shape, 1)
    return jnp.sum(jnp.where(same, row, 0.0), axis=1, keepdims=True)


def as_row(column):
    shape = (column.shape[0], column.shape[0])
    same = lax.broadcasted_iota(jnp.int32, shape, 0) == lax.broadcasted_iota(jnp.int32, shape, 1)
    return jnp.sum(jnp.where(same, column, 0.0), axis=0, keepdims=True)


def gate_pair(first, second):
    top = jnp.maximum(first, second)
    first, second = jnp.exp(first - top), jnp.exp(second - top)
    total = first + second
    return first / total, second / total


def allowed_mask(query_start, key_start, query_segment, key_segment, key_padding):
    shape = (query_segment.shape[0], key_segment.shape[1])
    query_at = query_start + lax.broadcasted_iota(jnp.int32, shape, 0)
    key_at = key_start + lax.broadcasted_iota(jnp.int32, shape, 1)
    distance = query_at - key_at
    return (
        (query_segment == key_segment)
        & (distance >= 0)
        & (distance < WINDOW)
        & ((key_padding == 1) | (distance == 0))
    )


def first_part(hidden, gains, dense, experts, segment, padding, cotangent, meta):
    tokens, width = hidden.shape
    bfloat, single = jnp.bfloat16, jnp.float32
    wq, wk, wv, wo, sg, su, sd = dense
    blocks = dict(hid=hidden, gains=jnp.pad(gains, ((0, 14), (0, 0))), wq=wq, wk=wk, wv=wv, wo=wo, sg=sg, su=su, sd=sd)
    blocks.update(zip(LATE, experts[:2]))
    blocks = [blocks[name] for name in NAMES]
    count = len(NAMES)
    cosine, sine = rotary_tables(4 * tokens, width // HEADS)
    in_hbm, in_vmem = pl.BlockSpec(memory_space=pl.ANY), pl.BlockSpec(memory_space=pltpu.VMEM)
    dma = pltpu.SemaphoreType.DMA
    shape = jax.ShapeDtypeStruct
    whole = {name: shape((4 * block.shape[0], block.shape[1]), block.dtype) for name, block in zip(NAMES, blocks)}
    middle = sg.shape[1]
    capacity = max(2, 2 * tokens * TOP // 8)
    routed = (8, capacity, width)
    halved = [(2,) + block.shape for block in (sg, su, sd)]
    inner = [
        shape((4 * tokens, width), bfloat),
        shape((tokens, width), bfloat),
        shape((4 * tokens, width), bfloat),
        shape((4 * tokens, width), bfloat),
        shape((HEADS, tokens, 1), single),
        shape((tokens, width), bfloat),
        shape((tokens, width), single),
        shape((tokens, width), bfloat),
    ]
    out = pl.pallas_call(
        first_kernel,
        out_shape=[whole[name] for name in LATE]
        + [whole[name] for name in EARLY]
        + inner[:7]
        + [
            shape((tokens, width), bfloat),
            shape((8, tokens), single),
            shape((16, width), single),
            shape(routed, bfloat),
            shape(routed, bfloat),
            shape((tokens, width), single),
            shape((tokens, width), single),
        ]
        + [shape(one, bfloat) for one in halved],
        in_specs=[in_vmem] * (count + 6),
        out_specs=[in_hbm] * (len(LATE) + SAVED) + [in_vmem] + [in_hbm] * 2 + [in_vmem] * 5,
        scratch_shapes=[pltpu.VMEM(whole[name].shape, whole[name].dtype) for name in PASSING]
        + [pltpu.VMEM(one.shape, one.dtype) for one in inner]
        + [pltpu.VMEM(one, bfloat) for one in halved]
        + [pltpu.VMEM(routed, bfloat)] * 2
        + [
            dma((count,)),
            dma((count,)),
            dma((count,)),
            dma((count,)),
            dma((count,)),
            dma((count, 3)),
            dma((count, 3)),
        ]
        + [dma((8,))] * 4
        + [dma((3, 4))] * 2
        + [
            dma((SAVED,)),
            dma((3,)),
            dma((3,)),
            pltpu.VMEM((2, 8, tokens), single),
            pltpu.VMEM((8, tokens), single),
            pltpu.VMEM((tokens, width), bfloat),
            pltpu.VMEM((tokens, width), bfloat),
        ],
        compiler_params=pltpu.CompilerParams(collective_id=0, has_side_effects=True, vmem_limit_bytes=60 << 20),
        cost_estimate=pl.CostEstimate(flops=15000000000, bytes_accessed=47000000, transcendentals=3000000),
    )(
        *blocks,
        segment[None, :],
        padding[None, :],
        jnp.asarray(cosine),
        jnp.asarray(sine),
        cotangent,
        meta,
    )
    return dict(zip(LATE + EARLY, out)), out[len(LATE + EARLY) :]


def add_into(target, first, second):
    rows = first.shape[-2]
    strip = math.gcd(rows, 64)

    def body(index, carry):
        at = pl.ds(pl.multiple_of(index * strip, strip), strip)
        for lead in range(first.shape[0]):
            total = first[lead, at, :].astype(jnp.float32) + second[lead, at, :].astype(jnp.float32)
            target[lead, at, :] = total.astype(target.dtype)
        return carry

    lax.fori_loop(0, rows // strip, body, 0)


class PlaneSum:
    def __init__(self, shape, work, receive, send_sem, recv_sem, bits, peers, order, out=None, done=0):
        self.work, self.receive, self.out = work, receive, out
        self.send_sem, self.recv_sem, self.bits, self.peers, self.order = send_sem, recv_sem, bits, peers, order
        self.at = [(0, size) for size in shape]
        self.inside = [0, 0, 0]
        self.trail = []
        for step in range(done):
            self.narrow(step)
        self.inside = [0, 0, 0]
        self.step = done

    def region(self, ref, starts, sizes):
        starts = [
            start if isinstance(start, int) or unit == 1 else pl.multiple_of(start, unit)
            for start, unit in zip(starts, (1, 16, 128))
        ]
        return ref.at[tuple(pl.ds(start, size) for start, size in zip(starts, sizes))]

    def working(self, bit_of):
        axis, dim = self.order[self.step]
        starts, sizes = list(self.inside), [size for _, size in self.at]
        sizes[dim] //= 2
        starts[dim] = starts[dim] + bit_of(self.bits[axis]) * sizes[dim]
        return self.region(self.work, starts, sizes)

    def final(self, at):
        return self.region(self.out, [0] + [start for start, _ in at[1:]], [1] + [size for _, size in at[1:]])

    def narrow(self, step):
        axis, dim = self.order[step]
        if axis != "y":
            self.trail.append((step, self.at))
        (start, size), self.at = self.at[dim], list(self.at)
        self.at[dim] = (start + self.bits[axis] * (size // 2), size // 2)
        self.inside[dim] = self.inside[dim] + self.bits[axis] * (size // 2)

    def start(self):
        step = self.step
        peer = self.peers[self.order[step][0]]
        send(self.working(lambda bit: 1 - bit), self.receive[step], self.send_sem.at[step], self.recv_sem.at[step], peer)

    def finish(self, target=None):
        step = self.step
        wait_for(self.receive[step], self.recv_sem.at[step])
        kept, gone = self.working(lambda bit: bit), self.working(lambda bit: 1 - bit)
        self.narrow(step)
        if step == len(self.order) - 1:
            target = self.final(self.at)
        add_into(kept if target is None else target, kept, self.receive[step])
        wait_for(gone, self.send_sem.at[step])
        self.step = step + 1

    def back_start(self):
        step, _ = self.trail[-1]
        part, at = self.final(self.at), self.step
        send(part, part, self.send_sem.at[at], self.recv_sem.at[at], self.peers[self.order[step][0]])

    def back_finish(self):
        step, whole = self.trail.pop()
        wait_for(self.final(self.at), self.send_sem.at[self.step])
        dim = self.order[step][1]
        start, size = self.at[dim]
        other = list(self.at)
        other[dim] = (2 * whole[dim][0] + size - start, size)
        wait_for(self.final(other), self.recv_sem.at[self.step])
        self.at = list(self.at)
        self.at[dim] = whole[dim]
        self.step += 1

    def advance(self):
        if self.step < len(self.order):
            self.finish()
        else:
            self.back_finish()
        if self.step < len(self.order):
            self.start()
        elif self.trail:
            self.back_start()


def receive_shapes(shape, order):
    result, shape = [], list(shape)
    for _, dim in order:
        shape[dim] //= 2
        result.append(tuple(shape))
    return result


def ordered(axes, dims):
    return tuple((axis, 0 if axis == "y" else dims[axis]) for axis in axes)


BY_COLUMNS, BY_ROWS = dict(x=2, z1=2, z2=2), dict(x=1, z1=1, z2=1)
BY_BOTH = dict(x=2, z1=1, z2=1)
SHARED_ORDER = (
    ordered(("y", "x", "z1", "z2"), BY_COLUMNS),
    ordered(("x", "y", "z1", "z2"), BY_COLUMNS),
    ordered(("z1", "y", "x", "z2"), BY_ROWS),
)
SHARED_DONE = 2
ATTENTION_ORDER = (
    ordered(("z1", "x", "y", "z2"), BY_BOTH),
    ordered(("y", "x", "z1", "z2"), BY_BOTH),
    ordered(("x", "y", "z1", "z2"), BY_BOTH),
    ordered(("x", "z1", "y", "z2"), BY_BOTH),
)


def plane_places():
    expert, shard = (lax.axis_index("expert"), lax.axis_index("shard"))
    zed, ex, why, core = (expert // 2, expert % 2, shard // 2, shard % 2)
    bits = {"x": ex, "z1": zed % 2, "z2": zed // 2, "y": why}
    peers = {
        "x": (expert + 1 - 2 * ex, shard),
        "z1": (expert + 2 - 4 * (zed % 2), shard),
        "z2": ((expert + 4) % 8, shard),
        "y": (expert, (shard + 2) % 4),
        "core": (expert, shard + 1 - 2 * core),
    }
    return expert, shard, zed, core, bits, peers


def enter(peers):
    barrier = pltpu.get_barrier_semaphore()
    for peer in peers:
        pl.semaphore_signal(barrier, inc=1, device_id=peer, device_id_type=MESH)
    pl.semaphore_wait(barrier, len(peers))


def second_kernel(*refs):
    rows_ref, grads_ref, meta_far, *weights_in, down_own = refs[:6]
    shared_in = refs[6:9]
    rows_back, grads_back, grads_far = refs[9:12]
    expert_core, shared_out = refs[12:15], refs[15:18]
    weights, shared_work = refs[18:21], refs[21:24]
    rows_put, grads_put, middle_ref, pre_ref, lin_ref, out_sum, grad_sum, far_put = refs[24:32]
    refs = refs[32:]
    receive = [refs[SHARED_DONE * index : SHARED_DONE * (index + 1)] for index in range(3)]
    refs = refs[3 * SHARED_DONE :]
    load_sem, shared_sem, out_send, out_recv, grad_send, grad_recv, core_send, core_recv, sum_send, sum_recv, far_send, far_recv, down_send, down_recv = refs
    expert, shard, zed, core, bits, peers = plane_places()
    def down_rows(slot):
        rows = down_own.shape[0]
        return weights[2].at[pl.ds(slot * rows, rows)]

    why = bits["y"]
    other, beside = (shard + 2) % 4, shard + 1 - 2 * core
    for index in range(2):
        pltpu.make_async_copy(weights_in[index], weights[index], load_sem.at[index]).start()
    for index in range(3):
        pltpu.make_async_copy(shared_in[index], shared_work[index], shared_sem.at[index]).start()
    pltpu.make_async_copy(down_own, down_rows(shard), load_sem.at[2]).start()
    enter((peers["y"], peers["core"]) + tuple(((expert + step) % 8, shard) for step in range(1, 8)))
    send(down_own, down_rows(shard), down_send.at[0], down_recv.at[0], peers["y"])
    send(down_own, down_rows(shard), down_send.at[1], down_recv.at[1], peers["core"])
    sums = [
        PlaneSum(
            shared_work[index].shape,
            shared_work[index],
            receive[index],
            sum_send.at[index],
            sum_recv.at[index],
            bits,
            peers,
            SHARED_ORDER[index],
        )
        for index in range(3)
    ]
    for index in range(3):
        pltpu.make_async_copy(shared_in[index], shared_work[index], shared_sem.at[index]).wait()
        sums[index].start()
    for index in range(2):
        pltpu.make_async_copy(weights_in[index], weights[index], load_sem.at[index]).wait()

    _, capacity, width = rows_ref.shape
    gate_ref, up_ref, down_ref = weights
    middle = gate_ref.shape[1]
    cuts = middle // 512

    half, in_half = expert // 4, expert % 4
    lot = 4 * capacity

    def hidden_units(index, carry):
        cut = pl.ds(pl.multiple_of(index * 512, 512), 512)
        rows = rows_ref[...].reshape(2 * lot, width)
        pre, lin = dense_product(rows, gate_ref[:, cut]), dense_product(rows, up_ref[:, cut])
        middle_ref[:, cut] = (jax.nn.silu(pre) * lin).astype(jnp.bfloat16)
        pre_ref[:, cut] = pre.astype(jnp.bfloat16)
        lin_ref[:, cut] = lin.astype(jnp.bfloat16)
        return carry

    def block(of_half, between=None):
        lots, here = pl.ds(4 * of_half, 4), pl.ds(pl.multiple_of(of_half * lot, lot), lot)
        grads = grads_ref[lots].reshape(lot, width)
        out_sum[...] = jnp.zeros_like(out_sum)
        grad_sum[...] = jnp.zeros_like(grad_sum)

        def body(index, carry):
            cut = pl.ds(pl.multiple_of((index + 2 * why) % 4 * 512, 512), 512)
            gate, up, down = gate_ref[:, cut], up_ref[:, cut], down_ref[cut, :]
            pre, lin = pre_ref[here, cut].astype(jnp.float32), lin_ref[here, cut].astype(jnp.float32)
            pre_grad, lin_grad = swiglu_back(product_t(grads, down), pre, lin)
            grad_sum[...] += product_t(pre_grad, gate) + product_t(lin_grad, up)
            out_sum[...] += dense_product(middle_ref[here, cut], down)
            pre_ref[here, cut] = pre_grad
            lin_ref[here, cut] = lin_grad
            return carry

        if between is None:
            lax.fori_loop(0, cuts, body, 0)
        else:
            lax.fori_loop(0, cuts // 2, body, 0)
            between()
            lax.fori_loop(cuts // 2, cuts, body, 0)
        rows_put[lots] = out_sum[...].astype(jnp.bfloat16).reshape(4, capacity, width)
        grads_put[lots] = grad_sum[...].astype(jnp.bfloat16).reshape(4, capacity, width)
        give_back(of_half, grads_put, grads_back, grad_send, grad_recv)
        give_back(of_half, rows_put, rows_back, out_send, out_recv)

    def give_back(of_half, put, back, send_sem, recv_sem):
        slot = 4 * ((of_half + half) % 2) + in_half
        for step in range(1, 4):
            there = (in_half + step) % 4
            source = 4 * of_half + there
            send(put.at[source], back.at[slot], send_sem.at[source], recv_sem.at[slot], (4 * half + there, shard))
        back[pl.ds(slot, 1)] = put[pl.ds(4 * of_half + in_half, 1)]

    def settle_back(put, back, send_sem, recv_sem, far):
        for step in range(1, 4):
            there = (in_half + step) % 4
            source = (4 * half + there + 4 * far) % 8
            wait_for(put.at[source], send_sem.at[source])
            wait_for(back.at[4 * far + there], recv_sem.at[4 * far + there])

    lax.fori_loop(0, cuts, hidden_units, 0)
    wait_for(down_rows(shard), load_sem.at[2])
    wait_for(down_rows(beside), down_recv.at[1])

    def rest_of_down():
        wait_for(down_rows(other), down_recv.at[0])
        send(down_rows(other), down_rows(other), down_send.at[2], down_recv.at[2], peers["core"])
        wait_for(down_rows((beside + 2) % 4), down_recv.at[2])

    block(1 - half, rest_of_down)
    for one in sums:
        one.advance()
    block(half)
    settle_back(grads_put, grads_back, grad_send, grad_recv, 1)
    taken = slots_in_half(meta_far[...], half, capacity)
    slot_at = lax.broadcasted_iota(jnp.int32, (taken[0].shape[0], 4 * capacity), 1)
    chosen = ((slot_at == taken[0]) | (slot_at == taken[1])).astype(jnp.bfloat16)
    far_put[...] = dense_product(chosen, grads_back[4:8].reshape(4 * capacity, width)).astype(jnp.bfloat16)
    send(far_put, grads_far, far_send, far_recv, ((expert + 4) % 8, shard))
    for index, ref in enumerate((down_rows(shard), down_rows(shard), down_rows(other))):
        wait_for(ref, down_send.at[index])

    rows_all, grads_all = rows_ref, grads_ref

    def weight_grad(index):
        def body(step, carry):
            cut = pl.ds(pl.multiple_of(step * 512, 512), 512)
            if index == 2:
                left, right = middle_ref[:, cut], grads_all[...].reshape(8 * capacity, width)
                down_ref[cut, :] = t_product(left, right).astype(jnp.bfloat16)
            else:
                left, right = rows_all[...].reshape(8 * capacity, width), (pre_ref, lin_ref)[index][:, cut]
                weights[index][:, cut] = t_product(left, right).astype(jnp.bfloat16)
            return carry

        lax.fori_loop(0, cuts, body, 0)

    def shard_rows(index, y_of, core_of):
        rows = weights[index].shape[0] // 4
        return weights[index].at[pl.ds((y_of * 2 + core_of) * rows, rows)]

    def core_start(index):
        for y_of in range(2):
            send(
                shard_rows(index, y_of, 1 - core),
                expert_core[index].at[y_of],
                core_send.at[index, y_of],
                core_recv.at[index, y_of],
                peers["core"],
            )

    def core_finish(index):
        for y_of in range(2):
            wait_for(expert_core[index].at[y_of], core_recv.at[index, y_of])
            wait_for(shard_rows(index, y_of, 1 - core), core_send.at[index, y_of])
        for y_of in range(2):
            kept = shard_rows(index, y_of, core)
            add_rows(expert_core[index].at[y_of], kept, expert_core[index].at[y_of])

    weight_grad(0)
    core_start(0)
    weight_grad(1)
    core_start(1)
    core_finish(0)
    for one, target in zip(sums, shared_out):
        one.finish(target)
    weight_grad(2)
    core_start(2)
    core_finish(1)
    settle_back(grads_put, grads_back, grad_send, grad_recv, 0)
    for far in range(2):
        settle_back(rows_put, rows_back, out_send, out_recv, far)
    wait_for(far_put, far_send)
    wait_for(grads_far, far_recv)
    core_finish(2)


def slots_in_half(meta, half, capacity):
    tokens = meta.shape[1]
    expert_at = lax.broadcasted_iota(jnp.int32, (tokens, 128), 1)
    choices = [as_column(meta[k : k + 1]).astype(jnp.int32) for k in range(TOP)]
    named = ((choices[0] == expert_at) | (choices[1] == expert_at)).astype(jnp.bfloat16)
    row_at = lax.broadcasted_iota(jnp.int32, (tokens, tokens), 0)
    before = lax.broadcasted_iota(jnp.int32, (tokens, tokens), 1) < row_at
    rank = dense_product(before.astype(jnp.bfloat16), named).astype(jnp.int32)
    slot = rank + (expert_at - 4 * half) * capacity
    columns = [jnp.sum(jnp.where(choice == expert_at, slot, 0).astype(jnp.float32), axis=1, keepdims=True) for choice in choices]
    return [jnp.where(choice // 4 == half, column.astype(jnp.int32), -1) for choice, column in zip(choices, columns)]


def add_rows(target, first, second):
    def body(index, carry):
        at = pl.ds(pl.multiple_of(index * 64, 64), 64)
        target[at, :] = (first[at, :].astype(jnp.float32) + second[at, :].astype(jnp.float32)).astype(target.dtype)
        return carry

    lax.fori_loop(0, first.shape[0] // 64, body, 0)


def second_part(rows, grads, meta_far, weights, shared):
    in_hbm, in_vmem = pl.BlockSpec(memory_space=pl.ANY), pl.BlockSpec(memory_space=pltpu.VMEM)
    dma, bfloat = pltpu.SemaphoreType.DMA, jnp.bfloat16
    shape = jax.ShapeDtypeStruct
    count, capacity, width = rows.shape
    middle = weights[0].shape[1]
    down_own = weights[2]
    whole = [weights[0].shape, weights[1].shape, (4 * down_own.shape[0], down_own.shape[1])]
    quarter = [(one[0] // 4, one[1]) for one in whole]
    steps = [receive_shapes(work.shape, order)[:SHARED_DONE] for work, order in zip(shared, SHARED_ORDER)]
    blocks = (count * capacity, middle)
    return pl.pallas_call(
        second_kernel,
        out_shape=[shape(rows.shape, bfloat)] * 2
        + [shape((meta_far.shape[1], width), bfloat)]
        + [shape((2,) + one, bfloat) for one in quarter]
        + [shape(one[-1], bfloat) for one in steps],
        in_specs=[in_vmem] * 3 + [in_hbm] * 6,
        out_specs=[in_vmem] * 9,
        scratch_shapes=[pltpu.VMEM(one, bfloat) for one in whole]
        + [pltpu.VMEM(work.shape, bfloat) for work in shared]
        + [pltpu.VMEM(rows.shape, bfloat)] * 2
        + [pltpu.VMEM(blocks, bfloat)] * 3
        + [pltpu.VMEM((4 * capacity, width), jnp.float32)] * 2
        + [pltpu.VMEM((meta_far.shape[1], width), bfloat)]
        + [pltpu.VMEM(one, bfloat) for group in steps for one in group]
        + [dma((3,)), dma((3,))]
        + [dma((8,))] * 4
        + [dma((3, 2)), dma((3, 2)), dma((3, SHARED_DONE)), dma((3, SHARED_DONE)), dma(()), dma(()), dma((3,)), dma((3,))],
        compiler_params=pltpu.CompilerParams(collective_id=1, has_side_effects=True, vmem_limit_bytes=62 << 20),
        cost_estimate=pl.CostEstimate(flops=29000000000, bytes_accessed=30000000, transcendentals=2000000),
    )(rows, grads, meta_far, *weights, *shared)


STORED = 15


def third_kernel(*refs):
    rows_back, grads_back, grads_far, mixed_ref, shared_ref, ffn_grad_ref, cot_ref, hidden_ref, gain_ref, meta_ref = refs[:10]
    segment_row, padding_row, cot_far, meta_far = refs[10:14]
    stored, left_over = refs[14 : 14 + STORED], refs[14 + STORED : 17 + STORED]
    output_ref, input_grad_ref, logit_grad_ref, gain_out = refs[32:36]
    sums_out, shared_out, expert_out = refs[36:40], refs[40:43], refs[43:46]
    query_grad, key_grad, value_grad, context_grad, attended_grad, mixed_grad_ref = refs[46:52]
    weight_grads, weight_work = refs[52:56], refs[56:60]
    context_core, context_y, far_got = refs[60:63]
    expert_y = refs[63:66]
    refs = refs[66:]
    receive = [refs[4 * index : 4 * index + 4] for index in range(4)]
    refs = refs[16:]
    rest = 4 - SHARED_DONE
    shared_receive = [(None,) * SHARED_DONE + refs[rest * index : rest * index + rest] for index in range(3)]
    refs = refs[3 * rest :]
    loaded, left_mine = refs[:STORED], refs[STORED : STORED + 3]
    wo_ref, attended_ref, cosine_ref, sine_ref, query_ref, key_ref, value_ref, lse_ref, normed_ref, wk_ref, wv_ref, wq_ref = loaded[3:]
    shared_work = loaded[:3]
    refs = refs[STORED + 3 :]
    gain_parts, gain_recv = refs[:2]
    core_send, core_recv, sum_send, sum_recv, share_send, share_recv, ctx_send, ctx_recv, gain_send, gain_got, late_send, late_recv, load_sem, left_sem, far_put, part_put, part_got = refs[2:]
    expert, shard, zed, core, bits, peers = plane_places()
    why = bits["y"]
    for index in range(STORED):
        pltpu.make_async_copy(stored[index], loaded[index], load_sem.at[index]).start()
    enter(tuple(peers[axis] for axis in ("core", "y", "x", "z1", "z2")))
    def send_left(index):
        send(left_over[index].at[1 - why], expert_y[index], ctx_send.at[3 + index], ctx_recv.at[3 + index], peers["y"])

    send_left(0)
    send_left(1)
    for index in range(3):
        pltpu.make_async_copy(left_over[index].at[why], left_mine[index], left_sem.at[index]).start()
    shared_sums = [
        PlaneSum(
            (2,) + shared_out[index].shape[1:],
            shared_work[index],
            shared_receive[index],
            share_send.at[index],
            share_recv.at[index],
            bits,
            peers,
            SHARED_ORDER[index],
            shared_out[index],
            SHARED_DONE,
        )
        for index in range(3)
    ]
    for index, one in enumerate(shared_sums):
        wait_for(loaded[index], load_sem.at[index])
        one.start()
    tokens, width = hidden_ref.shape
    here = pl.ds(pl.multiple_of(shard * tokens, tokens), tokens)
    single, bfloat = jnp.float32, jnp.bfloat16

    half, capacity = expert // 4, rows_back.shape[1]
    slots = 4 * capacity
    slot_at = lax.broadcasted_iota(jnp.int32, (tokens, slots), 1)
    slots_taken = slots_in_half(meta_ref[...], half, capacity)
    grad_out = cot_ref[...].astype(single)
    mixed = mixed_ref[...]
    picks = (slot_at == slots_taken[0]) | (slot_at == slots_taken[1])
    ffn_grad = ffn_grad_ref[...] + dense_product(picks.astype(bfloat), grads_back[0:4].reshape(slots, width))
    ffn_grad = ffn_grad + grads_far[...].astype(single)
    scale_second = rms_scale(mixed)
    gain_parts[0] = jnp.zeros_like(gain_parts[0])
    gain_parts[0, 1:2, :] = jnp.sum(ffn_grad * mixed * scale_second, axis=0, keepdims=True)
    scaled = ffn_grad * gain_ref[1:2, :]
    mixed_grad = (
        grad_out
        + scale_second * scaled
        - mixed * (scale_second * scale_second * scale_second) * jnp.mean(scaled * mixed, axis=-1, keepdims=True)
    )
    mixed_grad_ref[...] = mixed_grad
    mixed_low = mixed_grad.astype(bfloat)
    for index in range(3, 5):
        wait_for(loaded[index], load_sem.at[index])
    attended_grad[...] = product_t(mixed_low, wo_ref[...]).astype(bfloat)

    def shard_rows(ref, y_of, core_of):
        rows = ref.shape[0] // 4
        return ref.at[pl.ds((y_of * 2 + core_of) * rows, rows)]

    def core_start(index):
        for y_of in range(2):
            send(
                shard_rows(weight_grads[index], y_of, 1 - core),
                weight_work[index].at[y_of],
                core_send.at[index, y_of],
                core_recv.at[index, y_of],
                peers["core"],
            )

    def core_finish(index):
        for y_of in range(2):
            wait_for(weight_work[index].at[y_of], core_recv.at[index, y_of])
            wait_for(shard_rows(weight_grads[index], y_of, 1 - core), core_send.at[index, y_of])
            add_rows(weight_work[index].at[y_of], shard_rows(weight_grads[index], y_of, core), weight_work[index].at[y_of])

    sums = [
        PlaneSum(
            weight_work[index].shape,
            weight_work[index],
            receive[index],
            sum_send.at[index],
            sum_recv.at[index],
            bits,
            peers,
            ATTENTION_ORDER[index],
            sums_out[index],
        )
        for index in range(4)
    ]
    weight_grads[3][...] = t_product(attended_ref[...], mixed_low).astype(bfloat)
    core_start(3)

    for index in range(5, STORED):
        wait_for(loaded[index], load_sem.at[index])

    own_segment = as_column(segment_row[:, here].astype(single)).astype(jnp.int32)

    def head_pair(pair, carry):
        lanes = pl.ds(pl.multiple_of(pair * 128, 128), 128)
        query, keys, values, grads = query_ref[:, lanes], key_ref[:, lanes], value_ref[:, lanes], attended_grad[:, lanes]
        allowed = allowed_mask(shard * tokens, 0, own_segment, segment_row[...], padding_row[...])
        lane = lax.broadcasted_iota(jnp.int32, query.shape, 1)
        from_keys = []
        key_total = value_total = None
        for half in range(2):
            chosen = (lane >= 64) if half else (lane < 64)
            one_query = jnp.where(chosen, query, jnp.zeros_like(query))
            one_grad = jnp.where(chosen, grads, jnp.zeros_like(grads))
            scores = jnp.where(allowed, product_t(one_query, keys) * 0.125, neg_fill)
            probs = jnp.exp(scores - lse_ref[2 * pair + half])
            probs_grad = product_t(one_grad, values)
            delta = jnp.sum(probs * probs_grad, axis=1, keepdims=True)
            scores_grad = (probs * (probs_grad - delta)).astype(bfloat)
            from_keys.append(dense_product(scores_grad, keys))
            key_part = t_product(scores_grad, one_query)
            value_part = t_product(probs.astype(bfloat), one_grad)
            key_total = key_part if key_total is None else key_total + key_part
            value_total = value_part if value_total is None else value_total + value_part
        back = jnp.where(lane < 64, from_keys[0], from_keys[1]) * 0.125
        query_grad[:, lanes] = rotate_pair(back, cosine_ref[here, :], -sine_ref[here, :]).astype(bfloat)
        key_grad[:, lanes] = rotate_pair(key_total * 0.125, cosine_ref[...], -sine_ref[...]).astype(bfloat)
        value_grad[:, lanes] = value_total.astype(bfloat)
        return carry

    def group_grads(group):
        cut = slice(256 * group, 256 * group + 256)
        weight_grads[group][:, 0:256] = t_product(normed_ref[here, :], query_grad[:, cut]).astype(bfloat)
        weight_grads[group][:, 256:512] = t_product(normed_ref[...], key_grad[:, cut]).astype(bfloat)
        weight_grads[group][:, 512:768] = t_product(normed_ref[...], value_grad[:, cut]).astype(bfloat)
        core_start(group)

    def from_experts(block, taken, meta, grads):
        gates = [as_column(gate) for gate in gate_pair(meta[2:3], meta[3:4])]
        results = rows_back[4 * block : 4 * block + 4].reshape(slots, width)
        per_route = [dense_product((slot_at == slot).astype(bfloat), results) for slot in taken]
        routed = gates[0] * per_route[0] + gates[1] * per_route[1]
        return routed, [as_row(jnp.sum(rows * grads, axis=1, keepdims=True)) for rows in per_route]

    def serve_far():
        meta = meta_far[...]
        routed, contrib = from_experts(1, slots_in_half(meta, half, capacity), meta, cot_far[...].astype(single))
        far_put[...] = routed.astype(bfloat)
        part_put[...] = jnp.zeros_like(part_put)
        for k in range(TOP):
            part_put[k : k + 1, :] = contrib[k]
        send(far_put, far_got, late_send.at[0], late_recv.at[0], peers["z2"])
        send(part_put, part_got, late_send.at[1], late_recv.at[1], peers["z2"])

    def combine():
        meta = meta_ref[...]
        routed, contrib = from_experts(0, slots_taken, meta, grad_out)
        wait_for(far_got, late_recv.at[0])
        wait_for(part_got, late_recv.at[1])
        output_ref[...] = (mixed_ref[...] + shared_ref[...] + routed + far_got[...].astype(single)).astype(bfloat)
        gates = gate_pair(meta[2:3], meta[3:4])
        contrib = [contrib[k] + part_got[k : k + 1, :] for k in range(TOP)]
        mean_contrib = gates[0] * contrib[0] + gates[1] * contrib[1]
        for k in range(TOP):
            logit_grad_ref[k : k + 1, :] = gates[k] * (contrib[k] - mean_contrib)

    gate_sum, up_sum, down_sum = shared_sums
    first, second, third, out_sum = sums

    def take(*items):
        for one in items:
            if one.step < len(one.order) or one.trail:
                one.advance()

    lax.fori_loop(0, 2, head_pair, 0)
    take(gate_sum, up_sum, down_sum)
    core_finish(3)
    out_sum.start()
    group_grads(0)
    lax.fori_loop(2, 4, head_pair, 0)
    core_finish(0)
    first.start()
    take(out_sum, gate_sum, up_sum, down_sum)
    serve_far()
    group_grads(1)
    lax.fori_loop(4, 6, head_pair, 0)
    core_finish(1)
    second.start()
    group_grads(2)

    def context_block(block, carry):
        rows = pl.ds(pl.multiple_of(block * tokens, tokens), tokens)
        total = product_t(key_grad[rows, :], wk_ref[...]) + product_t(value_grad[rows, :], wv_ref[...])
        context_grad[rows, :] = total.astype(bfloat)
        return carry

    lax.fori_loop(0, 4, context_block, 0)
    for y_of in range(2):
        send(
            shard_rows(context_grad, y_of, 1 - core),
            context_core.at[y_of],
            ctx_send.at[y_of],
            ctx_recv.at[y_of],
            peers["core"],
        )
    core_finish(2)
    third.start()
    for y_of in range(2):
        wait_for(context_core.at[y_of], ctx_recv.at[y_of])
        wait_for(shard_rows(context_grad, y_of, 1 - core), ctx_send.at[y_of])
        add_rows(context_core.at[y_of], shard_rows(context_grad, y_of, core), context_core.at[y_of])
    send(context_core.at[1 - why], context_y, ctx_send.at[2], ctx_recv.at[2], peers["y"])
    normed_grad = product_t(query_grad[...], wq_ref[...])
    take(first, out_sum, gate_sum, up_sum)
    take(down_sum, third, second, first, out_sum)
    wait_for(context_y, ctx_recv.at[2])
    wait_for(context_core.at[1 - why], ctx_send.at[2])
    normed_grad = normed_grad + context_core[pl.ds(why, 1)].reshape(tokens, width).astype(single) + context_y[...].astype(single)
    rows_in = hidden_ref[...].astype(single)
    scale_first = rms_scale(rows_in)
    gain_parts[0, 0:1, :] = jnp.sum(normed_grad * rows_in * scale_first, axis=0, keepdims=True)

    def gain_start(step):
        peer = peers[("core", "y", "x", "z1", "z2")[step]]
        send(gain_parts.at[step], gain_recv.at[step], gain_send.at[step], gain_got.at[step], peer)

    def gain_finish(step):
        wait_for(gain_recv.at[step], gain_got.at[step])
        gain_parts[step + 1] = gain_parts[step] + gain_recv[step]

    gain_start(0)
    scaled = normed_grad * gain_ref[0:1, :]
    input_grad_ref[...] = (
        mixed_grad_ref[...]
        + scale_first * scaled
        - rows_in * (scale_first * scale_first * scale_first) * jnp.mean(scaled * rows_in, axis=-1, keepdims=True)
    )
    everything = (third, second, first, out_sum, gate_sum, up_sum, down_sum)
    for step in range(5):
        gain_finish(step)
        if step < 4:
            gain_start(step + 1)
        take(*everything)
        if step == 0:
            send_left(2)
        if step == 0:
            combine()
    left = [third, second, first, out_sum, gate_sum, up_sum, down_sum]
    while any(one.trail for one in left):
        take(*[one for one in left if one.trail])
    wait_for(far_put, late_send.at[0])
    wait_for(part_put, late_send.at[1])
    for index in range(3):
        wait_for(expert_y[index], ctx_recv.at[3 + index])
        wait_for(left_mine[index], left_sem.at[index])
        add_rows(expert_out[index], left_mine[index], expert_y[index])
        wait_for(left_over[index].at[1 - why], ctx_send.at[3 + index])
    gain_out[...] = gain_parts[5]
    for step in range(5):
        wait_for(gain_parts.at[step], gain_send.at[step])


def third_part(back, mixed, shared_out, ffn_grad, cotangent, hidden, gains, meta, kept, segment, padding, weights, left_over, shared, far, shared_own):
    tokens, width = hidden.shape
    bfloat, single = jnp.bfloat16, jnp.float32
    in_vmem = pl.BlockSpec(memory_space=pltpu.VMEM)
    dma, shape, vmem = pltpu.SemaphoreType.DMA, jax.ShapeDtypeStruct, pltpu.VMEM
    cosine, sine = rotary_tables(4 * tokens, width // HEADS)
    work = (2, width // 4, width)
    normed, query, keys, values, lse, attended = kept
    wq, wk, wv, wo = weights
    cosine, sine = jnp.asarray(cosine), jnp.asarray(sine)
    stored = (*shared, wo, attended, cosine, sine, query, keys, values, lse, normed, wk, wv, wq)
    arguments = (
        *back,
        mixed,
        shared_out,
        ffn_grad,
        cotangent,
        hidden,
        gains,
        meta,
        segment[None, :],
        padding[None, :],
        *far,
        *stored,
        *left_over,
    )
    in_hbm = pl.BlockSpec(memory_space=pl.ANY)
    return pl.pallas_call(
        third_kernel,
        out_shape=[
            shape((tokens, width), bfloat),
            shape((tokens, width), single),
            shape((TOP, tokens), single),
            shape((8, width), single),
        ]
        + [shape((1,) + work[1:], bfloat)] * 4
        + [shape((1,) + one, bfloat) for one in shared_own]
        + [shape(one.shape[1:], bfloat) for one in left_over],
        in_specs=[in_vmem] * 14 + [in_hbm] * (STORED + 3),
        out_specs=[in_vmem] * 14,
        scratch_shapes=[vmem((tokens, width), bfloat)]
        + [vmem((4 * tokens, width), bfloat)] * 3
        + [vmem((tokens, width), bfloat), vmem((tokens, width), single)]
        + [vmem((width, width), bfloat)] * 4
        + [vmem(work, bfloat)] * 4
        + [vmem((2, tokens, width), bfloat), vmem((tokens, width), bfloat), vmem((tokens, width), bfloat)]
        + [vmem(one.shape[1:], bfloat) for one in left_over]
        + [vmem(one, bfloat) for order in ATTENTION_ORDER for one in receive_shapes(work, order)]
        + [
            vmem(one, bfloat)
            for own, order in zip(shared_own, SHARED_ORDER)
            for one in receive_shapes((2,) + own, order)[SHARED_DONE:]
        ]
        + [vmem(one.shape, one.dtype) for one in stored]
        + [vmem(one.shape[1:], bfloat) for one in left_over]
        + [vmem((6, 8, width), single), vmem((5, 8, width), single)]
        + [dma((4, 2)), dma((4, 2)), dma((4, 7)), dma((4, 7)), dma((3, 7)), dma((3, 7)), dma((6,)), dma((6,)), dma((5,)), dma((5,)), dma((2,)), dma((2,)), dma((STORED,)), dma((3,))]
        + [vmem((tokens, width), bfloat), vmem((8, tokens), single), vmem((8, tokens), single)],
        compiler_params=pltpu.CompilerParams(collective_id=2, has_side_effects=True, vmem_limit_bytes=60 << 20),
        cost_estimate=pl.CostEstimate(flops=12000000000, bytes_accessed=25000000, transcendentals=3000000),
    )(*arguments)


def last_kernel(*refs):
    groups, rest_in, output_in, input_grad_in = refs[:3], refs[3:10], refs[10], refs[11]
    heads_out, rest_out, output_ref, input_grad_ref = refs[12:15], refs[15:22], refs[22], refs[23]
    for kind, target in enumerate(heads_out):
        for index, group in enumerate(groups):
            target[:, 256 * index : 256 * index + 256] = group[0, :, 256 * kind : 256 * kind + 256].astype(jnp.float32)
    for source, target in zip(rest_in, rest_out):
        target[...] = source[...].reshape(target.shape).astype(jnp.float32)
    output_ref[...] = output_in[...].reshape(output_ref.shape)
    input_grad_ref[...] = input_grad_in[...].reshape(input_grad_ref.shape)


def last_part(attention, shared, experts, output, input_grad):
    steps = 4
    inputs = [*attention, *shared, *experts, output, input_grad]

    def spec(shape):
        if len(shape) == 3:
            return pl.BlockSpec((1, shape[1] // steps, shape[2]), lambda step: (0, step, 0))
        return pl.BlockSpec((shape[0] // steps, shape[1]), lambda step: (step, 0))

    shapes = [one.shape[1:] for one in (attention[0], *attention[:3], *shared)]
    shapes = [shapes[0]] * 4 + shapes[4:] + [(1,) + one.shape for one in experts]
    out_shape = [jax.ShapeDtypeStruct(one, jnp.float32) for one in shapes]
    out_shape += [jax.ShapeDtypeStruct((1,) + one.shape, one.dtype) for one in (output, input_grad)]
    return pl.pallas_call(
        last_kernel,
        grid=(steps,),
        out_shape=out_shape,
        in_specs=[spec(one.shape) for one in inputs],
        out_specs=[spec(one.shape) for one in out_shape],
        compiler_params=pltpu.CompilerParams(vmem_limit_bytes=62 << 20),
    )(*inputs)


def swap(value, axis, bit):
    size = lax.axis_size(axis)
    return lax.ppermute(value, axis, [(index, index ^ bit) for index in range(size)])


def halves(value, bit_set, dim):
    half = value.shape[dim] // 2
    keep = lax.dynamic_slice_in_dim(value, bit_set * half, half, dim)
    give = lax.dynamic_slice_in_dim(value, (1 - bit_set) * half, half, dim)
    return keep, give


def fold(value, axis, bit, dim):
    bit_set = (lax.axis_index(axis) // bit) % 2
    keep, give = halves(value, bit_set, dim)
    return (keep.astype(jnp.float32) + swap(give.astype(jnp.bfloat16), axis, bit).astype(jnp.float32)).astype(jnp.bfloat16)


def unfold(value, axis, bit, dim):
    bit_set = (lax.axis_index(axis) // bit) % 2
    come = swap(value, axis, bit)
    return jnp.where(bit_set == 0, jnp.concatenate([value, come], dim), jnp.concatenate([come, value], dim))


def bits_of(axis):
    size = lax.axis_size(axis)
    return [1 << place for place in range(size.bit_length() - 1)]


def scatter_shards(value):
    count = lax.axis_size("shard")
    blocks = value.reshape((count // 2, 2, value.shape[0] // count) + value.shape[1:])
    blocks = fold(blocks, "shard", 1, 1)[:, 0]
    for bit in reversed(bits_of("shard")[1:]):
        blocks = fold(blocks, "shard", bit, 0)
    return blocks[0]


def sum_plane(value, dim):
    bits = bits_of("expert")
    for bit in bits:
        value = fold(value, "expert", bit, dim)
    for bit in reversed(bits):
        value = unfold(value, "expert", bit, dim)
    return value.astype(jnp.float32)


def shards(
    hidden_in,
    gain_attn,
    gain_ffn,
    w_query,
    w_key,
    w_value,
    w_out,
    shared_gate,
    shared_up,
    shared_down,
    expert_gate,
    expert_up,
    expert_down,
    gate_logits,
    routes,
    segment,
    padding,
    cotangent,
):
    bfloat = jnp.bfloat16
    tokens = hidden_in.shape[1]
    model_width = hidden_in.shape[2]
    head_size = model_width // HEADS
    experts = lax.axis_size("expert")
    capacity = max(2, 2 * tokens * TOP // experts)
    shard_count = lax.axis_size("shard")
    shard_index = lax.axis_index("shard")
    score_scale = head_size ** (-0.5)
    head_shape = (tokens, HEADS, head_size)
    fast = (experts, shard_count, WINDOW) == (8, 4, 4 * tokens)
    dense_own = (w_query, w_key, w_value, w_out, shared_gate, shared_up, shared_down)
    expert_own = (expert_gate[0], expert_up[0], expert_down[0])
    rows_in = hidden_in[0].astype(jnp.float32)
    scale_first = rms_scale(rows_in)
    positions = shard_index * tokens + jnp.arange(tokens, dtype=jnp.int32)
    segment_row, padding_row = segment[0], padding[0]
    query_segment = lax.dynamic_slice_in_dim(segment_row, shard_index * tokens, tokens)
    if fast:
        gain_own = lax.dynamic_update_slice(
            jnp.zeros((2, model_width), bfloat),
            jnp.stack([gain_attn, gain_ffn]),
            (0, shard_index * gain_attn.shape[0]),
        )
        meta = [routes[0].T.astype(jnp.float32), gate_logits[0].T, jnp.zeros((8 - 2 * TOP, tokens), jnp.float32)]
        meta = jnp.concatenate(meta, axis=0)
        full, rest = first_part(
            hidden_in[0],
            gain_own,
            dense_own,
            expert_own,
            segment_row,
            padding_row,
            cotangent[0],
            meta,
        )
        normed_ctx, query_low, keys_ctx, values_ctx, log_total, attended, mixed_rows = rest[:7]
        cot_far, meta_far, gains, received, grad_received, shared_out, ffn_grad_shared, *shared_work = rest[7:]
        normed_ffn = None
        gain_first, gain_second = gains[0], gains[1]
        w_q, w_k, w_v, w_o = (full[name] for name in ("wq", "wk", "wv", "wo"))
        e_gate, e_up = (full[name] for name in LATE)
        reach, key_start = shard_count - 1, 0
        key_segment, key_padding = segment_row, padding_row
        key_positions = jnp.arange(4 * tokens, dtype=jnp.int32)
        allowed = allowed_mask(shard_index * tokens, 0, query_segment[:, None], key_segment[None], key_padding[None])
    else:
        gather = functools.partial(lax.all_gather, axis_name="shard", tiled=True)
        w_q, w_k, w_v, w_o, s_gate, s_up, s_down = (gather(weight) for weight in dense_own)
        e_gate, e_up, e_down = (gather(weight) for weight in expert_own)
        gain_first, gain_second = (gather(gain).astype(jnp.float32) for gain in (gain_attn, gain_ffn))
        reach = min((WINDOW + tokens - 2) // tokens, shard_count - 1)
        lead_rows, key_rows = reach * tokens, (reach + 1) * tokens
        context = [from_behind(hidden_in[0], "shard", offset) for offset in range(reach, 0, -1)] + [hidden_in[0]]
        context = jnp.concatenate(context, axis=0).astype(jnp.float32)
        normed_ctx = (context * rms_scale(context) * gain_first).astype(bfloat)
        key_positions = (shard_index - reach) * tokens + jnp.arange(key_rows, dtype=jnp.int32)
        query_low = rotate(
            dense_product(normed_ctx[lead_rows:], w_q).reshape(head_shape), positions, 1.0
        ).astype(bfloat)
        keys_ctx = rotate(
            dense_product(normed_ctx, w_k).reshape(key_rows, HEADS, head_size), key_positions, 1.0
        ).astype(bfloat)
        values_ctx = dense_product(normed_ctx, w_v).astype(bfloat)
        segment_ext = jnp.concatenate([jnp.full((lead_rows,), -1, jnp.int32), segment_row])
        padding_ext = jnp.concatenate([jnp.zeros((lead_rows,), jnp.int32), padding_row])
        key_segment = lax.dynamic_slice_in_dim(segment_ext, shard_index * tokens, key_rows)
        key_padding = lax.dynamic_slice_in_dim(padding_ext, shard_index * tokens, key_rows)
        allowed = allowed_mask(
            shard_index * tokens,
            (shard_index - reach) * tokens,
            query_segment[:, None],
            key_segment[None],
            key_padding[None],
        )
    key_rows = (reach + 1) * tokens
    query_heads = query_low.reshape(head_shape)
    keys_all = keys_ctx.reshape(key_rows, HEADS, head_size)
    values_all = values_ctx.reshape(key_rows, HEADS, head_size)

    def score_block():
        raw_scores = (
            jnp.einsum("qhd,khd->hqk", query_heads, keys_all, preferred_element_type=jnp.float32)
            * score_scale
        )
        return jnp.where(allowed[None], raw_scores, neg_fill)

    if not fast:
        scores = score_block()
        top_score = jnp.max(scores, axis=-1, keepdims=True)
        exponent = jnp.exp(scores - top_score)
        exp_total = jnp.sum(exponent, axis=-1, keepdims=True)
        log_total = top_score + jnp.log(exp_total)
        attended = (
            jnp.einsum(
                "hqk,khd->qhd",
                (exponent / exp_total).astype(bfloat),
                values_all,
                preferred_element_type=jnp.float32,
            )
            .astype(bfloat)
            .reshape(tokens, model_width)
        )
        mixed_rows = rows_in + dense_product(attended, w_o)
        normed_ffn = (mixed_rows * rms_scale(mixed_rows) * gain_second).astype(bfloat)
    scale_second = rms_scale(mixed_rows)
    grad_low = cotangent[0]
    grad_out = grad_low.astype(jnp.float32)
    gate_probs = jax.nn.softmax(gate_logits[0], axis=-1)
    route_flat = routes[0].reshape(-1)
    route_total = tokens * TOP
    onehot = (route_flat[:, None] == jnp.arange(experts, dtype=jnp.int32)[None, :]).astype(
        jnp.int32
    )
    slot_rank = jnp.sum((jnp.cumsum(onehot, axis=0) - onehot) * onehot, axis=1)
    places = route_flat * capacity + slot_rank
    if not fast:
        shared_pre = dense_product(normed_ffn, s_gate)
        shared_lin = dense_product(normed_ffn, s_up)
        shared_mid = (jax.nn.silu(shared_pre) * shared_lin).astype(bfloat)
        shared_out = dense_product(shared_mid, s_down)
        grad_shared_mid = product_t(grad_low, s_down)
        grad_shared_pre, grad_shared_lin = swiglu_back(grad_shared_mid, shared_pre, shared_lin)
        shared_down_grad = dense_product(shared_mid.T, grad_low)
        shared_gate_grad = dense_product(normed_ffn.T, grad_shared_pre)
        shared_up_grad = dense_product(normed_ffn.T, grad_shared_lin)
        ffn_grad_shared = product_t(grad_shared_pre, s_gate) + product_t(grad_shared_lin, s_up)
        slot_table = (
            jnp.full((experts * capacity,), route_total, dtype=jnp.int32)
            .at[places]
            .set(jnp.arange(route_total, dtype=jnp.int32))
        )
        padded_rows = jnp.concatenate([normed_ffn, jnp.zeros((1, model_width), bfloat)], axis=0)
        send_rows = padded_rows[slot_table // TOP].reshape(experts, capacity, model_width)
        received = lax.all_to_all(send_rows, "expert", split_axis=0, concat_axis=0, tiled=True)
        route_grad = (
            (gate_probs[:, :, None] * grad_out[:, None, :])
            .astype(bfloat)
            .reshape(route_total, model_width)
        )
        route_padded = jnp.concatenate([route_grad, jnp.zeros((1, model_width), bfloat)], axis=0)
        send_grad = route_padded[slot_table].reshape(experts, capacity, model_width)
        grad_received = lax.all_to_all(send_grad, "expert", split_axis=0, concat_axis=0, tiled=True)
    if fast:
        results = second_part(received, grad_received, meta_far, (e_gate, e_up, expert_own[2]), shared_work)
        back, left_over, shared_work = results[:3], results[3:6], results[6:]
        output, input_grad, logit_grad, gain_grads, *sums = third_part(
            back,
            mixed_rows,
            shared_out,
            ffn_grad_shared,
            grad_low,
            hidden_in[0],
            gains,
            meta,
            (normed_ctx, query_low, keys_ctx, values_ctx, log_total, attended),
            segment_row,
            padding_row,
            (w_q, w_k, w_v, w_o),
            left_over,
            shared_work,
            (cot_far, meta_far),
            (shared_gate.shape, shared_up.shape, shared_down.shape),
        )
        *grads, output, input_grad = last_part(sums[:4], sums[4:7], sums[7:], output, input_grad)
        gain_grads = lax.dynamic_slice_in_dim(gain_grads, shard_index * gain_attn.shape[0], gain_attn.shape[0], 1)
        return (output, input_grad, logit_grad.T[None], gain_grads[0], gain_grads[1], *grads)
    else:
        gate_pre = jnp.einsum("sid,df->sif", received, e_gate, preferred_element_type=jnp.float32)
        up_pre = jnp.einsum("sid,df->sif", received, e_up, preferred_element_type=jnp.float32)
        middle = (jax.nn.silu(gate_pre) * up_pre).astype(bfloat)
        result = jnp.einsum("sif,fd->sid", middle, e_down, preferred_element_type=jnp.float32).astype(bfloat)
        returned = lax.all_to_all(result, "expert", split_axis=0, concat_axis=0, tiled=True)
        grad_middle = jnp.einsum(
            "sid,fd->sif", grad_received, e_down, preferred_element_type=jnp.float32
        )
        grad_gate_pre, grad_up_pre = swiglu_back(grad_middle, gate_pre, up_pre)
        expert_down_grad = jnp.einsum(
            "sif,sid->fd", middle, grad_received, preferred_element_type=jnp.float32
        )
        expert_gate_grad = jnp.einsum(
            "sid,sif->df", received, grad_gate_pre, preferred_element_type=jnp.float32
        )
        expert_up_grad = jnp.einsum(
            "sid,sif->df", received, grad_up_pre, preferred_element_type=jnp.float32
        )
        grad_rows = (
            jnp.einsum("sif,df->sid", grad_gate_pre, e_gate, preferred_element_type=jnp.float32)
            + jnp.einsum("sif,df->sid", grad_up_pre, e_up, preferred_element_type=jnp.float32)
        ).astype(bfloat)
        grad_back = lax.all_to_all(grad_rows, "expert", split_axis=0, concat_axis=0, tiled=True)
        expert_grads = tuple(
            scatter_shards(grad.astype(bfloat))[None].astype(jnp.float32)
            for grad in (expert_gate_grad, expert_up_grad, expert_down_grad)
        )
        shared_grads = (
            sum_plane(scatter_shards(shared_gate_grad.astype(bfloat)), 1),
            sum_plane(scatter_shards(shared_up_grad.astype(bfloat)), 1),
            sum_plane(scatter_shards(shared_down_grad.astype(bfloat)), 0),
        )
    per_route = (
        returned.reshape(experts * capacity, model_width)[places]
        .astype(jnp.float32)
        .reshape(tokens, TOP, model_width)
    )
    routed = jnp.sum(gate_probs[:, :, None] * per_route, axis=1)
    output = (mixed_rows + shared_out + routed).astype(bfloat)
    contrib = jnp.sum(per_route * grad_out[:, None, :], axis=-1)
    logit_grad = gate_probs * (contrib - jnp.sum(gate_probs * contrib, axis=-1, keepdims=True))
    grad_routes = (
        grad_back.reshape(experts * capacity, model_width)[places]
        .astype(jnp.float32)
        .reshape(tokens, TOP, model_width)
    )
    grad_normed_ffn = jnp.sum(grad_routes, axis=1) + ffn_grad_shared
    gain_ffn_grad = jnp.sum(grad_normed_ffn * mixed_rows * scale_second, axis=0)
    scaled_second = grad_normed_ffn * gain_second
    grad_mixed = (
        grad_out
        + scale_second * scaled_second
        - mixed_rows
        * scale_second**3
        * jnp.mean(scaled_second * mixed_rows, axis=-1, keepdims=True)
    )
    grad_mixed_low = grad_mixed.astype(bfloat)
    w_out_grad = dense_product(attended.T, grad_mixed_low)
    grad_attended = product_t(grad_mixed_low, w_o).astype(bfloat).reshape(head_shape)
    attn_probs = jnp.exp(score_block() - log_total)
    grad_probs = jnp.einsum(
        "qhd,khd->hqk", grad_attended, values_all, preferred_element_type=jnp.float32
    )
    delta_rows = jnp.sum(attn_probs * grad_probs, axis=-1, keepdims=True)
    grad_scores = (attn_probs * (grad_probs - delta_rows)).astype(bfloat)
    grad_query = (
        jnp.einsum("hqk,khd->qhd", grad_scores, keys_all, preferred_element_type=jnp.float32)
        * score_scale
    )
    grad_keys = (
        jnp.einsum("hqk,qhd->khd", grad_scores, query_heads, preferred_element_type=jnp.float32)
        * score_scale
    )
    grad_values = jnp.einsum(
        "hqk,qhd->khd", attn_probs.astype(bfloat), grad_attended, preferred_element_type=jnp.float32
    )
    grad_query_low = rotate(grad_query, positions, -1.0).astype(bfloat).reshape(tokens, model_width)
    grad_key_low = rotate(grad_keys, key_positions, -1.0).astype(bfloat).reshape(key_rows, model_width)
    grad_value_low = grad_values.astype(bfloat).reshape(key_rows, model_width)
    if fast:
        normed = lax.dynamic_slice_in_dim(normed_ctx, shard_index * tokens, tokens)
    else:
        normed = normed_ctx[reach * tokens :]
    w_query_grad = dense_product(normed.T, grad_query_low)
    w_key_grad = dense_product(normed_ctx.T, grad_key_low)
    w_value_grad = dense_product(normed_ctx.T, grad_value_low)
    grad_context = product_t(grad_key_low, w_k) + product_t(grad_value_low, w_v)
    grad_normed = product_t(grad_query_low, w_q)
    if fast:
        grad_normed = grad_normed + scatter_shards(grad_context.astype(bfloat)).astype(jnp.float32)
    else:
        grad_normed = grad_normed + grad_context[reach * tokens :]
        for offset in range(1, reach + 1):
            sent = grad_context[(reach - offset) * tokens :][:tokens].astype(bfloat)
            grad_normed = grad_normed + from_behind(sent, "shard", -offset).astype(jnp.float32)
    gain_attn_grad = jnp.sum(grad_normed * rows_in * scale_first, axis=0)
    scaled_first = grad_normed * gain_first
    input_grad = (
        grad_mixed
        + scale_first * scaled_first
        - rows_in * scale_first**3 * jnp.mean(scaled_first * rows_in, axis=-1, keepdims=True)
    )
    gain_rows = jnp.stack([gain_attn_grad, gain_ffn_grad], axis=1).astype(bfloat)
    gain_total = lax.psum(scatter_shards(gain_rows), "expert").astype(jnp.float32)
    attn_grads = jnp.stack([w_query_grad, w_key_grad, w_value_grad, w_out_grad]).astype(bfloat)
    attn_rows = scatter_shards(attn_grads.transpose(1, 0, 2)).transpose(1, 0, 2)
    attn_total = sum_plane(attn_rows.reshape(-1, model_width), 0).reshape(attn_rows.shape)
    return (
        output[None],
        input_grad[None],
        logit_grad[None],
        gain_total[:, 0],
        gain_total[:, 1],
        attn_total[0],
        attn_total[1],
        attn_total[2],
        attn_total[3],
        shared_grads[0],
        shared_grads[1],
        shared_grads[2],
        expert_grads[0],
        expert_grads[1],
        expert_grads[2],
    )


def solution(mesh):
    placed = (
        P("expert", "shard", None),
        P("shard"),
        P("shard"),
        P("shard", None),
        P("shard", None),
        P("shard", None),
        P("shard", None),
        P("shard", None),
        P("shard", None),
        P("shard", None),
        P("expert", "shard", None),
        P("expert", "shard", None),
        P("expert", "shard", None),
        P("expert", "shard", None),
        P("expert", "shard", None),
        P("expert", None),
        P("expert", None),
        P("expert", "shard", None),
    )
    return jax.shard_map(
        shards,
        mesh=mesh,
        in_specs=placed,
        out_specs=(
            P("expert", "shard", None),
            P("expert", "shard", None),
            P("expert", "shard", None),
            P("shard"),
            P("shard"),
            P("shard", None),
            P("shard", None),
            P("shard", None),
            P("shard", None),
            P("shard", None),
            P("shard", None),
            P("shard", None),
            P("expert", "shard", None),
            P("expert", "shard", None),
            P("expert", "shard", None),
        ),
        check_vma=False,
    )
```

```python
import functools
import math

import jax
import jax.numpy as jnp
import numpy as np
from jax import lax
from jax.experimental import pallas as pl
from jax.experimental.pallas import tpu as pltpu
from jax.sharding import PartitionSpec as P

HEADS = 12
TOP = 2
WINDOW = 1024
MESH = pl.DeviceIdType.MESH
norm_eps = 1e-06
neg_fill = -1e30
rope_base = 10000.0

DIRECT = ("hid", "gains")
EARLY = ("wk", "wv", "wq", "wo")
SHARED = ("sg", "su", "sd")
SWAP_Z = ("su",)
LATE = ("eg", "eu")
NAMES = DIRECT + EARLY + SHARED + LATE
PASSING = DIRECT + EARLY + SHARED
SAVED = 13


def dense_product(left, right):
    return jnp.dot(left, right, preferred_element_type=jnp.float32)


def product_t(left, right):
    return lax.dot_general(left, right, (((1,), (1,)), ((), ())), preferred_element_type=jnp.float32)


def t_product(left, right):
    return lax.dot_general(left, right, (((0,), (0,)), ((), ())), preferred_element_type=jnp.float32)


def rms_scale(values):
    return lax.rsqrt(jnp.mean(values * values, axis=-1, keepdims=True) + norm_eps)


def rotary_tables(length, head_size):
    half = head_size // 2
    frequency = np.float32(rope_base) ** (-np.arange(half, dtype=np.float32) / np.float32(half))
    angles = np.arange(length, dtype=np.float32)[:, None] * frequency[None, :]
    cosine, sine = np.cos(angles).astype(np.float32), np.sin(angles).astype(np.float32)
    return np.concatenate([cosine] * 4, axis=1), np.concatenate([-sine, sine] * 2, axis=1)


def rotate_pair(values, cosine, sine):
    lane = lax.broadcasted_iota(jnp.int32, values.shape, 1)
    partner = jnp.where(lane % 64 < 32, pltpu.roll(values, 96, 1), pltpu.roll(values, 32, 1))
    return values * cosine + partner * sine


def rotate(values, positions, direction):
    half_size = values.shape[-1] // 2
    frequency = rope_base ** (-jnp.arange(half_size, dtype=jnp.float32) / half_size)
    angles = positions.astype(jnp.float32)[:, None] * frequency[None, :]
    cosine = jnp.cos(angles)[:, None, :]
    sine_part = direction * jnp.sin(angles)[:, None, :]
    first_half = values[..., :half_size]
    second_half = values[..., half_size:]
    return jnp.concatenate(
        [
            first_half * cosine - second_half * sine_part,
            second_half * cosine + first_half * sine_part,
        ],
        axis=-1,
    )


def swiglu_back(grad_middle, gate_pre, up_pre):
    sigmoid_gate = jax.nn.sigmoid(gate_pre)
    activated = gate_pre * sigmoid_gate
    grad_gate = grad_middle * up_pre * sigmoid_gate * (1.0 + gate_pre * (1.0 - sigmoid_gate))
    grad_up = grad_middle * activated
    return (grad_gate.astype(jnp.bfloat16), grad_up.astype(jnp.bfloat16))


def from_behind(value, axis, steps):
    count = lax.axis_size(axis)
    first, last = (max(0, -steps), min(count, count - steps))
    return lax.ppermute(value, axis, [(source, source + steps) for source in range(first, last)])


def send(source, target, send_sem, recv_sem, peer):
    pltpu.make_async_remote_copy(
        src_ref=source,
        dst_ref=target,
        send_sem=send_sem,
        recv_sem=recv_sem,
        device_id=peer,
        device_id_type=MESH,
    ).start()


def wait_for(ref, sem):
    pltpu.make_async_copy(ref, ref, sem).wait()


def first_kernel(*refs):
    count = len(NAMES)
    own = dict(zip(NAMES, refs[:count]))
    segment_row, padding_row, cosine_ref, sine_ref, cot_ref, meta_ref = refs[count : count + 6]
    refs = refs[count + 6 :]
    full = dict(zip(LATE, refs[: len(LATE)]))
    refs = refs[len(LATE) :]
    saved, refs = refs[:SAVED], refs[SAVED:]
    gain_ref, rows_got, grads_got, shared_ref, ffn_grad_ref, *shared_work = refs[:8]
    refs = refs[8:]
    full.update(zip(PASSING, refs[: len(PASSING)]))
    refs = refs[len(PASSING) :]
    normed_ref, query_ref, key_ref, value_ref, lse_ref, attended_ref, mixed_ref, ffn_ref = refs[:8]
    refs = refs[8:]
    shared_core = refs[:3]
    refs = refs[3:]
    rows_put, grads_put = refs[:2]
    (own_sem, y_send, y_recv, swap_send, swap_recv, core_send, core_recv) = refs[2:9]
    row_sems, grad_sems, share_send, share_recv, save_sem = refs[9:11], refs[11:13], refs[13], refs[14], refs[15]
    far_send, far_recv, slot_ref, meta_far, cot_far, ffn_far = refs[16:]
    number = {name: index for index, name in enumerate(NAMES)}
    expert, shard = (lax.axis_index("expert"), lax.axis_index("shard"))
    zed, ex = (expert // 2, expert % 2)
    other = (shard + 2) % 4
    y_peer = (expert, other)
    core_peer = (expert, shard + 1 - 2 * (shard % 2))
    x_peer = (expert + 1 - 2 * ex, shard)
    z_peer = (expert + 2 - 4 * (zed % 2), shard)

    barrier = pltpu.get_barrier_semaphore()
    for peer in (y_peer, core_peer) + tuple(((expert + step) % 8, shard) for step in range(1, 8)):
        pl.semaphore_signal(barrier, inc=1, device_id=peer, device_id_type=MESH)
    pl.semaphore_wait(barrier, 9)

    def side(name):
        return (zed % 2, z_peer) if name in SWAP_Z else (ex, x_peer)

    def part_of(block, base, name, half):
        rows = own[name].shape[0]
        if half is None:
            return block.at[pl.ds(base, rows)]
        return block.at[pl.ds(base + half * (rows // 2), rows // 2)]

    def place(name, slot, half=None):
        return part_of(full[name], slot * own[name].shape[0], name, half)

    def mine(name, half=None):
        return part_of(own[name], 0, name, half)

    def cross(name, half=None):
        n = number[name]
        send(mine(name, half), place(name, shard, half), y_send.at[n], y_recv.at[n], y_peer)

    def to_core(name, step, half=None):
        n = number[name]
        part = place(name, other, half)
        send(part, part, core_send.at[n, 1 + step], core_recv.at[n, 1 + step], core_peer)

    far = shard + 1 - 2 * (shard % 2)
    far_other = (far + 2) % 4

    def settle_own(names):
        for name in names:
            n = number[name]
            pltpu.make_async_copy(own[name], place(name, shard), own_sem.at[n]).wait()
            wait_for(place(name, far), core_recv.at[n, 0])
            wait_for(own[name], core_send.at[n, 0])

    def settle_core(name, step, half=None):
        n = number[name]
        wait_for(place(name, far_other, half), core_recv.at[n, 1 + step])
        wait_for(place(name, other, half), core_send.at[n, 1 + step])

    def own_to_core(names):
        for name in names:
            n = number[name]
            send(own[name], place(name, shard), core_send.at[n, 0], core_recv.at[n, 0], core_peer)
            pltpu.make_async_copy(own[name], place(name, shard), own_sem.at[n]).start()

    for name in DIRECT:
        cross(name)
    for name in EARLY + SHARED:
        cross(name, side(name)[0])
    for name in LATE:
        cross(name)
    own_to_core(DIRECT + EARLY)

    tokens, width = own["hid"].shape
    capacity = rows_put.shape[1]
    far_expert, half_start, in_half = (expert + 4) % 8, 4 * (expert // 4), expert % 4
    far_peer = (far_expert, shard)

    def to_far(index, ref, target):
        send(ref, target, far_send.at[index], far_recv.at[index], far_peer)

    def settle_far(index, ref):
        wait_for(ref, far_send.at[index])
        wait_for(ref, far_recv.at[index])

    to_far(0, meta_ref, meta_far)
    to_far(1, cot_ref, cot_far)

    def fill_slots(block, meta):
        expert_at = lax.broadcasted_iota(jnp.int32, (8, tokens), 0).astype(jnp.float32)
        named = ((meta[0:1] == expert_at) | (meta[1:2] == expert_at)).astype(jnp.float32)
        row_at = lax.broadcasted_iota(jnp.int32, (tokens, tokens), 0)
        before = row_at < lax.broadcasted_iota(jnp.int32, (tokens, tokens), 1)
        rank = dense_product(named.astype(jnp.bfloat16), before.astype(jnp.bfloat16))
        slot_ref[block] = jnp.where(named > 0.0, rank, -1.0)

    def picks(block, target):
        slot_at = lax.broadcasted_iota(jnp.int32, (capacity, tokens), 0)
        return slot_at == slot_ref[block, pl.ds(target, 1), :].astype(jnp.int32)

    def put_grads(block, meta, cot):
        gates = [as_column(gate) for gate in gate_pair(meta[2:3], meta[3:4])]
        route_grads = [(gate * cot.astype(jnp.float32)).astype(jnp.bfloat16) for gate in gates]
        for index in range(4):
            target = half_start + index
            chosen = picks(block, target)
            grads_put[4 * block + index] = sum(
                dense_product(
                    (chosen & (meta[k : k + 1].astype(jnp.int32) == target)).astype(jnp.bfloat16), route_grads[k]
                )
                for k in range(TOP)
            ).astype(jnp.bfloat16)

    def put_rows(block, ffn):
        for index in range(4):
            chosen = picks(block, half_start + index).astype(jnp.bfloat16)
            rows_put[4 * block + index] = dense_product(chosen, ffn).astype(jnp.bfloat16)

    def dispatch(block, put, got, sems):
        source = far_expert if block else expert
        for step in range(1, 4):
            index = (in_half + step) % 4
            at = 4 * block + step
            send(put.at[4 * block + index], got.at[source], sems[0].at[at], sems[1].at[at], (half_start + index, shard))
        pltpu.make_async_copy(put.at[4 * block + in_half], got.at[source], sems[0].at[4 * block]).start()

    def settle_dispatch(put, got, sems):
        for block in range(2):
            for step in range(4):
                wait_for(put.at[4 * block + (in_half + step) % 4], sems[0].at[4 * block + step])
            for step in range(1, 4):
                sender = half_start + (in_half + 4 - step) % 4
                wait_for(got.at[(sender + 4 * block) % 8], sems[1].at[4 * block + step])

    fill_slots(0, meta_ref[...])
    put_grads(0, meta_ref[...], cot_ref[...])
    dispatch(0, grads_put, grads_got, grad_sems)
    for name in DIRECT:
        wait_for(place(name, other), y_recv.at[number[name]])
        to_core(name, 0)

    def early_out(name):
        n, (half, peer) = number[name], side(name)
        part = place(name, other, half)
        wait_for(part, y_recv.at[n])
        send(part, part, swap_send.at[n], swap_recv.at[n], peer)
        to_core(name, 0, half)

    def pass_early(name):
        half, _ = side(name)
        wait_for(place(name, other, 1 - half), swap_recv.at[number[name]])
        to_core(name, 1, 1 - half)

    def settle_early_far(name):
        half, _ = side(name)
        settle_core(name, 0, half)
        settle_core(name, 1, 1 - half)
        wait_for(mine(name, half), y_send.at[number[name]])
        wait_for(place(name, other, half), swap_send.at[number[name]])

    def settle_early(names):
        settle_own(names)
        for name in names:
            settle_early_far(name)

    for name in ("wk", "wv", "wq"):
        early_out(name)
    own_to_core(SHARED + LATE)

    settle_own(DIRECT)
    for name in DIRECT:
        settle_core(name, 0)
    gain_rows = sum(full["gains"][pl.ds(slot * 16, 16), :].astype(jnp.float32) for slot in range(4))
    gain_ref[...] = gain_rows
    gain_first, gain_second = gain_rows[0:1], gain_rows[1:2]

    def norm_block(block, carry):
        rows = pl.ds(pl.multiple_of(block * tokens, tokens), tokens)
        values = full["hid"][rows, :].astype(jnp.float32)
        normed_ref[rows, :] = (values * rms_scale(values) * gain_first).astype(jnp.bfloat16)
        return carry

    lax.fori_loop(0, 4, norm_block, 0)

    pass_early("wk")
    pass_early("wv")
    settle_early(("wk",))

    def key_block(block, carry):
        rows = pl.ds(pl.multiple_of(block * tokens, tokens), tokens)
        raw = dense_product(normed_ref[rows, :], full["wk"][...])
        cosine, sine = cosine_ref[rows, :], sine_ref[rows, :]
        for start in range(0, width, 128):
            key_ref[rows, start : start + 128] = rotate_pair(raw[:, start : start + 128], cosine, sine).astype(jnp.bfloat16)
        return carry

    def value_block(block, carry):
        rows = pl.ds(pl.multiple_of(block * tokens, tokens), tokens)
        value_ref[rows, :] = dense_product(normed_ref[rows, :], full["wv"][...]).astype(jnp.bfloat16)
        return carry

    lax.fori_loop(0, 4, key_block, 0)
    pass_early("wq")
    settle_early(("wv",))
    lax.fori_loop(0, 4, value_block, 0)
    settle_early(("wq",))
    here = pl.ds(pl.multiple_of(shard * tokens, tokens), tokens)
    raw = dense_product(normed_ref[here, :], full["wq"][...])
    cosine, sine = cosine_ref[here, :], sine_ref[here, :]
    for start in range(0, width, 128):
        query_ref[:, start : start + 128] = rotate_pair(raw[:, start : start + 128], cosine, sine).astype(jnp.bfloat16)
    early_out("wo")

    own_segment = as_column(segment_row[:, here].astype(jnp.float32)).astype(jnp.int32)

    def head_pair(pair, carry):
        lanes = pl.ds(pl.multiple_of(pair * 128, 128), 128)
        query, keys, values = query_ref[:, lanes], key_ref[:, lanes], value_ref[:, lanes]
        allowed = allowed_mask(shard * tokens, 0, own_segment, segment_row[...], padding_row[...])
        lane = lax.broadcasted_iota(jnp.int32, query.shape, 1)
        results = []
        for half in range(2):
            chosen = (lane >= 64) if half else (lane < 64)
            scores = product_t(jnp.where(chosen, query, jnp.zeros_like(query)), keys) * 0.125
            scores = jnp.where(allowed, scores, neg_fill)
            top_score = jnp.max(scores, axis=-1, keepdims=True)
            exponent = jnp.exp(scores - top_score)
            exp_total = jnp.sum(exponent, axis=-1, keepdims=True)
            lse_ref[2 * pair + half] = top_score + jnp.log(exp_total)
            results.append(dense_product((exponent / exp_total).astype(jnp.bfloat16), values))
        attended_ref[:, lanes] = jnp.where(lane < 64, results[0], results[1]).astype(jnp.bfloat16)
        return carry

    lax.fori_loop(0, 2, head_pair, 0)
    early_out("sg")
    pass_early("wo")
    lax.fori_loop(2, 5, head_pair, 0)
    early_out("su")
    pass_early("sg")
    lax.fori_loop(5, 6, head_pair, 0)
    settle_far(0, meta_far)
    settle_far(1, cot_far)
    fill_slots(1, meta_far[...])
    put_grads(1, meta_far[...], cot_far[...])
    settle_early(("wo",))
    rows_in = own["hid"][...].astype(jnp.float32)
    mixed = rows_in + dense_product(attended_ref[...], full["wo"][...])
    mixed_ref[...] = mixed
    ffn = (mixed * rms_scale(mixed) * gain_second).astype(jnp.bfloat16)
    ffn_ref[...] = ffn
    to_far(2, ffn_ref, ffn_far)
    put_rows(0, ffn)
    dispatch(0, rows_put, rows_got, row_sems)
    dispatch(1, grads_put, grads_got, grad_sems)
    keep = [full[name] for name in EARLY]
    keep += [normed_ref, query_ref, key_ref, value_ref, lse_ref, attended_ref, mixed_ref, cot_far, meta_far]
    for index, ref in enumerate(keep):
        pltpu.make_async_copy(ref, saved[index], save_sem.at[index]).start()
    early_out("sd")
    pass_early("su")
    settle_early(("sg", "su"))
    settle_own(("sd",))
    shared_ref[...] = jnp.zeros_like(shared_ref)
    ffn_grad_ref[...] = jnp.zeros_like(ffn_grad_ref)

    why = shard // 2

    def shared_block(block, carry):
        cut = pl.ds(pl.multiple_of((block + 2 * why) % 4 * 512, 512), 512)
        normed = ffn_ref[...]
        gate, up, down = full["sg"][:, cut], full["su"][:, cut], full["sd"][cut, :]
        pre, lin = dense_product(normed, gate), dense_product(normed, up)
        middle = (jax.nn.silu(pre) * lin).astype(jnp.bfloat16)
        shared_ref[...] += dense_product(middle, down)
        pre_grad, lin_grad = swiglu_back(product_t(cot_ref[...], down), pre, lin)
        ffn_grad_ref[...] += product_t(pre_grad, gate) + product_t(lin_grad, up)
        full["sg"][:, cut] = t_product(normed, pre_grad).astype(jnp.bfloat16)
        full["su"][:, cut] = t_product(normed, lin_grad).astype(jnp.bfloat16)
        full["sd"][cut, :] = t_product(middle, cot_ref[...]).astype(jnp.bfloat16)
        return carry

    core = shard % 2
    shared_grads = (full["sg"], full["su"], full["sd"])

    def halved(index, turn):
        ref, rows, columns = shared_grads[index], shared_grads[index].shape[0] // 4, shared_grads[index].shape[1]
        part = why if turn == 0 else 1 - why
        picked = (pl.ds(0, rows),)
        if index < 2:
            picked += (pl.ds(pl.multiple_of(part * (columns // 2), 128), columns // 2),)
        for y_of in (part,) if index == 2 else (0, 1):
            far_rows, near_rows = [pl.ds((y_of * 2 + of) * rows, rows) for of in (1 - core, core)]
            at = (y_of,) + picked
            place_of = 2 * turn if index == 2 else 2 * turn + y_of
            yield (
                ref.at[(far_rows,) + picked[1:]],
                shared_core[index].at[at],
                ref.at[(near_rows,) + picked[1:]],
                shared_work[index].at[at],
                place_of,
            )

    def share(part):
        for index in range(3):
            for away, landing, _, _, at in halved(index, part):
                send(away, landing, share_send.at[index, at], share_recv.at[index, at], core_peer)

    def take_share(part):
        for index in range(3):
            for away, landing, near, target, at in halved(index, part):
                wait_for(landing, share_recv.at[index, at])
                add_rows(target, near, landing)
                wait_for(away, share_send.at[index, at])

    cuts = full["sg"].shape[1] // 512
    lax.fori_loop(0, cuts // 2, shared_block, 0)
    share(0)
    pass_early("sd")
    settle_early_far("sd")
    lax.fori_loop(cuts // 2, cuts, shared_block, 0)
    wait_for(place(LATE[0], other), y_recv.at[number[LATE[0]]])
    to_core(LATE[0], 0)
    share(1)
    settle_far(2, ffn_far)
    put_rows(1, ffn_far[...])
    dispatch(1, rows_put, rows_got, row_sems)
    take_share(0)

    for name in LATE[1:]:
        wait_for(place(name, other), y_recv.at[number[name]])
        to_core(name, 0)

    for name in DIRECT:
        wait_for(own[name], y_send.at[number[name]])
    settle_own(LATE)
    for name in LATE:
        wait_for(own[name], y_send.at[number[name]])
        settle_core(name, 0)
    take_share(1)
    settle_dispatch(grads_put, grads_got, grad_sems)
    settle_dispatch(rows_put, rows_got, row_sems)
    for index, ref in enumerate(keep):
        wait_for(ref, save_sem.at[index])


def as_column(row):
    shape = (row.shape[1], row.shape[1])
    same = lax.broadcasted_iota(jnp.int32, shape, 0) == lax.broadcasted_iota(jnp.int32, shape, 1)
    return jnp.sum(jnp.where(same, row, 0.0), axis=1, keepdims=True)


def as_row(column):
    shape = (column.shape[0], column.shape[0])
    same = lax.broadcasted_iota(jnp.int32, shape, 0) == lax.broadcasted_iota(jnp.int32, shape, 1)
    return jnp.sum(jnp.where(same, column, 0.0), axis=0, keepdims=True)


def gate_pair(first, second):
    top = jnp.maximum(first, second)
    first, second = jnp.exp(first - top), jnp.exp(second - top)
    total = first + second
    return first / total, second / total


def allowed_mask(query_start, key_start, query_segment, key_segment, key_padding):
    shape = (query_segment.shape[0], key_segment.shape[1])
    query_at = query_start + lax.broadcasted_iota(jnp.int32, shape, 0)
    key_at = key_start + lax.broadcasted_iota(jnp.int32, shape, 1)
    distance = query_at - key_at
    return (
        (query_segment == key_segment)
        & (distance >= 0)
        & (distance < WINDOW)
        & ((key_padding == 1) | (distance == 0))
    )


def first_part(hidden, gains, dense, experts, segment, padding, cotangent, meta):
    tokens, width = hidden.shape
    bfloat, single = jnp.bfloat16, jnp.float32
    wq, wk, wv, wo, sg, su, sd = dense
    blocks = dict(hid=hidden, gains=jnp.pad(gains, ((0, 14), (0, 0))), wq=wq, wk=wk, wv=wv, wo=wo, sg=sg, su=su, sd=sd)
    blocks.update(zip(LATE, experts[:2]))
    blocks = [blocks[name] for name in NAMES]
    count = len(NAMES)
    cosine, sine = rotary_tables(4 * tokens, width // HEADS)
    in_hbm, in_vmem = pl.BlockSpec(memory_space=pl.ANY), pl.BlockSpec(memory_space=pltpu.VMEM)
    dma = pltpu.SemaphoreType.DMA
    shape = jax.ShapeDtypeStruct
    whole = {name: shape((4 * block.shape[0], block.shape[1]), block.dtype) for name, block in zip(NAMES, blocks)}
    middle = sg.shape[1]
    capacity = max(2, 2 * tokens * TOP // 8)
    routed = (8, capacity, width)
    halved = [(2,) + block.shape for block in (sg, su, sd)]
    inner = [
        shape((4 * tokens, width), bfloat),
        shape((tokens, width), bfloat),
        shape((4 * tokens, width), bfloat),
        shape((4 * tokens, width), bfloat),
        shape((HEADS, tokens, 1), single),
        shape((tokens, width), bfloat),
        shape((tokens, width), single),
        shape((tokens, width), bfloat),
    ]
    out = pl.pallas_call(
        first_kernel,
        out_shape=[whole[name] for name in LATE]
        + [whole[name] for name in EARLY]
        + inner[:7]
        + [
            shape((tokens, width), bfloat),
            shape((8, tokens), single),
            shape((16, width), single),
            shape(routed, bfloat),
            shape(routed, bfloat),
            shape((tokens, width), single),
            shape((tokens, width), single),
        ]
        + [shape(one, bfloat) for one in halved],
        in_specs=[in_vmem] * (count + 6),
        out_specs=[in_hbm] * (len(LATE) + SAVED) + [in_vmem] + [in_hbm] * 2 + [in_vmem] * 5,
        scratch_shapes=[pltpu.VMEM(whole[name].shape, whole[name].dtype) for name in PASSING]
        + [pltpu.VMEM(one.shape, one.dtype) for one in inner]
        + [pltpu.VMEM(one, bfloat) for one in halved]
        + [pltpu.VMEM(routed, bfloat)] * 2
        + [
            dma((count,)),
            dma((count,)),
            dma((count,)),
            dma((count,)),
            dma((count,)),
            dma((count, 3)),
            dma((count, 3)),
        ]
        + [dma((8,))] * 4
        + [dma((3, 4))] * 2
        + [
            dma((SAVED,)),
            dma((3,)),
            dma((3,)),
            pltpu.VMEM((2, 8, tokens), single),
            pltpu.VMEM((8, tokens), single),
            pltpu.VMEM((tokens, width), bfloat),
            pltpu.VMEM((tokens, width), bfloat),
        ],
        compiler_params=pltpu.CompilerParams(collective_id=0, has_side_effects=True, vmem_limit_bytes=60 << 20),
        cost_estimate=pl.CostEstimate(flops=15000000000, bytes_accessed=47000000, transcendentals=3000000),
    )(
        *blocks,
        segment[None, :],
        padding[None, :],
        jnp.asarray(cosine),
        jnp.asarray(sine),
        cotangent,
        meta,
    )
    return dict(zip(LATE + EARLY, out)), out[len(LATE + EARLY) :]


def add_into(target, first, second):
    rows = first.shape[-2]
    strip = math.gcd(rows, 64)

    def body(index, carry):
        at = pl.ds(pl.multiple_of(index * strip, strip), strip)
        for lead in range(first.shape[0]):
            total = first[lead, at, :].astype(jnp.float32) + second[lead, at, :].astype(jnp.float32)
            target[lead, at, :] = total.astype(target.dtype)
        return carry

    lax.fori_loop(0, rows // strip, body, 0)


class PlaneSum:
    def __init__(self, shape, work, receive, send_sem, recv_sem, bits, peers, order, out=None, done=0):
        self.work, self.receive, self.out = work, receive, out
        self.send_sem, self.recv_sem, self.bits, self.peers, self.order = send_sem, recv_sem, bits, peers, order
        self.at = [(0, size) for size in shape]
        self.inside = [0, 0, 0]
        self.trail = []
        for step in range(done):
            self.narrow(step)
        self.inside = [0, 0, 0]
        self.step = done

    def region(self, ref, starts, sizes):
        starts = [
            start if isinstance(start, int) or unit == 1 else pl.multiple_of(start, unit)
            for start, unit in zip(starts, (1, 16, 128))
        ]
        return ref.at[tuple(pl.ds(start, size) for start, size in zip(starts, sizes))]

    def working(self, bit_of):
        axis, dim = self.order[self.step]
        starts, sizes = list(self.inside), [size for _, size in self.at]
        sizes[dim] //= 2
        starts[dim] = starts[dim] + bit_of(self.bits[axis]) * sizes[dim]
        return self.region(self.work, starts, sizes)

    def final(self, at):
        return self.region(self.out, [0] + [start for start, _ in at[1:]], [1] + [size for _, size in at[1:]])

    def narrow(self, step):
        axis, dim = self.order[step]
        if axis != "y":
            self.trail.append((step, self.at))
        (start, size), self.at = self.at[dim], list(self.at)
        self.at[dim] = (start + self.bits[axis] * (size // 2), size // 2)
        self.inside[dim] = self.inside[dim] + self.bits[axis] * (size // 2)

    def start(self):
        step = self.step
        peer = self.peers[self.order[step][0]]
        send(self.working(lambda bit: 1 - bit), self.receive[step], self.send_sem.at[step], self.recv_sem.at[step], peer)

    def finish(self, target=None):
        step = self.step
        wait_for(self.receive[step], self.recv_sem.at[step])
        kept, gone = self.working(lambda bit: bit), self.working(lambda bit: 1 - bit)
        self.narrow(step)
        if step == len(self.order) - 1:
            target = self.final(self.at)
        add_into(kept if target is None else target, kept, self.receive[step])
        wait_for(gone, self.send_sem.at[step])
        self.step = step + 1

    def back_start(self):
        step, _ = self.trail[-1]
        part, at = self.final(self.at), self.step
        send(part, part, self.send_sem.at[at], self.recv_sem.at[at], self.peers[self.order[step][0]])

    def back_finish(self):
        step, whole = self.trail.pop()
        wait_for(self.final(self.at), self.send_sem.at[self.step])
        dim = self.order[step][1]
        start, size = self.at[dim]
        other = list(self.at)
        other[dim] = (2 * whole[dim][0] + size - start, size)
        wait_for(self.final(other), self.recv_sem.at[self.step])
        self.at = list(self.at)
        self.at[dim] = whole[dim]
        self.step += 1

    def advance(self):
        if self.step < len(self.order):
            self.finish()
        else:
            self.back_finish()
        if self.step < len(self.order):
            self.start()
        elif self.trail:
            self.back_start()


def receive_shapes(shape, order):
    result, shape = [], list(shape)
    for _, dim in order:
        shape[dim] //= 2
        result.append(tuple(shape))
    return result


def ordered(axes, dims):
    return tuple((axis, 0 if axis == "y" else dims[axis]) for axis in axes)


BY_COLUMNS, BY_ROWS = dict(x=2, z1=2, z2=2), dict(x=1, z1=1, z2=1)
BY_BOTH = dict(x=2, z1=1, z2=1)
SHARED_ORDER = (
    ordered(("y", "x", "z1", "z2"), BY_COLUMNS),
    ordered(("x", "y", "z1", "z2"), BY_COLUMNS),
    ordered(("z1", "y", "x", "z2"), BY_ROWS),
)
SHARED_DONE = 2
ATTENTION_ORDER = (
    ordered(("z1", "x", "y", "z2"), BY_BOTH),
    ordered(("y", "x", "z1", "z2"), BY_BOTH),
    ordered(("x", "y", "z1", "z2"), BY_BOTH),
    ordered(("x", "z1", "y", "z2"), BY_BOTH),
)


def plane_places():
    expert, shard = (lax.axis_index("expert"), lax.axis_index("shard"))
    zed, ex, why, core = (expert // 2, expert % 2, shard // 2, shard % 2)
    bits = {"x": ex, "z1": zed % 2, "z2": zed // 2, "y": why}
    peers = {
        "x": (expert + 1 - 2 * ex, shard),
        "z1": (expert + 2 - 4 * (zed % 2), shard),
        "z2": ((expert + 4) % 8, shard),
        "y": (expert, (shard + 2) % 4),
        "core": (expert, shard + 1 - 2 * core),
    }
    return expert, shard, zed, core, bits, peers


def enter(peers):
    barrier = pltpu.get_barrier_semaphore()
    for peer in peers:
        pl.semaphore_signal(barrier, inc=1, device_id=peer, device_id_type=MESH)
    pl.semaphore_wait(barrier, len(peers))


def second_kernel(*refs):
    rows_ref, grads_ref, meta_far, *weights_in, down_own = refs[:6]
    shared_in = refs[6:9]
    rows_back, grads_back, grads_far = refs[9:12]
    expert_core, shared_out = refs[12:15], refs[15:18]
    weights, shared_work = refs[18:21], refs[21:24]
    rows_put, grads_put, middle_ref, pre_ref, lin_ref, out_sum, grad_sum, far_put = refs[24:32]
    refs = refs[32:]
    receive = [refs[SHARED_DONE * index : SHARED_DONE * (index + 1)] for index in range(3)]
    refs = refs[3 * SHARED_DONE :]
    load_sem, shared_sem, out_send, out_recv, grad_send, grad_recv, core_send, core_recv, sum_send, sum_recv, far_send, far_recv, down_send, down_recv = refs
    expert, shard, zed, core, bits, peers = plane_places()
    def down_rows(slot):
        rows = down_own.shape[0]
        return weights[2].at[pl.ds(slot * rows, rows)]

    why = bits["y"]
    other, beside = (shard + 2) % 4, shard + 1 - 2 * core
    for index in range(2):
        pltpu.make_async_copy(weights_in[index], weights[index], load_sem.at[index]).start()
    for index in range(3):
        pltpu.make_async_copy(shared_in[index], shared_work[index], shared_sem.at[index]).start()
    pltpu.make_async_copy(down_own, down_rows(shard), load_sem.at[2]).start()
    enter((peers["y"], peers["core"]) + tuple(((expert + step) % 8, shard) for step in range(1, 8)))
    send(down_own, down_rows(shard), down_send.at[0], down_recv.at[0], peers["y"])
    send(down_own, down_rows(shard), down_send.at[1], down_recv.at[1], peers["core"])
    sums = [
        PlaneSum(
            shared_work[index].shape,
            shared_work[index],
            receive[index],
            sum_send.at[index],
            sum_recv.at[index],
            bits,
            peers,
            SHARED_ORDER[index],
        )
        for index in range(3)
    ]
    for index in range(3):
        pltpu.make_async_copy(shared_in[index], shared_work[index], shared_sem.at[index]).wait()
        sums[index].start()
    for index in range(2):
        pltpu.make_async_copy(weights_in[index], weights[index], load_sem.at[index]).wait()

    _, capacity, width = rows_ref.shape
    gate_ref, up_ref, down_ref = weights
    middle = gate_ref.shape[1]
    cuts = middle // 512

    half, in_half = expert // 4, expert % 4
    lot = 4 * capacity

    def hidden_units(index, carry):
        cut = pl.ds(pl.multiple_of(index * 512, 512), 512)
        rows = rows_ref[...].reshape(2 * lot, width)
        pre, lin = dense_product(rows, gate_ref[:, cut]), dense_product(rows, up_ref[:, cut])
        middle_ref[:, cut] = (jax.nn.silu(pre) * lin).astype(jnp.bfloat16)
        pre_ref[:, cut] = pre.astype(jnp.bfloat16)
        lin_ref[:, cut] = lin.astype(jnp.bfloat16)
        return carry

    def block(of_half, between=None):
        lots, here = pl.ds(4 * of_half, 4), pl.ds(pl.multiple_of(of_half * lot, lot), lot)
        grads = grads_ref[lots].reshape(lot, width)
        out_sum[...] = jnp.zeros_like(out_sum)
        grad_sum[...] = jnp.zeros_like(grad_sum)

        def body(index, carry):
            cut = pl.ds(pl.multiple_of((index + 2 * why) % 4 * 512, 512), 512)
            gate, up, down = gate_ref[:, cut], up_ref[:, cut], down_ref[cut, :]
            pre, lin = pre_ref[here, cut].astype(jnp.float32), lin_ref[here, cut].astype(jnp.float32)
            pre_grad, lin_grad = swiglu_back(product_t(grads, down), pre, lin)
            grad_sum[...] += product_t(pre_grad, gate) + product_t(lin_grad, up)
            out_sum[...] += dense_product(middle_ref[here, cut], down)
            pre_ref[here, cut] = pre_grad
            lin_ref[here, cut] = lin_grad
            return carry

        if between is None:
            lax.fori_loop(0, cuts, body, 0)
        else:
            lax.fori_loop(0, cuts // 2, body, 0)
            between()
            lax.fori_loop(cuts // 2, cuts, body, 0)
        rows_put[lots] = out_sum[...].astype(jnp.bfloat16).reshape(4, capacity, width)
        grads_put[lots] = grad_sum[...].astype(jnp.bfloat16).reshape(4, capacity, width)
        give_back(of_half, grads_put, grads_back, grad_send, grad_recv)
        give_back(of_half, rows_put, rows_back, out_send, out_recv)

    def give_back(of_half, put, back, send_sem, recv_sem):
        slot = 4 * ((of_half + half) % 2) + in_half
        for step in range(1, 4):
            there = (in_half + step) % 4
            source = 4 * of_half + there
            send(put.at[source], back.at[slot], send_sem.at[source], recv_sem.at[slot], (4 * half + there, shard))
        back[pl.ds(slot, 1)] = put[pl.ds(4 * of_half + in_half, 1)]

    def settle_back(put, back, send_sem, recv_sem, far):
        for step in range(1, 4):
            there = (in_half + step) % 4
            source = (4 * half + there + 4 * far) % 8
            wait_for(put.at[source], send_sem.at[source])
            wait_for(back.at[4 * far + there], recv_sem.at[4 * far + there])

    lax.fori_loop(0, cuts, hidden_units, 0)
    wait_for(down_rows(shard), load_sem.at[2])
    wait_for(down_rows(beside), down_recv.at[1])

    def rest_of_down():
        wait_for(down_rows(other), down_recv.at[0])
        send(down_rows(other), down_rows(other), down_send.at[2], down_recv.at[2], peers["core"])
        wait_for(down_rows((beside + 2) % 4), down_recv.at[2])

    block(1 - half, rest_of_down)
    for one in sums:
        one.advance()
    block(half)
    settle_back(grads_put, grads_back, grad_send, grad_recv, 1)
    taken = slots_in_half(meta_far[...], half, capacity)
    slot_at = lax.broadcasted_iota(jnp.int32, (taken[0].shape[0], 4 * capacity), 1)
    chosen = ((slot_at == taken[0]) | (slot_at == taken[1])).astype(jnp.bfloat16)
    far_put[...] = dense_product(chosen, grads_back[4:8].reshape(4 * capacity, width)).astype(jnp.bfloat16)
    send(far_put, grads_far, far_send, far_recv, ((expert + 4) % 8, shard))
    for index, ref in enumerate((down_rows(shard), down_rows(shard), down_rows(other))):
        wait_for(ref, down_send.at[index])

    rows_all, grads_all = rows_ref, grads_ref

    def weight_grad(index):
        def body(step, carry):
            cut = pl.ds(pl.multiple_of(step * 512, 512), 512)
            if index == 2:
                left, right = middle_ref[:, cut], grads_all[...].reshape(8 * capacity, width)
                down_ref[cut, :] = t_product(left, right).astype(jnp.bfloat16)
            else:
                left, right = rows_all[...].reshape(8 * capacity, width), (pre_ref, lin_ref)[index][:, cut]
                weights[index][:, cut] = t_product(left, right).astype(jnp.bfloat16)
            return carry

        lax.fori_loop(0, cuts, body, 0)

    def shard_rows(index, y_of, core_of):
        rows = weights[index].shape[0] // 4
        return weights[index].at[pl.ds((y_of * 2 + core_of) * rows, rows)]

    def core_start(index):
        for y_of in range(2):
            send(
                shard_rows(index, y_of, 1 - core),
                expert_core[index].at[y_of],
                core_send.at[index, y_of],
                core_recv.at[index, y_of],
                peers["core"],
            )

    def core_finish(index):
        for y_of in range(2):
            wait_for(expert_core[index].at[y_of], core_recv.at[index, y_of])
            wait_for(shard_rows(index, y_of, 1 - core), core_send.at[index, y_of])
        for y_of in range(2):
            kept = shard_rows(index, y_of, core)
            add_rows(expert_core[index].at[y_of], kept, expert_core[index].at[y_of])

    weight_grad(0)
    core_start(0)
    weight_grad(1)
    core_start(1)
    core_finish(0)
    for one, target in zip(sums, shared_out):
        one.finish(target)
    weight_grad(2)
    core_start(2)
    core_finish(1)
    settle_back(grads_put, grads_back, grad_send, grad_recv, 0)
    for far in range(2):
        settle_back(rows_put, rows_back, out_send, out_recv, far)
    wait_for(far_put, far_send)
    wait_for(grads_far, far_recv)
    core_finish(2)


def slots_in_half(meta, half, capacity):
    tokens = meta.shape[1]
    expert_at = lax.broadcasted_iota(jnp.int32, (tokens, 128), 1)
    choices = [as_column(meta[k : k + 1]).astype(jnp.int32) for k in range(TOP)]
    named = ((choices[0] == expert_at) | (choices[1] == expert_at)).astype(jnp.bfloat16)
    row_at = lax.broadcasted_iota(jnp.int32, (tokens, tokens), 0)
    before = lax.broadcasted_iota(jnp.int32, (tokens, tokens), 1) < row_at
    rank = dense_product(before.astype(jnp.bfloat16), named).astype(jnp.int32)
    slot = rank + (expert_at - 4 * half) * capacity
    columns = [jnp.sum(jnp.where(choice == expert_at, slot, 0).astype(jnp.float32), axis=1, keepdims=True) for choice in choices]
    return [jnp.where(choice // 4 == half, column.astype(jnp.int32), -1) for choice, column in zip(choices, columns)]


def add_rows(target, first, second):
    def body(index, carry):
        at = pl.ds(pl.multiple_of(index * 64, 64), 64)
        target[at, :] = (first[at, :].astype(jnp.float32) + second[at, :].astype(jnp.float32)).astype(target.dtype)
        return carry

    lax.fori_loop(0, first.shape[0] // 64, body, 0)


def second_part(rows, grads, meta_far, weights, shared):
    in_hbm, in_vmem = pl.BlockSpec(memory_space=pl.ANY), pl.BlockSpec(memory_space=pltpu.VMEM)
    dma, bfloat = pltpu.SemaphoreType.DMA, jnp.bfloat16
    shape = jax.ShapeDtypeStruct
    count, capacity, width = rows.shape
    middle = weights[0].shape[1]
    down_own = weights[2]
    whole = [weights[0].shape, weights[1].shape, (4 * down_own.shape[0], down_own.shape[1])]
    quarter = [(one[0] // 4, one[1]) for one in whole]
    steps = [receive_shapes(work.shape, order)[:SHARED_DONE] for work, order in zip(shared, SHARED_ORDER)]
    blocks = (count * capacity, middle)
    return pl.pallas_call(
        second_kernel,
        out_shape=[shape(rows.shape, bfloat)] * 2
        + [shape((meta_far.shape[1], width), bfloat)]
        + [shape((2,) + one, bfloat) for one in quarter]
        + [shape(one[-1], bfloat) for one in steps],
        in_specs=[in_vmem] * 3 + [in_hbm] * 6,
        out_specs=[in_vmem] * 9,
        scratch_shapes=[pltpu.VMEM(one, bfloat) for one in whole]
        + [pltpu.VMEM(work.shape, bfloat) for work in shared]
        + [pltpu.VMEM(rows.shape, bfloat)] * 2
        + [pltpu.VMEM(blocks, bfloat)] * 3
        + [pltpu.VMEM((4 * capacity, width), jnp.float32)] * 2
        + [pltpu.VMEM((meta_far.shape[1], width), bfloat)]
        + [pltpu.VMEM(one, bfloat) for group in steps for one in group]
        + [dma((3,)), dma((3,))]
        + [dma((8,))] * 4
        + [dma((3, 2)), dma((3, 2)), dma((3, SHARED_DONE)), dma((3, SHARED_DONE)), dma(()), dma(()), dma((3,)), dma((3,))],
        compiler_params=pltpu.CompilerParams(collective_id=1, has_side_effects=True, vmem_limit_bytes=62 << 20),
        cost_estimate=pl.CostEstimate(flops=29000000000, bytes_accessed=30000000, transcendentals=2000000),
    )(rows, grads, meta_far, *weights, *shared)


STORED = 15


def third_kernel(*refs):
    rows_back, grads_back, grads_far, mixed_ref, shared_ref, ffn_grad_ref, cot_ref, hidden_ref, gain_ref, meta_ref = refs[:10]
    segment_row, padding_row, cot_far, meta_far = refs[10:14]
    stored, left_over = refs[14 : 14 + STORED], refs[14 + STORED : 17 + STORED]
    output_ref, input_grad_ref, logit_grad_ref, gain_out = refs[32:36]
    sums_out, shared_out, expert_out = refs[36:40], refs[40:43], refs[43:46]
    query_grad, key_grad, value_grad, context_grad, attended_grad, mixed_grad_ref = refs[46:52]
    weight_grads, weight_work = refs[52:56], refs[56:60]
    context_core, context_y, far_got = refs[60:63]
    expert_y = refs[63:66]
    refs = refs[66:]
    receive = [refs[4 * index : 4 * index + 4] for index in range(4)]
    refs = refs[16:]
    rest = 4 - SHARED_DONE
    shared_receive = [(None,) * SHARED_DONE + refs[rest * index : rest * index + rest] for index in range(3)]
    refs = refs[3 * rest :]
    loaded, left_mine = refs[:STORED], refs[STORED : STORED + 3]
    wo_ref, attended_ref, cosine_ref, sine_ref, query_ref, key_ref, value_ref, lse_ref, normed_ref, wk_ref, wv_ref, wq_ref = loaded[3:]
    shared_work = loaded[:3]
    refs = refs[STORED + 3 :]
    gain_parts, gain_recv = refs[:2]
    core_send, core_recv, sum_send, sum_recv, share_send, share_recv, ctx_send, ctx_recv, gain_send, gain_got, late_send, late_recv, load_sem, left_sem, far_put, part_put, part_got = refs[2:]
    expert, shard, zed, core, bits, peers = plane_places()
    why = bits["y"]
    for index in range(STORED):
        pltpu.make_async_copy(stored[index], loaded[index], load_sem.at[index]).start()
    enter(tuple(peers[axis] for axis in ("core", "y", "x", "z1", "z2")))
    def send_left(index):
        send(left_over[index].at[1 - why], expert_y[index], ctx_send.at[3 + index], ctx_recv.at[3 + index], peers["y"])

    send_left(0)
    send_left(1)
    for index in range(3):
        pltpu.make_async_copy(left_over[index].at[why], left_mine[index], left_sem.at[index]).start()
    shared_sums = [
        PlaneSum(
            (2,) + shared_out[index].shape[1:],
            shared_work[index],
            shared_receive[index],
            share_send.at[index],
            share_recv.at[index],
            bits,
            peers,
            SHARED_ORDER[index],
            shared_out[index],
            SHARED_DONE,
        )
        for index in range(3)
    ]
    for index, one in enumerate(shared_sums):
        wait_for(loaded[index], load_sem.at[index])
        one.start()
    tokens, width = hidden_ref.shape
    here = pl.ds(pl.multiple_of(shard * tokens, tokens), tokens)
    single, bfloat = jnp.float32, jnp.bfloat16

    half, capacity = expert // 4, rows_back.shape[1]
    slots = 4 * capacity
    slot_at = lax.broadcasted_iota(jnp.int32, (tokens, slots), 1)
    slots_taken = slots_in_half(meta_ref[...], half, capacity)
    grad_out = cot_ref[...].astype(single)
    mixed = mixed_ref[...]
    picks = (slot_at == slots_taken[0]) | (slot_at == slots_taken[1])
    ffn_grad = ffn_grad_ref[...] + dense_product(picks.astype(bfloat), grads_back[0:4].reshape(slots, width))
    ffn_grad = ffn_grad + grads_far[...].astype(single)
    scale_second = rms_scale(mixed)
    gain_parts[0] = jnp.zeros_like(gain_parts[0])
    gain_parts[0, 1:2, :] = jnp.sum(ffn_grad * mixed * scale_second, axis=0, keepdims=True)
    scaled = ffn_grad * gain_ref[1:2, :]
    mixed_grad = (
        grad_out
        + scale_second * scaled
        - mixed * (scale_second * scale_second * scale_second) * jnp.mean(scaled * mixed, axis=-1, keepdims=True)
    )
    mixed_grad_ref[...] = mixed_grad
    mixed_low = mixed_grad.astype(bfloat)
    for index in range(3, 5):
        wait_for(loaded[index], load_sem.at[index])
    attended_grad[...] = product_t(mixed_low, wo_ref[...]).astype(bfloat)

    def shard_rows(ref, y_of, core_of):
        rows = ref.shape[0] // 4
        return ref.at[pl.ds((y_of * 2 + core_of) * rows, rows)]

    def core_start(index):
        for y_of in range(2):
            send(
                shard_rows(weight_grads[index], y_of, 1 - core),
                weight_work[index].at[y_of],
                core_send.at[index, y_of],
                core_recv.at[index, y_of],
                peers["core"],
            )

    def core_finish(index):
        for y_of in range(2):
            wait_for(weight_work[index].at[y_of], core_recv.at[index, y_of])
            wait_for(shard_rows(weight_grads[index], y_of, 1 - core), core_send.at[index, y_of])
            add_rows(weight_work[index].at[y_of], shard_rows(weight_grads[index], y_of, core), weight_work[index].at[y_of])

    sums = [
        PlaneSum(
            weight_work[index].shape,
            weight_work[index],
            receive[index],
            sum_send.at[index],
            sum_recv.at[index],
            bits,
            peers,
            ATTENTION_ORDER[index],
            sums_out[index],
        )
        for index in range(4)
    ]
    weight_grads[3][...] = t_product(attended_ref[...], mixed_low).astype(bfloat)
    core_start(3)

    for index in range(5, STORED):
        wait_for(loaded[index], load_sem.at[index])

    own_segment = as_column(segment_row[:, here].astype(single)).astype(jnp.int32)

    def head_pair(pair, carry):
        lanes = pl.ds(pl.multiple_of(pair * 128, 128), 128)
        query, keys, values, grads = query_ref[:, lanes], key_ref[:, lanes], value_ref[:, lanes], attended_grad[:, lanes]
        allowed = allowed_mask(shard * tokens, 0, own_segment, segment_row[...], padding_row[...])
        lane = lax.broadcasted_iota(jnp.int32, query.shape, 1)
        from_keys = []
        key_total = value_total = None
        for half in range(2):
            chosen = (lane >= 64) if half else (lane < 64)
            one_query = jnp.where(chosen, query, jnp.zeros_like(query))
            one_grad = jnp.where(chosen, grads, jnp.zeros_like(grads))
            scores = jnp.where(allowed, product_t(one_query, keys) * 0.125, neg_fill)
            probs = jnp.exp(scores - lse_ref[2 * pair + half])
            probs_grad = product_t(one_grad, values)
            delta = jnp.sum(probs * probs_grad, axis=1, keepdims=True)
            scores_grad = (probs * (probs_grad - delta)).astype(bfloat)
            from_keys.append(dense_product(scores_grad, keys))
            key_part = t_product(scores_grad, one_query)
            value_part = t_product(probs.astype(bfloat), one_grad)
            key_total = key_part if key_total is None else key_total + key_part
            value_total = value_part if value_total is None else value_total + value_part
        back = jnp.where(lane < 64, from_keys[0], from_keys[1]) * 0.125
        query_grad[:, lanes] = rotate_pair(back, cosine_ref[here, :], -sine_ref[here, :]).astype(bfloat)
        key_grad[:, lanes] = rotate_pair(key_total * 0.125, cosine_ref[...], -sine_ref[...]).astype(bfloat)
        value_grad[:, lanes] = value_total.astype(bfloat)
        return carry

    def group_grads(group):
        cut = slice(256 * group, 256 * group + 256)
        weight_grads[group][:, 0:256] = t_product(normed_ref[here, :], query_grad[:, cut]).astype(bfloat)
        weight_grads[group][:, 256:512] = t_product(normed_ref[...], key_grad[:, cut]).astype(bfloat)
        weight_grads[group][:, 512:768] = t_product(normed_ref[...], value_grad[:, cut]).astype(bfloat)
        core_start(group)

    def from_experts(block, taken, meta, grads):
        gates = [as_column(gate) for gate in gate_pair(meta[2:3], meta[3:4])]
        results = rows_back[4 * block : 4 * block + 4].reshape(slots, width)
        per_route = [dense_product((slot_at == slot).astype(bfloat), results) for slot in taken]
        routed = gates[0] * per_route[0] + gates[1] * per_route[1]
        return routed, [as_row(jnp.sum(rows * grads, axis=1, keepdims=True)) for rows in per_route]

    def serve_far():
        meta = meta_far[...]
        routed, contrib = from_experts(1, slots_in_half(meta, half, capacity), meta, cot_far[...].astype(single))
        far_put[...] = routed.astype(bfloat)
        part_put[...] = jnp.zeros_like(part_put)
        for k in range(TOP):
            part_put[k : k + 1, :] = contrib[k]
        send(far_put, far_got, late_send.at[0], late_recv.at[0], peers["z2"])
        send(part_put, part_got, late_send.at[1], late_recv.at[1], peers["z2"])

    def combine():
        meta = meta_ref[...]
        routed, contrib = from_experts(0, slots_taken, meta, grad_out)
        wait_for(far_got, late_recv.at[0])
        wait_for(part_got, late_recv.at[1])
        output_ref[...] = (mixed_ref[...] + shared_ref[...] + routed + far_got[...].astype(single)).astype(bfloat)
        gates = gate_pair(meta[2:3], meta[3:4])
        contrib = [contrib[k] + part_got[k : k + 1, :] for k in range(TOP)]
        mean_contrib = gates[0] * contrib[0] + gates[1] * contrib[1]
        for k in range(TOP):
            logit_grad_ref[k : k + 1, :] = gates[k] * (contrib[k] - mean_contrib)

    gate_sum, up_sum, down_sum = shared_sums
    first, second, third, out_sum = sums

    def take(*items):
        for one in items:
            if one.step < len(one.order) or one.trail:
                one.advance()

    lax.fori_loop(0, 2, head_pair, 0)
    take(gate_sum, up_sum, down_sum)
    core_finish(3)
    out_sum.start()
    group_grads(0)
    lax.fori_loop(2, 4, head_pair, 0)
    core_finish(0)
    first.start()
    take(out_sum, gate_sum, up_sum, down_sum)
    serve_far()
    group_grads(1)
    lax.fori_loop(4, 6, head_pair, 0)
    core_finish(1)
    second.start()
    group_grads(2)

    def context_block(block, carry):
        rows = pl.ds(pl.multiple_of(block * tokens, tokens), tokens)
        total = product_t(key_grad[rows, :], wk_ref[...]) + product_t(value_grad[rows, :], wv_ref[...])
        context_grad[rows, :] = total.astype(bfloat)
        return carry

    lax.fori_loop(0, 4, context_block, 0)
    for y_of in range(2):
        send(
            shard_rows(context_grad, y_of, 1 - core),
            context_core.at[y_of],
            ctx_send.at[y_of],
            ctx_recv.at[y_of],
            peers["core"],
        )
    core_finish(2)
    third.start()
    for y_of in range(2):
        wait_for(context_core.at[y_of], ctx_recv.at[y_of])
        wait_for(shard_rows(context_grad, y_of, 1 - core), ctx_send.at[y_of])
        add_rows(context_core.at[y_of], shard_rows(context_grad, y_of, core), context_core.at[y_of])
    send(context_core.at[1 - why], context_y, ctx_send.at[2], ctx_recv.at[2], peers["y"])
    normed_grad = product_t(query_grad[...], wq_ref[...])
    take(first, out_sum, gate_sum, up_sum)
    take(down_sum, third, second, first, out_sum)
    wait_for(context_y, ctx_recv.at[2])
    wait_for(context_core.at[1 - why], ctx_send.at[2])
    normed_grad = normed_grad + context_core[pl.ds(why, 1)].reshape(tokens, width).astype(single) + context_y[...].astype(single)
    rows_in = hidden_ref[...].astype(single)
    scale_first = rms_scale(rows_in)
    gain_parts[0, 0:1, :] = jnp.sum(normed_grad * rows_in * scale_first, axis=0, keepdims=True)

    def gain_start(step):
        peer = peers[("core", "y", "x", "z1", "z2")[step]]
        send(gain_parts.at[step], gain_recv.at[step], gain_send.at[step], gain_got.at[step], peer)

    def gain_finish(step):
        wait_for(gain_recv.at[step], gain_got.at[step])
        gain_parts[step + 1] = gain_parts[step] + gain_recv[step]

    gain_start(0)
    scaled = normed_grad * gain_ref[0:1, :]
    input_grad_ref[...] = (
        mixed_grad_ref[...]
        + scale_first * scaled
        - rows_in * (scale_first * scale_first * scale_first) * jnp.mean(scaled * rows_in, axis=-1, keepdims=True)
    )
    everything = (third, second, first, out_sum, gate_sum, up_sum, down_sum)
    for step in range(5):
        gain_finish(step)
        if step < 4:
            gain_start(step + 1)
        take(*everything)
        if step == 0:
            send_left(2)
        if step == 0:
            combine()
    left = [third, second, first, out_sum, gate_sum, up_sum, down_sum]
    while any(one.trail for one in left):
        take(*[one for one in left if one.trail])
    wait_for(far_put, late_send.at[0])
    wait_for(part_put, late_send.at[1])
    for index in range(3):
        wait_for(expert_y[index], ctx_recv.at[3 + index])
        wait_for(left_mine[index], left_sem.at[index])
        add_rows(expert_out[index], left_mine[index], expert_y[index])
        wait_for(left_over[index].at[1 - why], ctx_send.at[3 + index])
    gain_out[...] = gain_parts[5]
    for step in range(5):
        wait_for(gain_parts.at[step], gain_send.at[step])


def third_part(back, mixed, shared_out, ffn_grad, cotangent, hidden, gains, meta, kept, segment, padding, weights, left_over, shared, far, shared_own):
    tokens, width = hidden.shape
    bfloat, single = jnp.bfloat16, jnp.float32
    in_vmem = pl.BlockSpec(memory_space=pltpu.VMEM)
    dma, shape, vmem = pltpu.SemaphoreType.DMA, jax.ShapeDtypeStruct, pltpu.VMEM
    cosine, sine = rotary_tables(4 * tokens, width // HEADS)
    work = (2, width // 4, width)
    normed, query, keys, values, lse, attended = kept
    wq, wk, wv, wo = weights
    cosine, sine = jnp.asarray(cosine), jnp.asarray(sine)
    stored = (*shared, wo, attended, cosine, sine, query, keys, values, lse, normed, wk, wv, wq)
    arguments = (
        *back,
        mixed,
        shared_out,
        ffn_grad,
        cotangent,
        hidden,
        gains,
        meta,
        segment[None, :],
        padding[None, :],
        *far,
        *stored,
        *left_over,
    )
    in_hbm = pl.BlockSpec(memory_space=pl.ANY)
    return pl.pallas_call(
        third_kernel,
        out_shape=[
            shape((tokens, width), bfloat),
            shape((tokens, width), single),
            shape((TOP, tokens), single),
            shape((8, width), single),
        ]
        + [shape((1,) + work[1:], bfloat)] * 4
        + [shape((1,) + one, bfloat) for one in shared_own]
        + [shape(one.shape[1:], bfloat) for one in left_over],
        in_specs=[in_vmem] * 14 + [in_hbm] * (STORED + 3),
        out_specs=[in_vmem] * 14,
        scratch_shapes=[vmem((tokens, width), bfloat)]
        + [vmem((4 * tokens, width), bfloat)] * 3
        + [vmem((tokens, width), bfloat), vmem((tokens, width), single)]
        + [vmem((width, width), bfloat)] * 4
        + [vmem(work, bfloat)] * 4
        + [vmem((2, tokens, width), bfloat), vmem((tokens, width), bfloat), vmem((tokens, width), bfloat)]
        + [vmem(one.shape[1:], bfloat) for one in left_over]
        + [vmem(one, bfloat) for order in ATTENTION_ORDER for one in receive_shapes(work, order)]
        + [
            vmem(one, bfloat)
            for own, order in zip(shared_own, SHARED_ORDER)
            for one in receive_shapes((2,) + own, order)[SHARED_DONE:]
        ]
        + [vmem(one.shape, one.dtype) for one in stored]
        + [vmem(one.shape[1:], bfloat) for one in left_over]
        + [vmem((6, 8, width), single), vmem((5, 8, width), single)]
        + [dma((4, 2)), dma((4, 2)), dma((4, 7)), dma((4, 7)), dma((3, 7)), dma((3, 7)), dma((6,)), dma((6,)), dma((5,)), dma((5,)), dma((2,)), dma((2,)), dma((STORED,)), dma((3,))]
        + [vmem((tokens, width), bfloat), vmem((8, tokens), single), vmem((8, tokens), single)],
        compiler_params=pltpu.CompilerParams(collective_id=2, has_side_effects=True, vmem_limit_bytes=60 << 20),
        cost_estimate=pl.CostEstimate(flops=12000000000, bytes_accessed=25000000, transcendentals=3000000),
    )(*arguments)


def last_kernel(*refs):
    groups, rest_in, output_in, input_grad_in = refs[:3], refs[3:10], refs[10], refs[11]
    heads_out, rest_out, output_ref, input_grad_ref = refs[12:15], refs[15:22], refs[22], refs[23]
    for kind, target in enumerate(heads_out):
        for index, group in enumerate(groups):
            target[:, 256 * index : 256 * index + 256] = group[0, :, 256 * kind : 256 * kind + 256].astype(jnp.float32)
    for source, target in zip(rest_in, rest_out):
        target[...] = source[...].reshape(target.shape).astype(jnp.float32)
    output_ref[...] = output_in[...].reshape(output_ref.shape)
    input_grad_ref[...] = input_grad_in[...].reshape(input_grad_ref.shape)


def last_part(attention, shared, experts, output, input_grad):
    steps = 4
    inputs = [*attention, *shared, *experts, output, input_grad]

    def spec(shape):
        if len(shape) == 3:
            return pl.BlockSpec((1, shape[1] // steps, shape[2]), lambda step: (0, step, 0))
        return pl.BlockSpec((shape[0] // steps, shape[1]), lambda step: (step, 0))

    shapes = [one.shape[1:] for one in (attention[0], *attention[:3], *shared)]
    shapes = [shapes[0]] * 4 + shapes[4:] + [(1,) + one.shape for one in experts]
    out_shape = [jax.ShapeDtypeStruct(one, jnp.float32) for one in shapes]
    out_shape += [jax.ShapeDtypeStruct((1,) + one.shape, one.dtype) for one in (output, input_grad)]
    return pl.pallas_call(
        last_kernel,
        grid=(steps,),
        out_shape=out_shape,
        in_specs=[spec(one.shape) for one in inputs],
        out_specs=[spec(one.shape) for one in out_shape],
        compiler_params=pltpu.CompilerParams(vmem_limit_bytes=62 << 20),
    )(*inputs)


def swap(value, axis, bit):
    size = lax.axis_size(axis)
    return lax.ppermute(value, axis, [(index, index ^ bit) for index in range(size)])


def halves(value, bit_set, dim):
    half = value.shape[dim] // 2
    keep = lax.dynamic_slice_in_dim(value, bit_set * half, half, dim)
    give = lax.dynamic_slice_in_dim(value, (1 - bit_set) * half, half, dim)
    return keep, give


def fold(value, axis, bit, dim):
    bit_set = (lax.axis_index(axis) // bit) % 2
    keep, give = halves(value, bit_set, dim)
    return (keep.astype(jnp.float32) + swap(give.astype(jnp.bfloat16), axis, bit).astype(jnp.float32)).astype(jnp.bfloat16)


def unfold(value, axis, bit, dim):
    bit_set = (lax.axis_index(axis) // bit) % 2
    come = swap(value, axis, bit)
    return jnp.where(bit_set == 0, jnp.concatenate([value, come], dim), jnp.concatenate([come, value], dim))


def bits_of(axis):
    size = lax.axis_size(axis)
    return [1 << place for place in range(size.bit_length() - 1)]


def scatter_shards(value):
    count = lax.axis_size("shard")
    blocks = value.reshape((count // 2, 2, value.shape[0] // count) + value.shape[1:])
    blocks = fold(blocks, "shard", 1, 1)[:, 0]
    for bit in reversed(bits_of("shard")[1:]):
        blocks = fold(blocks, "shard", bit, 0)
    return blocks[0]


def sum_plane(value, dim):
    bits = bits_of("expert")
    for bit in bits:
        value = fold(value, "expert", bit, dim)
    for bit in reversed(bits):
        value = unfold(value, "expert", bit, dim)
    return value.astype(jnp.float32)


def shards(
    hidden_in,
    gain_attn,
    gain_ffn,
    w_query,
    w_key,
    w_value,
    w_out,
    shared_gate,
    shared_up,
    shared_down,
    expert_gate,
    expert_up,
    expert_down,
    gate_logits,
    routes,
    segment,
    padding,
    cotangent,
):
    bfloat = jnp.bfloat16
    tokens = hidden_in.shape[1]
    model_width = hidden_in.shape[2]
    head_size = model_width // HEADS
    experts = lax.axis_size("expert")
    capacity = max(2, 2 * tokens * TOP // experts)
    shard_count = lax.axis_size("shard")
    shard_index = lax.axis_index("shard")
    score_scale = head_size ** (-0.5)
    head_shape = (tokens, HEADS, head_size)
    fast = (experts, shard_count, WINDOW) == (8, 4, 4 * tokens)
    dense_own = (w_query, w_key, w_value, w_out, shared_gate, shared_up, shared_down)
    expert_own = (expert_gate[0], expert_up[0], expert_down[0])
    rows_in = hidden_in[0].astype(jnp.float32)
    scale_first = rms_scale(rows_in)
    positions = shard_index * tokens + jnp.arange(tokens, dtype=jnp.int32)
    segment_row, padding_row = segment[0], padding[0]
    query_segment = lax.dynamic_slice_in_dim(segment_row, shard_index * tokens, tokens)
    if fast:
        gain_own = lax.dynamic_update_slice(
            jnp.zeros((2, model_width), bfloat),
            jnp.stack([gain_attn, gain_ffn]),
            (0, shard_index * gain_attn.shape[0]),
        )
        meta = [routes[0].T.astype(jnp.float32), gate_logits[0].T, jnp.zeros((8 - 2 * TOP, tokens), jnp.float32)]
        meta = jnp.concatenate(meta, axis=0)
        full, rest = first_part(
            hidden_in[0],
            gain_own,
            dense_own,
            expert_own,
            segment_row,
            padding_row,
            cotangent[0],
            meta,
        )
        normed_ctx, query_low, keys_ctx, values_ctx, log_total, attended, mixed_rows = rest[:7]
        cot_far, meta_far, gains, received, grad_received, shared_out, ffn_grad_shared, *shared_work = rest[7:]
        normed_ffn = None
        gain_first, gain_second = gains[0], gains[1]
        w_q, w_k, w_v, w_o = (full[name] for name in ("wq", "wk", "wv", "wo"))
        e_gate, e_up = (full[name] for name in LATE)
        reach, key_start = shard_count - 1, 0
        key_segment, key_padding = segment_row, padding_row
        key_positions = jnp.arange(4 * tokens, dtype=jnp.int32)
        allowed = allowed_mask(shard_index * tokens, 0, query_segment[:, None], key_segment[None], key_padding[None])
    else:
        gather = functools.partial(lax.all_gather, axis_name="shard", tiled=True)
        w_q, w_k, w_v, w_o, s_gate, s_up, s_down = (gather(weight) for weight in dense_own)
        e_gate, e_up, e_down = (gather(weight) for weight in expert_own)
        gain_first, gain_second = (gather(gain).astype(jnp.float32) for gain in (gain_attn, gain_ffn))
        reach = min((WINDOW + tokens - 2) // tokens, shard_count - 1)
        lead_rows, key_rows = reach * tokens, (reach + 1) * tokens
        context = [from_behind(hidden_in[0], "shard", offset) for offset in range(reach, 0, -1)] + [hidden_in[0]]
        context = jnp.concatenate(context, axis=0).astype(jnp.float32)
        normed_ctx = (context * rms_scale(context) * gain_first).astype(bfloat)
        key_positions = (shard_index - reach) * tokens + jnp.arange(key_rows, dtype=jnp.int32)
        query_low = rotate(
            dense_product(normed_ctx[lead_rows:], w_q).reshape(head_shape), positions, 1.0
        ).astype(bfloat)
        keys_ctx = rotate(
            dense_product(normed_ctx, w_k).reshape(key_rows, HEADS, head_size), key_positions, 1.0
        ).astype(bfloat)
        values_ctx = dense_product(normed_ctx, w_v).astype(bfloat)
        segment_ext = jnp.concatenate([jnp.full((lead_rows,), -1, jnp.int32), segment_row])
        padding_ext = jnp.concatenate([jnp.zeros((lead_rows,), jnp.int32), padding_row])
        key_segment = lax.dynamic_slice_in_dim(segment_ext, shard_index * tokens, key_rows)
        key_padding = lax.dynamic_slice_in_dim(padding_ext, shard_index * tokens, key_rows)
        allowed = allowed_mask(
            shard_index * tokens,
            (shard_index - reach) * tokens,
            query_segment[:, None],
            key_segment[None],
            key_padding[None],
        )
    key_rows = (reach + 1) * tokens
    query_heads = query_low.reshape(head_shape)
    keys_all = keys_ctx.reshape(key_rows, HEADS, head_size)
    values_all = values_ctx.reshape(key_rows, HEADS, head_size)

    def score_block():
        raw_scores = (
            jnp.einsum("qhd,khd->hqk", query_heads, keys_all, preferred_element_type=jnp.float32)
            * score_scale
        )
        return jnp.where(allowed[None], raw_scores, neg_fill)

    if not fast:
        scores = score_block()
        top_score = jnp.max(scores, axis=-1, keepdims=True)
        exponent = jnp.exp(scores - top_score)
        exp_total = jnp.sum(exponent, axis=-1, keepdims=True)
        log_total = top_score + jnp.log(exp_total)
        attended = (
            jnp.einsum(
                "hqk,khd->qhd",
                (exponent / exp_total).astype(bfloat),
                values_all,
                preferred_element_type=jnp.float32,
            )
            .astype(bfloat)
            .reshape(tokens, model_width)
        )
        mixed_rows = rows_in + dense_product(attended, w_o)
        normed_ffn = (mixed_rows * rms_scale(mixed_rows) * gain_second).astype(bfloat)
    scale_second = rms_scale(mixed_rows)
    grad_low = cotangent[0]
    grad_out = grad_low.astype(jnp.float32)
    gate_probs = jax.nn.softmax(gate_logits[0], axis=-1)
    route_flat = routes[0].reshape(-1)
    route_total = tokens * TOP
    onehot = (route_flat[:, None] == jnp.arange(experts, dtype=jnp.int32)[None, :]).astype(
        jnp.int32
    )
    slot_rank = jnp.sum((jnp.cumsum(onehot, axis=0) - onehot) * onehot, axis=1)
    places = route_flat * capacity + slot_rank
    if not fast:
        shared_pre = dense_product(normed_ffn, s_gate)
        shared_lin = dense_product(normed_ffn, s_up)
        shared_mid = (jax.nn.silu(shared_pre) * shared_lin).astype(bfloat)
        shared_out = dense_product(shared_mid, s_down)
        grad_shared_mid = product_t(grad_low, s_down)
        grad_shared_pre, grad_shared_lin = swiglu_back(grad_shared_mid, shared_pre, shared_lin)
        shared_down_grad = dense_product(shared_mid.T, grad_low)
        shared_gate_grad = dense_product(normed_ffn.T, grad_shared_pre)
        shared_up_grad = dense_product(normed_ffn.T, grad_shared_lin)
        ffn_grad_shared = product_t(grad_shared_pre, s_gate) + product_t(grad_shared_lin, s_up)
        slot_table = (
            jnp.full((experts * capacity,), route_total, dtype=jnp.int32)
            .at[places]
            .set(jnp.arange(route_total, dtype=jnp.int32))
        )
        padded_rows = jnp.concatenate([normed_ffn, jnp.zeros((1, model_width), bfloat)], axis=0)
        send_rows = padded_rows[slot_table // TOP].reshape(experts, capacity, model_width)
        received = lax.all_to_all(send_rows, "expert", split_axis=0, concat_axis=0, tiled=True)
        route_grad = (
            (gate_probs[:, :, None] * grad_out[:, None, :])
            .astype(bfloat)
            .reshape(route_total, model_width)
        )
        route_padded = jnp.concatenate([route_grad, jnp.zeros((1, model_width), bfloat)], axis=0)
        send_grad = route_padded[slot_table].reshape(experts, capacity, model_width)
        grad_received = lax.all_to_all(send_grad, "expert", split_axis=0, concat_axis=0, tiled=True)
    if fast:
        results = second_part(received, grad_received, meta_far, (e_gate, e_up, expert_own[2]), shared_work)
        back, left_over, shared_work = results[:3], results[3:6], results[6:]
        output, input_grad, logit_grad, gain_grads, *sums = third_part(
            back,
            mixed_rows,
            shared_out,
            ffn_grad_shared,
            grad_low,
            hidden_in[0],
            gains,
            meta,
            (normed_ctx, query_low, keys_ctx, values_ctx, log_total, attended),
            segment_row,
            padding_row,
            (w_q, w_k, w_v, w_o),
            left_over,
            shared_work,
            (cot_far, meta_far),
            (shared_gate.shape, shared_up.shape, shared_down.shape),
        )
        *grads, output, input_grad = last_part(sums[:4], sums[4:7], sums[7:], output, input_grad)
        gain_grads = lax.dynamic_slice_in_dim(gain_grads, shard_index * gain_attn.shape[0], gain_attn.shape[0], 1)
        return (output, input_grad, logit_grad.T[None], gain_grads[0], gain_grads[1], *grads)
    else:
        gate_pre = jnp.einsum("sid,df->sif", received, e_gate, preferred_element_type=jnp.float32)
        up_pre = jnp.einsum("sid,df->sif", received, e_up, preferred_element_type=jnp.float32)
        middle = (jax.nn.silu(gate_pre) * up_pre).astype(bfloat)
        result = jnp.einsum("sif,fd->sid", middle, e_down, preferred_element_type=jnp.float32).astype(bfloat)
        returned = lax.all_to_all(result, "expert", split_axis=0, concat_axis=0, tiled=True)
        grad_middle = jnp.einsum(
            "sid,fd->sif", grad_received, e_down, preferred_element_type=jnp.float32
        )
        grad_gate_pre, grad_up_pre = swiglu_back(grad_middle, gate_pre, up_pre)
        expert_down_grad = jnp.einsum(
            "sif,sid->fd", middle, grad_received, preferred_element_type=jnp.float32
        )
        expert_gate_grad = jnp.einsum(
            "sid,sif->df", received, grad_gate_pre, preferred_element_type=jnp.float32
        )
        expert_up_grad = jnp.einsum(
            "sid,sif->df", received, grad_up_pre, preferred_element_type=jnp.float32
        )
        grad_rows = (
            jnp.einsum("sif,df->sid", grad_gate_pre, e_gate, preferred_element_type=jnp.float32)
            + jnp.einsum("sif,df->sid", grad_up_pre, e_up, preferred_element_type=jnp.float32)
        ).astype(bfloat)
        grad_back = lax.all_to_all(grad_rows, "expert", split_axis=0, concat_axis=0, tiled=True)
        expert_grads = tuple(
            scatter_shards(grad.astype(bfloat))[None].astype(jnp.float32)
            for grad in (expert_gate_grad, expert_up_grad, expert_down_grad)
        )
        shared_grads = (
            sum_plane(scatter_shards(shared_gate_grad.astype(bfloat)), 1),
            sum_plane(scatter_shards(shared_up_grad.astype(bfloat)), 1),
            sum_plane(scatter_shards(shared_down_grad.astype(bfloat)), 0),
        )
    per_route = (
        returned.reshape(experts * capacity, model_width)[places]
        .astype(jnp.float32)
        .reshape(tokens, TOP, model_width)
    )
    routed = jnp.sum(gate_probs[:, :, None] * per_route, axis=1)
    output = (mixed_rows + shared_out + routed).astype(bfloat)
    contrib = jnp.sum(per_route * grad_out[:, None, :], axis=-1)
    logit_grad = gate_probs * (contrib - jnp.sum(gate_probs * contrib, axis=-1, keepdims=True))
    grad_routes = (
        grad_back.reshape(experts * capacity, model_width)[places]
        .astype(jnp.float32)
        .reshape(tokens, TOP, model_width)
    )
    grad_normed_ffn = jnp.sum(grad_routes, axis=1) + ffn_grad_shared
    gain_ffn_grad = jnp.sum(grad_normed_ffn * mixed_rows * scale_second, axis=0)
    scaled_second = grad_normed_ffn * gain_second
    grad_mixed = (
        grad_out
        + scale_second * scaled_second
        - mixed_rows
        * scale_second**3
        * jnp.mean(scaled_second * mixed_rows, axis=-1, keepdims=True)
    )
    grad_mixed_low = grad_mixed.astype(bfloat)
    w_out_grad = dense_product(attended.T, grad_mixed_low)
    grad_attended = product_t(grad_mixed_low, w_o).astype(bfloat).reshape(head_shape)
    attn_probs = jnp.exp(score_block() - log_total)
    grad_probs = jnp.einsum(
        "qhd,khd->hqk", grad_attended, values_all, preferred_element_type=jnp.float32
    )
    delta_rows = jnp.sum(attn_probs * grad_probs, axis=-1, keepdims=True)
    grad_scores = (attn_probs * (grad_probs - delta_rows)).astype(bfloat)
    grad_query = (
        jnp.einsum("hqk,khd->qhd", grad_scores, keys_all, preferred_element_type=jnp.float32)
        * score_scale
    )
    grad_keys = (
        jnp.einsum("hqk,qhd->khd", grad_scores, query_heads, preferred_element_type=jnp.float32)
        * score_scale
    )
    grad_values = jnp.einsum(
        "hqk,qhd->khd", attn_probs.astype(bfloat), grad_attended, preferred_element_type=jnp.float32
    )
    grad_query_low = rotate(grad_query, positions, -1.0).astype(bfloat).reshape(tokens, model_width)
    grad_key_low = rotate(grad_keys, key_positions, -1.0).astype(bfloat).reshape(key_rows, model_width)
    grad_value_low = grad_values.astype(bfloat).reshape(key_rows, model_width)
    if fast:
        normed = lax.dynamic_slice_in_dim(normed_ctx, shard_index * tokens, tokens)
    else:
        normed = normed_ctx[reach * tokens :]
    w_query_grad = dense_product(normed.T, grad_query_low)
    w_key_grad = dense_product(normed_ctx.T, grad_key_low)
    w_value_grad = dense_product(normed_ctx.T, grad_value_low)
    grad_context = product_t(grad_key_low, w_k) + product_t(grad_value_low, w_v)
    grad_normed = product_t(grad_query_low, w_q)
    if fast:
        grad_normed = grad_normed + scatter_shards(grad_context.astype(bfloat)).astype(jnp.float32)
    else:
        grad_normed = grad_normed + grad_context[reach * tokens :]
        for offset in range(1, reach + 1):
            sent = grad_context[(reach - offset) * tokens :][:tokens].astype(bfloat)
            grad_normed = grad_normed + from_behind(sent, "shard", -offset).astype(jnp.float32)
    gain_attn_grad = jnp.sum(grad_normed * rows_in * scale_first, axis=0)
    scaled_first = grad_normed * gain_first
    input_grad = (
        grad_mixed
        + scale_first * scaled_first
        - rows_in * scale_first**3 * jnp.mean(scaled_first * rows_in, axis=-1, keepdims=True)
    )
    gain_rows = jnp.stack([gain_attn_grad, gain_ffn_grad], axis=1).astype(bfloat)
    gain_total = lax.psum(scatter_shards(gain_rows), "expert").astype(jnp.float32)
    attn_grads = jnp.stack([w_query_grad, w_key_grad, w_value_grad, w_out_grad]).astype(bfloat)
    attn_rows = scatter_shards(attn_grads.transpose(1, 0, 2)).transpose(1, 0, 2)
    attn_total = sum_plane(attn_rows.reshape(-1, model_width), 0).reshape(attn_rows.shape)
    return (
        output[None],
        input_grad[None],
        logit_grad[None],
        gain_total[:, 0],
        gain_total[:, 1],
        attn_total[0],
        attn_total[1],
        attn_total[2],
        attn_total[3],
        shared_grads[0],
        shared_grads[1],
        shared_grads[2],
        expert_grads[0],
        expert_grads[1],
        expert_grads[2],
    )


def solution(mesh):
    placed = (
        P("expert", "shard", None),
        P("shard"),
        P("shard"),
        P("shard", None),
        P("shard", None),
        P("shard", None),
        P("shard", None),
        P("shard", None),
        P("shard", None),
        P("shard", None),
        P("expert", "shard", None),
        P("expert", "shard", None),
        P("expert", "shard", None),
        P("expert", "shard", None),
        P("expert", "shard", None),
        P("expert", None),
        P("expert", None),
        P("expert", "shard", None),
    )
    return jax.shard_map(
        shards,
        mesh=mesh,
        in_specs=placed,
        out_specs=(
            P("expert", "shard", None),
            P("expert", "shard", None),
            P("expert", "shard", None),
            P("shard"),
            P("shard"),
            P("shard", None),
            P("shard", None),
            P("shard", None),
            P("shard", None),
            P("shard", None),
            P("shard", None),
            P("shard", None),
            P("expert", "shard", None),
            P("expert", "shard", None),
            P("expert", "shard", None),
        ),
        check_vma=False,
    )
```
